32 devices in a mesh: dp: 8 (over z, x), seq: 4 (over y, core).
Axes of the slice: x: 2, y: 2, z: 4, core: 2. Of those that a mesh axis runs over, the one named last changes fastest.
Arguments:
- inputs: bfloat16 [4, 8, 2048, 384], P(None, 'dp', 'seq'), may hold values from -6 to 6
- cotangent: bfloat16 [4, 8, 2048, 384], P(None, 'dp', 'seq'), may hold values from -6 to 6
- counts: int32 [8], P('dp'), may hold values from 2 to 4
- lead_steps: int32 [8, 4], P('dp'), may hold values from 0 to 15
- emb_table: bfloat16 [16, 384], replicated, may hold values from -6 to 6
- w_ada: bfloat16 [384, 2304], replicated, may hold values from -0.3125 to 0.3125
- b_ada: bfloat16 [2304], replicated, may hold values from -3 to 3
- w_qkv: bfloat16 [384, 1152], replicated, may hold values from -0.3125 to 0.3125
- w_out: bfloat16 [384, 384], replicated, may hold values from -1.25 to 1.25
- w_fc1: bfloat16 [384, 1536], replicated, may hold values from -0.3125 to 0.3125
- w_fc2: bfloat16 [1536, 384], replicated, may hold values from -0.15625 to 0.15625
Outputs:
- outputs: bfloat16 [4, 8, 2048, 384], P(None, 'dp', 'seq')
- grad_inputs: bfloat16 [4, 8, 2048, 384], P(None, 'dp', 'seq')
- grad_emb: float32 [16, 384], replicated
- grad_ada: float32 [384, 2304], replicated
- grad_bada: float32 [2304], replicated
- grad_qkv: float32 [384, 1152], replicated
- grad_out: float32 [384, 384], replicated
- grad_fc1: float32 [384, 1536], replicated
- grad_fc2: float32 [1536, 384], replicated
The draws below stay inside these ranges and needn't reach their ends.
Inputs may be any that keep to these rules, and one draw needn't show every extreme that they name: The step s of item i takes part when s < counts[i].
All inputs are finite; a program needn't handle non-finite values.
Results may differ from the reference program's by a relative error of at most 0.015.
The reference program's roundings to bfloat16 on the way count: a program that leaves them out, or rounds other values in their place, can miss the bound.
Values may be sent and summed in bfloat16 or wider, within the bound.
A program may use at most 256 MiB of HBM per device.

```python
import jax
import jax.numpy as jnp
from jax import lax

H = 6
HD = 64
D = 384
FF = 1536
NLEAD = 16
SLOTS = 4
LEN = 2048
ITEMS = 8


def with_ends(values, stream_key, low, largest):
    extent = values.shape
    spot = [jax.random.randint(jax.random.fold_in(stream_key, axis), (), 0, extent[axis]) for axis in range(len(extent))]
    values = values.at[tuple(spot)].set(low)
    longest = extent.index(max(extent))
    spot[longest] = (spot[longest] + 1) % extent[longest]
    return values.at[tuple(spot)].set(largest)


def block_levels(own_key, dims, split, least, top_value):
    def one(dim, blocks):
        draws = jax.random.uniform(jax.random.fold_in(jax.random.fold_in(own_key, 6), dim), (blocks,), jnp.float32, least / len(split), top_value / len(split))
        return jnp.repeat(jnp.exp(draws), dims[dim] // blocks).reshape((-1,) + (1,) * (len(dims) - dim - 1))

    factor_of = one(*split[0])
    for cut in split[1:]:
        factor_of = factor_of * one(*cut)
    return factor_of


def scatter_about(rng, extent, scale, limit, cuts=(), kind=jnp.bfloat16):
    entries = jax.random.normal(rng, extent, jnp.float32) * scale
    if len(cuts) > 0:
        entries = block_levels(rng, extent, cuts, -0.22, 0.18) * entries
    return jnp.clip(entries, min=-limit, max=limit).astype(kind)


def setup_inputs(seed: int = 0) -> dict:
    seeds = jax.random.split(jax.random.key(seed), 12)
    inputs = scatter_about(seeds[0], (SLOTS, ITEMS, LEN, D), 1.0, 6.0, ((1, 8), (2, 4)))
    cotangent = scatter_about(seeds[1], (SLOTS, ITEMS, LEN, D), 1.0, 6.0, ((1, 8), (2, 4)))
    counts = with_ends(jax.random.randint(seeds[2], (ITEMS,), 2, 5), jax.random.fold_in(seeds[2], 1), 2, 4).astype(jnp.int32)
    lead_steps = with_ends(jax.random.randint(seeds[3], (ITEMS, SLOTS), 0, NLEAD), jax.random.fold_in(seeds[3], 1), 0, NLEAD - 1).astype(jnp.int32)
    emb_table = scatter_about(seeds[4], (NLEAD, D), 1.0, 6.0)
    w_ada = scatter_about(seeds[5], (D, 6 * D), D ** -0.5, 0.3125)
    b_ada = scatter_about(seeds[6], (6 * D,), 0.5, 3.0)
    w_qkv = scatter_about(seeds[7], (D, 3 * D), D ** -0.5, 0.3125)
    w_out = scatter_about(seeds[8], (D, D), (D // 16) ** -0.5, 1.25)
    w_fc1 = scatter_about(seeds[9], (D, FF), D ** -0.5, 0.3125)
    w_fc2 = scatter_about(seeds[10], (FF, D), FF ** -0.5, 0.15625)
    return {"inputs": inputs, "cotangent": cotangent, "counts": counts, "lead_steps": lead_steps, "emb_table": emb_table, "w_ada": w_ada, "b_ada": b_ada, "w_qkv": w_qkv, "w_out": w_out, "w_fc1": w_fc1, "w_fc2": w_fc2}


EPSILON = 1e-06
HIGHEST = lax.Precision.HIGHEST

@jax.custom_vjp
def low(v):
    return lax.optimization_barrier(v.astype(jnp.bfloat16)).astype(jnp.float32)

@jax.custom_vjp
def low_back(v):
    return v

def low_keep(v):
    return (low(v), None)

def low_pass(kept, grad):
    return (grad,)

def back_keep(v):
    return (v, None)

def back_low(kept, grad):
    return (low(grad),)
low.defvjp(low_keep, low_pass)
low_back.defvjp(back_keep, back_low)

def modulate(values, shift_rows, scale_rows):
    center = values - lax.optimization_barrier(jnp.mean(values, axis=-1, keepdims=True))
    spread = lax.optimization_barrier(jnp.mean(center * center, axis=-1, keepdims=True))
    return center * lax.rsqrt(spread + EPSILON) * (1.0 + scale_rows[:, None, :]) + shift_rows[:, None, :]

def attention(queries, keys, values):
    item_count, head_count, length, head_depth = queries.shape
    block_rows = min(512, length)
    blocks = length // block_rows
    factor = head_depth ** (-0.5)
    query_blocks = queries.reshape(item_count, head_count, blocks, block_rows, head_depth).transpose(2, 0, 1, 3, 4)

    def one_block(query_rows):
        scores = low_back(jnp.einsum('nhre,nhke->nhrk', query_rows, keys, precision=HIGHEST) * factor)
        weights = low(jax.nn.softmax(scores, axis=-1))
        return jnp.einsum('nhrk,nhke->nhre', weights, values, precision=HIGHEST)
    results = lax.map(jax.checkpoint(one_block), query_blocks)
    return results.transpose(1, 2, 0, 3, 4).reshape(item_count, head_count, length, head_depth)

def block(states, lead_rows, active, emb_table, w_ada, b_ada, w_qkv, w_out, w_fc1, w_fc2):
    item_count, length, width = states.shape
    onehot = (lead_rows[:, None] == jnp.arange(NLEAD, dtype=jnp.int32)[None, :]).astype(jnp.float32)
    condition = jnp.dot(onehot, emb_table, precision=HIGHEST)
    cond_act = low(jax.nn.silu(condition))
    modulation = low_back(jnp.dot(cond_act, w_ada, precision=HIGHEST) + b_ada).reshape(item_count, 6, width)
    normed_one = low(modulate(states, modulation[:, 0], modulation[:, 1]))
    projected = jnp.einsum('npd,dthe->tnhpe', normed_one, w_qkv.reshape(width, 3, H, HD), precision=HIGHEST)
    projected = low(low_back(projected))
    mixed = low(low_back(attention(projected[0], projected[1], projected[2])))
    branch_one = low_back(jnp.einsum('nhpe,hef->npf', mixed, w_out.reshape(H, HD, width), precision=HIGHEST))
    middle = states + modulation[:, 2][:, None, :] * branch_one
    normed_two = low(modulate(middle, modulation[:, 3], modulation[:, 4]))
    hidden_pre = low_back(jnp.einsum('npd,df->npf', normed_two, w_fc1, precision=HIGHEST))
    hidden = low(jax.nn.gelu(hidden_pre, approximate=False))
    branch_two = low_back(jnp.einsum('npf,fd->npd', hidden, w_fc2, precision=HIGHEST))
    final = middle + modulation[:, 5][:, None, :] * branch_two
    return final * active[:, None, None]

def reference(inputs, cotangent, counts, lead_steps, emb_table, w_ada, b_ada, w_qkv, w_out, w_fc1, w_fc2):
    group_size = 2
    total_steps = SLOTS * ITEMS
    group_count = total_steps // group_size
    states = inputs.astype(jnp.float32).reshape(group_count, group_size, LEN, D)
    grad_given = cotangent.astype(jnp.float32).reshape(group_count, group_size, LEN, D)
    lead_flat = lead_steps.T.reshape(group_count, group_size)
    active_flat = (jnp.arange(SLOTS, dtype=jnp.int32)[:, None] < counts[None, :]).astype(jnp.float32)
    active_flat = active_flat.reshape(group_count, group_size)
    params = (emb_table.astype(jnp.float32), w_ada.astype(jnp.float32), b_ada.astype(jnp.float32), w_qkv.astype(jnp.float32), w_out.astype(jnp.float32), w_fc1.astype(jnp.float32), w_fc2.astype(jnp.float32))

    def forward(all_states, table, ada_weight, ada_bias, qkv_weight, out_weight, fc1_weight, fc2_weight):

        def one_group(pieces):
            state_rows, lead_rows, active_rows = pieces
            return block(state_rows, lead_rows, active_rows, table, ada_weight, ada_bias, qkv_weight, out_weight, fc1_weight, fc2_weight)
        return lax.map(jax.checkpoint(one_group), (all_states, lead_flat, active_flat))
    result, backward = jax.vjp(forward, states, *params)
    grads = backward(grad_given)
    return (result.reshape(SLOTS, ITEMS, LEN, D).astype(jnp.bfloat16), grads[0].reshape(SLOTS, ITEMS, LEN, D).astype(jnp.bfloat16), grads[1], grads[2], grads[3], grads[4], grads[5], grads[6], grads[7])
```

```python
import functools

import jax
import jax.numpy as jnp
from jax import lax
from jax.experimental import pallas as pl
from jax.experimental.pallas import tpu as pltpu
from jax.sharding import PartitionSpec as P

HD = 64
LANES = 128
EPSILON = 1e-06
LOG2E = 1.4426950408889634
LN2 = 0.6931471805599453
NN = (((1,), (0,)), ((), ()))
NT = (((1,), (1,)), ((), ()))
TN = (((0,), (0,)), ((), ()))
F32 = jnp.float32
BF16 = jnp.bfloat16
VMEM_BYTES = 56 * 1024 * 1024


def dot(a, b, dims=NN):
    return lax.dot_general(a, b, dims, preferred_element_type=F32)


def call(body, name, grid, in_specs, out_specs, out_shape, scratch=(), flops=0, moved=0, exps=0):
    return pl.pallas_call(
        body,
        name=name,
        grid=grid,
        in_specs=in_specs,
        out_specs=out_specs,
        out_shape=out_shape,
        scratch_shapes=list(scratch),
        cost_estimate=pl.CostEstimate(flops=flops, bytes_accessed=moved, transcendentals=exps),
        compiler_params=pltpu.CompilerParams(vmem_limit_bytes=VMEM_BYTES),
    )


def whole(shape):
    return pl.BlockSpec(shape, lambda *_: (0,) * len(shape))


def scalars():
    return pl.BlockSpec(memory_space=pltpu.SMEM)


def lane_index(shape):
    return lax.broadcasted_iota(jnp.int32, shape, 1)


def normalize(values):
    center = values - jnp.mean(values, axis=-1, keepdims=True)
    spread = jnp.mean(center * center, axis=-1, keepdims=True)
    inverse = lax.rsqrt(spread + EPSILON)
    return center * inverse, inverse


def norm_back(grad, xhat, inverse):
    first = jnp.mean(grad, axis=-1, keepdims=True)
    second = jnp.mean(grad * xhat, axis=-1, keepdims=True)
    return inverse * (grad - first - xhat * second)


def pick(refs, which):
    value = refs[0][0]
    for index in range(1, len(refs)):
        value = jnp.where(which == index, refs[index][0], value)
    return value


def modulation_kernel(lead_ref, emb_ref, ada_ref, bias_ref, mod_ref):
    rows = lax.broadcasted_iota(jnp.int32, (16, emb_ref.shape[0]), 0)
    columns = lane_index((16, emb_ref.shape[0]))
    onehot = jnp.zeros((16, emb_ref.shape[0]), F32)
    for step in range(lead_ref.shape[0]):
        onehot = jnp.where((rows == step) & (columns == lead_ref[step]), 1.0, onehot)
    condition = dot(onehot.astype(BF16), emb_ref[...])
    active = (condition * jax.nn.sigmoid(condition)).astype(BF16)
    mod_ref[...] = dot(active, ada_ref[...]) + bias_ref[...].astype(F32)


def project_kernel(sources, queries, *refs):
    x_refs = refs[:sources]
    mod_ref, w_ref = refs[sources : sources + 2]
    outs = refs[sources + 2 :]
    step, which = pl.program_id(0), pl.program_id(1)
    width = w_ref.shape[0]
    x = pick(x_refs, which).astype(F32)
    shift = mod_ref[pl.ds(step, 1), 0:width]
    scale = mod_ref[pl.ds(step, 1), width : 2 * width]
    xhat, _ = normalize(x)
    normed = (xhat * (1.0 + scale) + shift).astype(BF16)
    outs[0][0, 0] = normed
    start = 0 if queries else width
    projected = dot(normed, w_ref[:, start:])
    for part in range(len(outs) - 1):
        for pair in range(width // LANES):
            at = part * width + pair * LANES
            piece = projected[:, at : at + LANES]
            if queries and part == 0:
                piece = piece * (HD**-0.5 * LOG2E)
            outs[part + 1][0, pair, 0] = piece.astype(BF16)


def with_ones(values):
    low = lane_index(values.shape) < HD
    one = jnp.ones_like(values)
    return jnp.where(low, values, one), jnp.where(low, one, values)


def masked(values):
    low = lane_index(values.shape) < HD
    zero = jnp.zeros_like(values)
    return jnp.where(low, values, zero), jnp.where(low, zero, values)


def attend_local_kernel(rows, q_ref, k_ref, v_ref, acc_ref, ext_ref):
    ext_ref[0], ext_ref[1] = with_ones(v_ref[0, 0])

    def block(index, carry):
        at = pl.ds(pl.multiple_of(index * rows, rows), rows)
        for head, query in enumerate(masked(q_ref[0, 0, at, :])):
            weights = jnp.exp2(dot(query, k_ref[0, 0], NT)).astype(BF16)
            acc_ref[0, 0, head, at, :] = dot(weights, ext_ref[head])
        return carry

    lax.fori_loop(0, q_ref.shape[2] // rows, block, 0)


def attend_all_kernel(
    rows, q_ref, k_ref, v_ref, kr_ref, vr_ref, acc_ref, o_ref, qe_ref, ext_ref, total_ref
):
    ext_ref[0], ext_ref[1] = with_ones(vr_ref[0, 0])
    blocks = q_ref.shape[2] // rows

    def finish(at, query, first, second, top_first, top_second):
        lane = lane_index(query.shape)
        low = lane < HD
        swapped = jnp.where(low, second, first)
        total = pltpu.roll(swapped, HD, 1)
        o_ref[0, 0, at, :] = jnp.where(low, first, second) / total
        log_total = jnp.log2(swapped) + jnp.where(low, top_second, top_first)
        high = log_total.astype(BF16).astype(F32)
        middle = (log_total - high).astype(BF16).astype(F32)
        rest = log_total - high - middle
        spot = lane % HD
        extra = jnp.where(spot == 0, -high, jnp.where(spot == 1, -middle, -rest))
        extra = jnp.where(spot < 3, extra, 0.0).astype(BF16)
        qe_ref[0, 0, 0, at, :] = jnp.where(low, query, extra)
        qe_ref[0, 0, 1, at, :] = jnp.where(low, extra, query)
        return total

    def block(index, carry):
        at = pl.ds(pl.multiple_of(index * rows, rows), rows)
        query = q_ref[0, 0, at, :]
        sums = []
        for head, own in enumerate(masked(query)):
            weights = jnp.exp2(dot(own, kr_ref[0, 0], NT)).astype(BF16)
            sums.append(acc_ref[0, 0, head, at, :] + dot(weights, ext_ref[head]))
        total_ref[at, :] = finish(at, query, sums[0], sums[1], 0.0, 0.0)
        return carry

    lax.fori_loop(0, blocks, block, 0)
    total = total_ref[...]
    bad = jnp.sum(jnp.where((total > 1e-25) & (total < 1e25), 0.0, 1.0))

    @pl.when(bad > 0.0)
    def _():
        own_ext = with_ones(v_ref[0, 0])

        def again(index, carry):
            at = pl.ds(pl.multiple_of(index * rows, rows), rows)
            query = q_ref[0, 0, at, :]
            sums, tops = [], []
            for head, own in enumerate(masked(query)):
                scores = dot(own, k_ref[0, 0], NT)
                others = dot(own, kr_ref[0, 0], NT)
                top = jnp.maximum(
                    jnp.max(scores, axis=-1, keepdims=True),
                    jnp.max(others, axis=-1, keepdims=True),
                )
                sums.append(
                    dot(jnp.exp2(scores - top).astype(BF16), own_ext[head])
                    + dot(jnp.exp2(others - top).astype(BF16), ext_ref[head])
                )
                tops.append(top)
            finish(at, query, sums[0], sums[1], tops[0], tops[1])
            return carry

        lax.fori_loop(0, blocks, again, 0)


def gelu_parts(values):
    cumulative = 0.5 * (1.0 + lax.erf(values * 0.7071067811865476))
    density = jnp.exp2(values * values * (-0.5 * LOG2E)) * 0.3989422804014327
    return values * cumulative, cumulative + values * density


def patch_kernel(
    rows,
    chunk,
    active_ref,
    own_x,
    sib_x,
    own_ct,
    sib_ct,
    mod_ref,
    o_ref,
    out_w,
    fc1_w,
    fc2_w,
    final_ref,
    gm_ref,
    ge_ref,
    sums_ref,
    gout_ref,
    gfc1_ref,
    gfc2_ref,
    hidden_s,
    gpre_s,
    n2_s,
    g2_s,
    g1_s,
    mixed_s,
    gout_s,
    gfc1_s,
    gfc2_s,
):
    step, half = pl.program_id(0), pl.program_id(1)
    width, hidden_width = fc1_w.shape
    patches = own_x.shape[1]
    active = active_ref[step]

    def piece(index):
        return mod_ref[pl.ds(step, 1), index * width : (index + 1) * width]

    gate1, shift2, scale2, gate2 = piece(2), piece(3), piece(4), piece(5)

    @pl.when(half == 0)
    def _():
        sums_ref[...] = jnp.zeros_like(sums_ref)

    @pl.when((step == 0) & (half == 0))
    def _():
        gout_s[...] = jnp.zeros_like(gout_s)
        gfc1_s[...] = jnp.zeros_like(gfc1_s)
        gfc2_s[...] = jnp.zeros_like(gfc2_s)

    def block(index, carry):
        at = pl.ds(pl.multiple_of(index * rows, rows), rows)
        x = jnp.where(half == 0, own_x[0, at, :], sib_x[0, at, :]).astype(F32)
        final_grad = jnp.where(half == 0, own_ct[0, at, :], sib_ct[0, at, :]).astype(F32) * active
        outs = [o_ref[0, pair, at, :] for pair in range(width // LANES)]
        mixed = jnp.concatenate([o.astype(BF16) for o in outs], axis=-1)
        mixed_s[at, :] = mixed
        branch_one = dot(mixed, out_w[...])
        middle = x + gate1 * branch_one
        xhat, inverse = normalize(middle)
        n2 = (xhat * (1.0 + scale2) + shift2).astype(BF16)
        n2_s[at, :] = n2
        g2 = (gate2 * final_grad).astype(BF16)
        g2_s[at, :] = g2
        branch_two = jnp.zeros((rows, width), F32)
        gy = jnp.zeros((rows, width), F32)
        for start in range(0, hidden_width, chunk):
            columns = slice(start, start + chunk)
            pre = dot(n2, fc1_w[:, columns])
            grad_hidden = dot(g2, fc2_w[columns, :], NT)
            hidden, slope = gelu_parts(pre)
            hidden = hidden.astype(BF16)
            grad_pre = (slope * grad_hidden).astype(BF16)
            hidden_s[at, columns] = hidden
            gpre_s[at, columns] = grad_pre
            branch_two += dot(hidden, fc2_w[columns, :])
            gy += dot(grad_pre, fc1_w[:, columns], NT)
        final_ref[0, 0, at, :] = ((middle + gate2 * branch_two) * active).astype(BF16)
        gm = final_grad + norm_back(gy * (1.0 + scale2), xhat, inverse)
        gm_ref[0, 0, at, :] = gm
        g1 = (gate1 * gm).astype(BF16)
        g1_s[at, :] = g1
        sums = [branch_one * gm, gy, gy * xhat, branch_two * final_grad]
        for row, value in enumerate(sums):
            sums_ref[0, row : row + 1, :] += jnp.sum(value, axis=0, keepdims=True)
        grad_mixed = dot(g1, out_w[...], NT).astype(BF16)
        lane = lane_index((rows, LANES))
        low = lane < HD
        spot = lane % HD
        for pair, o in enumerate(outs):
            grad = grad_mixed[:, pair * LANES : (pair + 1) * LANES]
            product = grad.astype(F32) * o
            first = jnp.sum(jnp.where(low, product, 0.0), axis=-1, keepdims=True)
            second = jnp.sum(jnp.where(low, 0.0, product), axis=-1, keepdims=True)
            inner = jnp.where(low, second, first)
            high = inner.astype(BF16).astype(F32)
            mid = (inner - high).astype(BF16).astype(F32)
            extra = jnp.where(spot == 0, -high, jnp.where(spot == 1, -mid, high + mid - inner))
            extra = jnp.where(spot < 3, extra, 0.0).astype(BF16)
            ge_ref[0, pair, 0, at, :] = jnp.where(low, grad, extra)
            ge_ref[0, pair, 1, at, :] = jnp.where(low, extra, grad)
        return carry

    lax.fori_loop(0, patches // rows, block, 0)
    gout_s[...] += dot(mixed_s[...], g1_s[...], TN)
    for start in range(0, hidden_width, chunk):
        columns = slice(start, start + chunk)
        gfc1_s[:, columns] += dot(n2_s[...], gpre_s[:, columns], TN)
        gfc2_s[:, columns] += dot(g2_s[...], hidden_s[:, columns], TN)

    @pl.when((step == pl.num_programs(0) - 1) & (half == pl.num_programs(1) - 1))
    def _():
        gout_ref[...] = gout_s[...].astype(BF16)
        gfc1_ref[...] = gfc1_s[...].astype(BF16)
        gfc2_ref[...] = gfc2_s[...].astype(BF16)


def attend_back_kernel(rows, first_pass, *refs):
    if first_pass:
        qe_ref, ge_ref, k_ref, v_ref, dq_ref, dk_ref, dv_ref, acc_s = refs
    else:
        qe_ref, ge_ref, k_ref, v_ref, dq_in, dq_ref, dk_ref, dv_ref, acc_s = refs
    if first_pass:
        acc_s[...] = jnp.zeros_like(acc_s)
    else:
        acc_s[...] = dq_in[0, 0]

    def block(index, carry):
        at = pl.ds(pl.multiple_of(index * rows, rows), rows)
        keys = k_ref[0, 0, at, :]
        values = v_ref[0, 0, at, :]
        lane = lane_index(keys.shape)
        low = lane < HD
        ones = jnp.where(lane % HD < 3, 1.0, 0.0).astype(BF16)
        zero = jnp.zeros_like(keys)
        grads = []
        for head in range(2):
            own = low if head == 0 else jnp.logical_not(low)
            query = qe_ref[0, 0, head]
            grad = ge_ref[0, 0, head]
            probs = jnp.exp2(dot(jnp.where(own, keys, ones), query, NT))
            grad_probs = dot(jnp.where(own, values, ones), grad, NT)
            grad_scores = (probs * grad_probs).astype(BF16)
            grads.append((dot(grad_scores, query), dot(probs.astype(BF16), grad)))
            acc_s[...] += dot(grad_scores, jnp.where(own, keys, zero), TN)
        dk_ref[0, 0, at, :] = (jnp.where(low, grads[0][0], grads[1][0]) * LN2).astype(BF16)
        dv_ref[0, 0, at, :] = jnp.where(low, grads[0][1], grads[1][1]).astype(BF16)
        return carry

    lax.fori_loop(0, k_ref.shape[2] // rows, block, 0)
    if first_pass:
        dq_ref[0, 0] = acc_s[...]
    else:
        dq_ref[0, 0] = (acc_s[...] * HD**-0.5).astype(BF16)


def project_back_kernel(parts, last, *refs):
    grads = refs[:parts]
    normed_ref, w_ref = refs[parts : parts + 2]
    rest = refs[parts + 2 :]
    if last:
        add_ref, dx_ref, gw_ref, gw_s = rest
    else:
        dx_ref, gw_ref, gw_s = rest
    step, which = pl.program_id(0), pl.program_id(1)
    width = w_ref.shape[0]
    start = w_ref.shape[1] - parts * width
    joined = jnp.concatenate(
        [ref[0, pair] for ref in grads for pair in range(ref.shape[1])], axis=-1
    )
    dx_ref[0, 0] = dot(joined, w_ref[:, start:], NT).astype(dx_ref.dtype)

    @pl.when((step == 0) & (which == 0))
    def _():
        gw_s[...] = jnp.zeros_like(gw_s)
        if last:
            gw_s[:, width:] = add_ref[...]

    gw_s[...] += dot(normed_ref[0, 0], joined, TN)

    @pl.when((step == pl.num_programs(0) - 1) & (which == pl.num_programs(1) - 1))
    def _():
        gw_ref[...] = gw_s[...].astype(gw_ref.dtype)


def finish_kernel(remote, *refs):
    own_x, sib_x, mod_ref, gm_ref, sums_ref, dx_ref = refs[:6]
    others = refs[6 : 6 + remote]
    grad_ref, gmod_ref, acc_s = refs[6 + remote :]
    step, half = pl.program_id(0), pl.program_id(1)
    width = own_x.shape[2]
    x = jnp.where(half == 0, own_x[0], sib_x[0]).astype(F32)
    scale = mod_ref[pl.ds(step, 1), width : 2 * width]
    xhat, inverse = normalize(x)
    gy = dx_ref[0, 0]
    for other in others:
        gy = gy + other[0, 0].astype(F32)
    grad_ref[0, 0] = (gm_ref[0, 0] + norm_back(gy * (1.0 + scale), xhat, inverse)).astype(BF16)

    @pl.when((step == 0) & (half == 0))
    def _():
        acc_s[...] = jnp.zeros_like(acc_s)

    acc_s[pl.ds(step, 1), :] += jnp.sum(gy, axis=0, keepdims=True)
    acc_s[pl.ds(step + 2, 1), :] += jnp.sum(gy * xhat, axis=0, keepdims=True)

    @pl.when(half == 1)
    def _():
        for row in range(4):
            acc_s[pl.ds(step + 4 + 2 * row, 1), :] = sums_ref[0, row : row + 1, :]

    @pl.when((step == 1) & (half == 1))
    def _():
        gmod_ref[...] = acc_s[...].astype(BF16)


def modulation_back_kernel(lead_ref, gmod_ref, emb_ref, ada_ref, gemb_ref, gada_ref, gbada_ref):
    table_rows, width = emb_ref.shape
    count = gmod_ref.shape[0]
    table = emb_ref[...].astype(F32)
    gate = jax.nn.sigmoid(table)
    slope = gate * (1.0 + table * (1.0 - gate))
    table_act = (table * gate).astype(BF16)
    lead = lead_ref[...]
    piece = (lane_index((1, count)) % 16) // 2
    leads = lax.broadcasted_iota(jnp.int32, (table_rows, count), 0)
    grads = gmod_ref[...]
    total = jnp.zeros((table_rows, width), F32)
    for index in range(6):
        columns = slice(index * width, (index + 1) * width)
        chosen = jnp.where((leads == lead) & (piece == index), 1.0, 0.0).astype(BF16)
        acts = dot(table_act, chosen, TN).astype(BF16)
        gada_ref[:, columns] = dot(acts, grads)
        by_lead = dot(chosen, grads)
        gbada_ref[:, columns] = jnp.sum(by_lead, axis=0, keepdims=True)
        high = by_lead.astype(BF16)
        low = (by_lead - high.astype(F32)).astype(BF16)
        total += dot(high, ada_ref[:, columns], NT) + dot(low, ada_ref[:, columns], NT)
    gemb_ref[...] = total * slope


def local(
    chips, inputs, cotangent, counts, lead_steps, emb_table, w_ada, b_ada, w_qkv, w_out, w_fc1, w_fc2
):
    slots, items, patches, width = inputs.shape
    steps = slots * items // 2
    hidden_width = w_fc1.shape[1]
    pairs = width // LANES
    rows = 2 * patches
    remote = 2 * (chips - 1)
    far_rows = remote * patches
    spot = lax.axis_index("seq")
    core = lax.rem(spot, 2)
    devices = 2 * chips

    def send(values, shift, cross):
        pairs_list = []
        for source in range(devices):
            chip, side = source // 2, source % 2
            pairs_list.append((source, ((chip + shift) % chips) * 2 + (1 - side if cross else side)))
        return lax.ppermute(values, "seq", pairs_list)

    x_steps = inputs.reshape(2, steps, patches, width)
    ct_steps = cotangent.reshape(2, steps, patches, width)
    own_x = lax.dynamic_index_in_dim(x_steps, core, 0, keepdims=False)
    other_x = lax.dynamic_index_in_dim(x_steps, 1 - core, 0, keepdims=False)
    own_ct = lax.dynamic_index_in_dim(ct_steps, core, 0, keepdims=False)
    other_ct = lax.dynamic_index_in_dim(ct_steps, 1 - core, 0, keepdims=False)
    sib_x = send(other_x, 0, True)
    far_x = []
    for shift in range(1, chips):
        far_x.append(send(own_x, shift, False))
        far_x.append(send(other_x, shift, True))
    sib_ct = send(other_ct, 0, True)
    step_ids = core * steps + jnp.arange(steps, dtype=jnp.int32)
    active = (step_ids < counts[0]).astype(F32)
    leads_own = lax.dynamic_slice_in_dim(lead_steps[0], core * steps, steps)
    leads_all = lax.all_gather(lead_steps[0], "dp").reshape(-1, 1, 2, steps)
    leads_all = jnp.broadcast_to(leads_all, (leads_all.shape[0], chips, 2, steps))
    leads_all = jnp.broadcast_to(leads_all[:, :, :, None, :], leads_all.shape[:3] + (8, steps))
    leads_all = leads_all.reshape(1, -1)

    mod = call(
        modulation_kernel,
        "modulation",
        (),
        [scalars(), whole(emb_table.shape), whole(w_ada.shape), whole((1, 6 * width))],
        whole((16, 6 * width)),
        jax.ShapeDtypeStruct((16, 6 * width), F32),
        flops=2 * 16 * width * 6 * width,
        moved=2 * w_ada.size,
    )(leads_own, emb_table, w_ada, b_ada.reshape(1, -1))

    step_block = pl.BlockSpec((1, patches, width), lambda j, i: (j, 0, 0))
    patch_block = pl.BlockSpec((1, 1, patches, width), lambda j, i: (j, i, 0, 0))

    def project(sources, queries, name):
        parts = 3 if queries else 2
        count = len(sources)
        head_block = pl.BlockSpec((1, pairs, 1, patches, LANES), lambda j, i: (j, 0, i, 0, 0))
        outs = call(
            functools.partial(project_kernel, count, queries),
            name,
            (steps, count),
            [step_block] * count + [whole(mod.shape), whole(w_qkv.shape)],
            [patch_block] + [head_block] * parts,
            [jax.ShapeDtypeStruct((steps, count, patches, width), BF16)]
            + [jax.ShapeDtypeStruct((steps, pairs, count, patches, LANES), BF16)] * parts,
            flops=2 * steps * count * patches * width * parts * width,
            moved=2 * steps * count * patches * width * (2 + parts),
        )(*sources, mod, w_qkv)
        return [outs[0]] + [o.reshape(steps, pairs, count * patches, LANES) for o in outs[1:]]

    n1, q, k, v = project([own_x, sib_x], True, "project_near")

    def head_rows(count):
        return pl.BlockSpec((1, 1, count, LANES), lambda j, p: (j, p, 0, 0))

    both_heads = pl.BlockSpec((1, 1, 2, rows, LANES), lambda j, p: (j, p, 0, 0, 0))
    query_rows = min(256, rows)
    near_work = 4 * steps * pairs * 2 * rows * LANES * rows
    far_work = 4 * steps * pairs * 2 * rows * LANES * far_rows
    acc = call(
        functools.partial(attend_local_kernel, query_rows),
        "attend_near",
        (steps, pairs),
        [head_rows(rows)] * 3,
        both_heads,
        jax.ShapeDtypeStruct((steps, pairs, 2, rows, LANES), F32),
        [pltpu.VMEM((2, rows, LANES), BF16)],
        flops=near_work,
        exps=steps * pairs * 2 * rows * rows,
    )(q, k, v)

    n1r, kr, vr = project(far_x, False, "project_far")
    o, qe = call(
        functools.partial(attend_all_kernel, query_rows),
        "attend_far",
        (steps, pairs),
        [head_rows(rows)] * 3 + [head_rows(far_rows)] * 2 + [both_heads],
        [head_rows(rows), both_heads],
        [
            jax.ShapeDtypeStruct((steps, pairs, rows, LANES), F32),
            jax.ShapeDtypeStruct((steps, pairs, 2, rows, LANES), BF16),
        ],
        [pltpu.VMEM((2, far_rows, LANES), BF16), pltpu.VMEM((rows, LANES), F32)],
        flops=far_work,
        exps=steps * pairs * 2 * rows * far_rows,
    )(q, k, v, kr, vr, acc)

    block_rows = min(256, patches)
    outs = call(
        functools.partial(patch_kernel, block_rows, 512),
        "patchwise",
        (steps, 2),
        [scalars()]
        + [step_block] * 4
        + [
            whole(mod.shape),
            pl.BlockSpec((1, pairs, patches, LANES), lambda j, i: (j, 0, i, 0)),
            whole(w_out.shape),
            whole(w_fc1.shape),
            whole(w_fc2.shape),
        ],
        [
            patch_block,
            patch_block,
            pl.BlockSpec((1, pairs, 2, patches, LANES), lambda j, i: (j, 0, 0, i, 0)),
            pl.BlockSpec((1, 8, width), lambda j, i: (j, 0, 0)),
            whole((width, width)),
            whole((width, hidden_width)),
            whole((width, hidden_width)),
        ],
        [
            jax.ShapeDtypeStruct((steps, 2, patches, width), BF16),
            jax.ShapeDtypeStruct((steps, 2, patches, width), F32),
            jax.ShapeDtypeStruct((steps, pairs, 2, rows, LANES), BF16),
            jax.ShapeDtypeStruct((steps, 8, width), F32),
            jax.ShapeDtypeStruct((width, width), BF16),
            jax.ShapeDtypeStruct((width, hidden_width), BF16),
            jax.ShapeDtypeStruct((width, hidden_width), BF16),
        ],
        [pltpu.VMEM((patches, hidden_width), BF16)] * 2
        + [pltpu.VMEM((patches, width), BF16)] * 4
        + [
            pltpu.VMEM((width, width), F32),
            pltpu.VMEM((width, hidden_width), F32),
            pltpu.VMEM((width, hidden_width), F32),
        ],
        flops=6 * steps * rows * width * (2 * hidden_width + width),
        moved=steps * rows * width * 20,
        exps=2 * steps * rows * hidden_width,
    )(active, own_x, sib_x, own_ct, sib_ct, mod, o, w_out, w_fc1, w_fc2)
    final, gm, ge, sums, g_out, g_fc1, g_fc2 = outs
    final_other = send(final[:, 1], 0, True)
    g_out, g_fc1, g_fc2 = lax.psum((g_out, g_fc1, g_fc2), ("dp", "seq"))

    def attend_back(keys, values, before, name):
        count = keys.shape[2]
        first = before is None
        key_rows = min(512, count)
        return call(
            functools.partial(attend_back_kernel, key_rows, first),
            name,
            (steps, pairs),
            [both_heads] * 2 + [head_rows(count)] * 2 + ([] if first else [head_rows(rows)]),
            [head_rows(rows), head_rows(count), head_rows(count)],
            [
                jax.ShapeDtypeStruct((steps, pairs, rows, LANES), F32 if first else BF16),
                jax.ShapeDtypeStruct((steps, pairs, count, LANES), BF16),
                jax.ShapeDtypeStruct((steps, pairs, count, LANES), BF16),
            ],
            [pltpu.VMEM((rows, LANES), F32)],
            flops=10 * steps * pairs * 2 * rows * count * LANES,
            exps=steps * pairs * 2 * rows * count,
        )(*([qe, ge, keys, values] + ([] if first else [before])))

    def project_back(grads, normed, before, name):
        parts = len(grads)
        count = normed.shape[1]
        last = before is not None
        grad_block = pl.BlockSpec((1, pairs, patches, LANES), lambda j, i: (j, 0, i, 0))
        return call(
            functools.partial(project_back_kernel, parts, last),
            name,
            (steps, count),
            [grad_block] * parts
            + [patch_block, whole(w_qkv.shape)]
            + ([whole(before.shape)] if last else []),
            [patch_block, whole((width, parts * width))],
            [
                jax.ShapeDtypeStruct((steps, count, patches, width), F32 if last else BF16),
                jax.ShapeDtypeStruct((width, parts * width), BF16 if last else F32),
            ],
            [pltpu.VMEM((width, parts * width), F32)],
            flops=4 * steps * count * patches * width * parts * width,
            moved=steps * count * patches * width * 10,
        )(*(list(grads) + [normed, w_qkv] + ([before] if last else [])))

    dq_part, dkr, dvr = attend_back(kr, vr, None, "attend_back_far")
    dx_far, gw_part = project_back([dkr, dvr], n1r, None, "project_back_far")
    dx_got = [send(dx_far[:, 2 * r - 2 : 2 * r], -r, False) for r in range(1, chips)]
    dq, dk, dv = attend_back(k, v, dq_part, "attend_back_near")
    dx_near, g_qkv = project_back([dq, dk, dv], n1, gw_part, "project_back_near")
    g_qkv, g_out = lax.optimization_barrier((g_qkv, g_out))
    g_qkv = lax.psum(g_qkv, ("dp", "seq"))

    grad_x, gmod = call(
        functools.partial(finish_kernel, len(dx_got)),
        "finish",
        (steps, 2),
        [step_block, step_block, whole(mod.shape), patch_block]
        + [pl.BlockSpec((1, 8, width), lambda j, i: (j, 0, 0))]
        + [patch_block] * (1 + len(dx_got)),
        [patch_block, whole((16, width))],
        [
            jax.ShapeDtypeStruct((steps, 2, patches, width), BF16),
            jax.ShapeDtypeStruct((16, width), BF16),
        ],
        [pltpu.VMEM((16, width), F32)],
        flops=20 * steps * rows * width,
        moved=steps * rows * width * 16,
    )(own_x, sib_x, mod, gm, sums, dx_near, *dx_got)
    grad_other = send(grad_x[:, 1], 0, True)
    gathered = lax.all_gather(gmod, ("dp", "seq")).reshape(-1, width)
    g_emb, g_ada, g_bada = call(
        modulation_back_kernel,
        "modulation_back",
        (),
        [whole(leads_all.shape), whole(gathered.shape), whole(emb_table.shape), whole(w_ada.shape)],
        [whole(emb_table.shape), whole(w_ada.shape), whole((1, 6 * width))],
        [
            jax.ShapeDtypeStruct(emb_table.shape, F32),
            jax.ShapeDtypeStruct(w_ada.shape, F32),
            jax.ShapeDtypeStruct((1, 6 * width), F32),
        ],
        flops=2 * gathered.shape[0] * width * 6 * width,
        moved=6 * w_ada.size,
    )(leads_all, gathered, emb_table, w_ada)

    def join(mine, got):
        both = jnp.where(
            core == 0, jnp.concatenate([mine, got]), jnp.concatenate([got, mine])
        )
        return both.reshape(inputs.shape)

    return (
        join(final[:, 0], final_other),
        join(grad_x[:, 0], grad_other),
        g_emb,
        g_ada,
        g_bada.reshape(-1),
        g_qkv.astype(F32),
        g_out.astype(F32),
        g_fc1.astype(F32),
        g_fc2.astype(F32).T,
    )


def solution(mesh):
    tokens = P(None, "dp", "seq", None)
    return jax.shard_map(
        functools.partial(local, mesh.shape["seq"] // 2),
        mesh=mesh,
        in_specs=(tokens, tokens, P("dp"), P("dp", None)) + (P(),) * 7,
        out_specs=(tokens, tokens) + (P(),) * 7,
        check_vma=False,
    )
```

```python
import functools

import jax
import jax.numpy as jnp
from jax import lax
from jax.experimental import pallas as pl
from jax.experimental.pallas import tpu as pltpu
from jax.sharding import PartitionSpec as P

HD = 64
LANES = 128
EPSILON = 1e-06
LOG2E = 1.4426950408889634
LN2 = 0.6931471805599453
NN = (((1,), (0,)), ((), ()))
NT = (((1,), (1,)), ((), ()))
TN = (((0,), (0,)), ((), ()))
F32 = jnp.float32
BF16 = jnp.bfloat16
VMEM_BYTES = 56 * 1024 * 1024


def dot(a, b, dims=NN):
    return lax.dot_general(a, b, dims, preferred_element_type=F32)


def call(
    body,
    name,
    grid,
    in_specs,
    out_specs,
    out_shape,
    scratch=(),
    flops=0,
    moved=0,
    exps=0,
    collective=None,
):
    return pl.pallas_call(
        body,
        name=name,
        grid=grid,
        in_specs=in_specs,
        out_specs=out_specs,
        out_shape=out_shape,
        scratch_shapes=list(scratch),
        cost_estimate=pl.CostEstimate(flops=flops, bytes_accessed=moved, transcendentals=exps),
        compiler_params=pltpu.CompilerParams(
            vmem_limit_bytes=VMEM_BYTES,
            collective_id=collective,
            has_side_effects=collective is not None,
        ),
    )


def whole(shape):
    return pl.BlockSpec(shape, lambda *_: (0,) * len(shape))


def scalars():
    return pl.BlockSpec(memory_space=pltpu.SMEM)


def lane_index(shape):
    return lax.broadcasted_iota(jnp.int32, shape, 1)


def normalize(values):
    center = values - jnp.mean(values, axis=-1, keepdims=True)
    spread = jnp.mean(center * center, axis=-1, keepdims=True)
    inverse = lax.rsqrt(spread + EPSILON)
    return center * inverse, inverse


def norm_back(grad, xhat, inverse):
    first = jnp.mean(grad, axis=-1, keepdims=True)
    second = jnp.mean(grad * xhat, axis=-1, keepdims=True)
    return inverse * (grad - first - xhat * second)


def pick(refs, which):
    value = refs[0][0]
    for index in range(1, len(refs)):
        value = jnp.where(which == index, refs[index][0], value)
    return value


class Exchange:
    def __init__(self, mesh_shape, row_tiles):
        self.bits = []
        for axis in ("seq", "dp"):
            bit = 1
            while bit < mesh_shape[axis]:
                self.bits.append((axis, bit))
                bit *= 2
        self.levels = len(self.bits)
        self.even = 0
        while self.even < self.levels and row_tiles % 2 == 0:
            row_tiles //= 2
            self.even += 1
        unit = 2 ** (self.levels - self.even)
        self.groups = 2**self.even
        self.real = row_tiles * 16
        self.padded = -(-row_tiles // unit) * unit * 16
        self.shard = self.padded // unit

    def sizes(self, level):
        if level < self.even:
            return (self.groups >> (level + 1), self.real)
        return (1, self.padded >> (level - self.even + 1))

    def receive_scratch(self, width):
        return [pltpu.VMEM(self.sizes(level) + (width,), BF16) for level in range(self.levels)]

    def place(self, level):
        axis, bit = self.bits[level]
        here = lax.axis_index(axis)
        value = (here // bit) % 2
        return value, {axis: here + bit * (1 - 2 * value)}

    def spot(self, level, first, flip):
        group, row = 0, 0
        for index in range(first, level + 1):
            value, _ = self.place(index)
            if flip and index == level:
                value = 1 - value
            if index < self.even:
                group = group + value * (self.groups >> (index + 1))
            else:
                row = row + value * (self.padded >> (index - self.even + 1))
        if level >= self.even:
            row = pl.multiple_of(row, 16)
        count, rows = self.sizes(level)
        return pl.ds(group, count), pl.ds(row, rows)

    def barrier(self):
        semaphore = pltpu.get_barrier_semaphore()
        for level in range(self.levels):
            _, partner = self.place(level)
            pl.semaphore_signal(
                semaphore, inc=1, device_id=partner, device_id_type=pl.DeviceIdType.MESH
            )
        pl.semaphore_wait(semaphore, self.levels)

    def copy(self, source, target, sends, recvs, level):
        _, partner = self.place(level)
        return pltpu.make_async_remote_copy(
            src_ref=source,
            dst_ref=target,
            send_sem=sends.at[level],
            recv_sem=recvs.at[level],
            device_id=partner,
            device_id_type=pl.DeviceIdType.MESH,
        )

    def reduce_copy(self, level, start_ref, acc_ref, got, sends, recvs):
        groups, rows = self.spot(level, min(level, 1), True)
        source = start_ref if level == 0 else acc_ref
        return self.copy(source.at[groups, rows], got[level], sends, recvs, level)

    def reduce_start(self, level, *refs):
        self.reduce_copy(level, *refs).start()

    def reduce_finish(self, level, start_ref, acc_ref, got, sends, recvs):
        self.reduce_copy(level, start_ref, acc_ref, got, sends, recvs).wait()
        count, rows = self.sizes(level)
        groups, spots = self.spot(level, min(level, 1), False)
        if level == 0:
            target_groups, target_rows = pl.ds(0, count), pl.ds(0, rows)
            if self.padded > self.real:
                acc_ref[:, self.real :, :] = jnp.zeros_like(acc_ref[:, self.real :, :])
        else:
            target_groups, target_rows = groups, spots
        source = start_ref if level == 0 else acc_ref

        def add(index, carry):
            one = pl.ds(groups.start + index, 1)
            to = pl.ds(target_groups.start + index, 1)
            value = source[one, spots, :].astype(F32) + got[level][pl.ds(index, 1)].astype(F32)
            acc_ref[to, target_rows, :] = value.astype(BF16)
            return carry

        lax.fori_loop(0, count, add, 0)

    def own_shard(self, ref, first):
        if self.levels > self.even:
            return ref.at[self.spot(self.levels - 1, first, False)]
        groups, _ = self.spot(self.levels - 1, first, False)
        return ref.at[groups, pl.ds(0, self.shard)]

    def gather_copy(self, level, full_ref, sends, recvs):
        piece = full_ref.at[self.spot(level, 0, False)]
        return self.copy(piece, piece, sends, recvs, level)

    def gather_start(self, level, *refs):
        self.gather_copy(level, *refs).start()

    def gather_finish(self, level, *refs):
        self.gather_copy(level, *refs).wait()


def modulation_kernel(lead_ref, emb_ref, ada_ref, bias_ref, mod_ref):
    rows = lax.broadcasted_iota(jnp.int32, (16, emb_ref.shape[0]), 0)
    columns = lane_index((16, emb_ref.shape[0]))
    onehot = jnp.zeros((16, emb_ref.shape[0]), F32)
    for step in range(lead_ref.shape[0]):
        onehot = jnp.where((rows == step) & (columns == lead_ref[step]), 1.0, onehot)
    condition = dot(onehot.astype(BF16), emb_ref[...])
    active = (condition * jax.nn.sigmoid(condition)).astype(BF16)
    mod_ref[...] = dot(active, ada_ref[...]) + bias_ref[...].astype(F32)


def project_kernel(sources, queries, *refs):
    x_refs = refs[:sources]
    mod_ref, w_ref = refs[sources : sources + 2]
    outs = refs[sources + 2 :]
    step, which = pl.program_id(0), pl.program_id(1)
    width = w_ref.shape[0]
    x = pick(x_refs, which).astype(F32)
    shift = mod_ref[pl.ds(step, 1), 0:width]
    scale = mod_ref[pl.ds(step, 1), width : 2 * width]
    xhat, _ = normalize(x)
    normed = (xhat * (1.0 + scale) + shift).astype(BF16)
    outs[0][0, 0] = normed
    start = 0 if queries else width
    projected = dot(normed, w_ref[:, start:])
    for part in range(len(outs) - 1):
        for pair in range(width // LANES):
            at = part * width + pair * LANES
            piece = projected[:, at : at + LANES]
            if queries and part == 0:
                piece = piece * (HD**-0.5 * LOG2E)
            outs[part + 1][0, pair, 0] = piece.astype(BF16)


def with_ones(values):
    low = lane_index(values.shape) < HD
    one = jnp.ones_like(values)
    return jnp.where(low, values, one), jnp.where(low, one, values)


def masked(values):
    low = lane_index(values.shape) < HD
    zero = jnp.zeros_like(values)
    return jnp.where(low, values, zero), jnp.where(low, zero, values)


def attend_local_kernel(rows, q_ref, k_ref, v_ref, acc_ref, ext_ref):
    ext_ref[0], ext_ref[1] = with_ones(v_ref[0, 0])

    def block(index, carry):
        at = pl.ds(pl.multiple_of(index * rows, rows), rows)
        for head, query in enumerate(masked(q_ref[0, 0, at, :])):
            weights = jnp.exp2(dot(query, k_ref[0, 0], NT)).astype(BF16)
            acc_ref[0, 0, head, at, :] = dot(weights, ext_ref[head])
        return carry

    lax.fori_loop(0, q_ref.shape[2] // rows, block, 0)


def attend_all_kernel(
    rows, q_ref, k_ref, v_ref, kr_ref, vr_ref, acc_ref, o_ref, qe_ref, ext_ref, total_ref
):
    ext_ref[0], ext_ref[1] = with_ones(vr_ref[0, 0])
    blocks = q_ref.shape[2] // rows

    def finish(at, query, first, second, top_first, top_second):
        lane = lane_index(query.shape)
        low = lane < HD
        swapped = jnp.where(low, second, first)
        total = pltpu.roll(swapped, HD, 1)
        o_ref[0, 0, at, :] = jnp.where(low, first, second) / total
        log_total = jnp.log2(swapped) + jnp.where(low, top_second, top_first)
        high = log_total.astype(BF16).astype(F32)
        middle = (log_total - high).astype(BF16).astype(F32)
        rest = log_total - high - middle
        spot = lane % HD
        extra = jnp.where(spot == 0, -high, jnp.where(spot == 1, -middle, -rest))
        extra = jnp.where(spot < 3, extra, 0.0).astype(BF16)
        qe_ref[0, 0, 0, at, :] = jnp.where(low, query, extra)
        qe_ref[0, 0, 1, at, :] = jnp.where(low, extra, query)
        return total

    def block(index, carry):
        at = pl.ds(pl.multiple_of(index * rows, rows), rows)
        query = q_ref[0, 0, at, :]
        sums = []
        for head, own in enumerate(masked(query)):
            weights = jnp.exp2(dot(own, kr_ref[0, 0], NT)).astype(BF16)
            sums.append(acc_ref[0, 0, head, at, :] + dot(weights, ext_ref[head]))
        total_ref[at, :] = finish(at, query, sums[0], sums[1], 0.0, 0.0)
        return carry

    lax.fori_loop(0, blocks, block, 0)
    total = total_ref[...]
    bad = jnp.sum(jnp.where((total > 1e-25) & (total < 1e25), 0.0, 1.0))

    @pl.when(bad > 0.0)
    def _():
        own_ext = with_ones(v_ref[0, 0])

        def again(index, carry):
            at = pl.ds(pl.multiple_of(index * rows, rows), rows)
            query = q_ref[0, 0, at, :]
            sums, tops = [], []
            for head, own in enumerate(masked(query)):
                scores = dot(own, k_ref[0, 0], NT)
                others = dot(own, kr_ref[0, 0], NT)
                top = jnp.maximum(
                    jnp.max(scores, axis=-1, keepdims=True),
                    jnp.max(others, axis=-1, keepdims=True),
                )
                sums.append(
                    dot(jnp.exp2(scores - top).astype(BF16), own_ext[head])
                    + dot(jnp.exp2(others - top).astype(BF16), ext_ref[head])
                )
                tops.append(top)
            finish(at, query, sums[0], sums[1], tops[0], tops[1])
            return carry

        lax.fori_loop(0, blocks, again, 0)


def gelu_parts(values):
    cumulative = 0.5 * (1.0 + lax.erf(values * 0.7071067811865476))
    density = jnp.exp2(values * values * (-0.5 * LOG2E)) * 0.3989422804014327
    return values * cumulative, cumulative + values * density


def patch_kernel(
    rows,
    chunk,
    active_ref,
    own_x,
    sib_x,
    own_ct,
    sib_ct,
    mod_ref,
    o_ref,
    out_w,
    fc1_w,
    fc2_w,
    final_ref,
    gm_ref,
    ge_ref,
    sums_ref,
    stack_ref,
    hidden_s,
    gpre_s,
    n2_s,
    g2_s,
    g1_s,
    mixed_s,
    gout_s,
    gfc1_s,
    gfc2_s,
):
    step, half = pl.program_id(0), pl.program_id(1)
    width, hidden_width = fc1_w.shape
    patches = own_x.shape[1]
    active = active_ref[step]

    def piece(index):
        return mod_ref[pl.ds(step, 1), index * width : (index + 1) * width]

    gate1, shift2, scale2, gate2 = piece(2), piece(3), piece(4), piece(5)

    @pl.when(half == 0)
    def _():
        sums_ref[...] = jnp.zeros_like(sums_ref)

    @pl.when((step == 0) & (half == 0))
    def _():
        gout_s[...] = jnp.zeros_like(gout_s)
        gfc1_s[...] = jnp.zeros_like(gfc1_s)
        gfc2_s[...] = jnp.zeros_like(gfc2_s)

    def block(index, carry):
        at = pl.ds(pl.multiple_of(index * rows, rows), rows)
        x = jnp.where(half == 0, own_x[0, at, :], sib_x[0, at, :]).astype(F32)
        final_grad = jnp.where(half == 0, own_ct[0, at, :], sib_ct[0, at, :]).astype(F32) * active
        outs = [o_ref[0, pair, at, :] for pair in range(width // LANES)]
        mixed = jnp.concatenate([o.astype(BF16) for o in outs], axis=-1)
        mixed_s[at, :] = mixed
        branch_one = dot(mixed, out_w[...])
        middle = x + gate1 * branch_one
        xhat, inverse = normalize(middle)
        n2 = (xhat * (1.0 + scale2) + shift2).astype(BF16)
        n2_s[at, :] = n2
        g2 = (gate2 * final_grad).astype(BF16)
        g2_s[at, :] = g2
        branch_two = jnp.zeros((rows, width), F32)
        gy = jnp.zeros((rows, width), F32)
        for start in range(0, hidden_width, chunk):
            columns = slice(start, start + chunk)
            pre = dot(n2, fc1_w[:, columns])
            grad_hidden = dot(g2, fc2_w[columns, :], NT)
            hidden, slope = gelu_parts(pre)
            hidden = hidden.astype(BF16)
            grad_pre = (slope * grad_hidden).astype(BF16)
            hidden_s[at, columns] = hidden
            gpre_s[at, columns] = grad_pre
            branch_two += dot(hidden, fc2_w[columns, :])
            gy += dot(grad_pre, fc1_w[:, columns], NT)
        final_ref[0, 0, at, :] = ((middle + gate2 * branch_two) * active).astype(BF16)
        gm = final_grad + norm_back(gy * (1.0 + scale2), xhat, inverse)
        gm_ref[0, 0, at, :] = gm
        g1 = (gate1 * gm).astype(BF16)
        g1_s[at, :] = g1
        sums = [branch_one * gm, gy, gy * xhat, branch_two * final_grad]
        for row, value in enumerate(sums):
            sums_ref[0, row : row + 1, :] += jnp.sum(value, axis=0, keepdims=True)
        grad_mixed = dot(g1, out_w[...], NT).astype(BF16)
        lane = lane_index((rows, LANES))
        low = lane < HD
        spot = lane % HD
        for pair, o in enumerate(outs):
            grad = grad_mixed[:, pair * LANES : (pair + 1) * LANES]
            product = grad.astype(F32) * o
            first = jnp.sum(jnp.where(low, product, 0.0), axis=-1, keepdims=True)
            second = jnp.sum(jnp.where(low, 0.0, product), axis=-1, keepdims=True)
            inner = jnp.where(low, second, first)
            high = inner.astype(BF16).astype(F32)
            mid = (inner - high).astype(BF16).astype(F32)
            extra = jnp.where(spot == 0, -high, jnp.where(spot == 1, -mid, high + mid - inner))
            extra = jnp.where(spot < 3, extra, 0.0).astype(BF16)
            ge_ref[0, pair, 0, at, :] = jnp.where(low, grad, extra)
            ge_ref[0, pair, 1, at, :] = jnp.where(low, extra, grad)
        return carry

    lax.fori_loop(0, patches // rows, block, 0)
    gout_s[...] += dot(mixed_s[...], g1_s[...], TN)
    for start in range(0, hidden_width, chunk):
        columns = slice(start, start + chunk)
        gfc1_s[:, columns] += dot(n2_s[...], gpre_s[:, columns], TN)
        gfc2_s[:, columns] += dot(g2_s[...], hidden_s[:, columns], TN)

    @pl.when((step == pl.num_programs(0) - 1) & (half == pl.num_programs(1) - 1))
    def _():
        blocks = hidden_width // width
        for index in range(blocks):
            columns = slice(index * width, (index + 1) * width)
            stack_ref[index] = gfc1_s[:, columns].astype(BF16)
            stack_ref[blocks + index] = gfc2_s[:, columns].T.astype(BF16)
        stack_ref[2 * blocks] = gout_s[...].astype(BF16)


def attend_back_kernel(rows, first_pass, exchange, grid_steps, *refs):
    if first_pass:
        qe_ref, ge_ref, k_ref, v_ref, give_ref, dq_ref, dk_ref, dv_ref, shard_ref = refs[:9]
        acc_s, sum_s, sends, recvs, *got = refs[9:]
        acc_s[...] = jnp.zeros_like(acc_s)
    else:
        qe_ref, ge_ref, k_ref, v_ref, dq_in, shard_ref, dq_ref, dk_ref, dv_ref, full_ref = refs[:10]
        acc_s, full_s, sends, recvs, local_sem = refs[10:]
        acc_s[...] = dq_in[0, 0]
    per_step = k_ref.shape[2] // rows
    slots = pl.num_programs(0) * pl.num_programs(1) * per_step
    static_slots = grid_steps * per_step
    first_slot = (pl.program_id(0) * pl.num_programs(1) + pl.program_id(1)) * per_step
    levels = exchange.levels

    def reduce_action(level):
        refs_of = (give_ref, sum_s, got, sends, recvs)
        if level == 0:
            exchange.barrier()
        else:
            exchange.reduce_finish(level - 1, *refs_of)
        if level < levels:
            exchange.reduce_start(level, *refs_of)
        else:
            shard_ref[...] = exchange.own_shard(sum_s, 1)[...][0]

    def gather_action(order):
        level = levels - 1 - order
        refs_of = (full_s, sends, recvs)
        if order == 0:
            exchange.barrier()
            own = exchange.own_shard(full_s, 0)
            own[...] = shard_ref[...][None]
        else:
            exchange.gather_finish(level + 1, *refs_of)
        if order < levels:
            exchange.gather_start(level, *refs_of)
        else:
            copy = pltpu.make_async_copy(full_s, full_ref, local_sem)
            copy.start()
            copy.wait()

    action = reduce_action if first_pass else gather_action
    weights = [1.0] + [2.0 ** -(level - 1) * 6 for level in range(1, levels)]
    weights = [max(w, 1.5) for w in weights]
    if not first_pass:
        weights = weights[::-1]
    marks, total = [0], 0.0
    for w in weights:
        total += w
        marks.append(total)
    marks = [min(int(mark * (static_slots - 1) / total + 0.5), static_slots - 1) for mark in marks]

    def block(index, carry):
        for order, mark in enumerate(marks[:-1]):
            pl.when(first_slot + index == mark)(functools.partial(action, order))
        at = pl.ds(pl.multiple_of(index * rows, rows), rows)
        keys = k_ref[0, 0, at, :]
        values = v_ref[0, 0, at, :]
        lane = lane_index(keys.shape)
        low = lane < HD
        ones = jnp.where(lane % HD < 3, 1.0, 0.0).astype(BF16)
        zero = jnp.zeros_like(keys)
        grads = []
        for head in range(2):
            own = low if head == 0 else jnp.logical_not(low)
            query = qe_ref[0, 0, head]
            grad = ge_ref[0, 0, head]
            probs = jnp.exp2(dot(jnp.where(own, keys, ones), query, NT))
            grad_probs = dot(jnp.where(own, values, ones), grad, NT)
            grad_scores = (probs * grad_probs).astype(BF16)
            grads.append((dot(grad_scores, query), dot(probs.astype(BF16), grad)))
            acc_s[...] += dot(grad_scores, jnp.where(own, keys, zero), TN)
        dk_ref[0, 0, at, :] = (jnp.where(low, grads[0][0], grads[1][0]) * LN2).astype(BF16)
        dv_ref[0, 0, at, :] = jnp.where(low, grads[0][1], grads[1][1]).astype(BF16)
        return carry

    lax.fori_loop(0, per_step, block, 0)
    pl.when(first_slot + per_step == slots)(functools.partial(action, levels))
    if first_pass:
        dq_ref[0, 0] = acc_s[...]
    else:
        dq_ref[0, 0] = (acc_s[...] * HD**-0.5).astype(BF16)


def project_back_kernel(parts, last, *refs):
    grads = refs[:parts]
    normed_ref, w_ref = refs[parts : parts + 2]
    rest = refs[parts + 2 :]
    if last:
        add_ref, dx_ref, gw_ref, gw_s = rest
    else:
        dx_ref, gw_ref, gw_s = rest
    step, which = pl.program_id(0), pl.program_id(1)
    width = w_ref.shape[0]
    start = w_ref.shape[1] - parts * width
    joined = jnp.concatenate(
        [ref[0, pair] for ref in grads for pair in range(ref.shape[1])], axis=-1
    )
    dx_ref[0, 0] = dot(joined, w_ref[:, start:], NT).astype(dx_ref.dtype)

    @pl.when((step == 0) & (which == 0))
    def _():
        gw_s[...] = jnp.zeros_like(gw_s)
        if last:
            gw_s[:, width:] = add_ref[...]

    gw_s[...] += dot(normed_ref[0, 0], joined, TN)

    @pl.when((step == pl.num_programs(0) - 1) & (which == pl.num_programs(1) - 1))
    def _():
        if last:
            for part in range(parts):
                gw_ref[part] = gw_s[:, part * width : (part + 1) * width].astype(BF16)
        else:
            gw_ref[...] = gw_s[...]


def finish_kernel(remote, *refs):
    lead_ref, own_x, sib_x, mod_ref, gm_ref, sums_ref, dx_ref = refs[:7]
    others = refs[7 : 7 + remote]
    grad_ref, gmod_ref, acc_s = refs[7 + remote :]
    step, half = pl.program_id(0), pl.program_id(1)
    width = own_x.shape[2]
    x = jnp.where(half == 0, own_x[0], sib_x[0]).astype(F32)
    scale = mod_ref[pl.ds(step, 1), width : 2 * width]
    xhat, inverse = normalize(x)
    gy = dx_ref[0, 0]
    for other in others:
        gy = gy + other[0, 0].astype(F32)
    grad_ref[0, 0] = (gm_ref[0, 0] + norm_back(gy * (1.0 + scale), xhat, inverse)).astype(BF16)

    @pl.when((step == 0) & (half == 0))
    def _():
        acc_s[...] = jnp.zeros_like(acc_s)

    acc_s[pl.ds(step, 1), :] += jnp.sum(gy, axis=0, keepdims=True)
    acc_s[pl.ds(step + 2, 1), :] += jnp.sum(gy * xhat, axis=0, keepdims=True)

    @pl.when(half == 1)
    def _():
        for row in range(4):
            acc_s[pl.ds(step + 4 + 2 * row, 1), :] = sums_ref[0, row : row + 1, :]
        chosen = lane_index((1, width)) == lead_ref[step]
        acc_s[pl.ds(step + 12, 1), :] = jnp.where(chosen, 1.0, 0.0)

    @pl.when((step == 1) & (half == 1))
    def _():
        gmod_ref[...] = acc_s[...].astype(BF16)


def tail_kernel(exchange, give_ref, gmod_ref, full_ref, all_ref, sum_s, full_s, all_s, *refs):
    sends, recvs, back_sends, back_recvs, all_sends, all_recvs, *got = refs
    levels = exchange.levels
    index = 0
    scale = 1
    for level, (axis, bit) in enumerate(exchange.bits):
        value, _ = exchange.place(level)
        index = index + value * scale
        scale *= 2
    exchange.barrier()
    all_s[pl.ds(index, 1)] = gmod_ref[...][None]

    def gather_all(level):
        size = 1 << level
        piece = all_s.at[pl.ds((index // size) * size, size)]
        return exchange.copy(piece, piece, all_sends, all_recvs, level)

    refs_of = (give_ref, sum_s, got, sends, recvs)
    for level in range(levels):
        exchange.reduce_start(level, *refs_of)
        gather_all(level).start()
        exchange.reduce_finish(level, *refs_of)
        gather_all(level).wait()
    own = exchange.own_shard(full_s, 0)
    own[...] = exchange.own_shard(sum_s, 1)[...]
    for level in reversed(range(levels)):
        exchange.gather_start(level, full_s, back_sends, back_recvs)
        exchange.gather_finish(level, full_s, back_sends, back_recvs)
    all_ref[...] = all_s[...]
    full_ref[...] = full_s[...]


def unstack(exchange, full_ref, targets, width):
    row = 0
    end = exchange.groups * exchange.real
    while row < end:
        group, inside = divmod(row, exchange.real)
        block, place = divmod(row, width)
        count = min(exchange.real - inside, width - place)
        target, first_row, first_column = targets[block]
        target[
            first_row + place : first_row + place + count, first_column : first_column + width
        ] = full_ref[group, inside : inside + count, :].astype(F32)
        row += count


def final_kernel(early, late, gmod_ref, emb_ref, ada_ref, early_ref, late_ref, *outs):
    gemb_ref, gada_ref, gbada_ref, gqkv_ref, gout_ref, gfc1_ref, gfc2_ref = outs
    size = gout_ref.shape[0]
    blocks = gfc1_ref.shape[1] // size
    unstack(late, late_ref, [(gqkv_ref, 0, part * size) for part in range(3)], size)
    unstack(
        early,
        early_ref,
        [(gfc1_ref, 0, block * size) for block in range(blocks)]
        + [(gfc2_ref, block * size, 0) for block in range(blocks)]
        + [(gout_ref, 0, 0)],
        size,
    )
    table_rows, width = emb_ref.shape
    count = gmod_ref.shape[0]
    table = emb_ref[...].astype(F32)
    gate = jax.nn.sigmoid(table)
    slope = gate * (1.0 + table * (1.0 - gate))
    table_act = (table * gate).astype(BF16)
    piece = (lane_index((1, count)) % 16) // 2
    grads = gmod_ref[...]
    part = min(count, 512)
    row = lax.broadcasted_iota(jnp.int32, (part, part), 0)
    column = lane_index((part, part))
    spread = jnp.where(row == (column // 16) * 16 + 12 + column % 2, 1.0, 0.0).astype(BF16)
    leads = [
        dot(grads[start : start + part, :LANES], spread, TN)[:table_rows]
        for start in range(0, count, part)
    ]
    leads = jnp.concatenate(leads, axis=-1)
    total = jnp.zeros((table_rows, width), F32)
    for index in range(6):
        columns = slice(index * width, (index + 1) * width)
        chosen = jnp.where(piece == index, leads, 0.0).astype(BF16)
        acts = dot(table_act, chosen, TN).astype(BF16)
        gada_ref[:, columns] = dot(acts, grads)
        by_lead = dot(chosen, grads)
        gbada_ref[:, columns] = jnp.sum(by_lead, axis=0, keepdims=True)
        high = by_lead.astype(BF16)
        low = (by_lead - high.astype(F32)).astype(BF16)
        total += dot(high, ada_ref[:, columns], NT) + dot(low, ada_ref[:, columns], NT)
    gemb_ref[...] = total * slope


def local(
    mesh_shape, inputs, cotangent, counts, lead_steps, emb_table, w_ada, b_ada, w_qkv, w_out, w_fc1, w_fc2
):
    slots, items, patches, width = inputs.shape
    chips = mesh_shape["seq"] // 2
    stacked = 2 * w_fc1.shape[1] // w_fc1.shape[0] + 1
    steps = slots * items // 2
    hidden_width = w_fc1.shape[1]
    pairs = width // LANES
    rows = 2 * patches
    remote = 2 * (chips - 1)
    far_rows = remote * patches
    spot = lax.axis_index("seq")
    core = lax.rem(spot, 2)
    devices = 2 * chips

    def send(values, shift, cross):
        pairs_list = []
        for source in range(devices):
            chip, side = source // 2, source % 2
            pairs_list.append((source, ((chip + shift) % chips) * 2 + (1 - side if cross else side)))
        return lax.ppermute(values, "seq", pairs_list)

    x_steps = inputs.reshape(2, steps, patches, width)
    ct_steps = cotangent.reshape(2, steps, patches, width)
    own_x = lax.dynamic_index_in_dim(x_steps, core, 0, keepdims=False)
    other_x = lax.dynamic_index_in_dim(x_steps, 1 - core, 0, keepdims=False)
    own_ct = lax.dynamic_index_in_dim(ct_steps, core, 0, keepdims=False)
    other_ct = lax.dynamic_index_in_dim(ct_steps, 1 - core, 0, keepdims=False)
    sib_x = send(other_x, 0, True)
    far_x = []
    for shift in range(1, chips):
        far_x.append(send(own_x, shift, False))
        far_x.append(send(other_x, shift, True))
    sib_ct = send(other_ct, 0, True)
    step_ids = core * steps + jnp.arange(steps, dtype=jnp.int32)
    active = (step_ids < counts[0]).astype(F32)
    leads_own = lax.dynamic_slice_in_dim(lead_steps[0], core * steps, steps)
    mod = call(
        modulation_kernel,
        "modulation",
        (),
        [scalars(), whole(emb_table.shape), whole(w_ada.shape), whole((1, 6 * width))],
        whole((16, 6 * width)),
        jax.ShapeDtypeStruct((16, 6 * width), F32),
        flops=2 * 16 * width * 6 * width,
        moved=2 * w_ada.size,
    )(leads_own, emb_table, w_ada, b_ada.reshape(1, -1))

    step_block = pl.BlockSpec((1, patches, width), lambda j, i: (j, 0, 0))
    patch_block = pl.BlockSpec((1, 1, patches, width), lambda j, i: (j, i, 0, 0))

    def project(sources, queries, name):
        parts = 3 if queries else 2
        count = len(sources)
        head_block = pl.BlockSpec((1, pairs, 1, patches, LANES), lambda j, i: (j, 0, i, 0, 0))
        outs = call(
            functools.partial(project_kernel, count, queries),
            name,
            (steps, count),
            [step_block] * count + [whole(mod.shape), whole(w_qkv.shape)],
            [patch_block] + [head_block] * parts,
            [jax.ShapeDtypeStruct((steps, count, patches, width), BF16)]
            + [jax.ShapeDtypeStruct((steps, pairs, count, patches, LANES), BF16)] * parts,
            flops=2 * steps * count * patches * width * parts * width,
            moved=2 * steps * count * patches * width * (2 + parts),
        )(*sources, mod, w_qkv)
        return [outs[0]] + [o.reshape(steps, pairs, count * patches, LANES) for o in outs[1:]]

    n1, q, k, v = project([own_x, sib_x], True, "project_near")

    def head_rows(count):
        return pl.BlockSpec((1, 1, count, LANES), lambda j, p: (j, p, 0, 0))

    both_heads = pl.BlockSpec((1, 1, 2, rows, LANES), lambda j, p: (j, p, 0, 0, 0))
    query_rows = min(256, rows)
    near_work = 4 * steps * pairs * 2 * rows * LANES * rows
    far_work = 4 * steps * pairs * 2 * rows * LANES * far_rows
    acc = call(
        functools.partial(attend_local_kernel, query_rows),
        "attend_near",
        (steps, pairs),
        [head_rows(rows)] * 3,
        both_heads,
        jax.ShapeDtypeStruct((steps, pairs, 2, rows, LANES), F32),
        [pltpu.VMEM((2, rows, LANES), BF16)],
        flops=near_work,
        exps=steps * pairs * 2 * rows * rows,
    )(q, k, v)

    n1r, kr, vr = project(far_x, False, "project_far")
    o, qe = call(
        functools.partial(attend_all_kernel, query_rows),
        "attend_far",
        (steps, pairs),
        [head_rows(rows)] * 3 + [head_rows(far_rows)] * 2 + [both_heads],
        [head_rows(rows), both_heads],
        [
            jax.ShapeDtypeStruct((steps, pairs, rows, LANES), F32),
            jax.ShapeDtypeStruct((steps, pairs, 2, rows, LANES), BF16),
        ],
        [pltpu.VMEM((2, far_rows, LANES), BF16), pltpu.VMEM((rows, LANES), F32)],
        flops=far_work,
        exps=steps * pairs * 2 * rows * far_rows,
    )(q, k, v, kr, vr, acc)

    block_rows = min(256, patches)
    outs = call(
        functools.partial(patch_kernel, block_rows, 512),
        "patchwise",
        (steps, 2),
        [scalars()]
        + [step_block] * 4
        + [
            whole(mod.shape),
            pl.BlockSpec((1, pairs, patches, LANES), lambda j, i: (j, 0, i, 0)),
            whole(w_out.shape),
            whole(w_fc1.shape),
            whole(w_fc2.shape),
        ],
        [
            patch_block,
            patch_block,
            pl.BlockSpec((1, pairs, 2, patches, LANES), lambda j, i: (j, 0, 0, i, 0)),
            pl.BlockSpec((1, 8, width), lambda j, i: (j, 0, 0)),
            whole((stacked, width, width)),
        ],
        [
            jax.ShapeDtypeStruct((steps, 2, patches, width), BF16),
            jax.ShapeDtypeStruct((steps, 2, patches, width), F32),
            jax.ShapeDtypeStruct((steps, pairs, 2, rows, LANES), BF16),
            jax.ShapeDtypeStruct((steps, 8, width), F32),
            jax.ShapeDtypeStruct((stacked, width, width), BF16),
        ],
        [pltpu.VMEM((patches, hidden_width), BF16)] * 2
        + [pltpu.VMEM((patches, width), BF16)] * 4
        + [
            pltpu.VMEM((width, width), F32),
            pltpu.VMEM((width, hidden_width), F32),
            pltpu.VMEM((width, hidden_width), F32),
        ],
        flops=6 * steps * rows * width * (2 * hidden_width + width),
        moved=steps * rows * width * 20,
        exps=2 * steps * rows * hidden_width,
    )(active, own_x, sib_x, own_ct, sib_ct, mod, o, w_out, w_fc1, w_fc2)
    final, gm, ge, sums, stack = outs
    final_other = send(final[:, 1], 0, True)
    early = Exchange(mesh_shape, stacked * width // 16)
    late = Exchange(mesh_shape, 3 * width // 16)
    give = stack.reshape(early.groups, early.real, width)
    level_sems = [pltpu.SemaphoreType.DMA((early.levels,))] * 2

    def attend_back(keys, values, extra, first, name):
        count = keys.shape[2]
        key_rows = min(512, count)
        early_shape = (early.groups, early.padded, width)
        in_specs = [both_heads] * 2 + [head_rows(count)] * 2
        out_specs = [head_rows(rows), head_rows(count), head_rows(count)]
        out_shape = [
            jax.ShapeDtypeStruct((steps, pairs, rows, LANES), F32 if first else BF16),
            jax.ShapeDtypeStruct((steps, pairs, count, LANES), BF16),
            jax.ShapeDtypeStruct((steps, pairs, count, LANES), BF16),
        ]
        scratch = [pltpu.VMEM((rows, LANES), F32)]
        if first:
            in_specs += [whole(give.shape)]
            out_specs += [whole((early.shard, width))]
            out_shape += [jax.ShapeDtypeStruct((early.shard, width), BF16)]
            half = (early.groups // 2, early.padded, width)
            scratch += [pltpu.VMEM(half, BF16)] + level_sems + early.receive_scratch(width)
        else:
            in_specs += [head_rows(rows), whole((early.shard, width))]
            out_specs += [pl.BlockSpec(memory_space=pl.ANY)]
            out_shape += [jax.ShapeDtypeStruct(early_shape, BF16)]
            scratch += [pltpu.VMEM(early_shape, BF16)] + level_sems + [pltpu.SemaphoreType.DMA]
        return call(
            functools.partial(attend_back_kernel, key_rows, first, early, steps * pairs),
            name,
            (steps, pairs),
            in_specs,
            out_specs,
            out_shape,
            scratch,
            flops=10 * steps * pairs * 2 * rows * count * LANES,
            exps=steps * pairs * 2 * rows * count,
            collective=1 if first else 2,
        )(qe, ge, keys, values, *extra)

    def project_back(grads, normed, before, name):
        parts = len(grads)
        count = normed.shape[1]
        last = before is not None
        grad_block = pl.BlockSpec((1, pairs, patches, LANES), lambda j, i: (j, 0, i, 0))
        return call(
            functools.partial(project_back_kernel, parts, last),
            name,
            (steps, count),
            [grad_block] * parts
            + [patch_block, whole(w_qkv.shape)]
            + ([whole(before.shape)] if last else []),
            [patch_block, whole((parts, width, width) if last else (width, parts * width))],
            [
                jax.ShapeDtypeStruct((steps, count, patches, width), F32 if last else BF16),
                jax.ShapeDtypeStruct((parts, width, width), BF16)
                if last
                else jax.ShapeDtypeStruct((width, parts * width), F32),
            ],
            [pltpu.VMEM((width, parts * width), F32)],
            flops=4 * steps * count * patches * width * parts * width,
            moved=steps * count * patches * width * 10,
        )(*(list(grads) + [normed, w_qkv] + ([before] if last else [])))

    dq_part, dkr, dvr, shard = attend_back(kr, vr, [give], True, "attend_back_far")
    dx_far, gw_part = project_back([dkr, dvr], n1r, None, "project_back_far")
    dx_got = [send(dx_far[:, 2 * r - 2 : 2 * r], -r, False) for r in range(1, chips)]
    dq, dk, dv, early_sum = attend_back(k, v, [dq_part, shard], False, "attend_back_near")
    dx_near, g_qkv = project_back([dq, dk, dv], n1, gw_part, "project_back_near")

    grad_x, gmod = call(
        functools.partial(finish_kernel, len(dx_got)),
        "finish",
        (steps, 2),
        [scalars(), step_block, step_block, whole(mod.shape), patch_block]
        + [pl.BlockSpec((1, 8, width), lambda j, i: (j, 0, 0))]
        + [patch_block] * (1 + len(dx_got)),
        [patch_block, whole((16, width))],
        [
            jax.ShapeDtypeStruct((steps, 2, patches, width), BF16),
            jax.ShapeDtypeStruct((16, width), BF16),
        ],
        [pltpu.VMEM((16, width), F32)],
        flops=20 * steps * rows * width,
        moved=steps * rows * width * 16,
    )(leads_own, own_x, sib_x, mod, gm, sums, dx_near, *dx_got)
    grad_other = send(grad_x[:, 1], 0, True)

    late_shape = (late.groups, late.padded, width)
    all_shape = (mesh_shape["dp"] * mesh_shape["seq"], 16, width)
    late_sum, gathered = call(
        functools.partial(tail_kernel, late),
        "sum_late",
        (),
        [whole((late.groups, late.real, width)), whole(gmod.shape)],
        [whole(late_shape), whole(all_shape)],
        [jax.ShapeDtypeStruct(late_shape, BF16), jax.ShapeDtypeStruct(all_shape, BF16)],
        [
            pltpu.VMEM((late.groups // 2, late.padded, width), BF16),
            pltpu.VMEM(late_shape, BF16),
            pltpu.VMEM(all_shape, BF16),
        ]
        + [pltpu.SemaphoreType.DMA((late.levels,))] * 6
        + late.receive_scratch(width),
        collective=3,
    )(g_qkv.reshape(late.groups, late.real, width), gmod)
    gathered = gathered.reshape(-1, width)
    g_emb, g_ada, g_bada, g_qkv, g_out, g_fc1, g_fc2 = call(
        functools.partial(final_kernel, early, late),
        "final",
        (),
        [whole(gathered.shape), whole(emb_table.shape), whole(w_ada.shape)]
        + [whole(early_sum.shape), whole(late_sum.shape)],
        [whole(emb_table.shape), whole(w_ada.shape), whole((1, 6 * width))]
        + [whole(w.shape) for w in (w_qkv, w_out, w_fc1, w_fc2)],
        [
            jax.ShapeDtypeStruct(emb_table.shape, F32),
            jax.ShapeDtypeStruct(w_ada.shape, F32),
            jax.ShapeDtypeStruct((1, 6 * width), F32),
        ]
        + [jax.ShapeDtypeStruct(w.shape, F32) for w in (w_qkv, w_out, w_fc1, w_fc2)],
        flops=2 * gathered.shape[0] * width * 6 * width,
        moved=6 * w_ada.size,
    )(gathered, emb_table, w_ada, early_sum, late_sum)

    def join(mine, got):
        both = jnp.where(
            core == 0, jnp.concatenate([mine, got]), jnp.concatenate([got, mine])
        )
        return both.reshape(inputs.shape)

    return (
        join(final[:, 0], final_other),
        join(grad_x[:, 0], grad_other),
        g_emb,
        g_ada,
        g_bada.reshape(-1),
        g_qkv,
        g_out,
        g_fc1,
        g_fc2,
    )


def solution(mesh):
    tokens = P(None, "dp", "seq", None)
    return jax.shard_map(
        functools.partial(local, dict(mesh.shape)),
        mesh=mesh,
        in_specs=(tokens, tokens, P("dp"), P("dp", None)) + (P(),) * 7,
        out_specs=(tokens, tokens) + (P(),) * 7,
        check_vma=False,
    )
```

```python
import functools

import jax
import jax.numpy as jnp
from jax import lax
from jax.experimental import pallas as pl
from jax.experimental.pallas import tpu as pltpu
from jax.sharding import PartitionSpec as P

HD = 64
LANES = 128
EPSILON = 1e-06
LOG2E = 1.4426950408889634
LN2 = 0.6931471805599453
NN = (((1,), (0,)), ((), ()))
NT = (((1,), (1,)), ((), ()))
TN = (((0,), (0,)), ((), ()))
F32 = jnp.float32
BF16 = jnp.bfloat16
VMEM_BYTES = 56 * 1024 * 1024


def dot(a, b, dims=NN):
    return lax.dot_general(a, b, dims, preferred_element_type=F32)


def call(
    body,
    name,
    grid,
    in_specs,
    out_specs,
    out_shape,
    scratch=(),
    flops=0,
    moved=0,
    exps=0,
    collective=None,
):
    return pl.pallas_call(
        body,
        name=name,
        grid=grid,
        in_specs=in_specs,
        out_specs=out_specs,
        out_shape=out_shape,
        scratch_shapes=list(scratch),
        cost_estimate=pl.CostEstimate(flops=flops, bytes_accessed=moved, transcendentals=exps),
        compiler_params=pltpu.CompilerParams(
            vmem_limit_bytes=VMEM_BYTES,
            collective_id=collective,
            has_side_effects=collective is not None,
        ),
    )


def whole(shape):
    return pl.BlockSpec(shape, lambda *_: (0,) * len(shape))


def scalars():
    return pl.BlockSpec(memory_space=pltpu.SMEM)


def lane_index(shape):
    return lax.broadcasted_iota(jnp.int32, shape, 1)


def normalize(values):
    center = values - jnp.mean(values, axis=-1, keepdims=True)
    spread = jnp.mean(center * center, axis=-1, keepdims=True)
    inverse = lax.rsqrt(spread + EPSILON)
    return center * inverse, inverse


def norm_back(grad, xhat, inverse):
    first = jnp.mean(grad, axis=-1, keepdims=True)
    second = jnp.mean(grad * xhat, axis=-1, keepdims=True)
    return inverse * (grad - first - xhat * second)


def pick(refs, which):
    value = refs[0][0]
    for index in range(1, len(refs)):
        value = jnp.where(which == index, refs[index][0], value)
    return value


class Exchange:
    def __init__(self, mesh_shape, row_tiles, turn=0):
        bits = {"seq": [], "dp": []}
        for axis in bits:
            bit = 1
            while bit < mesh_shape[axis]:
                bits[axis].append((axis, bit))
                bit *= 2
        turned = bits["dp"][turn:] + bits["dp"][:turn]
        self.bits = bits["seq"][:1] + turned + bits["seq"][1:]
        self.levels = len(self.bits)
        self.even = 0
        while self.even < self.levels and row_tiles % 2 == 0:
            row_tiles //= 2
            self.even += 1
        unit = 2 ** (self.levels - self.even)
        self.groups = 2**self.even
        self.real = row_tiles * 16
        self.padded = -(-row_tiles // unit) * unit * 16
        self.shard = self.padded // unit

    def sizes(self, level):
        if level < self.even:
            return (self.groups >> (level + 1), self.real)
        return (1, self.padded >> (level - self.even + 1))

    def receive_scratch(self, width):
        return [pltpu.VMEM(self.sizes(level) + (width,), BF16) for level in range(self.levels)]

    def place(self, level):
        axis, bit = self.bits[level]
        here = lax.axis_index(axis)
        value = (here // bit) % 2
        return value, {axis: here + bit * (1 - 2 * value)}

    def spot(self, level, first, flip):
        group, row = 0, 0
        for index in range(first, level + 1):
            value, _ = self.place(index)
            if flip and index == level:
                value = 1 - value
            if index < self.even:
                group = group + value * (self.groups >> (index + 1))
            else:
                row = row + value * (self.padded >> (index - self.even + 1))
        if level >= self.even:
            row = pl.multiple_of(row, 16)
        count, rows = self.sizes(level)
        return pl.ds(group, count), pl.ds(row, rows)

    def barrier(self):
        semaphore = pltpu.get_barrier_semaphore()
        for level in range(self.levels):
            _, partner = self.place(level)
            pl.semaphore_signal(
                semaphore, inc=1, device_id=partner, device_id_type=pl.DeviceIdType.MESH
            )
        pl.semaphore_wait(semaphore, self.levels)

    def copy(self, source, target, sends, recvs, level):
        _, partner = self.place(level)
        return pltpu.make_async_remote_copy(
            src_ref=source,
            dst_ref=target,
            send_sem=sends.at[level],
            recv_sem=recvs.at[level],
            device_id=partner,
            device_id_type=pl.DeviceIdType.MESH,
        )

    def reduce_copy(self, level, start_ref, acc_ref, got, sends, recvs):
        groups, rows = self.spot(level, min(level, 1), True)
        source = start_ref if level == 0 else acc_ref
        return self.copy(source.at[groups, rows], got[level], sends, recvs, level)

    def reduce_start(self, level, *refs):
        self.reduce_copy(level, *refs).start()

    def reduce_finish(self, level, start_ref, acc_ref, got, sends, recvs):
        self.reduce_copy(level, start_ref, acc_ref, got, sends, recvs).wait()
        count, rows = self.sizes(level)
        groups, spots = self.spot(level, min(level, 1), False)
        if level == 0:
            target_groups, target_rows = pl.ds(0, count), pl.ds(0, rows)
            if self.padded > self.real:
                acc_ref[:, self.real :, :] = jnp.zeros_like(acc_ref[:, self.real :, :])
        else:
            target_groups, target_rows = groups, spots
        source = start_ref if level == 0 else acc_ref

        def add(index, carry):
            one = pl.ds(groups.start + index, 1)
            to = pl.ds(target_groups.start + index, 1)
            value = source[one, spots, :].astype(F32) + got[level][pl.ds(index, 1)].astype(F32)
            acc_ref[to, target_rows, :] = value.astype(BF16)
            return carry

        lax.fori_loop(0, count, add, 0)

    def own_shard(self, ref, first):
        if self.levels > self.even:
            return ref.at[self.spot(self.levels - 1, first, False)]
        groups, _ = self.spot(self.levels - 1, first, False)
        return ref.at[groups, pl.ds(0, self.shard)]

    def gather_copy(self, level, full_ref, sends, recvs):
        piece = full_ref.at[self.spot(level, 0, False)]
        return self.copy(piece, piece, sends, recvs, level)

    def gather_start(self, level, *refs):
        self.gather_copy(level, *refs).start()

    def gather_finish(self, level, *refs):
        self.gather_copy(level, *refs).wait()


def modulation_kernel(lead_ref, emb_ref, ada_ref, bias_ref, mod_ref):
    rows = lax.broadcasted_iota(jnp.int32, (16, emb_ref.shape[0]), 0)
    columns = lane_index((16, emb_ref.shape[0]))
    onehot = jnp.zeros((16, emb_ref.shape[0]), F32)
    for step in range(lead_ref.shape[0]):
        onehot = jnp.where((rows == step) & (columns == lead_ref[step]), 1.0, onehot)
    condition = dot(onehot.astype(BF16), emb_ref[...])
    active = (condition * jax.nn.sigmoid(condition)).astype(BF16)
    mod_ref[...] = dot(active, ada_ref[...]) + bias_ref[...].astype(F32)


def project_kernel(sources, queries, *refs):
    x_refs = refs[:sources]
    mod_ref, w_ref = refs[sources : sources + 2]
    outs = refs[sources + 2 :]
    step, which = pl.program_id(0), pl.program_id(1)
    width = w_ref.shape[0]
    x = pick(x_refs, which).astype(F32)
    shift = mod_ref[pl.ds(step, 1), 0:width]
    scale = mod_ref[pl.ds(step, 1), width : 2 * width]
    xhat, _ = normalize(x)
    normed = (xhat * (1.0 + scale) + shift).astype(BF16)
    outs[0][0, 0] = normed
    start = 0 if queries else width
    projected = dot(normed, w_ref[:, start:])
    for part in range(len(outs) - 1):
        for pair in range(width // LANES):
            at = part * width + pair * LANES
            piece = projected[:, at : at + LANES]
            if queries and part == 0:
                piece = piece * (HD**-0.5 * LOG2E)
            outs[part + 1][0, pair, 0] = piece.astype(BF16)


def with_ones(values):
    low = lane_index(values.shape) < HD
    one = jnp.ones_like(values)
    return jnp.where(low, values, one), jnp.where(low, one, values)


def masked(values):
    low = lane_index(values.shape) < HD
    zero = jnp.zeros_like(values)
    return jnp.where(low, values, zero), jnp.where(low, zero, values)


def attend_local_kernel(rows, q_ref, k_ref, v_ref, acc_ref, ext_ref):
    ext_ref[0], ext_ref[1] = with_ones(v_ref[0, 0])

    def block(index, carry):
        at = pl.ds(pl.multiple_of(index * rows, rows), rows)
        for head, query in enumerate(masked(q_ref[0, 0, at, :])):
            weights = jnp.exp2(dot(query, k_ref[0, 0], NT)).astype(BF16)
            acc_ref[0, 0, head, at, :] = dot(weights, ext_ref[head])
        return carry

    lax.fori_loop(0, q_ref.shape[2] // rows, block, 0, unroll=True)


def attend_all_kernel(
    rows, q_ref, k_ref, v_ref, kr_ref, vr_ref, acc_ref, o_ref, qe_ref, ext_ref, total_ref
):
    ext_ref[0], ext_ref[1] = with_ones(vr_ref[0, 0])
    blocks = q_ref.shape[2] // rows

    def finish(at, query, first, second, top_first, top_second):
        lane = lane_index(query.shape)
        low = lane < HD
        swapped = jnp.where(low, second, first)
        total = pltpu.roll(swapped, HD, 1)
        o_ref[0, 0, at, :] = jnp.where(low, first, second) / total
        log_total = jnp.log2(swapped) + jnp.where(low, top_second, top_first)
        high = log_total.astype(BF16).astype(F32)
        middle = (log_total - high).astype(BF16).astype(F32)
        rest = log_total - high - middle
        spot = lane % HD
        extra = jnp.where(spot == 0, -high, jnp.where(spot == 1, -middle, -rest))
        extra = jnp.where(spot < 3, extra, 0.0).astype(BF16)
        qe_ref[0, 0, 0, at, :] = jnp.where(low, query, extra)
        qe_ref[0, 0, 1, at, :] = jnp.where(low, extra, query)
        return total

    def block(index, carry):
        at = pl.ds(pl.multiple_of(index * rows, rows), rows)
        query = q_ref[0, 0, at, :]
        sums = []
        for head, own in enumerate(masked(query)):
            weights = jnp.exp2(dot(own, kr_ref[0, 0], NT)).astype(BF16)
            sums.append(acc_ref[0, 0, head, at, :] + dot(weights, ext_ref[head]))
        total_ref[at, :] = finish(at, query, sums[0], sums[1], 0.0, 0.0)
        return carry

    lax.fori_loop(0, blocks, block, 0, unroll=True)
    total = total_ref[...]
    bad = jnp.sum(jnp.where((total > 1e-25) & (total < 1e25), 0.0, 1.0))

    @pl.when(bad > 0.0)
    def _():
        own_ext = with_ones(v_ref[0, 0])

        def again(index, carry):
            at = pl.ds(pl.multiple_of(index * rows, rows), rows)
            query = q_ref[0, 0, at, :]
            sums, tops = [], []
            for head, own in enumerate(masked(query)):
                scores = dot(own, k_ref[0, 0], NT)
                others = dot(own, kr_ref[0, 0], NT)
                top = jnp.maximum(
                    jnp.max(scores, axis=-1, keepdims=True),
                    jnp.max(others, axis=-1, keepdims=True),
                )
                sums.append(
                    dot(jnp.exp2(scores - top).astype(BF16), own_ext[head])
                    + dot(jnp.exp2(others - top).astype(BF16), ext_ref[head])
                )
                tops.append(top)
            finish(at, query, sums[0], sums[1], tops[0], tops[1])
            return carry

        lax.fori_loop(0, blocks, again, 0)


def gelu_parts(values):
    cumulative = 0.5 * (1.0 + lax.erf(values * 0.7071067811865476))
    density = jnp.exp2(values * values * (-0.5 * LOG2E)) * 0.3989422804014327
    return values * cumulative, cumulative + values * density


def patch_kernel(
    rows,
    chunk,
    active_ref,
    own_x,
    sib_x,
    own_ct,
    sib_ct,
    mod_ref,
    o_ref,
    out_w,
    fc1_w,
    fc2_w,
    final_ref,
    gm_ref,
    ge_ref,
    sums_ref,
    stack_one,
    stack_two,
    hidden_s,
    gpre_s,
    n2_s,
    g2_s,
    g1_s,
    mixed_s,
    gout_s,
    gfc1_s,
    gfc2_s,
):
    step, half = pl.program_id(0), pl.program_id(1)
    width, hidden_width = fc1_w.shape
    patches = own_x.shape[1]
    active = active_ref[step]

    def piece(index):
        return mod_ref[pl.ds(step, 1), index * width : (index + 1) * width]

    gate1, shift2, scale2, gate2 = piece(2), piece(3), piece(4), piece(5)

    @pl.when(half == 0)
    def _():
        sums_ref[...] = jnp.zeros_like(sums_ref)

    @pl.when((step == 0) & (half == 0))
    def _():
        gout_s[...] = jnp.zeros_like(gout_s)
        gfc1_s[...] = jnp.zeros_like(gfc1_s)
        gfc2_s[...] = jnp.zeros_like(gfc2_s)

    def block(index, carry):
        at = pl.ds(pl.multiple_of(index * rows, rows), rows)
        x = jnp.where(half == 0, own_x[0, at, :], sib_x[0, at, :]).astype(F32)
        final_grad = jnp.where(half == 0, own_ct[0, at, :], sib_ct[0, at, :]).astype(F32) * active
        outs = [o_ref[0, pair, at, :] for pair in range(width // LANES)]
        mixed = jnp.concatenate([o.astype(BF16) for o in outs], axis=-1)
        mixed_s[at, :] = mixed
        branch_one = dot(mixed, out_w[...])
        middle = x + gate1 * branch_one
        xhat, inverse = normalize(middle)
        n2 = (xhat * (1.0 + scale2) + shift2).astype(BF16)
        n2_s[at, :] = n2
        g2 = (gate2 * final_grad).astype(BF16)
        g2_s[at, :] = g2
        branch_two = jnp.zeros((rows, width), F32)
        gy = jnp.zeros((rows, width), F32)
        for start in range(0, hidden_width, chunk):
            columns = slice(start, start + chunk)
            pre = dot(n2, fc1_w[:, columns])
            grad_hidden = dot(g2, fc2_w[columns, :], NT)
            hidden, slope = gelu_parts(pre)
            hidden = hidden.astype(BF16)
            grad_pre = (slope * grad_hidden).astype(BF16)
            hidden_s[at, columns] = hidden
            gpre_s[at, columns] = grad_pre
            branch_two += dot(hidden, fc2_w[columns, :])
            gy += dot(grad_pre, fc1_w[:, columns], NT)
        final_ref[0, 0, at, :] = ((middle + gate2 * branch_two) * active).astype(BF16)
        gm = final_grad + norm_back(gy * (1.0 + scale2), xhat, inverse)
        gm_ref[0, 0, at, :] = gm
        g1 = (gate1 * gm).astype(BF16)
        g1_s[at, :] = g1
        sums = [branch_one * gm, gy, gy * xhat, branch_two * final_grad]
        for row, value in enumerate(sums):
            sums_ref[0, row : row + 1, :] += jnp.sum(value, axis=0, keepdims=True)
        grad_mixed = dot(g1, out_w[...], NT).astype(BF16)
        lane = lane_index((rows, LANES))
        low = lane < HD
        spot = lane % HD
        for pair, o in enumerate(outs):
            grad = grad_mixed[:, pair * LANES : (pair + 1) * LANES]
            product = grad.astype(F32) * o
            first = jnp.sum(jnp.where(low, product, 0.0), axis=-1, keepdims=True)
            second = jnp.sum(jnp.where(low, 0.0, product), axis=-1, keepdims=True)
            inner = jnp.where(low, second, first)
            high = inner.astype(BF16).astype(F32)
            mid = (inner - high).astype(BF16).astype(F32)
            extra = jnp.where(spot == 0, -high, jnp.where(spot == 1, -mid, high + mid - inner))
            extra = jnp.where(spot < 3, extra, 0.0).astype(BF16)
            ge_ref[0, pair, 0, at, :] = jnp.where(low, grad, extra)
            ge_ref[0, pair, 1, at, :] = jnp.where(low, extra, grad)
        return carry

    lax.fori_loop(0, patches // rows, block, 0)
    gout_s[...] += dot(mixed_s[...], g1_s[...], TN)
    for start in range(0, hidden_width, chunk):
        columns = slice(start, start + chunk)
        gfc1_s[:, columns] += dot(n2_s[...], gpre_s[:, columns], TN)
        gfc2_s[:, columns] += dot(g2_s[...], hidden_s[:, columns], TN)

    @pl.when((step == pl.num_programs(0) - 1) & (half == pl.num_programs(1) - 1))
    def _():
        blocks = hidden_width // width
        for index in range(blocks):
            columns = slice(index * width, (index + 1) * width)
            stack_one[index] = gfc1_s[:, columns].astype(BF16)
            stack_two[index] = gfc2_s[:, columns].T.astype(BF16)
        stack_two[blocks] = gout_s[...].astype(BF16)


def attend_back_kernel(rows, first_pass, exchanges, grid_steps, *refs):
    count = len(exchanges)
    qe_ref, ge_ref, k_ref, v_ref = refs[:4]
    refs = refs[4:]
    if first_pass:
        gives, refs = refs[:count], refs[count:]
        dq_ref, dk_ref, dv_ref = refs[:3]
        shards, refs = refs[3 : 3 + count], refs[3 + count :]
    else:
        dq_in, shards, refs = refs[0], refs[1 : 1 + count], refs[1 + count :]
        dq_ref, dk_ref, dv_ref = refs[:3]
        fulls, refs = refs[3 : 3 + count], refs[3 + count :]
    acc_s, refs = refs[0], refs[1:]
    states = []
    for index, exchange in enumerate(exchanges):
        sends, recvs = refs[1], refs[2]
        if first_pass:
            got = refs[3 : 3 + exchange.levels]
            states.append((gives[index], refs[0], got, sends, recvs))
            refs = refs[3 + exchange.levels :]
        else:
            states.append((refs[0], sends, recvs))
            refs = refs[3:]
    per_step = k_ref.shape[2] // rows
    slots = pl.num_programs(0) * pl.num_programs(1) * per_step
    static_slots = grid_steps * per_step
    first_slot = (pl.program_id(0) * pl.num_programs(1) + pl.program_id(1)) * per_step
    levels = exchanges[0].levels
    if first_pass:
        acc_s[...] = jnp.zeros_like(acc_s)
    else:
        acc_s[...] = dq_in[0, 0].T

    def reduce_action(order):
        if order == 0:
            exchanges[0].barrier()
        for exchange, state, shard in zip(exchanges, states, shards):
            if order > 0:
                exchange.reduce_finish(order - 1, *state)
            if order < levels:
                exchange.reduce_start(order, *state)
            else:
                shard[...] = exchange.own_shard(state[1], 1)[...][0]

    def gather_action(order):
        if order == 0:
            exchanges[0].barrier()
        for exchange, state, shard in zip(exchanges, states, shards):
            if order == 0:
                own = exchange.own_shard(state[0], 0)
                own[...] = shard[...][None]
            else:
                exchange.gather_finish(levels - order, *state)
            if order < levels:
                exchange.gather_start(levels - 1 - order, *state)
        if order == levels:
            copies = [
                pltpu.make_async_copy(state[0], full, refs[index])
                for index, (state, full) in enumerate(zip(states, fulls))
            ]
            for copy in copies:
                copy.start()
            for copy in copies:
                copy.wait()

    action = reduce_action if first_pass else gather_action
    weights = [5.0, 10.0, 9.0, 6.0] + [4.0] * (levels - 4)
    if not first_pass:
        weights = weights[::-1]
    marks, total = [0], 0.0
    for weight in weights:
        total += weight
        marks.append(total)
    marks = [min(int(mark * (static_slots - 1) / total + 0.5), static_slots - 1) for mark in marks]

    def block(index, carry):
        for order, mark in enumerate(marks[:-1]):
            pl.when(first_slot + index == mark)(functools.partial(action, order))
        at = pl.ds(pl.multiple_of(index * rows, rows), rows)
        keys = k_ref[0, 0, at, :]
        values = v_ref[0, 0, at, :]
        lane = lane_index(keys.shape)
        low = lane < HD
        ones = jnp.where(lane % HD < 3, 1.0, 0.0).astype(BF16)
        zero = jnp.zeros_like(keys)
        grads = []
        for head in range(2):
            own = low if head == 0 else jnp.logical_not(low)
            query = qe_ref[0, 0, head]
            grad = ge_ref[0, 0, head]
            probs = jnp.exp2(dot(jnp.where(own, keys, ones), query, NT))
            grad_probs = dot(jnp.where(own, values, ones), grad, NT)
            grad_scores = (probs * grad_probs).astype(BF16)
            grads.append((dot(grad_scores, query), dot(probs.astype(BF16), grad)))
            acc_s[...] += dot(jnp.where(own, keys, zero), grad_scores, TN)
        dk_ref[0, 0, at, :] = (jnp.where(low, grads[0][0], grads[1][0]) * LN2).astype(BF16)
        dv_ref[0, 0, at, :] = jnp.where(low, grads[0][1], grads[1][1]).astype(BF16)
        return carry

    lax.fori_loop(0, per_step, block, 0)
    pl.when(first_slot + per_step == slots)(functools.partial(action, levels))
    if first_pass:
        dq_ref[0, 0] = acc_s[...].T
    else:
        dq_ref[0, 0] = (acc_s[...].T * HD**-0.5).astype(BF16)


def project_back_kernel(parts, last, *refs):
    grads = refs[:parts]
    normed_ref, w_ref = refs[parts : parts + 2]
    rest = refs[parts + 2 :]
    if last:
        add_ref, dx_ref, gw_ref, gw_s = rest
    else:
        dx_ref, gw_ref, gw_s = rest
    step, which = pl.program_id(0), pl.program_id(1)
    width = w_ref.shape[0]
    start = w_ref.shape[1] - parts * width
    joined = jnp.concatenate(
        [ref[0, pair] for ref in grads for pair in range(ref.shape[1])], axis=-1
    )
    dx_ref[0, 0] = dot(joined, w_ref[:, start:], NT).astype(dx_ref.dtype)

    @pl.when((step == 0) & (which == 0))
    def _():
        gw_s[...] = jnp.zeros_like(gw_s)
        if last:
            gw_s[:, width:] = add_ref[...]

    gw_s[...] += dot(normed_ref[0, 0], joined, TN)

    @pl.when((step == pl.num_programs(0) - 1) & (which == pl.num_programs(1) - 1))
    def _():
        if last:
            for part in range(parts):
                gw_ref[part] = gw_s[:, part * width : (part + 1) * width].astype(BF16)
        else:
            gw_ref[...] = gw_s[...]


def finish_kernel(remote, *refs):
    lead_ref, own_x, sib_x, mod_ref, gm_ref, sums_ref, dx_ref = refs[:7]
    others = refs[7 : 7 + remote]
    grad_ref, gmod_ref, acc_s = refs[7 + remote :]
    step, half = pl.program_id(0), pl.program_id(1)
    width = own_x.shape[2]
    x = jnp.where(half == 0, own_x[0], sib_x[0]).astype(F32)
    scale = mod_ref[pl.ds(step, 1), width : 2 * width]
    xhat, inverse = normalize(x)
    gy = dx_ref[0, 0]
    for other in others:
        gy = gy + other[0, 0].astype(F32)
    grad_ref[0, 0] = (gm_ref[0, 0] + norm_back(gy * (1.0 + scale), xhat, inverse)).astype(BF16)

    @pl.when((step == 0) & (half == 0))
    def _():
        acc_s[...] = jnp.zeros_like(acc_s)

    acc_s[pl.ds(step, 1), :] += jnp.sum(gy, axis=0, keepdims=True)
    acc_s[pl.ds(step + 2, 1), :] += jnp.sum(gy * xhat, axis=0, keepdims=True)

    @pl.when(half == 1)
    def _():
        for row in range(4):
            acc_s[pl.ds(step + 4 + 2 * row, 1), :] = sums_ref[0, row : row + 1, :]
        chosen = lane_index((1, width)) == lead_ref[step]
        acc_s[pl.ds(step + 12, 1), :] = jnp.where(chosen, 1.0, 0.0)

    @pl.when((step == 1) & (half == 1))
    def _():
        gmod_ref[...] = acc_s[...].astype(BF16)


def tail_kernel(exchange, give_ref, gmod_ref, full_ref, all_ref, sum_s, full_s, all_s, *refs):
    sends, recvs, back_sends, back_recvs, all_sends, all_recvs, *got = refs
    levels = exchange.levels
    index = 0
    scale = 1
    for level, (axis, bit) in enumerate(exchange.bits):
        value, _ = exchange.place(level)
        index = index + value * scale
        scale *= 2
    exchange.barrier()
    all_s[pl.ds(index, 1)] = gmod_ref[...][None]

    def gather_all(level):
        size = 1 << level
        piece = all_s.at[pl.ds((index // size) * size, size)]
        return exchange.copy(piece, piece, all_sends, all_recvs, level)

    refs_of = (give_ref, sum_s, got, sends, recvs)
    for level in range(levels):
        exchange.reduce_start(level, *refs_of)
        gather_all(level).start()
        exchange.reduce_finish(level, *refs_of)
        gather_all(level).wait()
    own = exchange.own_shard(full_s, 0)
    own[...] = exchange.own_shard(sum_s, 1)[...]
    for level in reversed(range(levels)):
        exchange.gather_start(level, full_s, back_sends, back_recvs)
        exchange.gather_finish(level, full_s, back_sends, back_recvs)
    all_ref[...] = all_s[...]
    full_ref[...] = full_s[...]


def unstack(exchange, full_ref, targets, width):
    row = 0
    end = exchange.groups * exchange.real
    while row < end:
        group, inside = divmod(row, exchange.real)
        block, place = divmod(row, width)
        count = min(exchange.real - inside, width - place)
        target, first_row, first_column = targets[block]
        target[
            first_row + place : first_row + place + count, first_column : first_column + width
        ] = full_ref[group, inside : inside + count, :].astype(F32)
        row += count


def final_kernel(early, late, gmod_ref, emb_ref, ada_ref, one_ref, two_ref, late_ref, *outs):
    gemb_ref, gada_ref, gbada_ref, gqkv_ref, gout_ref, gfc1_ref, gfc2_ref = outs
    size = gout_ref.shape[0]
    blocks = gfc1_ref.shape[1] // size
    unstack(late, late_ref, [(gqkv_ref, 0, part * size) for part in range(3)], size)
    unstack(early[0], one_ref, [(gfc1_ref, 0, block * size) for block in range(blocks)], size)
    rest = [(gfc2_ref, block * size, 0) for block in range(blocks)] + [(gout_ref, 0, 0)]
    unstack(early[1], two_ref, rest, size)
    table_rows, width = emb_ref.shape
    count = gmod_ref.shape[0]
    table = emb_ref[...].astype(F32)
    gate = jax.nn.sigmoid(table)
    slope = gate * (1.0 + table * (1.0 - gate))
    table_act = (table * gate).astype(BF16)
    piece = (lane_index((1, count)) % 16) // 2
    grads = gmod_ref[...]
    part = min(count, 512)
    row = lax.broadcasted_iota(jnp.int32, (part, part), 0)
    column = lane_index((part, part))
    spread = jnp.where(row == (column // 16) * 16 + 12 + column % 2, 1.0, 0.0).astype(BF16)
    leads = [
        dot(grads[start : start + part, :LANES], spread, TN)[:table_rows]
        for start in range(0, count, part)
    ]
    leads = jnp.concatenate(leads, axis=-1)
    total = jnp.zeros((table_rows, width), F32)
    for index in range(6):
        columns = slice(index * width, (index + 1) * width)
        chosen = jnp.where(piece == index, leads, 0.0).astype(BF16)
        acts = dot(table_act, chosen, TN).astype(BF16)
        gada_ref[:, columns] = dot(acts, grads)
        by_lead = dot(chosen, grads)
        gbada_ref[:, columns] = jnp.sum(by_lead, axis=0, keepdims=True)
        high = by_lead.astype(BF16)
        low = (by_lead - high.astype(F32)).astype(BF16)
        total += dot(high, ada_ref[:, columns], NT) + dot(low, ada_ref[:, columns], NT)
    gemb_ref[...] = total * slope


def local(
    mesh_shape, inputs, cotangent, counts, lead_steps, emb_table, w_ada, b_ada, w_qkv, w_out, w_fc1, w_fc2
):
    slots, items, patches, width = inputs.shape
    chips = mesh_shape["seq"] // 2
    blocks = w_fc1.shape[1] // w_fc1.shape[0]
    steps = slots * items // 2
    hidden_width = w_fc1.shape[1]
    pairs = width // LANES
    rows = 2 * patches
    remote = 2 * (chips - 1)
    far_rows = remote * patches
    spot = lax.axis_index("seq")
    core = lax.rem(spot, 2)
    devices = 2 * chips

    def send(values, shift, cross):
        pairs_list = []
        for source in range(devices):
            chip, side = source // 2, source % 2
            pairs_list.append((source, ((chip + shift) % chips) * 2 + (1 - side if cross else side)))
        return lax.ppermute(values, "seq", pairs_list)

    x_steps = inputs.reshape(2, steps, patches, width)
    ct_steps = cotangent.reshape(2, steps, patches, width)
    own_x = lax.dynamic_index_in_dim(x_steps, core, 0, keepdims=False)
    other_x = lax.dynamic_index_in_dim(x_steps, 1 - core, 0, keepdims=False)
    own_ct = lax.dynamic_index_in_dim(ct_steps, core, 0, keepdims=False)
    other_ct = lax.dynamic_index_in_dim(ct_steps, 1 - core, 0, keepdims=False)
    sib_x = send(other_x, 0, True)
    far_x = []
    for shift in range(1, chips):
        far_x.append(send(own_x, shift, False))
        far_x.append(send(other_x, shift, True))
    sib_ct = send(other_ct, 0, True)
    step_ids = core * steps + jnp.arange(steps, dtype=jnp.int32)
    active = (step_ids < counts[0]).astype(F32)
    leads_own = lax.dynamic_slice_in_dim(lead_steps[0], core * steps, steps)
    mod = call(
        modulation_kernel,
        "modulation",
        (),
        [scalars(), whole(emb_table.shape), whole(w_ada.shape), whole((1, 6 * width))],
        whole((16, 6 * width)),
        jax.ShapeDtypeStruct((16, 6 * width), F32),
        flops=2 * 16 * width * 6 * width,
        moved=2 * w_ada.size,
    )(leads_own, emb_table, w_ada, b_ada.reshape(1, -1))

    step_block = pl.BlockSpec((1, patches, width), lambda j, i: (j, 0, 0))
    patch_block = pl.BlockSpec((1, 1, patches, width), lambda j, i: (j, i, 0, 0))

    def project(sources, queries, name):
        parts = 3 if queries else 2
        count = len(sources)
        head_block = pl.BlockSpec((1, pairs, 1, patches, LANES), lambda j, i: (j, 0, i, 0, 0))
        outs = call(
            functools.partial(project_kernel, count, queries),
            name,
            (steps, count),
            [step_block] * count + [whole(mod.shape), whole(w_qkv.shape)],
            [patch_block] + [head_block] * parts,
            [jax.ShapeDtypeStruct((steps, count, patches, width), BF16)]
            + [jax.ShapeDtypeStruct((steps, pairs, count, patches, LANES), BF16)] * parts,
            flops=2 * steps * count * patches * width * parts * width,
            moved=2 * steps * count * patches * width * (2 + parts),
        )(*sources, mod, w_qkv)
        return [outs[0]] + [o.reshape(steps, pairs, count * patches, LANES) for o in outs[1:]]

    n1, q, k, v = project([own_x, sib_x], True, "project_near")

    def head_rows(count):
        return pl.BlockSpec((1, 1, count, LANES), lambda j, p: (j, p, 0, 0))

    both_heads = pl.BlockSpec((1, 1, 2, rows, LANES), lambda j, p: (j, p, 0, 0, 0))
    query_rows = min(512, rows)
    near_work = 4 * steps * pairs * 2 * rows * LANES * rows
    far_work = 4 * steps * pairs * 2 * rows * LANES * far_rows
    acc = call(
        functools.partial(attend_local_kernel, query_rows),
        "attend_near",
        (steps, pairs),
        [head_rows(rows)] * 3,
        both_heads,
        jax.ShapeDtypeStruct((steps, pairs, 2, rows, LANES), F32),
        [pltpu.VMEM((2, rows, LANES), BF16)],
        flops=near_work,
        exps=steps * pairs * 2 * rows * rows,
    )(q, k, v)

    n1r, kr, vr = project(far_x, False, "project_far")
    o, qe = call(
        functools.partial(attend_all_kernel, query_rows),
        "attend_far",
        (steps, pairs),
        [head_rows(rows)] * 3 + [head_rows(far_rows)] * 2 + [both_heads],
        [head_rows(rows), both_heads],
        [
            jax.ShapeDtypeStruct((steps, pairs, rows, LANES), F32),
            jax.ShapeDtypeStruct((steps, pairs, 2, rows, LANES), BF16),
        ],
        [pltpu.VMEM((2, far_rows, LANES), BF16), pltpu.VMEM((rows, LANES), F32)],
        flops=far_work,
        exps=steps * pairs * 2 * rows * far_rows,
    )(q, k, v, kr, vr, acc)

    block_rows = min(256, patches)
    outs = call(
        functools.partial(patch_kernel, block_rows, 512),
        "patchwise",
        (steps, 2),
        [scalars()]
        + [step_block] * 4
        + [
            whole(mod.shape),
            pl.BlockSpec((1, pairs, patches, LANES), lambda j, i: (j, 0, i, 0)),
            whole(w_out.shape),
            whole(w_fc1.shape),
            whole(w_fc2.shape),
        ],
        [
            patch_block,
            patch_block,
            pl.BlockSpec((1, pairs, 2, patches, LANES), lambda j, i: (j, 0, 0, i, 0)),
            pl.BlockSpec((1, 8, width), lambda j, i: (j, 0, 0)),
            whole((blocks, width, width)),
            whole((blocks + 1, width, width)),
        ],
        [
            jax.ShapeDtypeStruct((steps, 2, patches, width), BF16),
            jax.ShapeDtypeStruct((steps, 2, patches, width), F32),
            jax.ShapeDtypeStruct((steps, pairs, 2, rows, LANES), BF16),
            jax.ShapeDtypeStruct((steps, 8, width), F32),
            jax.ShapeDtypeStruct((blocks, width, width), BF16),
            jax.ShapeDtypeStruct((blocks + 1, width, width), BF16),
        ],
        [pltpu.VMEM((patches, hidden_width), BF16)] * 2
        + [pltpu.VMEM((patches, width), BF16)] * 4
        + [
            pltpu.VMEM((width, width), F32),
            pltpu.VMEM((width, hidden_width), F32),
            pltpu.VMEM((width, hidden_width), F32),
        ],
        flops=6 * steps * rows * width * (2 * hidden_width + width),
        moved=steps * rows * width * 20,
        exps=2 * steps * rows * hidden_width,
    )(active, own_x, sib_x, own_ct, sib_ct, mod, o, w_out, w_fc1, w_fc2)
    final, gm, ge, sums, stack_one, stack_two = outs
    final_other = send(final[:, 1], 0, True)
    early = [Exchange(mesh_shape, blocks * width // 16, 0), Exchange(mesh_shape, (blocks + 1) * width // 16, 1)]
    late = Exchange(mesh_shape, 3 * width // 16)
    gives = [g.reshape(e.groups, e.real, width) for e, g in zip(early, (stack_one, stack_two))]

    def attend_back(keys, values, extra, first, name):
        count = keys.shape[2]
        key_rows = min(512, count)
        in_specs = [both_heads] * 2 + [head_rows(count)] * 2
        out_specs = [head_rows(rows), head_rows(count), head_rows(count)]
        out_shape = [
            jax.ShapeDtypeStruct((steps, pairs, rows, LANES), F32 if first else BF16),
            jax.ShapeDtypeStruct((steps, pairs, count, LANES), BF16),
            jax.ShapeDtypeStruct((steps, pairs, count, LANES), BF16),
        ]
        scratch = [pltpu.VMEM((LANES, rows), F32)]
        if not first:
            in_specs += [head_rows(rows)]
        for exchange in early:
            shape = (exchange.groups, exchange.padded, width)
            shard = (exchange.shard, width)
            sems = [pltpu.SemaphoreType.DMA((exchange.levels,))] * 2
            if first:
                in_specs += [whole((exchange.groups, exchange.real, width))]
                out_specs += [whole(shard)]
                out_shape += [jax.ShapeDtypeStruct(shard, BF16)]
                half = (exchange.groups // 2, exchange.padded, width)
                scratch += [pltpu.VMEM(half, BF16)] + sems + exchange.receive_scratch(width)
            else:
                in_specs += [whole(shard)]
                out_specs += [pl.BlockSpec(memory_space=pl.ANY)]
                out_shape += [jax.ShapeDtypeStruct(shape, BF16)]
                scratch += [pltpu.VMEM(shape, BF16)] + sems
        if not first:
            scratch += [pltpu.SemaphoreType.DMA] * len(early)
        return call(
            functools.partial(attend_back_kernel, key_rows, first, early, steps * pairs),
            name,
            (steps, pairs),
            in_specs,
            out_specs,
            out_shape,
            scratch,
            flops=10 * steps * pairs * 2 * rows * count * LANES,
            exps=steps * pairs * 2 * rows * count,
            collective=1 if first else 2,
        )(qe, ge, keys, values, *extra)

    def project_back(grads, normed, before, name):
        parts = len(grads)
        count = normed.shape[1]
        last = before is not None
        grad_block = pl.BlockSpec((1, pairs, patches, LANES), lambda j, i: (j, 0, i, 0))
        return call(
            functools.partial(project_back_kernel, parts, last),
            name,
            (steps, count),
            [grad_block] * parts
            + [patch_block, whole(w_qkv.shape)]
            + ([whole(before.shape)] if last else []),
            [patch_block, whole((parts, width, width) if last else (width, parts * width))],
            [
                jax.ShapeDtypeStruct((steps, count, patches, width), F32 if last else BF16),
                jax.ShapeDtypeStruct((parts, width, width), BF16)
                if last
                else jax.ShapeDtypeStruct((width, parts * width), F32),
            ],
            [pltpu.VMEM((width, parts * width), F32)],
            flops=4 * steps * count * patches * width * parts * width,
            moved=steps * count * patches * width * 10,
        )(*(list(grads) + [normed, w_qkv] + ([before] if last else [])))

    dq_part, dkr, dvr, *shards = attend_back(kr, vr, gives, True, "attend_back_far")
    dx_far, gw_part = project_back([dkr, dvr], n1r, None, "project_back_far")
    dx_got = [send(dx_far[:, 2 * r - 2 : 2 * r], -r, False) for r in range(1, chips)]
    dq, dk, dv, *early_sums = attend_back(k, v, [dq_part, *shards], False, "attend_back_near")
    dx_near, g_qkv = project_back([dq, dk, dv], n1, gw_part, "project_back_near")

    grad_x, gmod = call(
        functools.partial(finish_kernel, len(dx_got)),
        "finish",
        (steps, 2),
        [scalars(), step_block, step_block, whole(mod.shape), patch_block]
        + [pl.BlockSpec((1, 8, width), lambda j, i: (j, 0, 0))]
        + [patch_block] * (1 + len(dx_got)),
        [patch_block, whole((16, width))],
        [
            jax.ShapeDtypeStruct((steps, 2, patches, width), BF16),
            jax.ShapeDtypeStruct((16, width), BF16),
        ],
        [pltpu.VMEM((16, width), F32)],
        flops=20 * steps * rows * width,
        moved=steps * rows * width * 16,
    )(leads_own, own_x, sib_x, mod, gm, sums, dx_near, *dx_got)
    grad_other = send(grad_x[:, 1], 0, True)

    late_shape = (late.groups, late.padded, width)
    all_shape = (mesh_shape["dp"] * mesh_shape["seq"], 16, width)
    late_sum, gathered = call(
        functools.partial(tail_kernel, late),
        "sum_late",
        (),
        [whole((late.groups, late.real, width)), whole(gmod.shape)],
        [whole(late_shape), whole(all_shape)],
        [jax.ShapeDtypeStruct(late_shape, BF16), jax.ShapeDtypeStruct(all_shape, BF16)],
        [
            pltpu.VMEM((late.groups // 2, late.padded, width), BF16),
            pltpu.VMEM(late_shape, BF16),
            pltpu.VMEM(all_shape, BF16),
        ]
        + [pltpu.SemaphoreType.DMA((late.levels,))] * 6
        + late.receive_scratch(width),
        collective=3,
    )(g_qkv.reshape(late.groups, late.real, width), gmod)
    gathered = gathered.reshape(-1, width)
    g_emb, g_ada, g_bada, g_qkv, g_out, g_fc1, g_fc2 = call(
        functools.partial(final_kernel, early, late),
        "final",
        (),
        [whole(gathered.shape), whole(emb_table.shape), whole(w_ada.shape)]
        + [whole(one.shape) for one in early_sums]
        + [whole(late_sum.shape)],
        [whole(emb_table.shape), whole(w_ada.shape), whole((1, 6 * width))]
        + [whole(w.shape) for w in (w_qkv, w_out, w_fc1, w_fc2)],
        [
            jax.ShapeDtypeStruct(emb_table.shape, F32),
            jax.ShapeDtypeStruct(w_ada.shape, F32),
            jax.ShapeDtypeStruct((1, 6 * width), F32),
        ]
        + [jax.ShapeDtypeStruct(w.shape, F32) for w in (w_qkv, w_out, w_fc1, w_fc2)],
        flops=2 * gathered.shape[0] * width * 6 * width,
        moved=6 * w_ada.size,
    )(gathered, emb_table, w_ada, *early_sums, late_sum)

    def join(mine, got):
        both = jnp.where(
            core == 0, jnp.concatenate([mine, got]), jnp.concatenate([got, mine])
        )
        return both.reshape(inputs.shape)

    return (
        join(final[:, 0], final_other),
        join(grad_x[:, 0], grad_other),
        g_emb,
        g_ada,
        g_bada.reshape(-1),
        g_qkv,
        g_out,
        g_fc1,
        g_fc2,
    )


def solution(mesh):
    tokens = P(None, "dp", "seq", None)
    return jax.shard_map(
        functools.partial(local, dict(mesh.shape)),
        mesh=mesh,
        in_specs=(tokens, tokens, P("dp"), P("dp", None)) + (P(),) * 7,
        out_specs=(tokens, tokens) + (P(),) * 7,
        check_vma=False,
    )
```

```python
import functools

import jax
import jax.numpy as jnp
from jax import lax
from jax.experimental import pallas as pl
from jax.experimental.pallas import tpu as pltpu
from jax.sharding import PartitionSpec as P

HD = 64
LANES = 128
EPSILON = 1e-06
LOG2E = 1.4426950408889634
LN2 = 0.6931471805599453
NN = (((1,), (0,)), ((), ()))
NT = (((1,), (1,)), ((), ()))
TN = (((0,), (0,)), ((), ()))
F32 = jnp.float32
BF16 = jnp.bfloat16
VMEM_BYTES = 56 * 1024 * 1024


def dot(a, b, dims=NN):
    return lax.dot_general(a, b, dims, preferred_element_type=F32)


def call(
    body,
    name,
    grid,
    in_specs,
    out_specs,
    out_shape,
    scratch=(),
    flops=0,
    moved=0,
    exps=0,
    collective=None,
):
    return pl.pallas_call(
        body,
        name=name,
        grid=grid,
        in_specs=in_specs,
        out_specs=out_specs,
        out_shape=out_shape,
        scratch_shapes=list(scratch),
        cost_estimate=pl.CostEstimate(flops=flops, bytes_accessed=moved, transcendentals=exps),
        compiler_params=pltpu.CompilerParams(
            vmem_limit_bytes=VMEM_BYTES,
            collective_id=collective,
            has_side_effects=collective is not None,
        ),
    )


def whole(shape):
    return pl.BlockSpec(shape, lambda *_: (0,) * len(shape))


def scalars():
    return pl.BlockSpec(memory_space=pltpu.SMEM)


def lane_index(shape):
    return lax.broadcasted_iota(jnp.int32, shape, 1)


def first_step(steps):
    return lax.rem(lax.axis_index("seq"), 2) * steps


def normalize(values):
    center = values - jnp.mean(values, axis=-1, keepdims=True)
    spread = jnp.mean(center * center, axis=-1, keepdims=True)
    inverse = lax.rsqrt(spread + EPSILON)
    return center * inverse, inverse


def norm_back(grad, xhat, inverse):
    first = jnp.mean(grad, axis=-1, keepdims=True)
    second = jnp.mean(grad * xhat, axis=-1, keepdims=True)
    return inverse * (grad - first - xhat * second)


def pick(refs, which):
    value = refs[0][0]
    for index in range(1, len(refs)):
        value = jnp.where(which == index, refs[index][0], value)
    return value


class Exchange:
    def __init__(self, mesh_shape, row_tiles, turn=0):
        bits = {"seq": [], "dp": []}
        for axis in bits:
            bit = 1
            while bit < mesh_shape[axis]:
                bits[axis].append((axis, bit))
                bit *= 2
        turned = bits["dp"][turn:] + bits["dp"][:turn]
        self.bits = bits["seq"][:1] + turned + bits["seq"][1:]
        self.all_levels = len(self.bits)
        self.levels = 1 + len(turned)
        self.even = 0
        while self.even < self.levels and row_tiles % 2 == 0:
            row_tiles //= 2
            self.even += 1
        unit = 2 ** (self.levels - self.even)
        self.groups = 2**self.even
        self.real = row_tiles * 16
        self.padded = -(-row_tiles // unit) * unit * 16
        self.shard = self.padded // unit

    def sizes(self, level):
        if level < self.even:
            return (self.groups >> (level + 1), self.real)
        return (1, self.padded >> (level - self.even + 1))

    def receive_scratch(self, width):
        last = self.levels - 1
        return [
            pltpu.VMEM(self.sizes(min(level, last)) + (width,), BF16)
            for level in range(self.all_levels)
        ]

    def place(self, level):
        axis, bit = self.bits[level]
        here = lax.axis_index(axis)
        value = (here // bit) % 2
        return value, {axis: here + bit * (1 - 2 * value)}

    def spot(self, level, first, flip):
        group, row = 0, 0
        for index in range(first, level + 1):
            value, _ = self.place(index)
            if flip and index == level:
                value = 1 - value
            if index < self.even:
                group = group + value * (self.groups >> (index + 1))
            else:
                row = row + value * (self.padded >> (index - self.even + 1))
        if level >= self.even:
            row = pl.multiple_of(row, 16)
        count, rows = self.sizes(level)
        return pl.ds(group, count), pl.ds(row, rows)

    def barrier(self):
        semaphore = pltpu.get_barrier_semaphore()
        for level in range(self.all_levels):
            _, partner = self.place(level)
            pl.semaphore_signal(
                semaphore, inc=1, device_id=partner, device_id_type=pl.DeviceIdType.MESH
            )
        pl.semaphore_wait(semaphore, self.all_levels)

    def copy(self, source, target, sends, recvs, level):
        _, partner = self.place(level)
        return pltpu.make_async_remote_copy(
            src_ref=source,
            dst_ref=target,
            send_sem=sends.at[level],
            recv_sem=recvs.at[level],
            device_id=partner,
            device_id_type=pl.DeviceIdType.MESH,
        )

    def reduce_copy(self, level, start_ref, acc_ref, got, sends, recvs):
        if level >= self.levels:
            return self.copy(self.own_shard(acc_ref, 1), got[level], sends, recvs, level)
        groups, rows = self.spot(level, min(level, 1), True)
        source = start_ref if level == 0 else acc_ref
        return self.copy(source.at[groups, rows], got[level], sends, recvs, level)

    def reduce_start(self, level, *refs):
        self.reduce_copy(level, *refs).start()

    def reduce_finish(self, level, start_ref, acc_ref, got, sends, recvs):
        self.reduce_copy(level, start_ref, acc_ref, got, sends, recvs).wait()
        if level >= self.levels:
            own = self.own_shard(acc_ref, 1)
            own[...] = (own[...].astype(F32) + got[level][...].astype(F32)).astype(BF16)
            return
        count, rows = self.sizes(level)
        groups, spots = self.spot(level, min(level, 1), False)
        if level == 0:
            target_groups, target_rows = pl.ds(0, count), pl.ds(0, rows)
            if self.padded > self.real:
                acc_ref[:, self.real :, :] = jnp.zeros_like(acc_ref[:, self.real :, :])
        else:
            target_groups, target_rows = groups, spots
        source = start_ref if level == 0 else acc_ref

        def add(index, carry):
            one = pl.ds(groups.start + index, 1)
            to = pl.ds(target_groups.start + index, 1)
            value = source[one, spots, :].astype(F32) + got[level][pl.ds(index, 1)].astype(F32)
            acc_ref[to, target_rows, :] = value.astype(BF16)
            return carry

        lax.fori_loop(0, count, add, 0)

    def own_shard(self, ref, first):
        if self.levels > self.even:
            return ref.at[self.spot(self.levels - 1, first, False)]
        groups, _ = self.spot(self.levels - 1, first, False)
        return ref.at[groups, pl.ds(0, self.shard)]

    def gather_copy(self, level, full_ref, sends, recvs):
        piece = full_ref.at[self.spot(level, 0, False)]
        return self.copy(piece, piece, sends, recvs, level)

    def gather_start(self, level, *refs):
        self.gather_copy(level, *refs).start()

    def gather_finish(self, level, *refs):
        self.gather_copy(level, *refs).wait()


def modulation_kernel(lead_ref, emb_ref, ada_ref, bias_ref, mod_ref):
    rows = lax.broadcasted_iota(jnp.int32, (16, emb_ref.shape[0]), 0)
    columns = lane_index((16, emb_ref.shape[0]))
    onehot = jnp.zeros((16, emb_ref.shape[0]), F32)
    for step in range(2):
        lead = lead_ref[0, first_step(2) + step]
        onehot = jnp.where((rows == step) & (columns == lead), 1.0, onehot)
    condition = dot(onehot.astype(BF16), emb_ref[...])
    active = (condition * jax.nn.sigmoid(condition)).astype(BF16)
    mod_ref[...] = dot(active, ada_ref[...]) + bias_ref[...].astype(F32)


def project_kernel(sources, queries, *refs):
    x_refs = refs[:sources]
    mod_ref, w_ref = refs[sources : sources + 2]
    outs = refs[sources + 2 :]
    step, which = pl.program_id(0), pl.program_id(1)
    width = w_ref.shape[0]
    x = pick(x_refs, which).astype(F32)
    shift = mod_ref[pl.ds(step, 1), 0:width]
    scale = mod_ref[pl.ds(step, 1), width : 2 * width]
    xhat, _ = normalize(x)
    normed = (xhat * (1.0 + scale) + shift).astype(BF16)
    outs[0][0, 0] = normed
    start = 0 if queries else width
    projected = dot(normed, w_ref[:, start:])
    for part in range(len(outs) - 1):
        for pair in range(width // LANES):
            at = part * width + pair * LANES
            piece = projected[:, at : at + LANES]
            if queries and part == 0:
                piece = piece * (HD**-0.5 * LOG2E)
            outs[part + 1][0, pair, 0] = piece.astype(BF16)


def with_ones(values):
    low = lane_index(values.shape) < HD
    one = jnp.ones_like(values)
    return jnp.where(low, values, one), jnp.where(low, one, values)


def masked(values):
    low = lane_index(values.shape) < HD
    zero = jnp.zeros_like(values)
    return jnp.where(low, values, zero), jnp.where(low, zero, values)


def attend_local_kernel(rows, q_ref, k_ref, v_ref, acc_ref, ext_ref):
    ext_ref[0], ext_ref[1] = with_ones(v_ref[0, 0])

    def block(index, carry):
        at = pl.ds(pl.multiple_of(index * rows, rows), rows)
        for head, query in enumerate(masked(q_ref[0, 0, at, :])):
            weights = jnp.exp2(dot(query, k_ref[0, 0], NT)).astype(BF16)
            acc_ref[0, 0, head, at, :] = dot(weights, ext_ref[head])
        return carry

    lax.fori_loop(0, q_ref.shape[2] // rows, block, 0, unroll=True)


def attend_all_kernel(
    rows, q_ref, k_ref, v_ref, kr_ref, vr_ref, acc_ref, o_ref, qe_ref, ext_ref, total_ref
):
    ext_ref[0], ext_ref[1] = with_ones(vr_ref[0, 0])
    blocks = q_ref.shape[2] // rows

    def finish(at, query, first, second, top_first, top_second):
        lane = lane_index(query.shape)
        low = lane < HD
        swapped = jnp.where(low, second, first)
        total = pltpu.roll(swapped, HD, 1)
        o_ref[0, 0, at, :] = jnp.where(low, first, second) / total
        log_total = jnp.log2(swapped) + jnp.where(low, top_second, top_first)
        high = log_total.astype(BF16).astype(F32)
        middle = (log_total - high).astype(BF16).astype(F32)
        rest = log_total - high - middle
        spot = lane % HD
        extra = jnp.where(spot == 0, -high, jnp.where(spot == 1, -middle, -rest))
        extra = jnp.where(spot < 3, extra, 0.0).astype(BF16)
        qe_ref[0, 0, 0, at, :] = jnp.where(low, query, extra)
        qe_ref[0, 0, 1, at, :] = jnp.where(low, extra, query)
        return total

    def block(index, carry):
        at = pl.ds(pl.multiple_of(index * rows, rows), rows)
        query = q_ref[0, 0, at, :]
        sums = []
        for head, own in enumerate(masked(query)):
            weights = jnp.exp2(dot(own, kr_ref[0, 0], NT)).astype(BF16)
            sums.append(acc_ref[0, 0, head, at, :] + dot(weights, ext_ref[head]))
        total_ref[at, :] = finish(at, query, sums[0], sums[1], 0.0, 0.0)
        return carry

    lax.fori_loop(0, blocks, block, 0, unroll=True)
    total = total_ref[...]
    bad = jnp.sum(jnp.where((total > 1e-25) & (total < 1e25), 0.0, 1.0))

    @pl.when(bad > 0.0)
    def _():
        own_ext = with_ones(v_ref[0, 0])

        def again(index, carry):
            at = pl.ds(pl.multiple_of(index * rows, rows), rows)
            query = q_ref[0, 0, at, :]
            sums, tops = [], []
            for head, own in enumerate(masked(query)):
                scores = dot(own, k_ref[0, 0], NT)
                others = dot(own, kr_ref[0, 0], NT)
                top = jnp.maximum(
                    jnp.max(scores, axis=-1, keepdims=True),
                    jnp.max(others, axis=-1, keepdims=True),
                )
                sums.append(
                    dot(jnp.exp2(scores - top).astype(BF16), own_ext[head])
                    + dot(jnp.exp2(others - top).astype(BF16), ext_ref[head])
                )
                tops.append(top)
            finish(at, query, sums[0], sums[1], tops[0], tops[1])
            return carry

        lax.fori_loop(0, blocks, again, 0)


def gelu_parts(values):
    t = 1.0 / (1.0 + jnp.abs(values) * (0.3275911 * 0.7071067811865476))
    bell = jnp.exp2(values * values * (-0.5 * LOG2E))
    series = 0.5 * 1.061405429
    for coefficient in (-1.453152027, 1.421413741, -0.284496736, 0.254829592):
        series = series * t + 0.5 * coefficient
    tail = series * t * bell
    cumulative = jnp.where(values < 0.0, tail, 1.0 - tail)
    return values * cumulative, cumulative + values * bell * 0.3989422804014327


def patch_kernel(
    rows,
    chunk,
    counts_ref,
    lead_ref,
    own_x,
    sib_x,
    own_ct,
    sib_ct,
    mod_ref,
    o_ref,
    out_w,
    fc1_w,
    fc2_w,
    final_ref,
    gm_ref,
    ge_ref,
    sums_ref,
    stack_one,
    stack_two,
    hidden_s,
    gpre_s,
    n2_s,
    g2_s,
    g1_s,
    mixed_s,
    gout_s,
    gfc1_s,
    gfc2_s,
    sums_s,
):
    step, half = pl.program_id(0), pl.program_id(1)
    width, hidden_width = fc1_w.shape
    patches = own_x.shape[1]
    slot = first_step(pl.num_programs(0)) + step
    active = (slot < counts_ref[0]).astype(F32)

    def piece(index):
        return mod_ref[pl.ds(step, 1), index * width : (index + 1) * width]

    gate1, shift2, scale2, gate2 = piece(2), piece(3), piece(4), piece(5)

    @pl.when((step == 0) & (half == 0))
    def _():
        sums_s[...] = jnp.zeros_like(sums_s)
        gout_s[...] = jnp.zeros_like(gout_s)
        gfc1_s[...] = jnp.zeros_like(gfc1_s)
        gfc2_s[...] = jnp.zeros_like(gfc2_s)

    def block(index, carry):
        at = pl.ds(pl.multiple_of(index * rows, rows), rows)
        x = jnp.where(half == 0, own_x[0, at, :], sib_x[0, at, :]).astype(F32)
        final_grad = jnp.where(half == 0, own_ct[0, at, :], sib_ct[0, at, :]).astype(F32) * active
        outs = [o_ref[0, pair, at, :] for pair in range(width // LANES)]
        mixed = jnp.concatenate([o.astype(BF16) for o in outs], axis=-1)
        mixed_s[at, :] = mixed
        branch_one = dot(mixed, out_w[...])
        middle = x + gate1 * branch_one
        xhat, inverse = normalize(middle)
        n2 = (xhat * (1.0 + scale2) + shift2).astype(BF16)
        n2_s[at, :] = n2
        g2 = (gate2 * final_grad).astype(BF16)
        g2_s[at, :] = g2
        branch_two = jnp.zeros((rows, width), F32)
        gy = jnp.zeros((rows, width), F32)
        for start in range(0, hidden_width, chunk):
            columns = slice(start, start + chunk)
            pre = dot(n2, fc1_w[:, columns])
            grad_hidden = dot(g2, fc2_w[columns, :], NT)
            hidden, slope = gelu_parts(pre)
            hidden = hidden.astype(BF16)
            grad_pre = (slope * grad_hidden).astype(BF16)
            hidden_s[at, columns] = hidden
            gpre_s[at, columns] = grad_pre
            branch_two += dot(hidden, fc2_w[columns, :])
            gy += dot(grad_pre, fc1_w[:, columns], NT)
        final_ref[0, 0, at, :] = ((middle + gate2 * branch_two) * active).astype(BF16)
        gm = final_grad + norm_back(gy * (1.0 + scale2), xhat, inverse)
        gm_ref[0, 0, at, :] = gm
        g1 = (gate1 * gm).astype(BF16)
        g1_s[at, :] = g1
        sums = [branch_one * gm, gy, gy * xhat, branch_two * final_grad]
        for row, value in enumerate(sums):
            place = pl.ds(2 * row + step, 1)
            sums_s[place, :] += jnp.sum(value, axis=0, keepdims=True)
        grad_mixed = dot(g1, out_w[...], NT).astype(BF16)
        lane = lane_index((rows, LANES))
        low = lane < HD
        spot = lane % HD
        for pair, o in enumerate(outs):
            grad = grad_mixed[:, pair * LANES : (pair + 1) * LANES]
            product = grad.astype(F32) * o
            first = jnp.sum(jnp.where(low, product, 0.0), axis=-1, keepdims=True)
            second = jnp.sum(jnp.where(low, 0.0, product), axis=-1, keepdims=True)
            inner = jnp.where(low, second, first)
            high = inner.astype(BF16).astype(F32)
            mid = (inner - high).astype(BF16).astype(F32)
            extra = jnp.where(spot == 0, -high, jnp.where(spot == 1, -mid, high + mid - inner))
            extra = jnp.where(spot < 3, extra, 0.0).astype(BF16)
            ge_ref[0, pair, 0, at, :] = jnp.where(low, grad, extra)
            ge_ref[0, pair, 1, at, :] = jnp.where(low, extra, grad)
        return carry

    lax.fori_loop(0, patches // rows, block, 0)
    gout_s[...] += dot(mixed_s[...], g1_s[...], TN)
    for start in range(0, hidden_width, chunk):
        columns = slice(start, start + chunk)
        gfc1_s[:, columns] += dot(n2_s[...], gpre_s[:, columns], TN)
        gfc2_s[:, columns] += dot(g2_s[...], hidden_s[:, columns], TN)

    @pl.when((step == pl.num_programs(0) - 1) & (half == pl.num_programs(1) - 1))
    def _():
        for index in range(2):
            lead = lead_ref[0, first_step(2) + index]
            sums_s[12 + index : 13 + index, :] = jnp.where(lane_index((1, width)) == lead, 1.0, 0.0)
        sums_ref[...] = sums_s[...].astype(BF16)
        blocks = hidden_width // width
        for index in range(blocks):
            columns = slice(index * width, (index + 1) * width)
            stack_one[index] = gfc1_s[:, columns].astype(BF16)
            stack_two[index] = gfc2_s[:, columns].T.astype(BF16)
        stack_two[blocks] = gout_s[...].astype(BF16)


def attend_back_kernel(rows, first_pass, exchanges, grid_steps, *refs):
    count = len(exchanges)
    qe_ref, ge_ref, k_ref, v_ref = refs[:4]
    refs = refs[4:]
    if first_pass:
        gives, sums_ref, refs = refs[:count], refs[count], refs[count + 1 :]
        dq_ref, dk_ref, dv_ref = refs[:3]
        shards, all_ref, refs = refs[3 : 3 + count], refs[3 + count], refs[4 + count :]
        all_s, all_sends, all_recvs = refs[-3:]
    else:
        dq_in, shards, refs = refs[0], refs[1 : 1 + count], refs[1 + count :]
        dq_ref, dk_ref, dv_ref = refs[:3]
        fulls, refs = refs[3 : 3 + count], refs[3 + count :]
    acc_s, refs = refs[0], refs[1:]
    states = []
    for index, exchange in enumerate(exchanges):
        sends, recvs = refs[1], refs[2]
        if first_pass:
            got = refs[3 : 3 + exchange.all_levels]
            states.append((gives[index], refs[0], got, sends, recvs))
            refs = refs[3 + exchange.all_levels :]
        else:
            states.append((refs[0], sends, recvs))
            refs = refs[3:]
    per_step = k_ref.shape[2] // rows
    slots = pl.num_programs(0) * pl.num_programs(1) * per_step
    static_slots = grid_steps * per_step
    first_slot = (pl.program_id(0) * pl.num_programs(1) + pl.program_id(1)) * per_step
    levels = exchanges[0].all_levels if first_pass else exchanges[0].levels
    if first_pass:
        acc_s[...] = jnp.zeros_like(acc_s)
    else:
        acc_s[...] = dq_in[0, 0].T

    def all_copy(level):
        index = 0
        for lower in range(len(exchanges[0].bits)):
            index = index + exchanges[0].place(lower)[0] * (1 << lower)
        if level < 0:
            return all_s.at[pl.ds(index, 1)]
        size = 1 << level
        piece = all_s.at[pl.ds((index // size) * size, size)]
        return exchanges[0].copy(piece, piece, all_sends, all_recvs, level)

    def reduce_action(order):
        if order == 0:
            exchanges[0].barrier()
            own = all_copy(-1)
            own[...] = sums_ref[...][None]
        else:
            all_copy(order - 1).wait()
        if order < levels:
            all_copy(order).start()
        else:
            all_ref[...] = all_s[...]
        for exchange, state, shard in zip(exchanges, states, shards):
            if order > 0:
                exchange.reduce_finish(order - 1, *state)
            if order < levels:
                exchange.reduce_start(order, *state)
            else:
                shard[...] = exchange.own_shard(state[1], 1)[...][0]

    def gather_action(order):
        if order == 0:
            exchanges[0].barrier()
        for exchange, state, shard in zip(exchanges, states, shards):
            if order == 0:
                exchange.own_shard(state[0], 0)[...] = shard[...][None]
            else:
                exchange.gather_finish(levels - order, *state)
            if order < levels:
                exchange.gather_start(levels - 1 - order, *state)
        if order == levels:
            copies = [
                pltpu.make_async_copy(state[0], full, refs[index])
                for index, (state, full) in enumerate(zip(states, fulls))
            ]
            for copy in copies:
                copy.start()
            for copy in copies:
                copy.wait()

    action = reduce_action if first_pass else gather_action
    weights = [5.0, 10.0, 9.0, 6.0] + [4.0] * levels
    weights = weights[:levels] if first_pass else weights[:levels][::-1]
    marks, total = [0], 0.0
    for weight in weights:
        total += weight
        marks.append(total)
    marks = [min(int(mark * (static_slots - 1) / total + 0.5), static_slots - 1) for mark in marks]

    def block(index, carry):
        for order, mark in enumerate(marks[:-1]):
            pl.when(first_slot + index == mark)(functools.partial(action, order))
        at = pl.ds(pl.multiple_of(index * rows, rows), rows)
        keys = k_ref[0, 0, at, :]
        values = v_ref[0, 0, at, :]
        lane = lane_index(keys.shape)
        low = lane < HD
        ones = jnp.where(lane % HD < 3, 1.0, 0.0).astype(BF16)
        zero = jnp.zeros_like(keys)
        grads = []
        for head in range(2):
            own = low if head == 0 else jnp.logical_not(low)
            query = qe_ref[0, 0, head]
            grad = ge_ref[0, 0, head]
            probs = jnp.exp2(dot(jnp.where(own, keys, ones), query, NT))
            grad_probs = dot(jnp.where(own, values, ones), grad, NT)
            grad_scores = (probs * grad_probs).astype(BF16)
            grads.append((dot(grad_scores, query), dot(probs.astype(BF16), grad)))
            acc_s[...] += dot(jnp.where(own, keys, zero), grad_scores, TN)
        dk_ref[0, 0, at, :] = (jnp.where(low, grads[0][0], grads[1][0]) * LN2).astype(BF16)
        dv_ref[0, 0, at, :] = jnp.where(low, grads[0][1], grads[1][1]).astype(BF16)
        return carry

    lax.fori_loop(0, per_step, block, 0)
    pl.when(first_slot + per_step == slots)(functools.partial(action, levels))
    if first_pass:
        dq_ref[0, 0] = acc_s[...].T
    else:
        dq_ref[0, 0] = (acc_s[...].T * HD**-0.5).astype(BF16)


def project_back_far_kernel(dk_ref, dv_ref, normed_ref, w_ref, dx_ref, gw_ref):
    width = w_ref.shape[0]
    joined = join_heads(dk_ref, dv_ref)
    dx_ref[0, 0] = dot(joined, w_ref[:, width:], NT).astype(BF16)

    @pl.when((pl.program_id(0) == 0) & (pl.program_id(1) == 0))
    def _():
        gw_ref[...] = jnp.zeros_like(gw_ref)

    gw_ref[...] += dot(normed_ref[0, 0], joined, TN)


def weight_back_kernel(dq_ref, dk_ref, dv_ref, normed_ref, far_ref, gw_ref, gw_s):
    step, which = pl.program_id(0), pl.program_id(1)
    width = normed_ref.shape[3]

    @pl.when((step == 0) & (which == 0))
    def _():
        gw_s[:, :width] = jnp.zeros_like(gw_s[:, :width])
        gw_s[:, width:] = far_ref[...]

    gw_s[...] += dot(normed_ref[0, 0], join_heads(dq_ref, dk_ref, dv_ref), TN)

    @pl.when((step == pl.num_programs(0) - 1) & (which == pl.num_programs(1) - 1))
    def _():
        for block in range(gw_ref.shape[0]):
            gw_ref[block] = gw_s[:, block * LANES : (block + 1) * LANES].astype(BF16)


def join_heads(*grads):
    return jnp.concatenate([ref[0, pair] for ref in grads for pair in range(ref.shape[1])], axis=-1)


class Direct:
    def __init__(self, mesh_shape, row_tiles):
        self.chips = mesh_shape["seq"] // 2
        self.peers = mesh_shape["dp"] * self.chips
        self.half = row_tiles * 8
        self.piece = -(-row_tiles // (2 * self.peers)) * 16
        self.padded = self.piece * self.peers

    def me(self):
        return lax.axis_index("dp") * self.chips + lax.axis_index("seq") // 2

    def core(self):
        return lax.axis_index("seq") % 2

    def sibling(self):
        return {"seq": lax.axis_index("seq") + 1 - 2 * self.core()}

    def peer(self, shift):
        other = (self.me() + shift) % self.peers
        device = {"dp": other // self.chips, "seq": (other % self.chips) * 2 + self.core()}
        return other, device

    def rows(self, index):
        return pl.ds(pl.multiple_of(index * self.piece, 16), self.piece)

    def barrier(self):
        semaphore = pltpu.get_barrier_semaphore()

        def signal(device):
            pl.semaphore_signal(semaphore, 1, device_id=device, device_id_type=pl.DeviceIdType.MESH)

        signal(self.sibling())

        def greet(shift, carry):
            signal(self.peer(shift)[1])
            return carry

        lax.fori_loop(1, self.peers, greet, 0)
        pl.semaphore_wait(semaphore, self.peers)

    def copy(self, source, target, send, recv, device):
        return pltpu.make_async_remote_copy(
            src_ref=source,
            dst_ref=target,
            send_sem=send,
            recv_sem=recv,
            device_id=device,
            device_id_type=pl.DeviceIdType.MESH,
        )

    def each_peer(self, do):
        def one(shift, carry):
            do(shift)
            return carry

        lax.fori_loop(1, self.peers, one, 0)


def tail_kernel(direct, remote, *refs):
    give_ref, own_x, sib_x, mod_ref, lead_ref, gm_ref, dq_ref, dk_ref, dv_ref, w_ref = refs[:10]
    others = refs[10 : 10 + remote]
    grad_ref, got_ref, full_ref, all_ref = refs[10 + remote : 14 + remote]
    sums_s, other_s, got_s, sum_s, core_s, pieces_s, full_s, all_s = refs[14 + remote : 22 + remote]
    core_sems, piece_sems, back_sems, all_sems, grad_sems, local_sem = refs[22 + remote :]
    step, half = pl.program_id(0), pl.program_id(1)
    width = own_x.shape[2]
    core, me = direct.core(), direct.me()

    core_copy = direct.copy(
        give_ref.at[1 - core], core_s, core_sems.at[0], core_sems.at[1], direct.sibling()
    )

    def piece_copy(shift):
        other, device = direct.peer(shift)
        return direct.copy(
            sum_s.at[direct.rows(other)],
            pieces_s.at[shift],
            piece_sems.at[0, shift],
            piece_sems.at[1, shift],
            device,
        )

    def full_copy(shift, arriving):
        _, device = direct.peer(shift)
        owner = (me + direct.peers - shift) % direct.peers if arriving else me
        place = full_s.at[core, direct.rows(owner)]
        return direct.copy(place, place, back_sems.at[0, shift], back_sems.at[1, shift], device)

    def sums_copy(shift, arriving):
        _, device = direct.peer(shift)
        owner = (me + direct.peers - shift) % direct.peers if arriving else me
        place = all_s.at[core, owner]
        return direct.copy(place, place, all_sems.at[0, shift], all_sems.at[1, shift], device)

    def side_copy(values, which, side):
        place = values.at[side]
        return direct.copy(
            place, place, core_sems.at[which], core_sems.at[which + 1], direct.sibling()
        )

    def grad_copy(index):
        return direct.copy(
            other_s.at[index],
            got_s.at[index],
            grad_sems.at[0, index],
            grad_sems.at[1, index],
            direct.sibling(),
        )

    @pl.when((step == 0) & (half == 0))
    def _():
        direct.barrier()
        core_copy.start()
        sums_s[...] = jnp.zeros_like(sums_s)

    @pl.when((step == 0) & (half == 1))
    def _():
        core_copy.wait()
        real = core_s.shape[0]
        sum_s[:real] = (give_ref[core].astype(F32) + core_s[...].astype(F32)).astype(BF16)
        if direct.padded > real:
            sum_s[real:] = jnp.zeros_like(sum_s[real:])
        direct.each_peer(lambda shift: piece_copy(shift).start())

    x = jnp.where(half == 0, own_x[0], sib_x[0]).astype(F32)
    scale = mod_ref[pl.ds(step, 1), width : 2 * width]
    xhat, inverse = normalize(x)
    gy = dot(join_heads(dq_ref, dk_ref, dv_ref), w_ref[...], NT)
    for other in others:
        gy = gy + other[0, 0].astype(F32)
    grad = (gm_ref[0, 0] + norm_back(gy * (1.0 + scale), xhat, inverse)).astype(BF16)

    @pl.when(half == 0)
    def _():
        grad_ref[0] = grad

    @pl.when(half == 1)
    def _():
        other_s[step] = grad
        grad_copy(step).start()

    for kind, value in enumerate((gy, gy * xhat)):
        total = jnp.sum(value, axis=0, keepdims=True)
        for index in range(width // LANES):
            place = pl.ds((kind * 2 + step) * (width // LANES) + index, 1)
            sums_s[place, :] += total[:, index * LANES : (index + 1) * LANES]

    @pl.when((step == 1) & (half == 1))
    def _():
        for index in range(2):
            chosen = lane_index((1, LANES)) == lead_ref[0, first_step(2) + index]
            sums_s[12 + index : 13 + index, :] = jnp.where(chosen, 1.0, 0.0)
        all_s[core, me] = sums_s[...].astype(BF16)
        direct.each_peer(lambda shift: sums_copy(shift, False).start())
        direct.each_peer(lambda shift: piece_copy(shift).wait())

        def add(shift, total):
            return total + pieces_s[shift].astype(F32)

        total = lax.fori_loop(1, direct.peers, add, sum_s[direct.rows(me)].astype(F32))
        full_s[core, direct.rows(me)] = total.astype(BF16)
        direct.each_peer(lambda shift: full_copy(shift, False).start())

        def arrived(shift):
            full_copy(shift, False).wait_send()
            full_copy(shift, True).wait_recv()
            sums_copy(shift, False).wait_send()
            sums_copy(shift, True).wait_recv()

        direct.each_peer(arrived)
        side_copy(full_s, 2, core).start()
        side_copy(all_s, 4, core).start()
        for index in range(2):
            grad_copy(index).wait()
        side_copy(full_s, 2, core).wait_send()
        side_copy(full_s, 2, 1 - core).wait_recv()
        side_copy(all_s, 4, core).wait_send()
        side_copy(all_s, 4, 1 - core).wait_recv()
        outs = [(got_s, got_ref), (full_s, full_ref), (all_s, all_ref)]
        copies = [
            pltpu.make_async_copy(source, target, local_sem.at[index])
            for index, (source, target) in enumerate(outs)
        ]
        for copy in copies:
            copy.start()
        for copy in copies:
            copy.wait()


def unstack(at, full_ref, targets, rows):
    row, end = 0, rows * len(targets)
    while row < end:
        group, inside, left = at(row)
        block, place = divmod(row, rows)
        count = min(left, rows - place)
        target, first_row, first_column = targets[block]
        columns = slice(first_column, first_column + full_ref.shape[2])
        value = full_ref[group, inside : inside + count, :].astype(F32)
        target[first_row + place : first_row + place + count, columns] = value
        row += count


def spread_leads(grads, step_of, table_rows):
    count = grads.shape[0]
    part = min(count, 512)
    row = lax.broadcasted_iota(jnp.int32, (part, part), 0)
    column = lane_index((part, part))
    chosen = (row // 16 == column // 16) & (row % 16 == 12 + step_of(column % 16))
    spread = jnp.where(chosen, 1.0, 0.0).astype(BF16)
    leads = [
        dot(grads[start : start + part, :LANES], spread, TN)[:table_rows]
        for start in range(0, count, part)
    ]
    return jnp.concatenate(leads, axis=-1)


def final_kernel(early, direct, *refs):
    early_sums, late_sums, emb_ref, ada_ref, one_ref, two_ref, late_ref = refs[:7]
    final_ref, final_got, grad_ref, grad_got = refs[7:11]
    outs = refs[11:20]
    gada_s, gqkv_s, gout_s, gfc1_s, gfc2_s, sems = refs[20:]
    final_out, grad_out, gemb_ref, gada_out, gbada_ref, gqkv_out, gout_out, gfc1_out, gfc2_out = outs
    size = gout_s.shape[0]
    blocks = gfc1_s.shape[1] // size
    copies = []

    def start(source, target):
        copy = pltpu.make_async_copy(source, target, sems.at[len(copies)])
        copy.start()
        copies.append(copy)

    mine = first_step(2)
    for index in range(2):
        start(final_ref.at[index, 0], final_out.at[mine + index])
        start(final_got.at[index], final_out.at[2 - mine + index])
        start(grad_ref.at[index], grad_out.at[mine + index])
        start(grad_got.at[index], grad_out.at[2 - mine + index])

    def grouped(exchange):
        def at(row):
            group, inside = divmod(row, exchange.real)
            return group, inside, exchange.real - inside

        return at

    def halved(row):
        group, inside = divmod(row, direct.half)
        return group, inside, direct.half - inside

    unstack(grouped(early[0]), one_ref, [(gfc1_s, 0, block * size) for block in range(blocks)], size)
    start(gfc1_s, gfc1_out)
    rest = [(gfc2_s, block * size, 0) for block in range(blocks)] + [(gout_s, 0, 0)]
    unstack(grouped(early[1]), two_ref, rest, size)
    start(gfc2_s, gfc2_out)
    start(gout_s, gout_out)
    columns = gqkv_s.shape[1] // LANES
    unstack(halved, late_ref, [(gqkv_s, 0, block * LANES) for block in range(columns)], size)
    start(gqkv_s, gqkv_out)

    table_rows = emb_ref.shape[0]
    table = emb_ref[...].astype(F32)
    gate = jax.nn.sigmoid(table)
    slope = gate * (1.0 + table * (1.0 - gate))
    table_act = (table * gate).astype(BF16)
    total = jnp.zeros((table_rows, size), F32)

    def one_piece(grads, leads, place, first):
        chosen = jnp.where(place, leads, 0.0).astype(BF16)
        acts = dot(table_act, chosen, TN).astype(BF16)
        where = slice(first, first + grads.shape[1])
        gada_s[:, where] = dot(acts, grads)
        by_lead = dot(chosen, grads)
        gbada_ref[:, where] = jnp.sum(by_lead, axis=0, keepdims=True)
        high = by_lead.astype(BF16)
        low = (by_lead - high.astype(F32)).astype(BF16)
        return dot(high, ada_ref[:, where], NT) + dot(low, ada_ref[:, where], NT)

    grads = early_sums[...]
    leads = spread_leads(grads, lambda row: row % 2, table_rows)
    row = lane_index((1, grads.shape[0])) % 16
    for index in range(4):
        total += one_piece(grads, leads, row // 2 == index, (2 + index) * size)
    grads = late_sums[...]
    parts = size // LANES
    leads = spread_leads(grads, lambda row: (row // parts) % 2, table_rows)
    row = lane_index((1, grads.shape[0])) % 16
    for index in range(2):
        for part in range(parts):
            place = (row // (2 * parts) == index) & (row % parts == part)
            total += one_piece(grads, leads, place, index * size + part * LANES)
    gemb_ref[...] = total * slope
    start(gada_s, gada_out)
    for copy in copies:
        copy.wait()


def local(
    mesh_shape, inputs, cotangent, counts, lead_steps, emb_table, w_ada, b_ada, w_qkv, w_out, w_fc1, w_fc2
):
    slots, items, patches, width = inputs.shape
    chips = mesh_shape["seq"] // 2
    blocks = w_fc1.shape[1] // w_fc1.shape[0]
    steps = slots * items // 2
    hidden_width = w_fc1.shape[1]
    pairs = width // LANES
    rows = 2 * patches
    remote = 2 * (chips - 1)
    far_rows = remote * patches
    spot = lax.axis_index("seq")
    core = lax.rem(spot, 2)
    devices = 2 * chips

    def send(values, shift, cross):
        pairs_list = []
        for source in range(devices):
            chip, side = source // 2, source % 2
            pairs_list.append((source, ((chip + shift) % chips) * 2 + (1 - side if cross else side)))
        return lax.ppermute(values, "seq", pairs_list)

    x_steps = inputs.reshape(2, steps, patches, width)
    ct_steps = cotangent.reshape(2, steps, patches, width)
    own_x = lax.dynamic_index_in_dim(x_steps, core, 0, keepdims=False)
    other_x = lax.dynamic_index_in_dim(x_steps, 1 - core, 0, keepdims=False)
    own_ct = lax.dynamic_index_in_dim(ct_steps, core, 0, keepdims=False)
    other_ct = lax.dynamic_index_in_dim(ct_steps, 1 - core, 0, keepdims=False)
    sib_x = send(other_x, 0, True)
    far_x = []
    for shift in range(1, chips):
        far_x.append(send(own_x, shift, False))
        far_x.append(send(other_x, shift, True))
    sib_ct = send(other_ct, 0, True)
    mod = call(
        modulation_kernel,
        "modulation",
        (),
        [scalars(), whole(emb_table.shape), whole(w_ada.shape), whole((1, 6 * width))],
        whole((16, 6 * width)),
        jax.ShapeDtypeStruct((16, 6 * width), F32),
        flops=2 * 16 * width * 6 * width,
        moved=2 * w_ada.size,
    )(lead_steps, emb_table, w_ada, b_ada.reshape(1, -1))

    step_block = pl.BlockSpec((1, patches, width), lambda j, i: (j, 0, 0))
    patch_block = pl.BlockSpec((1, 1, patches, width), lambda j, i: (j, i, 0, 0))

    def project(sources, queries, name):
        parts = 3 if queries else 2
        count = len(sources)
        head_block = pl.BlockSpec((1, pairs, 1, patches, LANES), lambda j, i: (j, 0, i, 0, 0))
        outs = call(
            functools.partial(project_kernel, count, queries),
            name,
            (steps, count),
            [step_block] * count + [whole(mod.shape), whole(w_qkv.shape)],
            [patch_block] + [head_block] * parts,
            [jax.ShapeDtypeStruct((steps, count, patches, width), BF16)]
            + [jax.ShapeDtypeStruct((steps, pairs, count, patches, LANES), BF16)] * parts,
            flops=2 * steps * count * patches * width * parts * width,
            moved=2 * steps * count * patches * width * (2 + parts),
        )(*sources, mod, w_qkv)
        return [outs[0]] + [o.reshape(steps, pairs, count * patches, LANES) for o in outs[1:]]

    n1, q, k, v = project([own_x, sib_x], True, "project_near")

    def head_rows(count):
        return pl.BlockSpec((1, 1, count, LANES), lambda j, p: (j, p, 0, 0))

    both_heads = pl.BlockSpec((1, 1, 2, rows, LANES), lambda j, p: (j, p, 0, 0, 0))
    query_rows = min(512, rows)
    near_work = 4 * steps * pairs * 2 * rows * LANES * rows
    far_work = 4 * steps * pairs * 2 * rows * LANES * far_rows
    acc = call(
        functools.partial(attend_local_kernel, query_rows),
        "attend_near",
        (steps, pairs),
        [head_rows(rows)] * 3,
        both_heads,
        jax.ShapeDtypeStruct((steps, pairs, 2, rows, LANES), F32),
        [pltpu.VMEM((2, rows, LANES), BF16)],
        flops=near_work,
        exps=steps * pairs * 2 * rows * rows,
    )(q, k, v)

    n1r, kr, vr = project(far_x, False, "project_far")
    o, qe = call(
        functools.partial(attend_all_kernel, query_rows),
        "attend_far",
        (steps, pairs),
        [head_rows(rows)] * 3 + [head_rows(far_rows)] * 2 + [both_heads],
        [head_rows(rows), both_heads],
        [
            jax.ShapeDtypeStruct((steps, pairs, rows, LANES), F32),
            jax.ShapeDtypeStruct((steps, pairs, 2, rows, LANES), BF16),
        ],
        [pltpu.VMEM((2, far_rows, LANES), BF16), pltpu.VMEM((rows, LANES), F32)],
        flops=far_work,
        exps=steps * pairs * 2 * rows * far_rows,
    )(q, k, v, kr, vr, acc)

    block_rows = min(256, patches)
    outs = call(
        functools.partial(patch_kernel, block_rows, 512),
        "patchwise",
        (steps, 2),
        [scalars()] * 2
        + [step_block] * 4
        + [
            whole(mod.shape),
            pl.BlockSpec((1, pairs, patches, LANES), lambda j, i: (j, 0, i, 0)),
            whole(w_out.shape),
            whole(w_fc1.shape),
            whole(w_fc2.shape),
        ],
        [
            patch_block,
            patch_block,
            pl.BlockSpec((1, pairs, 2, patches, LANES), lambda j, i: (j, 0, 0, i, 0)),
            whole((16, width)),
            whole((blocks, width, width)),
            whole((blocks + 1, width, width)),
        ],
        [
            jax.ShapeDtypeStruct((steps, 2, patches, width), BF16),
            jax.ShapeDtypeStruct((steps, 2, patches, width), F32),
            jax.ShapeDtypeStruct((steps, pairs, 2, rows, LANES), BF16),
            jax.ShapeDtypeStruct((16, width), BF16),
            jax.ShapeDtypeStruct((blocks, width, width), BF16),
            jax.ShapeDtypeStruct((blocks + 1, width, width), BF16),
        ],
        [pltpu.VMEM((patches, hidden_width), BF16)] * 2
        + [pltpu.VMEM((patches, width), BF16)] * 4
        + [
            pltpu.VMEM((width, width), F32),
            pltpu.VMEM((width, hidden_width), F32),
            pltpu.VMEM((width, hidden_width), F32),
            pltpu.VMEM((16, width), F32),
        ],
        flops=6 * steps * rows * width * (2 * hidden_width + width),
        moved=steps * rows * width * 20,
        exps=2 * steps * rows * hidden_width,
    )(counts, lead_steps, own_x, sib_x, own_ct, sib_ct, mod, o, w_out, w_fc1, w_fc2)
    final, gm, ge, sums, stack_one, stack_two = outs
    final_other = send(final[:, 1], 0, True)
    early = [Exchange(mesh_shape, blocks * width // 16, 0), Exchange(mesh_shape, (blocks + 1) * width // 16, 1)]
    gives = [g.reshape(e.groups, e.real, width) for e, g in zip(early, (stack_one, stack_two))]

    def attend_back(keys, values, extra, first, name):
        count = keys.shape[2]
        key_rows = min(512, count)
        in_specs = [both_heads] * 2 + [head_rows(count)] * 2
        out_specs = [head_rows(rows), head_rows(count), head_rows(count)]
        out_shape = [
            jax.ShapeDtypeStruct((steps, pairs, rows, LANES), F32 if first else BF16),
            jax.ShapeDtypeStruct((steps, pairs, count, LANES), BF16),
            jax.ShapeDtypeStruct((steps, pairs, count, LANES), BF16),
        ]
        scratch = [pltpu.VMEM((LANES, rows), F32)]
        if not first:
            in_specs += [head_rows(rows)]
        for exchange in early:
            shape = (exchange.groups, exchange.padded, width)
            shard = (exchange.shard, width)
            sems = [pltpu.SemaphoreType.DMA((exchange.all_levels,))] * 2
            if first:
                in_specs += [whole((exchange.groups, exchange.real, width))]
                out_specs += [whole(shard)]
                out_shape += [jax.ShapeDtypeStruct(shard, BF16)]
                half = (exchange.groups // 2, exchange.padded, width)
                scratch += [pltpu.VMEM(half, BF16)] + sems + exchange.receive_scratch(width)
            else:
                in_specs += [whole(shard)]
                out_specs += [pl.BlockSpec(memory_space=pl.ANY)]
                out_shape += [jax.ShapeDtypeStruct(shape, BF16)]
                scratch += [pltpu.VMEM(shape, BF16)] + sems
        if first:
            every = (mesh_shape["dp"] * mesh_shape["seq"], 16, width)
            in_specs += [whole(sums.shape)]
            out_specs += [whole(every)]
            out_shape += [jax.ShapeDtypeStruct(every, BF16)]
            sems = [pltpu.SemaphoreType.DMA((early[0].all_levels,))] * 2
            scratch += [pltpu.VMEM(every, BF16)] + sems
        else:
            scratch += [pltpu.SemaphoreType.DMA] * len(early)
        return call(
            functools.partial(attend_back_kernel, key_rows, first, early, steps * pairs),
            name,
            (steps, pairs),
            in_specs,
            out_specs,
            out_shape,
            scratch,
            flops=10 * steps * pairs * 2 * rows * count * LANES,
            exps=steps * pairs * 2 * rows * count,
            collective=1 if first else 2,
        )(qe, ge, keys, values, *extra)

    grad_block = pl.BlockSpec((1, pairs, patches, LANES), lambda j, i: (j, 0, i, 0))
    hbm = pl.BlockSpec(memory_space=pl.ANY)

    dq_part, dkr, dvr, shard_one, shard_two, early_all = attend_back(
        kr, vr, [*gives, sums], True, "attend_back_far"
    )
    dx_far, gw_part = call(
        project_back_far_kernel,
        "project_back_far",
        (steps, remote),
        [grad_block] * 2 + [patch_block, whole(w_qkv.shape)],
        [patch_block, whole((width, 2 * width))],
        [
            jax.ShapeDtypeStruct((steps, remote, patches, width), BF16),
            jax.ShapeDtypeStruct((width, 2 * width), F32),
        ],
        flops=4 * steps * far_rows * width * 2 * width,
        moved=steps * far_rows * width * 8,
    )(dkr, dvr, n1r, w_qkv)
    dx_got = [send(dx_far[:, 2 * r - 2 : 2 * r], -r, False) for r in range(1, chips)]
    dq, dk, dv, *early_sums = attend_back(
        k, v, [dq_part, shard_one, shard_two], False, "attend_back_near"
    )
    columns = w_qkv.shape[1] // LANES
    give_late = call(
        weight_back_kernel,
        "weight_back",
        (steps, 2),
        [grad_block] * 3 + [patch_block, whole(gw_part.shape)],
        whole((columns, width, LANES)),
        jax.ShapeDtypeStruct((columns, width, LANES), BF16),
        [pltpu.VMEM((width, columns * LANES), F32)],
        flops=2 * steps * rows * width * 3 * width,
        moved=steps * rows * width * 8,
    )(dq, dk, dv, n1, gw_part)

    direct = Direct(mesh_shape, columns * width // 16)
    full_shape = (2, direct.padded, LANES)
    late_all_shape = (2, direct.peers, 16, LANES)
    grad_own, grad_got, late_sum, late_all = call(
        functools.partial(tail_kernel, direct, len(dx_got)),
        "tail",
        (steps, 2),
        [whole((2, direct.half, LANES)), step_block, step_block, whole(mod.shape), scalars()]
        + [patch_block]
        + [grad_block] * 3
        + [whole(w_qkv.shape)]
        + [patch_block] * len(dx_got),
        [step_block, hbm, hbm, hbm],
        [
            jax.ShapeDtypeStruct((steps, patches, width), BF16),
            jax.ShapeDtypeStruct((steps, patches, width), BF16),
            jax.ShapeDtypeStruct(full_shape, BF16),
            jax.ShapeDtypeStruct(late_all_shape, BF16),
        ],
        [
            pltpu.VMEM((16, LANES), F32),
            pltpu.VMEM((steps, patches, width), BF16),
            pltpu.VMEM((steps, patches, width), BF16),
            pltpu.VMEM((direct.padded, LANES), BF16),
            pltpu.VMEM((direct.half, LANES), BF16),
            pltpu.VMEM((direct.peers, direct.piece, LANES), BF16),
            pltpu.VMEM(full_shape, BF16),
            pltpu.VMEM(late_all_shape, BF16),
            pltpu.SemaphoreType.DMA((6,)),
            pltpu.SemaphoreType.DMA((2, direct.peers)),
            pltpu.SemaphoreType.DMA((2, direct.peers)),
            pltpu.SemaphoreType.DMA((2, direct.peers)),
            pltpu.SemaphoreType.DMA((2, steps)),
            pltpu.SemaphoreType.DMA((3,)),
        ],
        flops=2 * steps * rows * width * 3 * width,
        collective=3,
    )(
        give_late.reshape(2, direct.half, LANES),
        own_x,
        sib_x,
        mod,
        lead_steps,
        gm,
        dq,
        dk,
        dv,
        w_qkv,
        *dx_got,
    )

    early_all = early_all.reshape(-1, width)
    late_all = late_all.reshape(-1, LANES)
    small = [early_all, late_all, emb_table, w_ada, *early_sums, late_sum]
    out_shapes = [(slots * items, patches, width)] * 2 + [emb_table.shape, w_ada.shape]
    out_shapes += [(1, 6 * width), w_qkv.shape, w_out.shape, w_fc1.shape, w_fc2.shape]
    outs = call(
        functools.partial(final_kernel, early, direct),
        "final",
        (),
        [whole(value.shape) for value in small] + [hbm] * 4,
        [hbm] * 2 + [whole(emb_table.shape), hbm, whole((1, 6 * width))] + [hbm] * 4,
        [
            jax.ShapeDtypeStruct(shape, BF16 if index < 2 else F32)
            for index, shape in enumerate(out_shapes)
        ],
        [pltpu.VMEM(w.shape, F32) for w in (w_ada, w_qkv, w_out, w_fc1, w_fc2)]
        + [pltpu.SemaphoreType.DMA((4 * 2 + 5,))],
        flops=2 * early_all.shape[0] * width * 6 * width,
        moved=6 * w_ada.size,
    )(*small, final, final_other, grad_own, grad_got)
    outputs, grad_inputs, g_emb, g_ada, g_bada, g_qkv, g_out, g_fc1, g_fc2 = outs
    return (
        outputs.reshape(inputs.shape),
        grad_inputs.reshape(inputs.shape),
        g_emb,
        g_ada,
        g_bada.reshape(-1),
        g_qkv,
        g_out,
        g_fc1,
        g_fc2,
    )


def solution(mesh):
    tokens = P(None, "dp", "seq", None)
    return jax.shard_map(
        functools.partial(local, dict(mesh.shape)),
        mesh=mesh,
        in_specs=(tokens, tokens, P("dp"), P("dp", None)) + (P(),) * 7,
        out_specs=(tokens, tokens) + (P(),) * 7,
        check_vma=False,
    )
```

```python
import functools

import jax
import jax.numpy as jnp
from jax import lax
from jax.experimental import pallas as pl
from jax.experimental.pallas import tpu as pltpu
from jax.sharding import PartitionSpec as P

HD = 64
LANES = 128
EPSILON = 1e-06
LOG2E = 1.4426950408889634
LN2 = 0.6931471805599453
NN = (((1,), (0,)), ((), ()))
NT = (((1,), (1,)), ((), ()))
TN = (((0,), (0,)), ((), ()))
F32 = jnp.float32
BF16 = jnp.bfloat16
VMEM_BYTES = 56 * 1024 * 1024


def dot(a, b, dims=NN):
    return lax.dot_general(a, b, dims, preferred_element_type=F32)


def call(
    body,
    name,
    grid,
    in_specs,
    out_specs,
    out_shape,
    scratch=(),
    flops=0,
    moved=0,
    exps=0,
    collective=None,
):
    return pl.pallas_call(
        body,
        name=name,
        grid=grid,
        in_specs=in_specs,
        out_specs=out_specs,
        out_shape=out_shape,
        scratch_shapes=list(scratch),
        cost_estimate=pl.CostEstimate(flops=flops, bytes_accessed=moved, transcendentals=exps),
        compiler_params=pltpu.CompilerParams(
            vmem_limit_bytes=VMEM_BYTES,
            collective_id=collective,
            has_side_effects=collective is not None,
        ),
    )


def whole(shape):
    return pl.BlockSpec(shape, lambda *_: (0,) * len(shape))


def scalars():
    return pl.BlockSpec(memory_space=pltpu.SMEM)


def lane_index(shape):
    return lax.broadcasted_iota(jnp.int32, shape, 1)


def first_step(steps):
    return lax.rem(lax.axis_index("seq"), 2) * steps


def normalize(values):
    center = values - jnp.mean(values, axis=-1, keepdims=True)
    spread = jnp.mean(center * center, axis=-1, keepdims=True)
    inverse = lax.rsqrt(spread + EPSILON)
    return center * inverse, inverse


def norm_back(grad, xhat, inverse):
    first = jnp.mean(grad, axis=-1, keepdims=True)
    second = jnp.mean(grad * xhat, axis=-1, keepdims=True)
    return inverse * (grad - first - xhat * second)


def pick(refs, which):
    value = refs[0][0]
    for index in range(1, len(refs)):
        value = jnp.where(which == index, refs[index][0], value)
    return value


class Exchange:
    def __init__(self, mesh_shape, row_tiles, turn=0):
        bits = {"seq": [], "dp": []}
        for axis in bits:
            bit = 1
            while bit < mesh_shape[axis]:
                bits[axis].append((axis, bit))
                bit *= 2
        turned = bits["dp"][turn:] + bits["dp"][:turn]
        self.bits = bits["seq"][:1] + turned + bits["seq"][1:]
        self.all_levels = len(self.bits)
        self.levels = 1 + len(turned)
        self.even = 0
        while self.even < self.levels and row_tiles % 2 == 0:
            row_tiles //= 2
            self.even += 1
        unit = 2 ** (self.levels - self.even)
        self.groups = 2**self.even
        self.real = row_tiles * 16
        self.padded = -(-row_tiles // unit) * unit * 16
        self.shard = self.padded // unit

    def sizes(self, level):
        if level < self.even:
            return (self.groups >> (level + 1), self.real)
        return (1, self.padded >> (level - self.even + 1))

    def receive_scratch(self, width):
        last = self.levels - 1
        return [
            pltpu.VMEM(self.sizes(min(level, last)) + (width,), BF16)
            for level in range(self.all_levels)
        ]

    def place(self, level):
        axis, bit = self.bits[level]
        here = lax.axis_index(axis)
        value = (here // bit) % 2
        return value, {axis: here + bit * (1 - 2 * value)}

    def spot(self, level, first, flip):
        group, row = 0, 0
        for index in range(first, level + 1):
            value, _ = self.place(index)
            if flip and index == level:
                value = 1 - value
            if index < self.even:
                group = group + value * (self.groups >> (index + 1))
            else:
                row = row + value * (self.padded >> (index - self.even + 1))
        if level >= self.even:
            row = pl.multiple_of(row, 16)
        count, rows = self.sizes(level)
        return pl.ds(group, count), pl.ds(row, rows)

    def barrier(self):
        semaphore = pltpu.get_barrier_semaphore()
        for level in range(self.all_levels):
            _, partner = self.place(level)
            pl.semaphore_signal(
                semaphore, inc=1, device_id=partner, device_id_type=pl.DeviceIdType.MESH
            )
        pl.semaphore_wait(semaphore, self.all_levels)

    def copy(self, source, target, sends, recvs, level):
        _, partner = self.place(level)
        return pltpu.make_async_remote_copy(
            src_ref=source,
            dst_ref=target,
            send_sem=sends.at[level],
            recv_sem=recvs.at[level],
            device_id=partner,
            device_id_type=pl.DeviceIdType.MESH,
        )

    def reduce_copy(self, level, start_ref, acc_ref, got, sends, recvs):
        if level >= self.levels:
            return self.copy(self.own_shard(acc_ref, 1), got[level], sends, recvs, level)
        groups, rows = self.spot(level, min(level, 1), True)
        source = start_ref if level == 0 else acc_ref
        return self.copy(source.at[groups, rows], got[level], sends, recvs, level)

    def reduce_start(self, level, *refs):
        self.reduce_copy(level, *refs).start()

    def reduce_finish(self, level, start_ref, acc_ref, got, sends, recvs):
        self.reduce_copy(level, start_ref, acc_ref, got, sends, recvs).wait()
        if level >= self.levels:
            own = self.own_shard(acc_ref, 1)
            own[...] = (own[...].astype(F32) + got[level][...].astype(F32)).astype(BF16)
            return
        count, rows = self.sizes(level)
        groups, spots = self.spot(level, min(level, 1), False)
        if level == 0:
            target_groups, target_rows = pl.ds(0, count), pl.ds(0, rows)
            if self.padded > self.real:
                acc_ref[:, self.real :, :] = jnp.zeros_like(acc_ref[:, self.real :, :])
        else:
            target_groups, target_rows = groups, spots
        source = start_ref if level == 0 else acc_ref

        def add(index, carry):
            one = pl.ds(groups.start + index, 1)
            to = pl.ds(target_groups.start + index, 1)
            value = source[one, spots, :].astype(F32) + got[level][pl.ds(index, 1)].astype(F32)
            acc_ref[to, target_rows, :] = value.astype(BF16)
            return carry

        lax.fori_loop(0, count, add, 0)

    def own_shard(self, ref, first):
        if self.levels > self.even:
            return ref.at[self.spot(self.levels - 1, first, False)]
        groups, _ = self.spot(self.levels - 1, first, False)
        return ref.at[groups, pl.ds(0, self.shard)]

    def gather_copy(self, level, full_ref, sends, recvs):
        piece = full_ref.at[self.spot(level, 0, False)]
        return self.copy(piece, piece, sends, recvs, level)

    def gather_start(self, level, *refs):
        self.gather_copy(level, *refs).start()

    def gather_finish(self, level, *refs):
        self.gather_copy(level, *refs).wait()


def modulation_kernel(lead_ref, emb_ref, ada_ref, bias_ref, mod_ref):
    rows = lax.broadcasted_iota(jnp.int32, (16, emb_ref.shape[0]), 0)
    columns = lane_index((16, emb_ref.shape[0]))
    onehot = jnp.zeros((16, emb_ref.shape[0]), F32)
    for step in range(2):
        lead = lead_ref[0, first_step(2) + step]
        onehot = jnp.where((rows == step) & (columns == lead), 1.0, onehot)
    condition = dot(onehot.astype(BF16), emb_ref[...])
    active = (condition * jax.nn.sigmoid(condition)).astype(BF16)
    mod_ref[...] = dot(active, ada_ref[...]) + bias_ref[...].astype(F32)


def project_kernel(sources, queries, *refs):
    x_refs = refs[:sources]
    mod_ref, w_ref = refs[sources : sources + 2]
    outs = refs[sources + 2 :]
    step, which = pl.program_id(0), pl.program_id(1)
    width = w_ref.shape[0]
    x = pick(x_refs, which).astype(F32)
    shift = mod_ref[pl.ds(step, 1), 0:width]
    scale = mod_ref[pl.ds(step, 1), width : 2 * width]
    xhat, _ = normalize(x)
    normed = (xhat * (1.0 + scale) + shift).astype(BF16)
    outs[0][0, 0] = normed
    start = 0 if queries else width
    projected = dot(normed, w_ref[:, start:])
    for part in range(len(outs) - 1):
        for pair in range(width // LANES):
            at = part * width + pair * LANES
            piece = projected[:, at : at + LANES]
            if queries and part == 0:
                piece = piece * (HD**-0.5 * LOG2E)
            outs[part + 1][0, pair, 0] = piece.astype(BF16)


def with_ones(values):
    low = lane_index(values.shape) < HD
    one = jnp.ones_like(values)
    return jnp.where(low, values, one), jnp.where(low, one, values)


def exponentials(query, keys_ref, width=256):
    count = keys_ref.shape[2]
    width = min(width, count)
    return jnp.concatenate(
        [
            jnp.exp2(dot(query, keys_ref[0, 0, start : start + width, :], NT)).astype(BF16)
            for start in range(0, count, width)
        ],
        axis=-1,
    )


def masked(values):
    low = lane_index(values.shape) < HD
    zero = jnp.zeros_like(values)
    return jnp.where(low, values, zero), jnp.where(low, zero, values)


def attend_local_kernel(rows, q_ref, k_ref, v_ref, acc_ref, ext_ref):
    ext_ref[0], ext_ref[1] = with_ones(v_ref[0, 0])

    def block(index, carry):
        at = pl.ds(pl.multiple_of(index * rows, rows), rows)
        for head, query in enumerate(masked(q_ref[0, 0, at, :])):
            acc_ref[0, 0, head, at, :] = dot(exponentials(query, k_ref), ext_ref[head])
        return carry

    lax.fori_loop(0, q_ref.shape[2] // rows, block, 0, unroll=True)


def attend_all_kernel(
    rows, q_ref, k_ref, v_ref, kr_ref, vr_ref, acc_ref, o_ref, qe_ref, ext_ref, total_ref
):
    ext_ref[0], ext_ref[1] = with_ones(vr_ref[0, 0])
    blocks = q_ref.shape[2] // rows

    def finish(at, query, first, second, top_first, top_second):
        lane = lane_index(query.shape)
        low = lane < HD
        swapped = jnp.where(low, second, first)
        total = pltpu.roll(swapped, HD, 1)
        o_ref[0, 0, at, :] = jnp.where(low, first, second) / total
        log_total = jnp.log2(swapped) + jnp.where(low, top_second, top_first)
        high = log_total.astype(BF16).astype(F32)
        middle = (log_total - high).astype(BF16).astype(F32)
        rest = log_total - high - middle
        spot = lane % HD
        extra = jnp.where(spot == 0, -high, jnp.where(spot == 1, -middle, -rest))
        extra = jnp.where(spot < 3, extra, 0.0).astype(BF16)
        qe_ref[0, 0, 0, at, :] = jnp.where(low, query, extra)
        qe_ref[0, 0, 1, at, :] = jnp.where(low, extra, query)
        return total

    def block(index, carry):
        at = pl.ds(pl.multiple_of(index * rows, rows), rows)
        query = q_ref[0, 0, at, :]
        sums = []
        for head, own in enumerate(masked(query)):
            more = dot(exponentials(own, kr_ref), ext_ref[head])
            sums.append(acc_ref[0, 0, head, at, :] + more)
        total_ref[at, :] = finish(at, query, sums[0], sums[1], 0.0, 0.0)
        return carry

    lax.fori_loop(0, blocks, block, 0, unroll=True)
    total = total_ref[...]
    bad = jnp.sum(jnp.where((total > 1e-25) & (total < 1e25), 0.0, 1.0))

    @pl.when(bad > 0.0)
    def _():
        own_ext = with_ones(v_ref[0, 0])

        def again(index, carry):
            at = pl.ds(pl.multiple_of(index * rows, rows), rows)
            query = q_ref[0, 0, at, :]
            sums, tops = [], []
            for head, own in enumerate(masked(query)):
                scores = dot(own, k_ref[0, 0], NT)
                others = dot(own, kr_ref[0, 0], NT)
                top = jnp.maximum(
                    jnp.max(scores, axis=-1, keepdims=True),
                    jnp.max(others, axis=-1, keepdims=True),
                )
                sums.append(
                    dot(jnp.exp2(scores - top).astype(BF16), own_ext[head])
                    + dot(jnp.exp2(others - top).astype(BF16), ext_ref[head])
                )
                tops.append(top)
            finish(at, query, sums[0], sums[1], tops[0], tops[1])
            return carry

        lax.fori_loop(0, blocks, again, 0)


def gelu_parts(values):
    cumulative = 0.5 * lax.erf(values * 0.7071067811865476) + 0.5
    bell = jnp.exp2(values * values * (-0.5 * LOG2E))
    return values * cumulative, cumulative + values * bell * 0.3989422804014327


def patch_kernel(
    rows,
    chunk,
    counts_ref,
    lead_ref,
    own_x,
    sib_x,
    own_ct,
    sib_ct,
    mod_ref,
    o_ref,
    out_w,
    fc1_w,
    fc2_w,
    final_own,
    final_sib,
    gm_ref,
    ge_ref,
    sums_ref,
    stack_one,
    stack_two,
    hidden_s,
    gpre_s,
    n2_s,
    g2_s,
    g1_s,
    mixed_s,
    gout_s,
    gfc1_s,
    gfc2_s,
    sums_s,
):
    step, half = pl.program_id(0), pl.program_id(1)
    width, hidden_width = fc1_w.shape
    patches = own_x.shape[1]
    slot = first_step(pl.num_programs(0)) + step
    active = (slot < counts_ref[0]).astype(F32)

    def piece(index):
        return mod_ref[pl.ds(step, 1), index * width : (index + 1) * width]

    gate1, shift2, scale2, gate2 = piece(2), piece(3), piece(4), piece(5)

    @pl.when((step == 0) & (half == 0))
    def _():
        sums_s[...] = jnp.zeros_like(sums_s)
        gout_s[...] = jnp.zeros_like(gout_s)
        gfc1_s[...] = jnp.zeros_like(gfc1_s)
        gfc2_s[...] = jnp.zeros_like(gfc2_s)

    def block(index, carry):
        at = pl.ds(pl.multiple_of(index * rows, rows), rows)
        x = jnp.where(half == 0, own_x[0, at, :], sib_x[0, at, :]).astype(F32)
        final_grad = jnp.where(half == 0, own_ct[0, at, :], sib_ct[0, at, :]).astype(F32) * active
        outs = [o_ref[0, pair, at, :] for pair in range(width // LANES)]
        mixed = jnp.concatenate([o.astype(BF16) for o in outs], axis=-1)
        mixed_s[at, :] = mixed
        branch_one = dot(mixed, out_w[...])
        middle = x + gate1 * branch_one
        xhat, inverse = normalize(middle)
        n2 = (xhat * (1.0 + scale2) + shift2).astype(BF16)
        n2_s[at, :] = n2
        g2 = (gate2 * final_grad).astype(BF16)
        g2_s[at, :] = g2
        branch_two = jnp.zeros((rows, width), F32)
        gy = jnp.zeros((rows, width), F32)

        def products(start):
            columns = slice(start, start + chunk)
            return dot(n2, fc1_w[:, columns]), dot(g2, fc2_w[columns, :], NT)

        ahead = products(0)
        for start in range(0, hidden_width, chunk):
            columns = slice(start, start + chunk)
            pre, grad_hidden = ahead
            if start + chunk < hidden_width:
                ahead = products(start + chunk)
            hidden, slope = gelu_parts(pre)
            hidden = hidden.astype(BF16)
            grad_pre = (slope * grad_hidden).astype(BF16)
            hidden_s[at, columns] = hidden
            gpre_s[at, columns] = grad_pre
            branch_two += dot(hidden, fc2_w[columns, :])
            gy += dot(grad_pre, fc1_w[:, columns], NT)
        final = ((middle + gate2 * branch_two) * active).astype(BF16)

        @pl.when(half == 0)
        def _():
            final_own[0, at, :] = final

        @pl.when(half == 1)
        def _():
            final_sib[0, at, :] = final

        gm = final_grad + norm_back(gy * (1.0 + scale2), xhat, inverse)
        gm_ref[0, 0, at, :] = gm
        g1 = (gate1 * gm).astype(BF16)
        g1_s[at, :] = g1
        sums = [branch_one * gm, gy, gy * xhat, branch_two * final_grad]
        for row, value in enumerate(sums):
            place = pl.ds(2 * row + step, 1)
            sums_s[place, :] += jnp.sum(value, axis=0, keepdims=True)
        grad_mixed = dot(g1, out_w[...], NT).astype(BF16)
        lane = lane_index((rows, LANES))
        low = lane < HD
        spot = lane % HD
        for pair, o in enumerate(outs):
            grad = grad_mixed[:, pair * LANES : (pair + 1) * LANES]
            product = grad.astype(F32) * o
            first = jnp.sum(jnp.where(low, product, 0.0), axis=-1, keepdims=True)
            second = jnp.sum(jnp.where(low, 0.0, product), axis=-1, keepdims=True)
            inner = jnp.where(low, second, first)
            high = inner.astype(BF16).astype(F32)
            mid = (inner - high).astype(BF16).astype(F32)
            extra = jnp.where(spot == 0, -high, jnp.where(spot == 1, -mid, high + mid - inner))
            extra = jnp.where(spot < 3, extra, 0.0).astype(BF16)
            ge_ref[0, pair, 0, at, :] = jnp.where(low, grad, extra)
            ge_ref[0, pair, 1, at, :] = jnp.where(low, extra, grad)
        return carry

    lax.fori_loop(0, patches // rows, block, 0)
    gout_s[...] += dot(mixed_s[...], g1_s[...], TN)
    for start in range(0, hidden_width, chunk):
        columns = slice(start, start + chunk)
        gfc1_s[:, columns] += dot(n2_s[...], gpre_s[:, columns], TN)
        gfc2_s[:, columns] += dot(g2_s[...], hidden_s[:, columns], TN)

    @pl.when((step == pl.num_programs(0) - 1) & (half == pl.num_programs(1) - 1))
    def _():
        for index in range(2):
            lead = lead_ref[0, first_step(2) + index]
            sums_s[12 + index : 13 + index, :] = jnp.where(lane_index((1, width)) == lead, 1.0, 0.0)
        sums_ref[...] = sums_s[...].astype(BF16)
        blocks = hidden_width // width
        for index in range(blocks):
            columns = slice(index * width, (index + 1) * width)
            stack_one[index] = gfc1_s[:, columns].astype(BF16)
            stack_two[index] = gfc2_s[:, columns].T.astype(BF16)
        stack_two[blocks] = gout_s[...].astype(BF16)


def attend_back_kernel(rows, first_pass, exchanges, grid_steps, *refs):
    count = len(exchanges)
    qe_ref, ge_ref, k_ref, v_ref = refs[:4]
    refs = refs[4:]
    if first_pass:
        gives, sums_ref, refs = refs[:count], refs[count], refs[count + 1 :]
        dq_ref, dk_ref, dv_ref = refs[:3]
        shards, all_ref, refs = refs[3 : 3 + count], refs[3 + count], refs[4 + count :]
        all_s, all_sends, all_recvs = refs[-3:]
    else:
        dq_in, shards, refs = refs[0], refs[1 : 1 + count], refs[1 + count :]
        dq_ref, dk_ref, dv_ref = refs[:3]
        fulls, refs = refs[3 : 3 + count], refs[3 + count :]
    acc_s, refs = refs[0], refs[1:]
    states = []
    for index, exchange in enumerate(exchanges):
        sends, recvs = refs[1], refs[2]
        if first_pass:
            got = refs[3 : 3 + exchange.all_levels]
            states.append((gives[index], refs[0], got, sends, recvs))
            refs = refs[3 + exchange.all_levels :]
        else:
            states.append((refs[0], sends, recvs))
            refs = refs[3:]
    per_step = k_ref.shape[2] // rows
    queries = qe_ref.shape[3]
    piece = min(256, queries)
    slots = pl.num_programs(0) * pl.num_programs(1) * per_step
    static_slots = grid_steps * per_step
    first_slot = (pl.program_id(0) * pl.num_programs(1) + pl.program_id(1)) * per_step
    levels = exchanges[0].all_levels if first_pass else exchanges[0].levels
    if first_pass:
        acc_s[...] = jnp.zeros_like(acc_s)
    else:
        acc_s[...] = dq_in[0, 0].T

    def all_copy(level):
        index = 0
        for lower in range(len(exchanges[0].bits)):
            index = index + exchanges[0].place(lower)[0] * (1 << lower)
        if level < 0:
            return all_s.at[pl.ds(index, 1)]
        size = 1 << level
        piece = all_s.at[pl.ds((index // size) * size, size)]
        return exchanges[0].copy(piece, piece, all_sends, all_recvs, level)

    def reduce_action(order):
        if order == 0:
            exchanges[0].barrier()
            own = all_copy(-1)
            own[...] = sums_ref[...][None]
        else:
            all_copy(order - 1).wait()
        if order < levels:
            all_copy(order).start()
        else:
            all_ref[...] = all_s[...]
        for exchange, state, shard in zip(exchanges, states, shards):
            if order > 0:
                exchange.reduce_finish(order - 1, *state)
            if order < levels:
                exchange.reduce_start(order, *state)
            else:
                shard[...] = exchange.own_shard(state[1], 1)[...][0]

    def gather_action(order):
        if order == 0:
            exchanges[0].barrier()
        for exchange, state, shard in zip(exchanges, states, shards):
            if order == 0:
                exchange.own_shard(state[0], 0)[...] = shard[...][None]
            else:
                exchange.gather_finish(levels - order, *state)
            if order < levels:
                exchange.gather_start(levels - 1 - order, *state)
        if order == levels:
            copies = [
                pltpu.make_async_copy(state[0], full, refs[index])
                for index, (state, full) in enumerate(zip(states, fulls))
            ]
            for copy in copies:
                copy.start()
            for copy in copies:
                copy.wait()

    action = reduce_action if first_pass else gather_action
    weights = [5.0, 10.0, 9.0, 6.0] + [4.0] * levels
    weights = weights[:levels] if first_pass else weights[:levels][::-1]
    marks, total = [0], 0.0
    for weight in weights:
        total += weight
        marks.append(total)
    last = static_slots - (2 if first_pass else 1)
    marks = [min(int(mark * last / total + 0.5), last) for mark in marks]

    def block(index, carry):
        for order, mark in enumerate(marks[:-1]):
            pl.when(first_slot + index == mark)(functools.partial(action, order))
        at = pl.ds(pl.multiple_of(index * rows, rows), rows)
        keys = k_ref[0, 0, at, :]
        values = v_ref[0, 0, at, :]
        lane = lane_index(keys.shape)
        low = lane < HD
        ones = jnp.where(lane % HD < 3, 1.0, 0.0).astype(BF16)
        turned = keys.T
        grads = []
        for head in range(2):
            own = low if head == 0 else jnp.logical_not(low)
            own_keys = jnp.where(own, keys, ones)
            own_values = jnp.where(own, values, ones)
            probs, grad_scores = [], []
            for start in range(0, queries, piece):
                some = slice(start, start + piece)
                prob = jnp.exp2(dot(own_keys, qe_ref[0, 0, head, some, :], NT))
                grad_prob = dot(own_values, ge_ref[0, 0, head, some, :], NT)
                probs.append(prob.astype(BF16))
                grad_scores.append((prob * grad_prob).astype(BF16))
            probs = jnp.concatenate(probs, axis=-1)
            grad_scores = jnp.concatenate(grad_scores, axis=-1)
            grads.append((dot(grad_scores, qe_ref[0, 0, head]), dot(probs, ge_ref[0, 0, head])))
            mine = slice(head * HD, (head + 1) * HD)
            acc_s[mine, :] += dot(turned[mine, :], grad_scores)
        dk_ref[0, 0, at, :] = (jnp.where(low, grads[0][0], grads[1][0]) * LN2).astype(BF16)
        dv_ref[0, 0, at, :] = jnp.where(low, grads[0][1], grads[1][1]).astype(BF16)
        return carry

    lax.fori_loop(0, per_step, block, 0)
    pl.when(first_slot + per_step == slots)(functools.partial(action, levels))
    if first_pass:
        dq_ref[0, 0] = acc_s[...].T
    else:
        dq_ref[0, 0] = (acc_s[...].T * HD**-0.5).astype(BF16)


def project_back_far_kernel(dk_ref, dv_ref, normed_ref, w_ref, dx_ref, gw_ref):
    width = w_ref.shape[0]
    joined = join_heads(dk_ref, dv_ref)
    dx_ref[0, 0] = dot(joined, w_ref[:, width:], NT).astype(BF16)

    @pl.when((pl.program_id(0) == 0) & (pl.program_id(1) == 0))
    def _():
        gw_ref[...] = jnp.zeros_like(gw_ref)

    gw_ref[...] += dot(normed_ref[0, 0], joined, TN)


def weight_back_kernel(dq_ref, dk_ref, dv_ref, normed_ref, far_ref, gw_ref, gw_s):
    step, which = pl.program_id(0), pl.program_id(1)
    width = normed_ref.shape[3]

    @pl.when((step == 0) & (which == 0))
    def _():
        gw_s[:, :width] = jnp.zeros_like(gw_s[:, :width])
        gw_s[:, width:] = far_ref[...]

    gw_s[...] += dot(normed_ref[0, 0], join_heads(dq_ref, dk_ref, dv_ref), TN)

    @pl.when((step == pl.num_programs(0) - 1) & (which == pl.num_programs(1) - 1))
    def _():
        for block in range(gw_ref.shape[0]):
            gw_ref[block] = gw_s[:, block * LANES : (block + 1) * LANES].astype(BF16)


def join_heads(*grads):
    return jnp.concatenate([ref[0, pair] for ref in grads for pair in range(ref.shape[1])], axis=-1)


class Direct:
    def __init__(self, mesh_shape, row_tiles):
        self.chips = mesh_shape["seq"] // 2
        self.peers = mesh_shape["dp"] * self.chips
        self.half = row_tiles * 8
        self.piece = -(-row_tiles // (2 * self.peers)) * 16
        self.padded = self.piece * self.peers

    def me(self):
        return lax.axis_index("dp") * self.chips + lax.axis_index("seq") // 2

    def core(self):
        return lax.axis_index("seq") % 2

    def sibling(self):
        return {"seq": lax.axis_index("seq") + 1 - 2 * self.core()}

    def peer(self, shift):
        other = (self.me() + shift) % self.peers
        device = {"dp": other // self.chips, "seq": (other % self.chips) * 2 + self.core()}
        return other, device

    def rows(self, index):
        return pl.ds(pl.multiple_of(index * self.piece, 16), self.piece)

    def barrier(self):
        semaphore = pltpu.get_barrier_semaphore()

        def signal(device):
            pl.semaphore_signal(semaphore, 1, device_id=device, device_id_type=pl.DeviceIdType.MESH)

        signal(self.sibling())

        def greet(shift, carry):
            signal(self.peer(shift)[1])
            return carry

        lax.fori_loop(1, self.peers, greet, 0)
        pl.semaphore_wait(semaphore, self.peers)

    def copy(self, source, target, send, recv, device):
        return pltpu.make_async_remote_copy(
            src_ref=source,
            dst_ref=target,
            send_sem=send,
            recv_sem=recv,
            device_id=device,
            device_id_type=pl.DeviceIdType.MESH,
        )

    def each_peer(self, do):
        def one(shift, carry):
            do(shift)
            return carry

        lax.fori_loop(1, self.peers, one, 0)


def tail_kernel(direct, remote, *refs):
    give_ref, own_x, sib_x, mod_ref, lead_ref, gm_ref, dq_ref, dk_ref, dv_ref, w_ref = refs[:10]
    others = refs[10 : 10 + remote]
    grad_ref, got_ref, full_ref, all_ref = refs[10 + remote : 14 + remote]
    sums_s, other_s, got_s, sum_s, core_s, pieces_s, full_s, all_s = refs[14 + remote : 22 + remote]
    core_sems, piece_sems, back_sems, all_sems, grad_sems, local_sem = refs[22 + remote :]
    step, half = pl.program_id(0), pl.program_id(1)
    width = own_x.shape[2]
    core, me = direct.core(), direct.me()

    core_copy = direct.copy(
        give_ref.at[1 - core], core_s, core_sems.at[0], core_sems.at[1], direct.sibling()
    )

    def piece_copy(shift):
        other, device = direct.peer(shift)
        return direct.copy(
            sum_s.at[direct.rows(other)],
            pieces_s.at[shift],
            piece_sems.at[0, shift],
            piece_sems.at[1, shift],
            device,
        )

    def full_copy(shift, arriving):
        _, device = direct.peer(shift)
        owner = (me + direct.peers - shift) % direct.peers if arriving else me
        place = full_s.at[core, direct.rows(owner)]
        return direct.copy(place, place, back_sems.at[0, shift], back_sems.at[1, shift], device)

    def sums_copy(shift, arriving):
        _, device = direct.peer(shift)
        owner = (me + direct.peers - shift) % direct.peers if arriving else me
        place = all_s.at[core, owner]
        return direct.copy(place, place, all_sems.at[0, shift], all_sems.at[1, shift], device)

    def side_copy(values, which, side):
        place = values.at[side]
        return direct.copy(
            place, place, core_sems.at[which], core_sems.at[which + 1], direct.sibling()
        )

    def grad_copy(index):
        return direct.copy(
            other_s.at[index],
            got_s.at[index],
            grad_sems.at[0, index],
            grad_sems.at[1, index],
            direct.sibling(),
        )

    @pl.when((step == 0) & (half == 0))
    def _():
        direct.barrier()
        core_copy.start()
        sums_s[...] = jnp.zeros_like(sums_s)

    @pl.when((step == 0) & (half == 1))
    def _():
        core_copy.wait()
        real = core_s.shape[0]
        sum_s[:real] = (give_ref[core].astype(F32) + core_s[...].astype(F32)).astype(BF16)
        if direct.padded > real:
            sum_s[real:] = jnp.zeros_like(sum_s[real:])
        direct.each_peer(lambda shift: piece_copy(shift).start())

    x = jnp.where(half == 0, own_x[0], sib_x[0]).astype(F32)
    scale = mod_ref[pl.ds(step, 1), width : 2 * width]
    xhat, inverse = normalize(x)
    gy = dot(join_heads(dq_ref, dk_ref, dv_ref), w_ref[...], NT)
    for other in others:
        gy = gy + other[0, 0].astype(F32)
    grad = (gm_ref[0, 0] + norm_back(gy * (1.0 + scale), xhat, inverse)).astype(BF16)

    @pl.when(half == 0)
    def _():
        grad_ref[0] = grad

    @pl.when(half == 1)
    def _():
        other_s[step] = grad
        grad_copy(step).start()

    for kind, value in enumerate((gy, gy * xhat)):
        total = jnp.sum(value, axis=0, keepdims=True)
        for index in range(width // LANES):
            place = pl.ds((kind * 2 + step) * (width // LANES) + index, 1)
            sums_s[place, :] += total[:, index * LANES : (index + 1) * LANES]

    @pl.when((step == 1) & (half == 1))
    def _():
        for index in range(2):
            chosen = lane_index((1, LANES)) == lead_ref[0, first_step(2) + index]
            sums_s[12 + index : 13 + index, :] = jnp.where(chosen, 1.0, 0.0)
        all_s[core, me] = sums_s[...].astype(BF16)
        direct.each_peer(lambda shift: sums_copy(shift, False).start())
        direct.each_peer(lambda shift: piece_copy(shift).wait())

        def add(shift, total):
            return total + pieces_s[shift].astype(F32)

        total = lax.fori_loop(1, direct.peers, add, sum_s[direct.rows(me)].astype(F32))
        full_s[core, direct.rows(me)] = total.astype(BF16)
        direct.each_peer(lambda shift: full_copy(shift, False).start())

        def arrived(shift):
            full_copy(shift, False).wait_send()
            full_copy(shift, True).wait_recv()
            sums_copy(shift, False).wait_send()
            sums_copy(shift, True).wait_recv()

        direct.each_peer(arrived)
        side_copy(full_s, 2, core).start()
        side_copy(all_s, 4, core).start()
        for index in range(2):
            grad_copy(index).wait()
        side_copy(full_s, 2, core).wait_send()
        side_copy(full_s, 2, 1 - core).wait_recv()
        side_copy(all_s, 4, core).wait_send()
        side_copy(all_s, 4, 1 - core).wait_recv()
        outs = [(got_s, got_ref), (full_s, full_ref), (all_s, all_ref)]
        copies = [
            pltpu.make_async_copy(source, target, local_sem.at[index])
            for index, (source, target) in enumerate(outs)
        ]
        for copy in copies:
            copy.start()
        for copy in copies:
            copy.wait()


def unstack(at, full_ref, targets, rows):
    row, end = 0, rows * len(targets)
    while row < end:
        group, inside, left = at(row)
        block, place = divmod(row, rows)
        count = min(left, rows - place)
        target, first_row, first_column = targets[block]
        columns = slice(first_column, first_column + full_ref.shape[2])
        value = full_ref[group, inside : inside + count, :].astype(F32)
        target[first_row + place : first_row + place + count, columns] = value
        row += count


def spread_leads(grads, step_of, table_rows):
    count = grads.shape[0]
    part = min(count, 512)
    row = lax.broadcasted_iota(jnp.int32, (part, part), 0)
    column = lane_index((part, part))
    chosen = (row // 16 == column // 16) & (row % 16 == 12 + step_of(column % 16))
    spread = jnp.where(chosen, 1.0, 0.0).astype(BF16)
    leads = [
        dot(grads[start : start + part, :LANES], spread, TN)[:table_rows]
        for start in range(0, count, part)
    ]
    return jnp.concatenate(leads, axis=-1)


def final_kernel(early, direct, *refs):
    early_sums, late_sums, emb_ref, ada_ref, one_ref, two_ref, late_ref = refs[:7]
    final_ref, final_got, grad_ref, grad_got = refs[7:11]
    outs = refs[11:20]
    gada_s, gqkv_s, gout_s, gfc1_s, gfc2_s, sems = refs[20:]
    final_out, grad_out, gemb_ref, gada_out, gbada_ref, gqkv_out, gout_out, gfc1_out, gfc2_out = outs
    size = gout_s.shape[0]
    blocks = gfc1_s.shape[1] // size
    copies = []

    def start(source, target):
        copy = pltpu.make_async_copy(source, target, sems.at[len(copies)])
        copy.start()
        copies.append(copy)

    mine = first_step(2)
    for index in range(2):
        start(final_ref.at[index], final_out.at[mine + index])
        start(final_got.at[index], final_out.at[2 - mine + index])
        start(grad_ref.at[index], grad_out.at[mine + index])
        start(grad_got.at[index], grad_out.at[2 - mine + index])

    def grouped(exchange):
        def at(row):
            group, inside = divmod(row, exchange.real)
            return group, inside, exchange.real - inside

        return at

    def halved(row):
        group, inside = divmod(row, direct.half)
        return group, inside, direct.half - inside

    unstack(grouped(early[0]), one_ref, [(gfc1_s, 0, block * size) for block in range(blocks)], size)
    start(gfc1_s, gfc1_out)
    rest = [(gfc2_s, block * size, 0) for block in range(blocks)] + [(gout_s, 0, 0)]
    unstack(grouped(early[1]), two_ref, rest, size)
    start(gfc2_s, gfc2_out)
    start(gout_s, gout_out)
    columns = gqkv_s.shape[1] // LANES
    unstack(halved, late_ref, [(gqkv_s, 0, block * LANES) for block in range(columns)], size)
    start(gqkv_s, gqkv_out)

    table_rows = emb_ref.shape[0]
    table = emb_ref[...].astype(F32)
    gate = jax.nn.sigmoid(table)
    slope = gate * (1.0 + table * (1.0 - gate))
    table_act = (table * gate).astype(BF16)
    total = jnp.zeros((table_rows, size), F32)

    def one_piece(grads, leads, place, first):
        chosen = jnp.where(place, leads, 0.0).astype(BF16)
        acts = dot(table_act, chosen, TN).astype(BF16)
        where = slice(first, first + grads.shape[1])
        gada_s[:, where] = dot(acts, grads)
        by_lead = dot(chosen, grads)
        gbada_ref[:, where] = jnp.sum(by_lead, axis=0, keepdims=True)
        high = by_lead.astype(BF16)
        low = (by_lead - high.astype(F32)).astype(BF16)
        return dot(high, ada_ref[:, where], NT) + dot(low, ada_ref[:, where], NT)

    grads = early_sums[...]
    leads = spread_leads(grads, lambda row: row % 2, table_rows)
    row = lane_index((1, grads.shape[0])) % 16
    for index in range(4):
        total += one_piece(grads, leads, row // 2 == index, (2 + index) * size)
    grads = late_sums[...]
    parts = size // LANES
    leads = spread_leads(grads, lambda row: (row // parts) % 2, table_rows)
    row = lane_index((1, grads.shape[0])) % 16
    for index in range(2):
        for part in range(parts):
            place = (row // (2 * parts) == index) & (row % parts == part)
            total += one_piece(grads, leads, place, index * size + part * LANES)
    gemb_ref[...] = total * slope
    start(gada_s, gada_out)
    for copy in copies:
        copy.wait()


def local(
    mesh_shape, inputs, cotangent, counts, lead_steps, emb_table, w_ada, b_ada, w_qkv, w_out, w_fc1, w_fc2
):
    slots, items, patches, width = inputs.shape
    chips = mesh_shape["seq"] // 2
    blocks = w_fc1.shape[1] // w_fc1.shape[0]
    steps = slots * items // 2
    hidden_width = w_fc1.shape[1]
    pairs = width // LANES
    rows = 2 * patches
    remote = 2 * (chips - 1)
    far_rows = remote * patches
    spot = lax.axis_index("seq")
    core = lax.rem(spot, 2)
    devices = 2 * chips

    def send(values, shift, cross):
        pairs_list = []
        for source in range(devices):
            chip, side = source // 2, source % 2
            pairs_list.append((source, ((chip + shift) % chips) * 2 + (1 - side if cross else side)))
        return lax.ppermute(values, "seq", pairs_list)

    x_steps = inputs.reshape(2, steps, patches, width)
    ct_steps = cotangent.reshape(2, steps, patches, width)
    own_x = lax.dynamic_index_in_dim(x_steps, core, 0, keepdims=False)
    other_x = lax.dynamic_index_in_dim(x_steps, 1 - core, 0, keepdims=False)
    own_ct = lax.dynamic_index_in_dim(ct_steps, core, 0, keepdims=False)
    other_ct = lax.dynamic_index_in_dim(ct_steps, 1 - core, 0, keepdims=False)
    sib_x = send(other_x, 0, True)
    far_x = []
    for shift in range(1, chips):
        far_x.append(send(own_x, shift, False))
        far_x.append(send(other_x, shift, True))
    sib_ct = send(other_ct, 0, True)
    mod = call(
        modulation_kernel,
        "modulation",
        (),
        [scalars(), whole(emb_table.shape), whole(w_ada.shape), whole((1, 6 * width))],
        whole((16, 6 * width)),
        jax.ShapeDtypeStruct((16, 6 * width), F32),
        flops=2 * 16 * width * 6 * width,
        moved=2 * w_ada.size,
    )(lead_steps, emb_table, w_ada, b_ada.reshape(1, -1))

    step_block = pl.BlockSpec((1, patches, width), lambda j, i: (j, 0, 0))
    patch_block = pl.BlockSpec((1, 1, patches, width), lambda j, i: (j, i, 0, 0))

    def project(sources, queries, name):
        parts = 3 if queries else 2
        count = len(sources)
        head_block = pl.BlockSpec((1, pairs, 1, patches, LANES), lambda j, i: (j, 0, i, 0, 0))
        outs = call(
            functools.partial(project_kernel, count, queries),
            name,
            (steps, count),
            [step_block] * count + [whole(mod.shape), whole(w_qkv.shape)],
            [patch_block] + [head_block] * parts,
            [jax.ShapeDtypeStruct((steps, count, patches, width), BF16)]
            + [jax.ShapeDtypeStruct((steps, pairs, count, patches, LANES), BF16)] * parts,
            flops=2 * steps * count * patches * width * parts * width,
            moved=2 * steps * count * patches * width * (2 + parts),
        )(*sources, mod, w_qkv)
        return [outs[0]] + [o.reshape(steps, pairs, count * patches, LANES) for o in outs[1:]]

    n1, q, k, v = project([own_x, sib_x], True, "project_near")

    def head_rows(count):
        return pl.BlockSpec((1, 1, count, LANES), lambda j, p: (j, p, 0, 0))

    both_heads = pl.BlockSpec((1, 1, 2, rows, LANES), lambda j, p: (j, p, 0, 0, 0))
    query_rows = min(256, rows)
    near_work = 4 * steps * pairs * 2 * rows * LANES * rows
    far_work = 4 * steps * pairs * 2 * rows * LANES * far_rows
    acc = call(
        functools.partial(attend_local_kernel, query_rows),
        "attend_near",
        (steps, pairs),
        [head_rows(rows)] * 3,
        both_heads,
        jax.ShapeDtypeStruct((steps, pairs, 2, rows, LANES), F32),
        [pltpu.VMEM((2, rows, LANES), BF16)],
        flops=near_work,
        exps=steps * pairs * 2 * rows * rows,
    )(q, k, v)

    n1r, kr, vr = project(far_x, False, "project_far")
    o, qe = call(
        functools.partial(attend_all_kernel, query_rows),
        "attend_far",
        (steps, pairs),
        [head_rows(rows)] * 3 + [head_rows(far_rows)] * 2 + [both_heads],
        [head_rows(rows), both_heads],
        [
            jax.ShapeDtypeStruct((steps, pairs, rows, LANES), F32),
            jax.ShapeDtypeStruct((steps, pairs, 2, rows, LANES), BF16),
        ],
        [pltpu.VMEM((2, far_rows, LANES), BF16), pltpu.VMEM((rows, LANES), F32)],
        flops=far_work,
        exps=steps * pairs * 2 * rows * far_rows,
    )(q, k, v, kr, vr, acc)

    block_rows = min(256, patches)
    outs = call(
        functools.partial(patch_kernel, block_rows, 512),
        "patchwise",
        (steps, 2),
        [scalars()] * 2
        + [step_block] * 4
        + [
            whole(mod.shape),
            pl.BlockSpec((1, pairs, patches, LANES), lambda j, i: (j, 0, i, 0)),
            whole(w_out.shape),
            whole(w_fc1.shape),
            whole(w_fc2.shape),
        ],
        [
            step_block,
            step_block,
            patch_block,
            pl.BlockSpec((1, pairs, 2, patches, LANES), lambda j, i: (j, 0, 0, i, 0)),
            whole((16, width)),
            whole((blocks, width, width)),
            whole((blocks + 1, width, width)),
        ],
        [
            jax.ShapeDtypeStruct((steps, patches, width), BF16),
            jax.ShapeDtypeStruct((steps, patches, width), BF16),
            jax.ShapeDtypeStruct((steps, 2, patches, width), F32),
            jax.ShapeDtypeStruct((steps, pairs, 2, rows, LANES), BF16),
            jax.ShapeDtypeStruct((16, width), BF16),
            jax.ShapeDtypeStruct((blocks, width, width), BF16),
            jax.ShapeDtypeStruct((blocks + 1, width, width), BF16),
        ],
        [pltpu.VMEM((patches, hidden_width), BF16)] * 2
        + [pltpu.VMEM((patches, width), BF16)] * 4
        + [
            pltpu.VMEM((width, width), F32),
            pltpu.VMEM((width, hidden_width), F32),
            pltpu.VMEM((width, hidden_width), F32),
            pltpu.VMEM((16, width), F32),
        ],
        flops=6 * steps * rows * width * (2 * hidden_width + width),
        moved=steps * rows * width * 20,
        exps=2 * steps * rows * hidden_width,
    )(counts, lead_steps, own_x, sib_x, own_ct, sib_ct, mod, o, w_out, w_fc1, w_fc2)
    final_own, final_sib, gm, ge, sums, stack_one, stack_two = outs
    final_got = send(final_sib, 0, True)
    early = [Exchange(mesh_shape, blocks * width // 16, 0), Exchange(mesh_shape, (blocks + 1) * width // 16, 1)]
    gives = [g.reshape(e.groups, e.real, width) for e, g in zip(early, (stack_one, stack_two))]

    def attend_back(keys, values, extra, first, name):
        count = keys.shape[2]
        key_rows = min(256, count)
        in_specs = [both_heads] * 2 + [head_rows(count)] * 2
        out_specs = [head_rows(rows), head_rows(count), head_rows(count)]
        out_shape = [
            jax.ShapeDtypeStruct((steps, pairs, rows, LANES), F32 if first else BF16),
            jax.ShapeDtypeStruct((steps, pairs, count, LANES), BF16),
            jax.ShapeDtypeStruct((steps, pairs, count, LANES), BF16),
        ]
        scratch = [pltpu.VMEM((LANES, rows), F32)]
        if not first:
            in_specs += [head_rows(rows)]
        for exchange in early:
            shape = (exchange.groups, exchange.padded, width)
            shard = (exchange.shard, width)
            sems = [pltpu.SemaphoreType.DMA((exchange.all_levels,))] * 2
            if first:
                in_specs += [whole((exchange.groups, exchange.real, width))]
                out_specs += [whole(shard)]
                out_shape += [jax.ShapeDtypeStruct(shard, BF16)]
                half = (exchange.groups // 2, exchange.padded, width)
                scratch += [pltpu.VMEM(half, BF16)] + sems + exchange.receive_scratch(width)
            else:
                in_specs += [whole(shard)]
                out_specs += [pl.BlockSpec(memory_space=pl.ANY)]
                out_shape += [jax.ShapeDtypeStruct(shape, BF16)]
                scratch += [pltpu.VMEM(shape, BF16)] + sems
        if first:
            every = (mesh_shape["dp"] * mesh_shape["seq"], 16, width)
            in_specs += [whole(sums.shape)]
            out_specs += [whole(every)]
            out_shape += [jax.ShapeDtypeStruct(every, BF16)]
            sems = [pltpu.SemaphoreType.DMA((early[0].all_levels,))] * 2
            scratch += [pltpu.VMEM(every, BF16)] + sems
        else:
            scratch += [pltpu.SemaphoreType.DMA] * len(early)
        return call(
            functools.partial(attend_back_kernel, key_rows, first, early, steps * pairs),
            name,
            (steps, pairs),
            in_specs,
            out_specs,
            out_shape,
            scratch,
            flops=10 * steps * pairs * 2 * rows * count * LANES,
            exps=steps * pairs * 2 * rows * count,
            collective=1 if first else 2,
        )(qe, ge, keys, values, *extra)

    grad_block = pl.BlockSpec((1, pairs, patches, LANES), lambda j, i: (j, 0, i, 0))
    hbm = pl.BlockSpec(memory_space=pl.ANY)

    dq_part, dkr, dvr, shard_one, shard_two, early_all = attend_back(
        kr, vr, [*gives, sums], True, "attend_back_far"
    )
    dx_far, gw_part = call(
        project_back_far_kernel,
        "project_back_far",
        (steps, remote),
        [grad_block] * 2 + [patch_block, whole(w_qkv.shape)],
        [patch_block, whole((width, 2 * width))],
        [
            jax.ShapeDtypeStruct((steps, remote, patches, width), BF16),
            jax.ShapeDtypeStruct((width, 2 * width), F32),
        ],
        flops=4 * steps * far_rows * width * 2 * width,
        moved=steps * far_rows * width * 8,
    )(dkr, dvr, n1r, w_qkv)
    dx_got = [send(dx_far[:, 2 * r - 2 : 2 * r], -r, False) for r in range(1, chips)]
    dq, dk, dv, *early_sums = attend_back(
        k, v, [dq_part, shard_one, shard_two], False, "attend_back_near"
    )
    columns = w_qkv.shape[1] // LANES
    give_late = call(
        weight_back_kernel,
        "weight_back",
        (steps, 2),
        [grad_block] * 3 + [patch_block, whole(gw_part.shape)],
        whole((columns, width, LANES)),
        jax.ShapeDtypeStruct((columns, width, LANES), BF16),
        [pltpu.VMEM((width, columns * LANES), F32)],
        flops=2 * steps * rows * width * 3 * width,
        moved=steps * rows * width * 8,
    )(dq, dk, dv, n1, gw_part)

    direct = Direct(mesh_shape, columns * width // 16)
    full_shape = (2, direct.padded, LANES)
    late_all_shape = (2, direct.peers, 16, LANES)
    grad_own, grad_got, late_sum, late_all = call(
        functools.partial(tail_kernel, direct, len(dx_got)),
        "tail",
        (steps, 2),
        [whole((2, direct.half, LANES)), step_block, step_block, whole(mod.shape), scalars()]
        + [patch_block]
        + [grad_block] * 3
        + [whole(w_qkv.shape)]
        + [patch_block] * len(dx_got),
        [step_block, hbm, hbm, hbm],
        [
            jax.ShapeDtypeStruct((steps, patches, width), BF16),
            jax.ShapeDtypeStruct((steps, patches, width), BF16),
            jax.ShapeDtypeStruct(full_shape, BF16),
            jax.ShapeDtypeStruct(late_all_shape, BF16),
        ],
        [
            pltpu.VMEM((16, LANES), F32),
            pltpu.VMEM((steps, patches, width), BF16),
            pltpu.VMEM((steps, patches, width), BF16),
            pltpu.VMEM((direct.padded, LANES), BF16),
            pltpu.VMEM((direct.half, LANES), BF16),
            pltpu.VMEM((direct.peers, direct.piece, LANES), BF16),
            pltpu.VMEM(full_shape, BF16),
            pltpu.VMEM(late_all_shape, BF16),
            pltpu.SemaphoreType.DMA((6,)),
            pltpu.SemaphoreType.DMA((2, direct.peers)),
            pltpu.SemaphoreType.DMA((2, direct.peers)),
            pltpu.SemaphoreType.DMA((2, direct.peers)),
            pltpu.SemaphoreType.DMA((2, steps)),
            pltpu.SemaphoreType.DMA((3,)),
        ],
        flops=2 * steps * rows * width * 3 * width,
        collective=3,
    )(
        give_late.reshape(2, direct.half, LANES),
        own_x,
        sib_x,
        mod,
        lead_steps,
        gm,
        dq,
        dk,
        dv,
        w_qkv,
        *dx_got,
    )

    early_all = early_all.reshape(-1, width)
    late_all = late_all.reshape(-1, LANES)
    small = [early_all, late_all, emb_table, w_ada, *early_sums, late_sum]
    out_shapes = [(slots * items, patches, width)] * 2 + [emb_table.shape, w_ada.shape]
    out_shapes += [(1, 6 * width), w_qkv.shape, w_out.shape, w_fc1.shape, w_fc2.shape]
    outs = call(
        functools.partial(final_kernel, early, direct),
        "final",
        (),
        [whole(value.shape) for value in small] + [whole((steps, patches, width))] * 4,
        [hbm] * 2 + [whole(emb_table.shape), hbm, whole((1, 6 * width))] + [hbm] * 4,
        [
            jax.ShapeDtypeStruct(shape, BF16 if index < 2 else F32)
            for index, shape in enumerate(out_shapes)
        ],
        [pltpu.VMEM(w.shape, F32) for w in (w_ada, w_qkv, w_out, w_fc1, w_fc2)]
        + [pltpu.SemaphoreType.DMA((4 * 2 + 5,))],
        flops=2 * early_all.shape[0] * width * 6 * width,
        moved=6 * w_ada.size,
    )(*small, final_own, final_got, grad_own, grad_got)
    outputs, grad_inputs, g_emb, g_ada, g_bada, g_qkv, g_out, g_fc1, g_fc2 = outs
    return (
        outputs.reshape(inputs.shape),
        grad_inputs.reshape(inputs.shape),
        g_emb,
        g_ada,
        g_bada.reshape(-1),
        g_qkv,
        g_out,
        g_fc1,
        g_fc2,
    )


def solution(mesh):
    tokens = P(None, "dp", "seq", None)
    return jax.shard_map(
        functools.partial(local, dict(mesh.shape)),
        mesh=mesh,
        in_specs=(tokens, tokens, P("dp"), P("dp", None)) + (P(),) * 7,
        out_specs=(tokens, tokens) + (P(),) * 7,
        check_vma=False,
    )
```

```python
import functools

import jax
import jax.numpy as jnp
from jax import lax
from jax.experimental import pallas as pl
from jax.experimental.pallas import tpu as pltpu
from jax.sharding import PartitionSpec as P

HD = 64
LANES = 128
EPSILON = 1e-06
LOG2E = 1.4426950408889634
LN2 = 0.6931471805599453
NN = (((1,), (0,)), ((), ()))
NT = (((1,), (1,)), ((), ()))
TN = (((0,), (0,)), ((), ()))
F32 = jnp.float32
BF16 = jnp.bfloat16
VMEM_BYTES = 56 * 1024 * 1024


def dot(a, b, dims=NN):
    return lax.dot_general(a, b, dims, preferred_element_type=F32)


def call(
    body,
    name,
    grid,
    in_specs,
    out_specs,
    out_shape,
    scratch=(),
    flops=0,
    moved=0,
    exps=0,
    collective=None,
    aliases=None,
):
    return pl.pallas_call(
        body,
        name=name,
        grid=grid,
        in_specs=in_specs,
        out_specs=out_specs,
        out_shape=out_shape,
        scratch_shapes=list(scratch),
        input_output_aliases=aliases or {},
        cost_estimate=pl.CostEstimate(flops=flops, bytes_accessed=moved, transcendentals=exps),
        compiler_params=pltpu.CompilerParams(
            vmem_limit_bytes=VMEM_BYTES,
            collective_id=collective,
            has_side_effects=collective is not None,
        ),
    )


def whole(shape):
    return pl.BlockSpec(shape, lambda *_: (0,) * len(shape))


def scalars():
    return pl.BlockSpec(memory_space=pltpu.SMEM)


def lane_index(shape):
    return lax.broadcasted_iota(jnp.int32, shape, 1)


def first_step(steps):
    return lax.rem(lax.axis_index("seq"), 2) * steps


def normalize(values):
    center = values - jnp.mean(values, axis=-1, keepdims=True)
    spread = jnp.mean(center * center, axis=-1, keepdims=True)
    inverse = lax.rsqrt(spread + EPSILON)
    return center * inverse, inverse


def norm_back(grad, xhat, inverse):
    first = jnp.mean(grad, axis=-1, keepdims=True)
    second = jnp.mean(grad * xhat, axis=-1, keepdims=True)
    return inverse * (grad - first - xhat * second)


def pick(refs, which):
    value = refs[0][0]
    for index in range(1, len(refs)):
        value = jnp.where(which == index, refs[index][0], value)
    return value


class Exchange:
    def __init__(self, mesh_shape, row_tiles, turn=0):
        bits = {"seq": [], "dp": []}
        for axis in bits:
            bit = 1
            while bit < mesh_shape[axis]:
                bits[axis].append((axis, bit))
                bit *= 2
        turned = bits["dp"][turn:] + bits["dp"][:turn]
        self.bits = bits["seq"][:1] + turned + bits["seq"][1:]
        self.all_levels = len(self.bits)
        self.levels = 1 + len(turned)
        self.even = 0
        while self.even < self.levels and row_tiles % 2 == 0:
            row_tiles //= 2
            self.even += 1
        unit = 2 ** (self.levels - self.even)
        self.groups = 2**self.even
        self.real = row_tiles * 16
        self.padded = -(-row_tiles // unit) * unit * 16
        self.shard = self.padded // unit

    def sizes(self, level):
        if level < self.even:
            return (self.groups >> (level + 1), self.real)
        return (1, self.padded >> (level - self.even + 1))

    def receive_scratch(self, width):
        last = self.levels - 1
        return [
            pltpu.VMEM(self.sizes(min(level, last)) + (width,), BF16)
            for level in range(self.all_levels)
        ]

    def place(self, level):
        axis, bit = self.bits[level]
        here = lax.axis_index(axis)
        value = (here // bit) % 2
        return value, {axis: here + bit * (1 - 2 * value)}

    def spot(self, level, first, flip):
        group, row = 0, 0
        for index in range(first, level + 1):
            value, _ = self.place(index)
            if flip and index == level:
                value = 1 - value
            if index < self.even:
                group = group + value * (self.groups >> (index + 1))
            else:
                row = row + value * (self.padded >> (index - self.even + 1))
        if level >= self.even:
            row = pl.multiple_of(row, 16)
        count, rows = self.sizes(level)
        return pl.ds(group, count), pl.ds(row, rows)

    def barrier(self):
        semaphore = pltpu.get_barrier_semaphore()
        for level in range(self.all_levels):
            _, partner = self.place(level)
            pl.semaphore_signal(
                semaphore, inc=1, device_id=partner, device_id_type=pl.DeviceIdType.MESH
            )
        pl.semaphore_wait(semaphore, self.all_levels)

    def copy(self, source, target, sends, recvs, level):
        _, partner = self.place(level)
        return pltpu.make_async_remote_copy(
            src_ref=source,
            dst_ref=target,
            send_sem=sends.at[level],
            recv_sem=recvs.at[level],
            device_id=partner,
            device_id_type=pl.DeviceIdType.MESH,
        )

    def reduce_copy(self, level, start_ref, acc_ref, got, sends, recvs):
        if level >= self.levels:
            return self.copy(self.own_shard(acc_ref, 1), got[level], sends, recvs, level)
        groups, rows = self.spot(level, min(level, 1), True)
        source = start_ref if level == 0 else acc_ref
        return self.copy(source.at[groups, rows], got[level], sends, recvs, level)

    def reduce_start(self, level, *refs):
        self.reduce_copy(level, *refs).start()

    def reduce_finish(self, level, start_ref, acc_ref, got, sends, recvs):
        self.reduce_copy(level, start_ref, acc_ref, got, sends, recvs).wait()
        if level >= self.levels:
            own = self.own_shard(acc_ref, 1)
            own[...] = (own[...].astype(F32) + got[level][...].astype(F32)).astype(BF16)
            return
        count, rows = self.sizes(level)
        groups, spots = self.spot(level, min(level, 1), False)
        if level == 0:
            target_groups, target_rows = pl.ds(0, count), pl.ds(0, rows)
            if self.padded > self.real:
                acc_ref[:, self.real :, :] = jnp.zeros_like(acc_ref[:, self.real :, :])
        else:
            target_groups, target_rows = groups, spots
        source = start_ref if level == 0 else acc_ref

        def add(index, carry):
            one = pl.ds(groups.start + index, 1)
            to = pl.ds(target_groups.start + index, 1)
            value = source[one, spots, :].astype(F32) + got[level][pl.ds(index, 1)].astype(F32)
            acc_ref[to, target_rows, :] = value.astype(BF16)
            return carry

        lax.fori_loop(0, count, add, 0)

    def own_shard(self, ref, first):
        if self.levels > self.even:
            return ref.at[self.spot(self.levels - 1, first, False)]
        groups, _ = self.spot(self.levels - 1, first, False)
        return ref.at[groups, pl.ds(0, self.shard)]

    def gather_copy(self, level, full_ref, sends, recvs):
        piece = full_ref.at[self.spot(level, 0, False)]
        return self.copy(piece, piece, sends, recvs, level)

    def gather_start(self, level, *refs):
        self.gather_copy(level, *refs).start()

    def gather_finish(self, level, *refs):
        self.gather_copy(level, *refs).wait()


def modulation(lead_ref, emb_ref, ada_ref, bias_ref):
    shape = (16, emb_ref.shape[0])
    rows = lax.broadcasted_iota(jnp.int32, shape, 0)
    columns = lane_index(shape)
    onehot = jnp.zeros(shape, F32)
    for step in range(2):
        lead = lead_ref[0, first_step(2) + step]
        onehot = jnp.where((rows == step) & (columns == lead), 1.0, onehot)
    condition = dot(onehot.astype(BF16), emb_ref[...])
    active = (condition * jax.nn.sigmoid(condition)).astype(BF16)
    return dot(active, ada_ref[...]) + bias_ref[...].astype(F32)


def project(x_refs, mod_ref, step, w_ref, normed_ref, head_refs):
    width = w_ref.shape[0]
    patches = x_refs[0].shape[1]
    shift = mod_ref[pl.ds(step, 1), 0:width]
    scale = mod_ref[pl.ds(step, 1), width : 2 * width]
    queries = len(head_refs) == 3
    for index, x_ref in enumerate(x_refs):
        at = slice(index * patches, (index + 1) * patches)
        xhat, _ = normalize(x_ref[0].astype(F32))
        normed = (xhat * (1.0 + scale) + shift).astype(BF16)
        normed_ref[0, at, :] = normed
        for part, head_ref in enumerate(head_refs):
            start = (part + (0 if queries else 1)) * width
            projected = dot(normed, w_ref[:, start : start + width])
            if queries and part == 0:
                projected = projected * (HD**-0.5 * LOG2E)
            projected = projected.astype(BF16)
            for pair in range(width // LANES):
                head_ref[0, pair, at, :] = projected[:, pair * LANES : (pair + 1) * LANES]


def with_ones(values):
    low = lane_index(values.shape) < HD
    one = jnp.ones_like(values)
    return jnp.where(low, values, one), jnp.where(low, one, values)


def exponentials(query, keys_ref, pair, width=256):
    count = keys_ref.shape[2]
    width = min(width, count)
    return jnp.concatenate(
        [
            jnp.exp2(dot(query, keys_ref[0, pair, start : start + width, :], NT)).astype(BF16)
            for start in range(0, count, width)
        ],
        axis=-1,
    )


def masked(values):
    low = lane_index(values.shape) < HD
    zero = jnp.zeros_like(values)
    return jnp.where(low, values, zero), jnp.where(low, zero, values)


def near_kernel(rows, *refs):
    lead_ref, emb_ref, ada_ref, bias_ref, own_x, sib_x, w_ref = refs[:7]
    mod_ref, normed_ref, q_ref, k_ref, v_ref, acc_ref = refs[7:]
    step, pair = pl.program_id(0), pl.program_id(1)

    @pl.when((step == 0) & (pair == 0))
    def _():
        mod_ref[...] = modulation(lead_ref, emb_ref, ada_ref, bias_ref)

    @pl.when(pair == 0)
    def _():
        project([own_x, sib_x], mod_ref, step, w_ref, normed_ref, [q_ref, k_ref, v_ref])

    ext = with_ones(v_ref[0, pair])
    for start in range(0, q_ref.shape[2], rows):
        at = slice(start, start + rows)
        for head, query in enumerate(masked(q_ref[0, pair, at, :])):
            acc_ref[0, 0, head, at, :] = dot(exponentials(query, k_ref, pair), ext[head])


def far_kernel(rows, step, sources, *refs):
    x_refs, refs = refs[:sources], refs[sources:]
    mod_ref, w_ref, q_ref, k_ref, v_ref, acc_ref = refs[:6]
    normed_ref, kr_ref, vr_ref, o_ref, qe_ref, ext_ref, total_ref = refs[-7:]
    pair = pl.program_id(0)

    @pl.when(pair == 0)
    def _():
        project(x_refs, mod_ref, step, w_ref, normed_ref, [kr_ref, vr_ref])

    ext_ref[0], ext_ref[1] = with_ones(vr_ref[0, pair])
    def finish(at, query, first, second, top_first, top_second):
        lane = lane_index(query.shape)
        low = lane < HD
        swapped = jnp.where(low, second, first)
        total = pltpu.roll(swapped, HD, 1)
        o_ref[0, 0, at, :] = jnp.where(low, first, second) / total
        log_total = jnp.log2(swapped) + jnp.where(low, top_second, top_first)
        high = log_total.astype(BF16).astype(F32)
        middle = (log_total - high).astype(BF16).astype(F32)
        rest = log_total - high - middle
        spot = lane % HD
        extra = jnp.where(spot == 0, -high, jnp.where(spot == 1, -middle, -rest))
        extra = jnp.where(spot < 3, extra, 0.0).astype(BF16)
        qe_ref[0, 0, 0, at, :] = jnp.where(low, query, extra)
        qe_ref[0, 0, 1, at, :] = jnp.where(low, extra, query)
        return total

    for start in range(0, q_ref.shape[2], rows):
        at = slice(start, start + rows)
        query = q_ref[0, 0, at, :]
        sums = []
        for head, own in enumerate(masked(query)):
            more = dot(exponentials(own, kr_ref, pair), ext_ref[head])
            sums.append(acc_ref[0, 0, head, at, :] + more)
        total_ref[at, :] = finish(at, query, sums[0], sums[1], 0.0, 0.0)

    total = total_ref[...]
    bad = jnp.sum(jnp.where((total > 1e-25) & (total < 1e25), 0.0, 1.0))

    @pl.when(bad > 0.0)
    def _():
        own_ext = with_ones(v_ref[0, 0])

        again_rows = min(256, rows)

        def again(index, carry):
            at = pl.ds(pl.multiple_of(index * again_rows, again_rows), again_rows)
            query = q_ref[0, 0, at, :]
            sums, tops = [], []
            for head, own in enumerate(masked(query)):
                scores = dot(own, k_ref[0, 0], NT)
                others = dot(own, kr_ref[0, pair], NT)
                top = jnp.maximum(
                    jnp.max(scores, axis=-1, keepdims=True),
                    jnp.max(others, axis=-1, keepdims=True),
                )
                sums.append(
                    dot(jnp.exp2(scores - top).astype(BF16), own_ext[head])
                    + dot(jnp.exp2(others - top).astype(BF16), ext_ref[head])
                )
                tops.append(top)
            finish(at, query, sums[0], sums[1], tops[0], tops[1])
            return carry

        lax.fori_loop(0, q_ref.shape[2] // again_rows, again, 0)


def gelu_parts(values):
    cumulative = 0.5 * lax.erf(values * 0.7071067811865476) + 0.5
    bell = jnp.exp2(values * values * (-0.5 * LOG2E))
    return values * cumulative, cumulative + values * bell * 0.3989422804014327


def patch_kernel(
    rows,
    chunk,
    counts_ref,
    lead_ref,
    own_x,
    sib_x,
    own_ct,
    sib_ct,
    mod_ref,
    o_ref,
    out_w,
    fc1_w,
    fc2_w,
    final_own,
    final_sib,
    gm_ref,
    ge_ref,
    sums_ref,
    stack_one,
    stack_two,
    hidden_s,
    gpre_s,
    n2_s,
    g2_s,
    g1_s,
    mixed_s,
    gout_s,
    gfc1_s,
    gfc2_s,
    sums_s,
):
    step, half = pl.program_id(0), pl.program_id(1)
    width, hidden_width = fc1_w.shape
    patches = own_x.shape[1]
    slot = first_step(pl.num_programs(0)) + step
    active = (slot < counts_ref[0]).astype(F32)

    def piece(index):
        return mod_ref[pl.ds(step, 1), index * width : (index + 1) * width]

    gate1, shift2, scale2, gate2 = piece(2), piece(3), piece(4), piece(5)

    @pl.when((step == 0) & (half == 0))
    def _():
        sums_s[...] = jnp.zeros_like(sums_s)
        gout_s[...] = jnp.zeros_like(gout_s)
        gfc1_s[...] = jnp.zeros_like(gfc1_s)
        gfc2_s[...] = jnp.zeros_like(gfc2_s)

    def block(index, carry):
        at = pl.ds(pl.multiple_of(index * rows, rows), rows)
        x = jnp.where(half == 0, own_x[0, at, :], sib_x[0, at, :]).astype(F32)
        final_grad = jnp.where(half == 0, own_ct[0, at, :], sib_ct[0, at, :]).astype(F32) * active
        outs = [o_ref[0, pair, at, :] for pair in range(width // LANES)]
        mixed = jnp.concatenate([o.astype(BF16) for o in outs], axis=-1)
        mixed_s[at, :] = mixed
        branch_one = dot(mixed, out_w[...])
        middle = x + gate1 * branch_one
        xhat, inverse = normalize(middle)
        n2 = (xhat * (1.0 + scale2) + shift2).astype(BF16)
        n2_s[at, :] = n2
        g2 = (gate2 * final_grad).astype(BF16)
        g2_s[at, :] = g2
        branch_two = jnp.zeros((rows, width), F32)
        gy = jnp.zeros((rows, width), F32)

        def products(start):
            columns = slice(start, start + chunk)
            return dot(n2, fc1_w[:, columns]), dot(g2, fc2_w[columns, :], NT)

        ahead = products(0)
        for start in range(0, hidden_width, chunk):
            columns = slice(start, start + chunk)
            pre, grad_hidden = ahead
            if start + chunk < hidden_width:
                ahead = products(start + chunk)
            hidden, slope = gelu_parts(pre)
            hidden = hidden.astype(BF16)
            grad_pre = (slope * grad_hidden).astype(BF16)
            hidden_s[at, columns] = hidden
            gpre_s[at, columns] = grad_pre
            branch_two += dot(hidden, fc2_w[columns, :])
            gy += dot(grad_pre, fc1_w[:, columns], NT)
        final = ((middle + gate2 * branch_two) * active).astype(BF16)

        @pl.when(half == 0)
        def _():
            final_own[0, at, :] = final

        @pl.when(half == 1)
        def _():
            final_sib[0, at, :] = final

        gm = final_grad + norm_back(gy * (1.0 + scale2), xhat, inverse)
        gm_ref[0, 0, at, :] = gm
        g1 = (gate1 * gm).astype(BF16)
        g1_s[at, :] = g1
        sums = [branch_one * gm, gy, gy * xhat, branch_two * final_grad]
        for row, value in enumerate(sums):
            place = pl.ds(2 * row + step, 1)
            sums_s[place, :] += jnp.sum(value, axis=0, keepdims=True)
        grad_mixed = dot(g1, out_w[...], NT).astype(BF16)
        lane = lane_index((rows, LANES))
        low = lane < HD
        spot = lane % HD
        for pair, o in enumerate(outs):
            grad = grad_mixed[:, pair * LANES : (pair + 1) * LANES]
            product = grad.astype(F32) * o
            first = jnp.sum(jnp.where(low, product, 0.0), axis=-1, keepdims=True)
            second = jnp.sum(jnp.where(low, 0.0, product), axis=-1, keepdims=True)
            inner = jnp.where(low, second, first)
            high = inner.astype(BF16).astype(F32)
            mid = (inner - high).astype(BF16).astype(F32)
            extra = jnp.where(spot == 0, -high, jnp.where(spot == 1, -mid, high + mid - inner))
            extra = jnp.where(spot < 3, extra, 0.0).astype(BF16)
            ge_ref[0, pair, 0, at, :] = jnp.where(low, grad, extra)
            ge_ref[0, pair, 1, at, :] = jnp.where(low, extra, grad)
        return carry

    lax.fori_loop(0, patches // rows, block, 0)
    gout_s[...] += dot(mixed_s[...], g1_s[...], TN)
    for start in range(0, hidden_width, chunk):
        columns = slice(start, start + chunk)
        gfc1_s[:, columns] += dot(n2_s[...], gpre_s[:, columns], TN)
        gfc2_s[:, columns] += dot(g2_s[...], hidden_s[:, columns], TN)

    @pl.when((step == pl.num_programs(0) - 1) & (half == pl.num_programs(1) - 1))
    def _():
        for index in range(2):
            lead = lead_ref[0, first_step(2) + index]
            sums_s[12 + index : 13 + index, :] = jnp.where(lane_index((1, width)) == lead, 1.0, 0.0)
        sums_ref[...] = sums_s[...].astype(BF16)
        blocks = hidden_width // width
        for index in range(blocks):
            columns = slice(index * width, (index + 1) * width)
            stack_one[index] = gfc1_s[:, columns].astype(BF16)
            stack_two[index] = gfc2_s[:, columns].T.astype(BF16)
        stack_two[blocks] = gout_s[...].astype(BF16)


def attend_back_kernel(first_pass, exchanges, grid_steps, *refs):
    count = len(exchanges)
    qe_ref, ge_ref, k_ref, v_ref = refs[:4]
    refs = refs[4:]
    if first_pass:
        gives, sums_ref, refs = refs[:count], refs[count], refs[count + 1 :]
        dq_ref, dk_ref, dv_ref = refs[:3]
        shards, all_ref, refs = refs[3 : 3 + count], refs[3 + count], refs[4 + count :]
        all_s, all_sends, all_recvs = refs[-3:]
    else:
        dq_in, shards, refs = refs[0], refs[1 : 1 + count], refs[1 + count :]
        dq_ref, dk_ref, dv_ref = refs[:3]
        fulls, refs = refs[3 : 3 + count], refs[3 + count :]
    states = []
    for index, exchange in enumerate(exchanges):
        sends, recvs = refs[1], refs[2]
        if first_pass:
            got = refs[3 : 3 + exchange.all_levels]
            states.append((gives[index], refs[0], got, sends, recvs))
            refs = refs[3 + exchange.all_levels :]
        else:
            states.append((refs[0], sends, recvs))
            refs = refs[3:]
    queries = qe_ref.shape[3]
    piece = min(256, queries)
    static_slots = grid_steps * 2
    first_slot = (pl.program_id(0) * pl.num_programs(1) + pl.program_id(1)) * 2
    levels = exchanges[0].all_levels if first_pass else exchanges[0].levels

    def all_copy(level):
        index = 0
        for lower in range(len(exchanges[0].bits)):
            index = index + exchanges[0].place(lower)[0] * (1 << lower)
        if level < 0:
            return all_s.at[pl.ds(index, 1)]
        size = 1 << level
        piece = all_s.at[pl.ds((index // size) * size, size)]
        return exchanges[0].copy(piece, piece, all_sends, all_recvs, level)

    def reduce_action(order):
        if order == 0:
            exchanges[0].barrier()
            own = all_copy(-1)
            own[...] = sums_ref[...][None]
        else:
            all_copy(order - 1).wait()
        if order < levels:
            all_copy(order).start()
        else:
            all_ref[...] = all_s[...]
        for exchange, state, shard in zip(exchanges, states, shards):
            if order > 0:
                exchange.reduce_finish(order - 1, *state)
            if order < levels:
                exchange.reduce_start(order, *state)
            else:
                shard[...] = exchange.own_shard(state[1], 1)[...][0]

    def gather_action(order):
        if order == 0:
            exchanges[0].barrier()
        for exchange, state, shard in zip(exchanges, states, shards):
            if order == 0:
                exchange.own_shard(state[0], 0)[...] = shard[...][None]
            else:
                exchange.gather_finish(levels - order, *state)
            if order < levels:
                exchange.gather_start(levels - 1 - order, *state)
        if order == levels:
            copies = [
                pltpu.make_async_copy(state[0], full, refs[index])
                for index, (state, full) in enumerate(zip(states, fulls))
            ]
            for copy in copies:
                copy.start()
            for copy in copies:
                copy.wait()

    action = reduce_action if first_pass else gather_action
    weights = [5.0, 10.0, 9.0, 6.0] + [4.0] * levels
    weights = weights[:levels] if first_pass else weights[:levels][::-1]
    marks, total = [0], 0.0
    for weight in weights:
        total += weight
        marks.append(total)
    last = static_slots - (2 if first_pass else 1)
    marks = [min(int(mark * last / total + 0.5), last) for mark in marks]

    keys = k_ref[0, 0]
    values = v_ref[0, 0]
    lane = lane_index(keys.shape)
    low = lane < HD
    ones = jnp.where(lane % HD < 3, 1.0, 0.0).astype(BF16)
    turned = keys.T
    grads, query_grads = [], []
    for head in range(2):
        for order, mark in enumerate(marks[:-1]):
            pl.when(first_slot + head == mark)(functools.partial(action, order))
        own = low if head == 0 else jnp.logical_not(low)
        own_keys = jnp.where(own, keys, ones)
        own_values = jnp.where(own, values, ones)
        mine = turned[head * HD : (head + 1) * HD]
        probs, grad_scores, query_grad = [], [], []
        for start in range(0, queries, piece):
            some = slice(start, start + piece)
            prob = jnp.exp2(dot(own_keys, qe_ref[0, 0, head, some, :], NT))
            grad_prob = dot(own_values, ge_ref[0, 0, head, some, :], NT)
            probs.append(prob.astype(BF16))
            grad_scores.append((prob * grad_prob).astype(BF16))
            query_grad.append(dot(mine, grad_scores[-1]))
        probs = jnp.concatenate(probs, axis=-1)
        grad_scores = jnp.concatenate(grad_scores, axis=-1)
        grads.append((dot(grad_scores, qe_ref[0, 0, head]), dot(probs, ge_ref[0, 0, head])))
        query_grads.append(jnp.concatenate(query_grad, axis=-1))
    dk_ref[0, 0] = (jnp.where(low, grads[0][0], grads[1][0]) * LN2).astype(BF16)
    dv_ref[0, 0] = jnp.where(low, grads[0][1], grads[1][1]).astype(BF16)
    query_grads = jnp.concatenate(query_grads, axis=0).T
    if first_pass:
        dq_ref[0, 0] = query_grads
    else:
        dq_ref[0, 0] = ((dq_in[0, 0] + query_grads) * HD**-0.5).astype(BF16)
    pl.when(first_slot + 2 == static_slots)(functools.partial(action, levels))


def project_back_far_kernel(dk_ref, dv_ref, normed_ref, w_ref, dx_ref, gw_ref):
    width = w_ref.shape[0]
    joined = join_heads(dk_ref, dv_ref)
    dx_ref[0, 0] = dot(joined, w_ref[:, width:], NT).astype(BF16)

    @pl.when((pl.program_id(0) == 0) & (pl.program_id(1) == 0))
    def _():
        gw_ref[...] = jnp.zeros_like(gw_ref)

    gw_ref[...] += dot(normed_ref[0, 0], joined, TN)


def weight_back_kernel(dq_ref, dk_ref, dv_ref, normed_ref, far_ref, gw_ref, gw_s):
    step, which = pl.program_id(0), pl.program_id(1)
    width = normed_ref.shape[3]

    @pl.when((step == 0) & (which == 0))
    def _():
        gw_s[:, :width] = jnp.zeros_like(gw_s[:, :width])
        gw_s[:, width:] = far_ref[...]

    gw_s[...] += dot(normed_ref[0, 0], join_heads(dq_ref, dk_ref, dv_ref), TN)

    @pl.when((step == pl.num_programs(0) - 1) & (which == pl.num_programs(1) - 1))
    def _():
        for block in range(gw_ref.shape[0]):
            gw_ref[block] = gw_s[:, block * LANES : (block + 1) * LANES].astype(BF16)


def join_heads(*grads):
    return jnp.concatenate([ref[0, pair] for ref in grads for pair in range(ref.shape[1])], axis=-1)


class Direct:
    def __init__(self, mesh_shape, row_tiles):
        self.chips = mesh_shape["seq"] // 2
        self.peers = mesh_shape["dp"] * self.chips
        self.half = row_tiles * 8
        self.piece = -(-row_tiles // (2 * self.peers)) * 16
        self.padded = self.piece * self.peers

    def me(self):
        return lax.axis_index("dp") * self.chips + lax.axis_index("seq") // 2

    def core(self):
        return lax.axis_index("seq") % 2

    def sibling(self):
        return {"seq": lax.axis_index("seq") + 1 - 2 * self.core()}

    def peer(self, shift):
        other = (self.me() + shift) % self.peers
        device = {"dp": other // self.chips, "seq": (other % self.chips) * 2 + self.core()}
        return other, device

    def rows(self, index):
        return pl.ds(pl.multiple_of(index * self.piece, 16), self.piece)

    def barrier(self):
        semaphore = pltpu.get_barrier_semaphore()

        def signal(device):
            pl.semaphore_signal(semaphore, 1, device_id=device, device_id_type=pl.DeviceIdType.MESH)

        signal(self.sibling())

        def greet(shift, carry):
            signal(self.peer(shift)[1])
            return carry

        lax.fori_loop(1, self.peers, greet, 0)
        pl.semaphore_wait(semaphore, self.peers)

    def copy(self, source, target, send, recv, device):
        return pltpu.make_async_remote_copy(
            src_ref=source,
            dst_ref=target,
            send_sem=send,
            recv_sem=recv,
            device_id=device,
            device_id_type=pl.DeviceIdType.MESH,
        )

    def each_peer(self, do):
        def one(shift, carry):
            do(shift)
            return carry

        lax.fori_loop(1, self.peers, one, 0)


def tail_kernel(direct, remote, *refs):
    give_ref, own_x, sib_x, mod_ref, lead_ref, gm_ref, dq_ref, dk_ref, dv_ref, w_ref = refs[:10]
    others = refs[10 : 10 + remote]
    grad_ref, got_ref, full_ref, all_ref = refs[10 + remote : 14 + remote]
    sums_s, other_s, got_s, sum_s, core_s, pieces_s, full_s, all_s = refs[14 + remote : 22 + remote]
    core_sems, piece_sems, back_sems, all_sems, grad_sems, local_sem = refs[22 + remote :]
    step, half = pl.program_id(0), pl.program_id(1)
    width = own_x.shape[2]
    core, me = direct.core(), direct.me()

    core_copy = direct.copy(
        give_ref.at[1 - core], core_s, core_sems.at[0], core_sems.at[1], direct.sibling()
    )

    def piece_copy(shift):
        other, device = direct.peer(shift)
        return direct.copy(
            sum_s.at[direct.rows(other)],
            pieces_s.at[shift],
            piece_sems.at[0, shift],
            piece_sems.at[1, shift],
            device,
        )

    def full_copy(shift, arriving):
        _, device = direct.peer(shift)
        owner = (me + direct.peers - shift) % direct.peers if arriving else me
        place = full_s.at[core, direct.rows(owner)]
        return direct.copy(place, place, back_sems.at[0, shift], back_sems.at[1, shift], device)

    def sums_copy(shift, arriving):
        _, device = direct.peer(shift)
        owner = (me + direct.peers - shift) % direct.peers if arriving else me
        place = all_s.at[core, owner]
        return direct.copy(place, place, all_sems.at[0, shift], all_sems.at[1, shift], device)

    def side_copy(values, which, side):
        place = values.at[side]
        return direct.copy(
            place, place, core_sems.at[which], core_sems.at[which + 1], direct.sibling()
        )

    def grad_copy(index):
        return direct.copy(
            other_s.at[index],
            got_s.at[index],
            grad_sems.at[0, index],
            grad_sems.at[1, index],
            direct.sibling(),
        )

    @pl.when((step == 0) & (half == 0))
    def _():
        direct.barrier()
        core_copy.start()
        sums_s[...] = jnp.zeros_like(sums_s)

    @pl.when((step == 0) & (half == 1))
    def _():
        core_copy.wait()
        real = core_s.shape[0]
        sum_s[:real] = (give_ref[core].astype(F32) + core_s[...].astype(F32)).astype(BF16)
        if direct.padded > real:
            sum_s[real:] = jnp.zeros_like(sum_s[real:])
        direct.each_peer(lambda shift: piece_copy(shift).start())

    x = jnp.where(half == 0, own_x[0], sib_x[0]).astype(F32)
    scale = mod_ref[pl.ds(step, 1), width : 2 * width]
    xhat, inverse = normalize(x)
    gy = dot(join_heads(dq_ref, dk_ref, dv_ref), w_ref[...], NT)
    for other in others:
        gy = gy + other[0, 0].astype(F32)
    grad = (gm_ref[0, 0] + norm_back(gy * (1.0 + scale), xhat, inverse)).astype(BF16)

    @pl.when(half == 0)
    def _():
        grad_ref[0] = grad

    @pl.when(half == 1)
    def _():
        other_s[step] = grad
        grad_copy(step).start()

    for kind, value in enumerate((gy, gy * xhat)):
        total = jnp.sum(value, axis=0, keepdims=True)
        for index in range(width // LANES):
            place = pl.ds((kind * 2 + step) * (width // LANES) + index, 1)
            sums_s[place, :] += total[:, index * LANES : (index + 1) * LANES]

    @pl.when((step == 1) & (half == 1))
    def _():
        for index in range(2):
            chosen = lane_index((1, LANES)) == lead_ref[0, first_step(2) + index]
            sums_s[12 + index : 13 + index, :] = jnp.where(chosen, 1.0, 0.0)
        all_s[core, me] = sums_s[...].astype(BF16)
        direct.each_peer(lambda shift: sums_copy(shift, False).start())
        direct.each_peer(lambda shift: piece_copy(shift).wait())

        def add(shift, total):
            return total + pieces_s[shift].astype(F32)

        total = lax.fori_loop(1, direct.peers, add, sum_s[direct.rows(me)].astype(F32))
        full_s[core, direct.rows(me)] = total.astype(BF16)
        direct.each_peer(lambda shift: full_copy(shift, False).start())

        def arrived(shift):
            full_copy(shift, False).wait_send()
            full_copy(shift, True).wait_recv()
            sums_copy(shift, False).wait_send()
            sums_copy(shift, True).wait_recv()

        direct.each_peer(arrived)
        side_copy(full_s, 2, core).start()
        side_copy(all_s, 4, core).start()
        for index in range(2):
            grad_copy(index).wait()
        side_copy(full_s, 2, core).wait_send()
        side_copy(full_s, 2, 1 - core).wait_recv()
        side_copy(all_s, 4, core).wait_send()
        side_copy(all_s, 4, 1 - core).wait_recv()
        outs = [(got_s, got_ref), (full_s, full_ref), (all_s, all_ref)]
        copies = [
            pltpu.make_async_copy(source, target, local_sem.at[index])
            for index, (source, target) in enumerate(outs)
        ]
        for copy in copies:
            copy.start()
        for copy in copies:
            copy.wait()


def unstack(at, full_ref, targets, rows):
    row, end = 0, rows * len(targets)
    while row < end:
        group, inside, left = at(row)
        block, place = divmod(row, rows)
        count = min(left, rows - place)
        target, first_row, first_column = targets[block]
        columns = slice(first_column, first_column + full_ref.shape[2])
        value = full_ref[group, inside : inside + count, :].astype(F32)
        target[first_row + place : first_row + place + count, columns] = value
        row += count


def spread_leads(grads, step_of, table_rows):
    count = grads.shape[0]
    part = min(count, 512)
    row = lax.broadcasted_iota(jnp.int32, (part, part), 0)
    column = lane_index((part, part))
    chosen = (row // 16 == column // 16) & (row % 16 == 12 + step_of(column % 16))
    spread = jnp.where(chosen, 1.0, 0.0).astype(BF16)
    leads = [
        dot(grads[start : start + part, :LANES], spread, TN)[:table_rows]
        for start in range(0, count, part)
    ]
    return jnp.concatenate(leads, axis=-1)


def final_kernel(early, direct, *refs):
    early_sums, late_sums, emb_ref, ada_ref, one_ref, two_ref, late_ref = refs[:7]
    final_ref, final_got, grad_ref, grad_got = refs[7:11]
    outs = refs[11:20]
    gada_s, gqkv_s, gout_s, gfc1_s, gfc2_s, sems = refs[20:]
    final_out, grad_out, gemb_ref, gada_out, gbada_ref, gqkv_out, gout_out, gfc1_out, gfc2_out = outs
    size = gout_s.shape[0]
    blocks = gfc1_s.shape[1] // size
    copies = []

    def start(source, target):
        copy = pltpu.make_async_copy(source, target, sems.at[len(copies)])
        copy.start()
        copies.append(copy)

    mine = first_step(2)
    for index in range(2):
        start(final_ref.at[index], final_out.at[mine + index])
        start(final_got.at[index], final_out.at[2 - mine + index])
        start(grad_ref.at[index], grad_out.at[mine + index])
        start(grad_got.at[index], grad_out.at[2 - mine + index])

    def grouped(exchange):
        def at(row):
            group, inside = divmod(row, exchange.real)
            return group, inside, exchange.real - inside

        return at

    def halved(row):
        group, inside = divmod(row, direct.half)
        return group, inside, direct.half - inside

    unstack(grouped(early[0]), one_ref, [(gfc1_s, 0, block * size) for block in range(blocks)], size)
    start(gfc1_s, gfc1_out)
    rest = [(gfc2_s, block * size, 0) for block in range(blocks)] + [(gout_s, 0, 0)]
    unstack(grouped(early[1]), two_ref, rest, size)
    start(gfc2_s, gfc2_out)
    start(gout_s, gout_out)
    columns = gqkv_s.shape[1] // LANES
    unstack(halved, late_ref, [(gqkv_s, 0, block * LANES) for block in range(columns)], size)
    start(gqkv_s, gqkv_out)

    table_rows = emb_ref.shape[0]
    table = emb_ref[...].astype(F32)
    gate = jax.nn.sigmoid(table)
    slope = gate * (1.0 + table * (1.0 - gate))
    table_act = (table * gate).astype(BF16)
    total = jnp.zeros((table_rows, size), F32)

    def one_piece(grads, leads, place, first):
        chosen = jnp.where(place, leads, 0.0).astype(BF16)
        acts = dot(table_act, chosen, TN).astype(BF16)
        where = slice(first, first + grads.shape[1])
        gada_s[:, where] = dot(acts, grads)
        by_lead = dot(chosen, grads)
        gbada_ref[:, where] = jnp.sum(by_lead, axis=0, keepdims=True)
        high = by_lead.astype(BF16)
        low = (by_lead - high.astype(F32)).astype(BF16)
        return dot(high, ada_ref[:, where], NT) + dot(low, ada_ref[:, where], NT)

    grads = early_sums[...]
    leads = spread_leads(grads, lambda row: row % 2, table_rows)
    row = lane_index((1, grads.shape[0])) % 16
    for index in range(4):
        total += one_piece(grads, leads, row // 2 == index, (2 + index) * size)
    grads = late_sums[...]
    parts = size // LANES
    leads = spread_leads(grads, lambda row: (row // parts) % 2, table_rows)
    row = lane_index((1, grads.shape[0])) % 16
    for index in range(2):
        for part in range(parts):
            place = (row // (2 * parts) == index) & (row % parts == part)
            total += one_piece(grads, leads, place, index * size + part * LANES)
    gemb_ref[...] = total * slope
    start(gada_s, gada_out)
    for copy in copies:
        copy.wait()


def local(
    mesh_shape, inputs, cotangent, counts, lead_steps, emb_table, w_ada, b_ada, w_qkv, w_out, w_fc1, w_fc2
):
    slots, items, patches, width = inputs.shape
    chips = mesh_shape["seq"] // 2
    blocks = w_fc1.shape[1] // w_fc1.shape[0]
    steps = slots * items // 2
    hidden_width = w_fc1.shape[1]
    pairs = width // LANES
    rows = 2 * patches
    remote = 2 * (chips - 1)
    far_rows = remote * patches
    spot = lax.axis_index("seq")
    core = lax.rem(spot, 2)
    devices = 2 * chips

    def send(values, shift, cross):
        pairs_list = []
        for source in range(devices):
            chip, side = source // 2, source % 2
            pairs_list.append((source, ((chip + shift) % chips) * 2 + (1 - side if cross else side)))
        return lax.ppermute(values, "seq", pairs_list)

    x_steps = inputs.reshape(2, steps, patches, width)
    ct_steps = cotangent.reshape(2, steps, patches, width)
    own_x = lax.dynamic_index_in_dim(x_steps, core, 0, keepdims=False)
    other_x = lax.dynamic_index_in_dim(x_steps, 1 - core, 0, keepdims=False)
    own_ct = lax.dynamic_index_in_dim(ct_steps, core, 0, keepdims=False)
    other_ct = lax.dynamic_index_in_dim(ct_steps, 1 - core, 0, keepdims=False)
    sib_x = send(other_x, 0, True)
    far_x = []
    for step in range(steps):
        some = slice(step, step + 1)
        for shift in range(1, chips):
            far_x.append(send(own_x[some], shift, False))
            far_x.append(send(other_x[some], shift, True))
    sib_ct = send(other_ct, 0, True)

    step_block = pl.BlockSpec((1, patches, width), lambda j, i: (j, 0, 0))
    patch_block = pl.BlockSpec((1, 1, patches, width), lambda j, i: (j, i, 0, 0))

    def head_rows(count):
        return pl.BlockSpec((1, 1, count, LANES), lambda j, p: (j, p, 0, 0))

    def of_step(*shape):
        return pl.BlockSpec((1,) + shape, lambda j, p: (j,) + (0,) * len(shape))

    both_heads = pl.BlockSpec((1, 1, 2, rows, LANES), lambda j, p: (j, p, 0, 0, 0))
    near_work = 4 * steps * pairs * 2 * rows * LANES * rows
    near_heads = jax.ShapeDtypeStruct((steps, pairs, rows, LANES), BF16)
    mod, n1, q, k, v, acc = call(
        functools.partial(near_kernel, rows),
        "near",
        (steps, pairs),
        [scalars(), whole(emb_table.shape), whole(w_ada.shape), whole((1, 6 * width))]
        + [step_block] * 2
        + [whole(w_qkv.shape)],
        [whole((16, 6 * width)), of_step(rows, width)]
        + [of_step(pairs, rows, LANES)] * 3
        + [both_heads],
        [
            jax.ShapeDtypeStruct((16, 6 * width), F32),
            jax.ShapeDtypeStruct((steps, rows, width), BF16),
            near_heads,
            near_heads,
            near_heads,
            jax.ShapeDtypeStruct((steps, pairs, 2, rows, LANES), F32),
        ],
        flops=near_work + 6 * steps * rows * width * width,
        exps=steps * pairs * 2 * rows * rows,
    )(lead_steps, emb_table, w_ada, b_ada.reshape(1, -1), own_x, sib_x, w_qkv)

    def far(step, before):
        some_x = far_x[step * remote : (step + 1) * remote]

        def at_step(*shape):
            return pl.BlockSpec((1,) + shape, lambda p: (step,) + (0,) * len(shape))

        def at_pair(*shape):
            return pl.BlockSpec((1, 1) + shape, lambda p: (step, p) + (0,) * len(shape))

        operands = [*some_x, mod, w_qkv, q, k, v, acc]
        return call(
            functools.partial(far_kernel, rows, step, remote),
            "far",
            (pairs,),
            [whole((1, patches, width))] * remote
            + [whole(mod.shape), whole(w_qkv.shape)]
            + [at_pair(rows, LANES)] * 3
            + [at_pair(2, rows, LANES)]
            + [pl.BlockSpec(memory_space=pl.ANY)] * len(before),
            [at_step(far_rows, width)]
            + [at_step(pairs, far_rows, LANES)] * 2
            + [at_pair(rows, LANES), at_pair(2, rows, LANES)],
            [
                jax.ShapeDtypeStruct((steps, far_rows, width), BF16),
                jax.ShapeDtypeStruct((steps, pairs, far_rows, LANES), BF16),
                jax.ShapeDtypeStruct((steps, pairs, far_rows, LANES), BF16),
                jax.ShapeDtypeStruct((steps, pairs, rows, LANES), F32),
                jax.ShapeDtypeStruct((steps, pairs, 2, rows, LANES), BF16),
            ],
            [pltpu.VMEM((2, far_rows, LANES), BF16), pltpu.VMEM((rows, LANES), F32)],
            flops=near_work // 2,
            exps=pairs * 2 * rows * far_rows,
            aliases={len(operands) + index: index for index in range(len(before))},
        )(*operands, *before)

    far_results = []
    for step in range(steps):
        far_results = far(step, far_results)
    n1r, kr, vr, o, qe = far_results

    block_rows = min(256, patches)
    outs = call(
        functools.partial(patch_kernel, block_rows, 512),
        "patchwise",
        (steps, 2),
        [scalars()] * 2
        + [step_block] * 4
        + [
            whole(mod.shape),
            pl.BlockSpec((1, pairs, patches, LANES), lambda j, i: (j, 0, i, 0)),
            whole(w_out.shape),
            whole(w_fc1.shape),
            whole(w_fc2.shape),
        ],
        [
            step_block,
            step_block,
            patch_block,
            pl.BlockSpec((1, pairs, 2, patches, LANES), lambda j, i: (j, 0, 0, i, 0)),
            whole((16, width)),
            whole((blocks, width, width)),
            whole((blocks + 1, width, width)),
        ],
        [
            jax.ShapeDtypeStruct((steps, patches, width), BF16),
            jax.ShapeDtypeStruct((steps, patches, width), BF16),
            jax.ShapeDtypeStruct((steps, 2, patches, width), F32),
            jax.ShapeDtypeStruct((steps, pairs, 2, rows, LANES), BF16),
            jax.ShapeDtypeStruct((16, width), BF16),
            jax.ShapeDtypeStruct((blocks, width, width), BF16),
            jax.ShapeDtypeStruct((blocks + 1, width, width), BF16),
        ],
        [pltpu.VMEM((patches, hidden_width), BF16)] * 2
        + [pltpu.VMEM((patches, width), BF16)] * 4
        + [
            pltpu.VMEM((width, width), F32),
            pltpu.VMEM((width, hidden_width), F32),
            pltpu.VMEM((width, hidden_width), F32),
            pltpu.VMEM((16, width), F32),
        ],
        flops=6 * steps * rows * width * (2 * hidden_width + width),
        moved=steps * rows * width * 20,
        exps=2 * steps * rows * hidden_width,
    )(counts, lead_steps, own_x, sib_x, own_ct, sib_ct, mod, o, w_out, w_fc1, w_fc2)
    final_own, final_sib, gm, ge, sums, stack_one, stack_two = outs
    final_got = send(final_sib, 0, True)
    early = [Exchange(mesh_shape, blocks * width // 16, 0), Exchange(mesh_shape, (blocks + 1) * width // 16, 1)]
    gives = [g.reshape(e.groups, e.real, width) for e, g in zip(early, (stack_one, stack_two))]

    def attend_back(keys, values, extra, first, name):
        count = keys.shape[2]
        in_specs = [both_heads] * 2 + [head_rows(count)] * 2
        out_specs = [head_rows(rows), head_rows(count), head_rows(count)]
        out_shape = [
            jax.ShapeDtypeStruct((steps, pairs, rows, LANES), F32 if first else BF16),
            jax.ShapeDtypeStruct((steps, pairs, count, LANES), BF16),
            jax.ShapeDtypeStruct((steps, pairs, count, LANES), BF16),
        ]
        scratch = []
        if not first:
            in_specs += [head_rows(rows)]
        for exchange in early:
            shape = (exchange.groups, exchange.padded, width)
            shard = (exchange.shard, width)
            sems = [pltpu.SemaphoreType.DMA((exchange.all_levels,))] * 2
            if first:
                in_specs += [whole((exchange.groups, exchange.real, width))]
                out_specs += [whole(shard)]
                out_shape += [jax.ShapeDtypeStruct(shard, BF16)]
                half = (exchange.groups // 2, exchange.padded, width)
                scratch += [pltpu.VMEM(half, BF16)] + sems + exchange.receive_scratch(width)
            else:
                in_specs += [whole(shard)]
                out_specs += [pl.BlockSpec(memory_space=pl.ANY)]
                out_shape += [jax.ShapeDtypeStruct(shape, BF16)]
                scratch += [pltpu.VMEM(shape, BF16)] + sems
        if first:
            every = (mesh_shape["dp"] * mesh_shape["seq"], 16, width)
            in_specs += [whole(sums.shape)]
            out_specs += [whole(every)]
            out_shape += [jax.ShapeDtypeStruct(every, BF16)]
            sems = [pltpu.SemaphoreType.DMA((early[0].all_levels,))] * 2
            scratch += [pltpu.VMEM(every, BF16)] + sems
        else:
            scratch += [pltpu.SemaphoreType.DMA] * len(early)
        return call(
            functools.partial(attend_back_kernel, first, early, steps * pairs),
            name,
            (steps, pairs),
            in_specs,
            out_specs,
            out_shape,
            scratch,
            flops=10 * steps * pairs * 2 * rows * count * LANES,
            exps=steps * pairs * 2 * rows * count,
            collective=1 if first else 2,
        )(qe, ge, keys, values, *extra)

    grad_block = pl.BlockSpec((1, pairs, patches, LANES), lambda j, i: (j, 0, i, 0))
    hbm = pl.BlockSpec(memory_space=pl.ANY)

    dq_part, dkr, dvr, shard_one, shard_two, early_all = attend_back(
        kr, vr, [*gives, sums], True, "attend_back_far"
    )
    dx_far, gw_part = call(
        project_back_far_kernel,
        "project_back_far",
        (steps, remote),
        [grad_block] * 2 + [patch_block, whole(w_qkv.shape)],
        [patch_block, whole((width, 2 * width))],
        [
            jax.ShapeDtypeStruct((steps, remote, patches, width), BF16),
            jax.ShapeDtypeStruct((width, 2 * width), F32),
        ],
        flops=4 * steps * far_rows * width * 2 * width,
        moved=steps * far_rows * width * 8,
    )(dkr, dvr, n1r.reshape(steps, remote, patches, width), w_qkv)
    dx_got = [send(dx_far[:, 2 * r - 2 : 2 * r], -r, False) for r in range(1, chips)]
    dq, dk, dv, *early_sums = attend_back(
        k, v, [dq_part, shard_one, shard_two], False, "attend_back_near"
    )
    columns = w_qkv.shape[1] // LANES
    give_late = call(
        weight_back_kernel,
        "weight_back",
        (steps, 2),
        [grad_block] * 3 + [patch_block, whole(gw_part.shape)],
        whole((columns, width, LANES)),
        jax.ShapeDtypeStruct((columns, width, LANES), BF16),
        [pltpu.VMEM((width, columns * LANES), F32)],
        flops=2 * steps * rows * width * 3 * width,
        moved=steps * rows * width * 8,
    )(dq, dk, dv, n1.reshape(steps, 2, patches, width), gw_part)

    direct = Direct(mesh_shape, columns * width // 16)
    full_shape = (2, direct.padded, LANES)
    late_all_shape = (2, direct.peers, 16, LANES)
    grad_own, grad_got, late_sum, late_all = call(
        functools.partial(tail_kernel, direct, len(dx_got)),
        "tail",
        (steps, 2),
        [whole((2, direct.half, LANES)), step_block, step_block, whole(mod.shape), scalars()]
        + [patch_block]
        + [grad_block] * 3
        + [whole(w_qkv.shape)]
        + [patch_block] * len(dx_got),
        [step_block, hbm, hbm, hbm],
        [
            jax.ShapeDtypeStruct((steps, patches, width), BF16),
            jax.ShapeDtypeStruct((steps, patches, width), BF16),
            jax.ShapeDtypeStruct(full_shape, BF16),
            jax.ShapeDtypeStruct(late_all_shape, BF16),
        ],
        [
            pltpu.VMEM((16, LANES), F32),
            pltpu.VMEM((steps, patches, width), BF16),
            pltpu.VMEM((steps, patches, width), BF16),
            pltpu.VMEM((direct.padded, LANES), BF16),
            pltpu.VMEM((direct.half, LANES), BF16),
            pltpu.VMEM((direct.peers, direct.piece, LANES), BF16),
            pltpu.VMEM(full_shape, BF16),
            pltpu.VMEM(late_all_shape, BF16),
            pltpu.SemaphoreType.DMA((6,)),
            pltpu.SemaphoreType.DMA((2, direct.peers)),
            pltpu.SemaphoreType.DMA((2, direct.peers)),
            pltpu.SemaphoreType.DMA((2, direct.peers)),
            pltpu.SemaphoreType.DMA((2, steps)),
            pltpu.SemaphoreType.DMA((3,)),
        ],
        flops=2 * steps * rows * width * 3 * width,
        collective=3,
    )(
        give_late.reshape(2, direct.half, LANES),
        own_x,
        sib_x,
        mod,
        lead_steps,
        gm,
        dq,
        dk,
        dv,
        w_qkv,
        *dx_got,
    )

    early_all = early_all.reshape(-1, width)
    late_all = late_all.reshape(-1, LANES)
    small = [early_all, late_all, emb_table, w_ada, *early_sums, late_sum]
    out_shapes = [(slots * items, patches, width)] * 2 + [emb_table.shape, w_ada.shape]
    out_shapes += [(1, 6 * width), w_qkv.shape, w_out.shape, w_fc1.shape, w_fc2.shape]
    outs = call(
        functools.partial(final_kernel, early, direct),
        "final",
        (),
        [whole(value.shape) for value in small] + [whole((steps, patches, width))] * 4,
        [hbm] * 2 + [whole(emb_table.shape), hbm, whole((1, 6 * width))] + [hbm] * 4,
        [
            jax.ShapeDtypeStruct(shape, BF16 if index < 2 else F32)
            for index, shape in enumerate(out_shapes)
        ],
        [pltpu.VMEM(w.shape, F32) for w in (w_ada, w_qkv, w_out, w_fc1, w_fc2)]
        + [pltpu.SemaphoreType.DMA((4 * 2 + 5,))],
        flops=2 * early_all.shape[0] * width * 6 * width,
        moved=6 * w_ada.size,
    )(*small, final_own, final_got, grad_own, grad_got)
    outputs, grad_inputs, g_emb, g_ada, g_bada, g_qkv, g_out, g_fc1, g_fc2 = outs
    return (
        outputs.reshape(inputs.shape),
        grad_inputs.reshape(inputs.shape),
        g_emb,
        g_ada,
        g_bada.reshape(-1),
        g_qkv,
        g_out,
        g_fc1,
        g_fc2,
    )


def solution(mesh):
    tokens = P(None, "dp", "seq", None)
    return jax.shard_map(
        functools.partial(local, dict(mesh.shape)),
        mesh=mesh,
        in_specs=(tokens, tokens, P("dp"), P("dp", None)) + (P(),) * 7,
        out_specs=(tokens, tokens) + (P(),) * 7,
        check_vma=False,
    )
```

```python
import functools

import jax
import jax.numpy as jnp
from jax import lax
from jax.experimental import pallas as pl
from jax.experimental.pallas import tpu as pltpu
from jax.sharding import PartitionSpec as P

HD = 64
LANES = 128
EPSILON = 1e-06
LOG2E = 1.4426950408889634
NN = (((1,), (0,)), ((), ()))
NT = (((1,), (1,)), ((), ()))
TN = (((0,), (0,)), ((), ()))
F32 = jnp.float32
BF16 = jnp.bfloat16
VMEM_BYTES = 56 * 1024 * 1024


def dot(a, b, dims=NN):
    return lax.dot_general(a, b, dims, preferred_element_type=F32)


def call(
    body,
    name,
    grid,
    in_specs,
    out_specs,
    out_shape,
    scratch=(),
    flops=0,
    moved=0,
    exps=0,
    collective=None,
    aliases=None,
):
    return pl.pallas_call(
        body,
        name=name,
        grid=grid,
        in_specs=in_specs,
        out_specs=out_specs,
        out_shape=out_shape,
        scratch_shapes=list(scratch),
        input_output_aliases=aliases or {},
        cost_estimate=pl.CostEstimate(flops=flops, bytes_accessed=moved, transcendentals=exps),
        compiler_params=pltpu.CompilerParams(
            vmem_limit_bytes=VMEM_BYTES,
            collective_id=collective,
            has_side_effects=collective is not None,
        ),
    )


def whole(shape):
    return pl.BlockSpec(shape, lambda *_: (0,) * len(shape))


def scalars():
    return pl.BlockSpec(memory_space=pltpu.SMEM)


def lane_index(shape):
    return lax.broadcasted_iota(jnp.int32, shape, 1)


def first_step(steps):
    return lax.rem(lax.axis_index("seq"), 2) * steps


def normalize(values):
    center = values - jnp.mean(values, axis=-1, keepdims=True)
    spread = jnp.mean(center * center, axis=-1, keepdims=True)
    inverse = lax.rsqrt(spread + EPSILON)
    return center * inverse, inverse


def norm_back(grad, xhat, inverse):
    first = jnp.mean(grad, axis=-1, keepdims=True)
    second = jnp.mean(grad * xhat, axis=-1, keepdims=True)
    return inverse * (grad - first - xhat * second)


def pick(refs, which):
    value = refs[0][0]
    for index in range(1, len(refs)):
        value = jnp.where(which == index, refs[index][0], value)
    return value


class Exchange:
    def __init__(self, mesh_shape, row_tiles, turn=0):
        bits = {"seq": [], "dp": []}
        for axis in bits:
            bit = 1
            while bit < mesh_shape[axis]:
                bits[axis].append((axis, bit))
                bit *= 2
        turned = bits["dp"][turn:] + bits["dp"][:turn]
        self.bits = bits["seq"][:1] + turned + bits["seq"][1:]
        self.all_levels = len(self.bits)
        self.levels = 1 + len(turned)
        self.even = 0
        while self.even < self.levels and row_tiles % 2 == 0:
            row_tiles //= 2
            self.even += 1
        unit = 2 ** (self.levels - self.even)
        self.groups = 2**self.even
        self.real = row_tiles * 16
        self.padded = -(-row_tiles // unit) * unit * 16
        self.shard = self.padded // unit

    def sizes(self, level):
        if level < self.even:
            return (self.groups >> (level + 1), self.real)
        return (1, self.padded >> (level - self.even + 1))

    def receive_scratch(self, width):
        last = self.levels - 1
        return [
            pltpu.VMEM(self.sizes(min(level, last)) + (width,), BF16)
            for level in range(self.all_levels)
        ]

    def place(self, level):
        axis, bit = self.bits[level]
        here = lax.axis_index(axis)
        value = (here // bit) % 2
        return value, {axis: here + bit * (1 - 2 * value)}

    def spot(self, level, first, flip):
        group, row = 0, 0
        for index in range(first, level + 1):
            value, _ = self.place(index)
            if flip and index == level:
                value = 1 - value
            if index < self.even:
                group = group + value * (self.groups >> (index + 1))
            else:
                row = row + value * (self.padded >> (index - self.even + 1))
        if level >= self.even:
            row = pl.multiple_of(row, 16)
        count, rows = self.sizes(level)
        return pl.ds(group, count), pl.ds(row, rows)

    def barrier(self):
        semaphore = pltpu.get_barrier_semaphore()
        for level in range(self.all_levels):
            _, partner = self.place(level)
            pl.semaphore_signal(
                semaphore, inc=1, device_id=partner, device_id_type=pl.DeviceIdType.MESH
            )
        pl.semaphore_wait(semaphore, self.all_levels)

    def copy(self, source, target, sends, recvs, level):
        _, partner = self.place(level)
        return pltpu.make_async_remote_copy(
            src_ref=source,
            dst_ref=target,
            send_sem=sends.at[level],
            recv_sem=recvs.at[level],
            device_id=partner,
            device_id_type=pl.DeviceIdType.MESH,
        )

    def reduce_copy(self, level, start_ref, acc_ref, got, sends, recvs):
        if level >= self.levels:
            return self.copy(self.own_shard(acc_ref, 1), got[level], sends, recvs, level)
        groups, rows = self.spot(level, min(level, 1), True)
        source = start_ref if level == 0 else acc_ref
        return self.copy(source.at[groups, rows], got[level], sends, recvs, level)

    def reduce_start(self, level, *refs):
        self.reduce_copy(level, *refs).start()

    def reduce_finish(self, level, start_ref, acc_ref, got, sends, recvs):
        self.reduce_copy(level, start_ref, acc_ref, got, sends, recvs).wait()
        if level >= self.levels:
            own = self.own_shard(acc_ref, 1)
            own[...] = (own[...].astype(F32) + got[level][...].astype(F32)).astype(BF16)
            return
        count, rows = self.sizes(level)
        groups, spots = self.spot(level, min(level, 1), False)
        if level == 0:
            target_groups, target_rows = pl.ds(0, count), pl.ds(0, rows)
            if self.padded > self.real:
                acc_ref[:, self.real :, :] = jnp.zeros_like(acc_ref[:, self.real :, :])
        else:
            target_groups, target_rows = groups, spots
        source = start_ref if level == 0 else acc_ref

        def add(index, carry):
            one = pl.ds(groups.start + index, 1)
            to = pl.ds(target_groups.start + index, 1)
            value = source[one, spots, :].astype(F32) + got[level][pl.ds(index, 1)].astype(F32)
            acc_ref[to, target_rows, :] = value.astype(BF16)
            return carry

        lax.fori_loop(0, count, add, 0)

    def own_shard(self, ref, first):
        if self.levels > self.even:
            return ref.at[self.spot(self.levels - 1, first, False)]
        groups, _ = self.spot(self.levels - 1, first, False)
        return ref.at[groups, pl.ds(0, self.shard)]

    def gather_copy(self, level, full_ref, sends, recvs):
        piece = full_ref.at[self.spot(level, 0, False)]
        return self.copy(piece, piece, sends, recvs, level)

    def gather_start(self, level, *refs):
        self.gather_copy(level, *refs).start()

    def gather_finish(self, level, *refs):
        self.gather_copy(level, *refs).wait()


def modulation(lead_ref, emb_ref, ada_ref, bias_ref):
    shape = (16, emb_ref.shape[0])
    rows = lax.broadcasted_iota(jnp.int32, shape, 0)
    columns = lane_index(shape)
    onehot = jnp.zeros(shape, F32)
    for step in range(2):
        lead = lead_ref[0, first_step(2) + step]
        onehot = jnp.where((rows == step) & (columns == lead), 1.0, onehot)
    condition = dot(onehot.astype(BF16), emb_ref[...])
    active = (condition * jax.nn.sigmoid(condition)).astype(BF16)
    return dot(active, ada_ref[...]) + bias_ref[...].astype(F32)


def project(x_refs, mod_ref, step, w_ref, normed_ref, head_refs):
    width = w_ref.shape[0]
    patches = x_refs[0].shape[1]
    shift = mod_ref[pl.ds(step, 1), 0:width]
    scale = mod_ref[pl.ds(step, 1), width : 2 * width]
    queries = len(head_refs) == 3
    for index, x_ref in enumerate(x_refs):
        at = slice(index * patches, (index + 1) * patches)
        xhat, _ = normalize(x_ref[0].astype(F32))
        normed = (xhat * (1.0 + scale) + shift).astype(BF16)
        normed_ref[0, at, :] = normed
        for part, head_ref in enumerate(head_refs):
            start = (part + (0 if queries else 1)) * width
            projected = dot(normed, w_ref[:, start : start + width])
            if queries and part == 0:
                projected = projected.astype(BF16).astype(F32) * HD**-0.5
            projected = projected.astype(BF16)
            for pair in range(width // LANES):
                head_ref[0, pair, at, :] = projected[:, pair * LANES : (pair + 1) * LANES]


def with_ones(values):
    low = lane_index(values.shape) < HD
    one = jnp.ones_like(values)
    return jnp.where(low, values, one), jnp.where(low, one, values)


def attend(queries, keys_ref, ext_ref, pair, scores_s, weights_s, sum_s, start):
    count = keys_ref.shape[2]
    piece = scores_s.shape[2]
    steps = [(head, at) for head in range(2) for at in range(0, count, piece)]
    for head in range(2):
        sum_s[head] = start(head)
    for index in range(len(steps) + 2):
        if index < len(steps):
            head, at = steps[index]
            keys = keys_ref[0, pair, at : at + piece, :]
            scores_s[index % 2] = dot(queries[head], keys, NT)
        if 0 < index <= len(steps):
            weights_s[(index - 1) % 2] = jnp.exp(scores_s[(index - 1) % 2]).astype(BF16)
        if index > 1:
            head, at = steps[index - 2]
            sum_s[head] += dot(weights_s[index % 2], ext_ref[head, at : at + piece, :])


def masked(values):
    low = lane_index(values.shape) < HD
    zero = jnp.zeros_like(values)
    return jnp.where(low, values, zero), jnp.where(low, zero, values)


def near_kernel(*refs):
    lead_ref, emb_ref, ada_ref, bias_ref, own_x, sib_x, w_ref = refs[:7]
    mod_ref, normed_ref, q_ref, k_ref, v_ref, acc_ref, ext_ref, scores_s, weights_s = refs[7:]
    step, pair = pl.program_id(0), pl.program_id(1)

    @pl.when((step == 0) & (pair == 0))
    def _():
        mod_ref[...] = modulation(lead_ref, emb_ref, ada_ref, bias_ref)

    @pl.when(pair == 0)
    def _():
        project([own_x, sib_x], mod_ref, step, w_ref, normed_ref, [q_ref, k_ref, v_ref])

    ext_ref[0], ext_ref[1] = with_ones(v_ref[0, pair])
    queries = masked(q_ref[0, pair])
    zero = jnp.zeros(acc_ref.shape[3:], F32)
    attend(queries, k_ref, ext_ref, pair, scores_s, weights_s, acc_ref.at[0, 0], lambda head: zero)


def far_kernel(step, sources, *refs):
    x_refs, refs = refs[:sources], refs[sources:]
    mod_ref, w_ref, q_ref, k_ref, v_ref, acc_ref = refs[:6]
    normed_ref, kr_ref, vr_ref, o_ref, qe_ref = refs[-10:-5]
    ext_ref, total_ref, scores_s, weights_s, sum_s = refs[-5:]
    pair = pl.program_id(0)

    @pl.when(pair == 0)
    def _():
        project(x_refs, mod_ref, step, w_ref, normed_ref, [kr_ref, vr_ref])

    ext_ref[0], ext_ref[1] = with_ones(vr_ref[0, pair])
    def finish(at, query, first, second, top_first, top_second):
        lane = lane_index(query.shape)
        low = lane < HD
        swapped = jnp.where(low, second, first)
        total = pltpu.roll(swapped, HD, 1)
        o_ref[0, 0, at, :] = jnp.where(low, first, second) / total
        log_total = jnp.log(swapped) + jnp.where(low, top_second, top_first)
        high = log_total.astype(BF16).astype(F32)
        middle = (log_total - high).astype(BF16).astype(F32)
        rest = log_total - high - middle
        spot = lane % HD
        extra = jnp.where(spot == 0, -high, jnp.where(spot == 1, -middle, -rest))
        extra = jnp.where(spot < 3, extra, 0.0).astype(BF16)
        qe_ref[0, 0, 0, at, :] = jnp.where(low, query, extra)
        qe_ref[0, 0, 1, at, :] = jnp.where(low, extra, query)
        return total

    query = q_ref[0, 0]
    queries = masked(query)
    attend(
        queries, kr_ref, ext_ref, pair, scores_s, weights_s, sum_s, lambda head: acc_ref[0, 0, head]
    )
    total_ref[...] = finish(slice(None), query, sum_s[0], sum_s[1], 0.0, 0.0)
    total = total_ref[...]
    bad = jnp.sum(jnp.where((total > 1e-25) & (total < 1e25), 0.0, 1.0))

    @pl.when(bad > 0.0)
    def _():
        own_ext = with_ones(v_ref[0, 0])

        again_rows = min(256, q_ref.shape[2])

        def again(index, carry):
            at = pl.ds(pl.multiple_of(index * again_rows, again_rows), again_rows)
            query = q_ref[0, 0, at, :]
            sums, tops = [], []
            for head, own in enumerate(masked(query)):
                scores = dot(own, k_ref[0, 0], NT)
                others = dot(own, kr_ref[0, pair], NT)
                top = jnp.maximum(
                    jnp.max(scores, axis=-1, keepdims=True),
                    jnp.max(others, axis=-1, keepdims=True),
                )
                sums.append(
                    dot(jnp.exp(scores - top).astype(BF16), own_ext[head])
                    + dot(jnp.exp(others - top).astype(BF16), ext_ref[head])
                )
                tops.append(top)
            finish(at, query, sums[0], sums[1], tops[0], tops[1])
            return carry

        lax.fori_loop(0, q_ref.shape[2] // again_rows, again, 0)


def gelu_parts(values):
    cumulative = 0.5 * lax.erf(values * 0.7071067811865476) + 0.5
    bell = jnp.exp2(values * values * (-0.5 * LOG2E))
    return values * cumulative, cumulative + values * bell * 0.3989422804014327


def patch_kernel(
    rows,
    chunk,
    counts_ref,
    lead_ref,
    own_x,
    sib_x,
    own_ct,
    sib_ct,
    mod_ref,
    o_ref,
    out_w,
    fc1_w,
    fc2_w,
    final_own,
    final_sib,
    gm_ref,
    ge_ref,
    sums_ref,
    stack_one,
    stack_two,
    hidden_s,
    gpre_s,
    n2_s,
    g2_s,
    g1_s,
    mixed_s,
    gout_s,
    gfc1_s,
    gfc2_s,
    sums_s,
):
    step, half = pl.program_id(0), pl.program_id(1)
    width, hidden_width = fc1_w.shape
    patches = own_x.shape[1]
    slot = first_step(pl.num_programs(0)) + step
    active = (slot < counts_ref[0]).astype(F32)

    def piece(index):
        return mod_ref[pl.ds(step, 1), index * width : (index + 1) * width]

    gate1, shift2, scale2, gate2 = piece(2), piece(3), piece(4), piece(5)

    @pl.when((step == 0) & (half == 0))
    def _():
        sums_s[...] = jnp.zeros_like(sums_s)
        gout_s[...] = jnp.zeros_like(gout_s)
        gfc1_s[...] = jnp.zeros_like(gfc1_s)
        gfc2_s[...] = jnp.zeros_like(gfc2_s)

    def block(index, carry):
        at = pl.ds(pl.multiple_of(index * rows, rows), rows)
        x = jnp.where(half == 0, own_x[0, at, :], sib_x[0, at, :]).astype(F32)
        final_grad = jnp.where(half == 0, own_ct[0, at, :], sib_ct[0, at, :]).astype(F32) * active
        outs = [o_ref[0, pair, at, :] for pair in range(width // LANES)]
        mixed = jnp.concatenate([o.astype(BF16) for o in outs], axis=-1)
        mixed_s[at, :] = mixed
        branch_one = dot(mixed, out_w[...])
        middle = x + gate1 * branch_one
        xhat, inverse = normalize(middle)
        n2 = (xhat * (1.0 + scale2) + shift2).astype(BF16)
        n2_s[at, :] = n2
        g2 = (gate2 * final_grad).astype(BF16)
        g2_s[at, :] = g2
        branch_two = jnp.zeros((rows, width), F32)
        gy = jnp.zeros((rows, width), F32)

        def products(start):
            columns = slice(start, start + chunk)
            return dot(n2, fc1_w[:, columns]), dot(g2, fc2_w[columns, :], NT)

        ahead = products(0)
        for start in range(0, hidden_width, chunk):
            columns = slice(start, start + chunk)
            pre, grad_hidden = ahead
            if start + chunk < hidden_width:
                ahead = products(start + chunk)
            hidden, slope = gelu_parts(pre)
            hidden = hidden.astype(BF16)
            grad_pre = (slope * grad_hidden).astype(BF16)
            hidden_s[at, columns] = hidden
            gpre_s[at, columns] = grad_pre
            branch_two += dot(hidden, fc2_w[columns, :])
            gy += dot(grad_pre, fc1_w[:, columns], NT)
        final = ((middle + gate2 * branch_two) * active).astype(BF16)

        @pl.when(half == 0)
        def _():
            final_own[0, at, :] = final

        @pl.when(half == 1)
        def _():
            final_sib[0, at, :] = final

        gm = final_grad + norm_back(gy * (1.0 + scale2), xhat, inverse)
        gm_ref[0, 0, at, :] = gm
        g1 = (gate1 * gm).astype(BF16)
        g1_s[at, :] = g1
        sums = [branch_one * gm, gy, gy * xhat, branch_two * final_grad]
        for row, value in enumerate(sums):
            place = pl.ds(2 * row + step, 1)
            sums_s[place, :] += jnp.sum(value, axis=0, keepdims=True)
        grad_mixed = dot(g1, out_w[...], NT).astype(BF16)
        lane = lane_index((rows, LANES))
        low = lane < HD
        spot = lane % HD
        for pair, o in enumerate(outs):
            grad = grad_mixed[:, pair * LANES : (pair + 1) * LANES]
            product = grad.astype(F32) * o
            first = jnp.sum(jnp.where(low, product, 0.0), axis=-1, keepdims=True)
            second = jnp.sum(jnp.where(low, 0.0, product), axis=-1, keepdims=True)
            inner = jnp.where(low, second, first)
            high = inner.astype(BF16).astype(F32)
            mid = (inner - high).astype(BF16).astype(F32)
            extra = jnp.where(spot == 0, -high, jnp.where(spot == 1, -mid, high + mid - inner))
            extra = jnp.where(spot < 3, extra, 0.0).astype(BF16)
            ge_ref[0, pair, 0, at, :] = jnp.where(low, grad, extra)
            ge_ref[0, pair, 1, at, :] = jnp.where(low, extra, grad)
        return carry

    lax.fori_loop(0, patches // rows, block, 0)
    gout_s[...] += dot(mixed_s[...], g1_s[...], TN)
    for start in range(0, hidden_width, chunk):
        columns = slice(start, start + chunk)
        gfc1_s[:, columns] += dot(n2_s[...], gpre_s[:, columns], TN)
        gfc2_s[:, columns] += dot(g2_s[...], hidden_s[:, columns], TN)

    @pl.when((step == pl.num_programs(0) - 1) & (half == pl.num_programs(1) - 1))
    def _():
        for index in range(2):
            lead = lead_ref[0, first_step(2) + index]
            sums_s[12 + index : 13 + index, :] = jnp.where(lane_index((1, width)) == lead, 1.0, 0.0)
        sums_ref[...] = sums_s[...].astype(BF16)
        blocks = hidden_width // width
        for index in range(blocks):
            columns = slice(index * width, (index + 1) * width)
            stack_one[index] = gfc1_s[:, columns].astype(BF16)
            stack_two[index] = gfc2_s[:, columns].T.astype(BF16)
        stack_two[blocks] = gout_s[...].astype(BF16)


def attend_back_kernel(first_pass, exchanges, grid_steps, *refs):
    count = len(exchanges)
    qe_ref, ge_ref, k_ref, v_ref = refs[:4]
    refs = refs[4:]
    if first_pass:
        gives, sums_ref, refs = refs[:count], refs[count], refs[count + 1 :]
        dq_ref, dk_ref, dv_ref = refs[:3]
        shards, all_ref, refs = refs[3 : 3 + count], refs[3 + count], refs[4 + count :]
        all_s, all_sends, all_recvs = refs[-3:]
    else:
        dq_in, shards, refs = refs[0], refs[1 : 1 + count], refs[1 + count :]
        dq_ref, dk_ref, dv_ref = refs[:3]
        fulls, refs = refs[3 : 3 + count], refs[3 + count :]
    scores_s, grads_s, probs_s, grad_scores_s, dq_s, dk_s, dv_s = refs[:7]
    refs = refs[7:]
    states = []
    for index, exchange in enumerate(exchanges):
        sends, recvs = refs[1], refs[2]
        if first_pass:
            got = refs[3 : 3 + exchange.all_levels]
            states.append((gives[index], refs[0], got, sends, recvs))
            refs = refs[3 + exchange.all_levels :]
        else:
            states.append((refs[0], sends, recvs))
            refs = refs[3:]
    queries = qe_ref.shape[3]
    piece = min(256, queries)
    static_slots = grid_steps * 2
    first_slot = (pl.program_id(0) * pl.num_programs(1) + pl.program_id(1)) * 2
    levels = exchanges[0].all_levels if first_pass else exchanges[0].levels

    def all_copy(level):
        index = 0
        for lower in range(len(exchanges[0].bits)):
            index = index + exchanges[0].place(lower)[0] * (1 << lower)
        if level < 0:
            return all_s.at[pl.ds(index, 1)]
        size = 1 << level
        piece = all_s.at[pl.ds((index // size) * size, size)]
        return exchanges[0].copy(piece, piece, all_sends, all_recvs, level)

    def reduce_action(order):
        if order == 0:
            exchanges[0].barrier()
            own = all_copy(-1)
            own[...] = sums_ref[...][None]
        else:
            all_copy(order - 1).wait()
        if order < levels:
            all_copy(order).start()
        else:
            all_ref[...] = all_s[...]
        for exchange, state, shard in zip(exchanges, states, shards):
            if order > 0:
                exchange.reduce_finish(order - 1, *state)
            if order < levels:
                exchange.reduce_start(order, *state)
            else:
                shard[...] = exchange.own_shard(state[1], 1)[...][0]

    def gather_action(order):
        if order == 0:
            exchanges[0].barrier()
        for exchange, state, shard in zip(exchanges, states, shards):
            if order == 0:
                exchange.own_shard(state[0], 0)[...] = shard[...][None]
            else:
                exchange.gather_finish(levels - order, *state)
            if order < levels:
                exchange.gather_start(levels - 1 - order, *state)
        if order == levels:
            copies = [
                pltpu.make_async_copy(state[0], full, refs[index])
                for index, (state, full) in enumerate(zip(states, fulls))
            ]
            for copy in copies:
                copy.start()
            for copy in copies:
                copy.wait()

    action = reduce_action if first_pass else gather_action
    weights = [5.0, 10.0, 9.0, 6.0] + [4.0] * levels
    weights = weights[:levels] if first_pass else weights[:levels][::-1]
    marks, total = [0], 0.0
    for weight in weights:
        total += weight
        marks.append(total)
    last = static_slots - (2 if first_pass else 1)
    marks = [min(int(mark * last / total + 0.5), last) for mark in marks]

    keys = k_ref[0, 0]
    values = v_ref[0, 0]
    lane = lane_index(keys.shape)
    low = lane < HD
    ones = jnp.where(lane % HD < 3, 1.0, 0.0).astype(BF16)
    turned = keys.T
    own_keys = (jnp.where(low, keys, ones), jnp.where(low, ones, keys))
    own_values = (jnp.where(low, values, ones), jnp.where(low, ones, values))
    dk_s[...] = jnp.zeros_like(dk_s)
    dv_s[...] = jnp.zeros_like(dv_s)
    steps = [(head, slice(at, at + piece)) for head in range(2) for at in range(0, queries, piece)]
    for index in range(len(steps) + 2):
        if index % (len(steps) // 2) == 0 and index < len(steps):
            for order, mark in enumerate(marks[:-1]):
                half = first_slot + index // (len(steps) // 2)
                pl.when(half == mark)(functools.partial(action, order))
        if index < len(steps):
            head, some = steps[index]
            slot = index % 2
            scores_s[slot] = dot(own_keys[head], qe_ref[0, 0, head, some, :], NT)
            grads_s[slot] = dot(own_values[head], ge_ref[0, 0, head, some, :], NT)
        if 0 < index <= len(steps):
            slot = (index - 1) % 2
            probs = jnp.exp(scores_s[slot])
            probs_s[slot] = probs.astype(BF16)
            grad_scores_s[slot] = (probs * grads_s[slot]).astype(BF16)
        if index > 1:
            head, some = steps[index - 2]
            slot = index % 2
            own = masked(qe_ref[0, 0, head, some, :])[head]
            grad = masked(ge_ref[0, 0, head, some, :])[head]
            mine = slice(head * HD, (head + 1) * HD)
            dk_s[...] += dot(grad_scores_s[slot], own)
            dv_s[...] += dot(probs_s[slot], grad)
            dq_s[mine, some] = dot(turned[mine], grad_scores_s[slot])
    dk_ref[0, 0] = dk_s[...].astype(BF16)
    dv_ref[0, 0] = dv_s[...].astype(BF16)
    if first_pass:
        dq_ref[0, 0] = dq_s[...].T
    else:
        dq_ref[0, 0] = ((dq_in[0, 0] + dq_s[...].T) * HD**-0.5).astype(BF16)
    pl.when(first_slot + 2 == static_slots)(functools.partial(action, levels))


def project_back_far_kernel(dk_ref, dv_ref, normed_ref, w_ref, dx_ref, gw_ref):
    width = w_ref.shape[0]
    joined = join_heads(dk_ref, dv_ref)
    dx_ref[0, 0] = dot(joined, w_ref[:, width:], NT).astype(BF16)

    @pl.when((pl.program_id(0) == 0) & (pl.program_id(1) == 0))
    def _():
        gw_ref[...] = jnp.zeros_like(gw_ref)

    gw_ref[...] += dot(normed_ref[0, 0], joined, TN)


def weight_back_kernel(dq_ref, dk_ref, dv_ref, normed_ref, far_ref, gw_ref, gw_s):
    step, which = pl.program_id(0), pl.program_id(1)
    width = normed_ref.shape[3]

    @pl.when((step == 0) & (which == 0))
    def _():
        gw_s[:, :width] = jnp.zeros_like(gw_s[:, :width])
        gw_s[:, width:] = far_ref[...]

    gw_s[...] += dot(normed_ref[0, 0], join_heads(dq_ref, dk_ref, dv_ref), TN)

    @pl.when((step == pl.num_programs(0) - 1) & (which == pl.num_programs(1) - 1))
    def _():
        for block in range(gw_ref.shape[0]):
            gw_ref[block] = gw_s[:, block * LANES : (block + 1) * LANES].astype(BF16)


def join_heads(*grads):
    return jnp.concatenate([ref[0, pair] for ref in grads for pair in range(ref.shape[1])], axis=-1)


class Direct:
    def __init__(self, mesh_shape, row_tiles):
        self.chips = mesh_shape["seq"] // 2
        self.peers = mesh_shape["dp"] * self.chips
        self.half = row_tiles * 8
        self.piece = -(-row_tiles // (2 * self.peers)) * 16
        self.padded = self.piece * self.peers

    def me(self):
        return lax.axis_index("dp") * self.chips + lax.axis_index("seq") // 2

    def core(self):
        return lax.axis_index("seq") % 2

    def sibling(self):
        return {"seq": lax.axis_index("seq") + 1 - 2 * self.core()}

    def peer(self, shift):
        other = (self.me() + shift) % self.peers
        device = {"dp": other // self.chips, "seq": (other % self.chips) * 2 + self.core()}
        return other, device

    def rows(self, index):
        return pl.ds(pl.multiple_of(index * self.piece, 16), self.piece)

    def barrier(self):
        semaphore = pltpu.get_barrier_semaphore()

        def signal(device):
            pl.semaphore_signal(semaphore, 1, device_id=device, device_id_type=pl.DeviceIdType.MESH)

        signal(self.sibling())

        def greet(shift, carry):
            signal(self.peer(shift)[1])
            return carry

        lax.fori_loop(1, self.peers, greet, 0)
        pl.semaphore_wait(semaphore, self.peers)

    def copy(self, source, target, send, recv, device):
        return pltpu.make_async_remote_copy(
            src_ref=source,
            dst_ref=target,
            send_sem=send,
            recv_sem=recv,
            device_id=device,
            device_id_type=pl.DeviceIdType.MESH,
        )

    def each_peer(self, do):
        def one(shift, carry):
            do(shift)
            return carry

        lax.fori_loop(1, self.peers, one, 0)


def tail_kernel(direct, remote, *refs):
    give_ref, own_x, sib_x, mod_ref, lead_ref, gm_ref, dq_ref, dk_ref, dv_ref, w_ref = refs[:10]
    others = refs[10 : 10 + remote]
    grad_ref, got_ref, full_ref, all_ref = refs[10 + remote : 14 + remote]
    sums_s, other_s, got_s, sum_s, core_s, pieces_s, full_s, all_s = refs[14 + remote : 22 + remote]
    core_sems, piece_sems, back_sems, all_sems, grad_sems, local_sem = refs[22 + remote :]
    step, half = pl.program_id(0), pl.program_id(1)
    width = own_x.shape[2]
    core, me = direct.core(), direct.me()

    core_copy = direct.copy(
        give_ref.at[1 - core], core_s, core_sems.at[0], core_sems.at[1], direct.sibling()
    )

    def piece_copy(shift):
        other, device = direct.peer(shift)
        return direct.copy(
            sum_s.at[direct.rows(other)],
            pieces_s.at[shift],
            piece_sems.at[0, shift],
            piece_sems.at[1, shift],
            device,
        )

    def full_copy(shift, arriving):
        _, device = direct.peer(shift)
        owner = (me + direct.peers - shift) % direct.peers if arriving else me
        place = full_s.at[core, direct.rows(owner)]
        return direct.copy(place, place, back_sems.at[0, shift], back_sems.at[1, shift], device)

    def sums_copy(shift, arriving):
        _, device = direct.peer(shift)
        owner = (me + direct.peers - shift) % direct.peers if arriving else me
        place = all_s.at[core, owner]
        return direct.copy(place, place, all_sems.at[0, shift], all_sems.at[1, shift], device)

    def side_copy(values, which, side):
        place = values.at[side]
        return direct.copy(
            place, place, core_sems.at[which], core_sems.at[which + 1], direct.sibling()
        )

    def grad_copy(index):
        return direct.copy(
            other_s.at[index],
            got_s.at[index],
            grad_sems.at[0, index],
            grad_sems.at[1, index],
            direct.sibling(),
        )

    @pl.when((step == 0) & (half == 0))
    def _():
        direct.barrier()
        core_copy.start()
        sums_s[...] = jnp.zeros_like(sums_s)

    @pl.when((step == 0) & (half == 1))
    def _():
        core_copy.wait()
        real = core_s.shape[0]
        sum_s[:real] = (give_ref[core].astype(F32) + core_s[...].astype(F32)).astype(BF16)
        if direct.padded > real:
            sum_s[real:] = jnp.zeros_like(sum_s[real:])
        direct.each_peer(lambda shift: piece_copy(shift).start())

    x = jnp.where(half == 0, own_x[0], sib_x[0]).astype(F32)
    scale = mod_ref[pl.ds(step, 1), width : 2 * width]
    xhat, inverse = normalize(x)
    gy = dot(join_heads(dq_ref, dk_ref, dv_ref), w_ref[...], NT)
    for other in others:
        gy = gy + other[0, 0].astype(F32)
    grad = (gm_ref[0, 0] + norm_back(gy * (1.0 + scale), xhat, inverse)).astype(BF16)

    @pl.when(half == 0)
    def _():
        grad_ref[0] = grad

    @pl.when(half == 1)
    def _():
        other_s[step] = grad
        grad_copy(step).start()

    for kind, value in enumerate((gy, gy * xhat)):
        total = jnp.sum(value, axis=0, keepdims=True)
        for index in range(width // LANES):
            place = pl.ds((kind * 2 + step) * (width // LANES) + index, 1)
            sums_s[place, :] += total[:, index * LANES : (index + 1) * LANES]

    @pl.when((step == 1) & (half == 1))
    def _():
        for index in range(2):
            chosen = lane_index((1, LANES)) == lead_ref[0, first_step(2) + index]
            sums_s[12 + index : 13 + index, :] = jnp.where(chosen, 1.0, 0.0)
        all_s[core, me] = sums_s[...].astype(BF16)
        direct.each_peer(lambda shift: sums_copy(shift, False).start())
        direct.each_peer(lambda shift: piece_copy(shift).wait())

        def add(shift, total):
            return total + pieces_s[shift].astype(F32)

        total = lax.fori_loop(1, direct.peers, add, sum_s[direct.rows(me)].astype(F32))
        full_s[core, direct.rows(me)] = total.astype(BF16)
        direct.each_peer(lambda shift: full_copy(shift, False).start())

        def arrived(shift):
            full_copy(shift, False).wait_send()
            full_copy(shift, True).wait_recv()
            sums_copy(shift, False).wait_send()
            sums_copy(shift, True).wait_recv()

        direct.each_peer(arrived)
        side_copy(full_s, 2, core).start()
        side_copy(all_s, 4, core).start()
        for index in range(2):
            grad_copy(index).wait()
        side_copy(full_s, 2, core).wait_send()
        side_copy(full_s, 2, 1 - core).wait_recv()
        side_copy(all_s, 4, core).wait_send()
        side_copy(all_s, 4, 1 - core).wait_recv()
        outs = [(got_s, got_ref), (full_s, full_ref), (all_s, all_ref)]
        copies = [
            pltpu.make_async_copy(source, target, local_sem.at[index])
            for index, (source, target) in enumerate(outs)
        ]
        for copy in copies:
            copy.start()
        for copy in copies:
            copy.wait()


def unstack(at, full_ref, targets, rows):
    row, end = 0, rows * len(targets)
    while row < end:
        group, inside, left = at(row)
        block, place = divmod(row, rows)
        count = min(left, rows - place)
        target, first_row, first_column = targets[block]
        columns = slice(first_column, first_column + full_ref.shape[2])
        value = full_ref[group, inside : inside + count, :].astype(F32)
        target[first_row + place : first_row + place + count, columns] = value
        row += count


def spread_leads(grads, step_of, table_rows):
    count = grads.shape[0]
    part = min(count, 512)
    row = lax.broadcasted_iota(jnp.int32, (part, part), 0)
    column = lane_index((part, part))
    chosen = (row // 16 == column // 16) & (row % 16 == 12 + step_of(column % 16))
    spread = jnp.where(chosen, 1.0, 0.0).astype(BF16)
    leads = [
        dot(grads[start : start + part, :LANES], spread, TN)[:table_rows]
        for start in range(0, count, part)
    ]
    return jnp.concatenate(leads, axis=-1)


def final_kernel(early, direct, *refs):
    early_sums, late_sums, emb_ref, ada_ref, one_ref, two_ref, late_ref = refs[:7]
    final_ref, final_got, grad_ref, grad_got = refs[7:11]
    outs = refs[11:20]
    gada_s, gqkv_s, gout_s, gfc1_s, gfc2_s, sems = refs[20:]
    final_out, grad_out, gemb_ref, gada_out, gbada_ref, gqkv_out, gout_out, gfc1_out, gfc2_out = outs
    size = gout_s.shape[0]
    blocks = gfc1_s.shape[1] // size
    copies = []

    def start(source, target):
        copy = pltpu.make_async_copy(source, target, sems.at[len(copies)])
        copy.start()
        copies.append(copy)

    mine = first_step(2)
    for index in range(2):
        start(final_ref.at[index], final_out.at[mine + index])
        start(final_got.at[index], final_out.at[2 - mine + index])
        start(grad_ref.at[index], grad_out.at[mine + index])
        start(grad_got.at[index], grad_out.at[2 - mine + index])

    def grouped(exchange):
        def at(row):
            group, inside = divmod(row, exchange.real)
            return group, inside, exchange.real - inside

        return at

    def halved(row):
        group, inside = divmod(row, direct.half)
        return group, inside, direct.half - inside

    unstack(grouped(early[0]), one_ref, [(gfc1_s, 0, block * size) for block in range(blocks)], size)
    start(gfc1_s, gfc1_out)
    rest = [(gfc2_s, block * size, 0) for block in range(blocks)] + [(gout_s, 0, 0)]
    unstack(grouped(early[1]), two_ref, rest, size)
    start(gfc2_s, gfc2_out)
    start(gout_s, gout_out)
    columns = gqkv_s.shape[1] // LANES
    unstack(halved, late_ref, [(gqkv_s, 0, block * LANES) for block in range(columns)], size)
    start(gqkv_s, gqkv_out)

    table_rows = emb_ref.shape[0]
    table = emb_ref[...].astype(F32)
    gate = jax.nn.sigmoid(table)
    slope = gate * (1.0 + table * (1.0 - gate))
    table_act = (table * gate).astype(BF16)
    total = jnp.zeros((table_rows, size), F32)

    def one_piece(grads, leads, place, first):
        chosen = jnp.where(place, leads, 0.0).astype(BF16)
        acts = dot(table_act, chosen, TN).astype(BF16)
        where = slice(first, first + grads.shape[1])
        gada_s[:, where] = dot(acts, grads)
        by_lead = dot(chosen, grads)
        gbada_ref[:, where] = jnp.sum(by_lead, axis=0, keepdims=True)
        high = by_lead.astype(BF16)
        low = (by_lead - high.astype(F32)).astype(BF16)
        return dot(high, ada_ref[:, where], NT) + dot(low, ada_ref[:, where], NT)

    grads = early_sums[...]
    leads = spread_leads(grads, lambda row: row % 2, table_rows)
    row = lane_index((1, grads.shape[0])) % 16
    for index in range(4):
        total += one_piece(grads, leads, row // 2 == index, (2 + index) * size)
    grads = late_sums[...]
    parts = size // LANES
    leads = spread_leads(grads, lambda row: (row // parts) % 2, table_rows)
    row = lane_index((1, grads.shape[0])) % 16
    for index in range(2):
        for part in range(parts):
            place = (row // (2 * parts) == index) & (row % parts == part)
            total += one_piece(grads, leads, place, index * size + part * LANES)
    gemb_ref[...] = total * slope
    start(gada_s, gada_out)
    for copy in copies:
        copy.wait()


def local(
    mesh_shape, inputs, cotangent, counts, lead_steps, emb_table, w_ada, b_ada, w_qkv, w_out, w_fc1, w_fc2
):
    slots, items, patches, width = inputs.shape
    chips = mesh_shape["seq"] // 2
    blocks = w_fc1.shape[1] // w_fc1.shape[0]
    steps = slots * items // 2
    hidden_width = w_fc1.shape[1]
    pairs = width // LANES
    rows = 2 * patches
    remote = 2 * (chips - 1)
    far_rows = remote * patches
    spot = lax.axis_index("seq")
    core = lax.rem(spot, 2)
    devices = 2 * chips

    def send(values, shift, cross):
        pairs_list = []
        for source in range(devices):
            chip, side = source // 2, source % 2
            pairs_list.append((source, ((chip + shift) % chips) * 2 + (1 - side if cross else side)))
        return lax.ppermute(values, "seq", pairs_list)

    x_steps = inputs.reshape(2, steps, patches, width)
    ct_steps = cotangent.reshape(2, steps, patches, width)
    own_x = lax.dynamic_index_in_dim(x_steps, core, 0, keepdims=False)
    other_x = lax.dynamic_index_in_dim(x_steps, 1 - core, 0, keepdims=False)
    own_ct = lax.dynamic_index_in_dim(ct_steps, core, 0, keepdims=False)
    other_ct = lax.dynamic_index_in_dim(ct_steps, 1 - core, 0, keepdims=False)
    sib_x = send(other_x, 0, True)
    far_x = []
    for step in range(steps):
        some = slice(step, step + 1)
        for shift in range(1, chips):
            far_x.append(send(own_x[some], shift, False))
            far_x.append(send(other_x[some], shift, True))
    sib_ct = send(other_ct, 0, True)

    step_block = pl.BlockSpec((1, patches, width), lambda j, i: (j, 0, 0))
    patch_block = pl.BlockSpec((1, 1, patches, width), lambda j, i: (j, i, 0, 0))

    def head_rows(count):
        return pl.BlockSpec((1, 1, count, LANES), lambda j, p: (j, p, 0, 0))

    def of_step(*shape):
        return pl.BlockSpec((1,) + shape, lambda j, p: (j,) + (0,) * len(shape))

    both_heads = pl.BlockSpec((1, 1, 2, rows, LANES), lambda j, p: (j, p, 0, 0, 0))
    piece = min(256, rows)
    near_work = 4 * steps * pairs * 2 * rows * LANES * rows
    near_heads = jax.ShapeDtypeStruct((steps, pairs, rows, LANES), BF16)
    mod, n1, q, k, v, acc = call(
        near_kernel,
        "near",
        (steps, pairs),
        [scalars(), whole(emb_table.shape), whole(w_ada.shape), whole((1, 6 * width))]
        + [step_block] * 2
        + [whole(w_qkv.shape)],
        [whole((16, 6 * width)), of_step(rows, width)]
        + [of_step(pairs, rows, LANES)] * 3
        + [both_heads],
        [
            jax.ShapeDtypeStruct((16, 6 * width), F32),
            jax.ShapeDtypeStruct((steps, rows, width), BF16),
            near_heads,
            near_heads,
            near_heads,
            jax.ShapeDtypeStruct((steps, pairs, 2, rows, LANES), F32),
        ],
        [
            pltpu.VMEM((2, rows, LANES), BF16),
            pltpu.VMEM((2, rows, piece), F32),
            pltpu.VMEM((2, rows, piece), BF16),
        ],
        flops=near_work + 6 * steps * rows * width * width,
        exps=steps * pairs * 2 * rows * rows,
    )(lead_steps, emb_table, w_ada, b_ada.reshape(1, -1), own_x, sib_x, w_qkv)

    def far(step, before):
        some_x = far_x[step * remote : (step + 1) * remote]

        def at_step(*shape):
            return pl.BlockSpec((1,) + shape, lambda p: (step,) + (0,) * len(shape))

        def at_pair(*shape):
            return pl.BlockSpec((1, 1) + shape, lambda p: (step, p) + (0,) * len(shape))

        operands = [*some_x, mod, w_qkv, q, k, v, acc]
        return call(
            functools.partial(far_kernel, step, remote),
            "far",
            (pairs,),
            [whole((1, patches, width))] * remote
            + [whole(mod.shape), whole(w_qkv.shape)]
            + [at_pair(rows, LANES)] * 3
            + [at_pair(2, rows, LANES)]
            + [pl.BlockSpec(memory_space=pl.ANY)] * len(before),
            [at_step(far_rows, width)]
            + [at_step(pairs, far_rows, LANES)] * 2
            + [at_pair(rows, LANES), at_pair(2, rows, LANES)],
            [
                jax.ShapeDtypeStruct((steps, far_rows, width), BF16),
                jax.ShapeDtypeStruct((steps, pairs, far_rows, LANES), BF16),
                jax.ShapeDtypeStruct((steps, pairs, far_rows, LANES), BF16),
                jax.ShapeDtypeStruct((steps, pairs, rows, LANES), F32),
                jax.ShapeDtypeStruct((steps, pairs, 2, rows, LANES), BF16),
            ],
            [
                pltpu.VMEM((2, far_rows, LANES), BF16),
                pltpu.VMEM((rows, LANES), F32),
                pltpu.VMEM((2, rows, piece), F32),
                pltpu.VMEM((2, rows, piece), BF16),
                pltpu.VMEM((2, rows, LANES), F32),
            ],
            flops=near_work // 2,
            exps=pairs * 2 * rows * far_rows,
            aliases={len(operands) + index: index for index in range(len(before))},
        )(*operands, *before)

    far_results = []
    for step in range(steps):
        far_results = far(step, far_results)
    n1r, kr, vr, o, qe = far_results

    block_rows = min(256, patches)
    outs = call(
        functools.partial(patch_kernel, block_rows, 512),
        "patchwise",
        (steps, 2),
        [scalars()] * 2
        + [step_block] * 4
        + [
            whole(mod.shape),
            pl.BlockSpec((1, pairs, patches, LANES), lambda j, i: (j, 0, i, 0)),
            whole(w_out.shape),
            whole(w_fc1.shape),
            whole(w_fc2.shape),
        ],
        [
            step_block,
            step_block,
            patch_block,
            pl.BlockSpec((1, pairs, 2, patches, LANES), lambda j, i: (j, 0, 0, i, 0)),
            whole((16, width)),
            whole((blocks, width, width)),
            whole((blocks + 1, width, width)),
        ],
        [
            jax.ShapeDtypeStruct((steps, patches, width), BF16),
            jax.ShapeDtypeStruct((steps, patches, width), BF16),
            jax.ShapeDtypeStruct((steps, 2, patches, width), F32),
            jax.ShapeDtypeStruct((steps, pairs, 2, rows, LANES), BF16),
            jax.ShapeDtypeStruct((16, width), BF16),
            jax.ShapeDtypeStruct((blocks, width, width), BF16),
            jax.ShapeDtypeStruct((blocks + 1, width, width), BF16),
        ],
        [pltpu.VMEM((patches, hidden_width), BF16)] * 2
        + [pltpu.VMEM((patches, width), BF16)] * 4
        + [
            pltpu.VMEM((width, width), F32),
            pltpu.VMEM((width, hidden_width), F32),
            pltpu.VMEM((width, hidden_width), F32),
            pltpu.VMEM((16, width), F32),
        ],
        flops=6 * steps * rows * width * (2 * hidden_width + width),
        moved=steps * rows * width * 20,
        exps=2 * steps * rows * hidden_width,
    )(counts, lead_steps, own_x, sib_x, own_ct, sib_ct, mod, o, w_out, w_fc1, w_fc2)
    final_own, final_sib, gm, ge, sums, stack_one, stack_two = outs
    final_got = send(final_sib, 0, True)
    early = [Exchange(mesh_shape, blocks * width // 16, 0), Exchange(mesh_shape, (blocks + 1) * width // 16, 1)]
    gives = [g.reshape(e.groups, e.real, width) for e, g in zip(early, (stack_one, stack_two))]

    def attend_back(keys, values, extra, first, name):
        count = keys.shape[2]
        in_specs = [both_heads] * 2 + [head_rows(count)] * 2
        out_specs = [head_rows(rows), head_rows(count), head_rows(count)]
        out_shape = [
            jax.ShapeDtypeStruct((steps, pairs, rows, LANES), F32 if first else BF16),
            jax.ShapeDtypeStruct((steps, pairs, count, LANES), BF16),
            jax.ShapeDtypeStruct((steps, pairs, count, LANES), BF16),
        ]
        scratch = [pltpu.VMEM((2, count, piece), F32)] * 2
        scratch += [pltpu.VMEM((2, count, piece), BF16)] * 2
        scratch += [pltpu.VMEM((LANES, rows), F32)] + [pltpu.VMEM((count, LANES), F32)] * 2
        if not first:
            in_specs += [head_rows(rows)]
        for exchange in early:
            shape = (exchange.groups, exchange.padded, width)
            shard = (exchange.shard, width)
            sems = [pltpu.SemaphoreType.DMA((exchange.all_levels,))] * 2
            if first:
                in_specs += [whole((exchange.groups, exchange.real, width))]
                out_specs += [whole(shard)]
                out_shape += [jax.ShapeDtypeStruct(shard, BF16)]
                half = (exchange.groups // 2, exchange.padded, width)
                scratch += [pltpu.VMEM(half, BF16)] + sems + exchange.receive_scratch(width)
            else:
                in_specs += [whole(shard)]
                out_specs += [pl.BlockSpec(memory_space=pl.ANY)]
                out_shape += [jax.ShapeDtypeStruct(shape, BF16)]
                scratch += [pltpu.VMEM(shape, BF16)] + sems
        if first:
            every = (mesh_shape["dp"] * mesh_shape["seq"], 16, width)
            in_specs += [whole(sums.shape)]
            out_specs += [whole(every)]
            out_shape += [jax.ShapeDtypeStruct(every, BF16)]
            sems = [pltpu.SemaphoreType.DMA((early[0].all_levels,))] * 2
            scratch += [pltpu.VMEM(every, BF16)] + sems
        else:
            scratch += [pltpu.SemaphoreType.DMA] * len(early)
        return call(
            functools.partial(attend_back_kernel, first, early, steps * pairs),
            name,
            (steps, pairs),
            in_specs,
            out_specs,
            out_shape,
            scratch,
            flops=10 * steps * pairs * 2 * rows * count * LANES,
            exps=steps * pairs * 2 * rows * count,
            collective=1 if first else 2,
        )(qe, ge, keys, values, *extra)

    grad_block = pl.BlockSpec((1, pairs, patches, LANES), lambda j, i: (j, 0, i, 0))
    hbm = pl.BlockSpec(memory_space=pl.ANY)

    dq_part, dkr, dvr, shard_one, shard_two, early_all = attend_back(
        kr, vr, [*gives, sums], True, "attend_back_far"
    )
    dx_far, gw_part = call(
        project_back_far_kernel,
        "project_back_far",
        (steps, remote),
        [grad_block] * 2 + [patch_block, whole(w_qkv.shape)],
        [patch_block, whole((width, 2 * width))],
        [
            jax.ShapeDtypeStruct((steps, remote, patches, width), BF16),
            jax.ShapeDtypeStruct((width, 2 * width), F32),
        ],
        flops=4 * steps * far_rows * width * 2 * width,
        moved=steps * far_rows * width * 8,
    )(dkr, dvr, n1r.reshape(steps, remote, patches, width), w_qkv)
    dx_got = [send(dx_far[:, 2 * r - 2 : 2 * r], -r, False) for r in range(1, chips)]
    dq, dk, dv, *early_sums = attend_back(
        k, v, [dq_part, shard_one, shard_two], False, "attend_back_near"
    )
    columns = w_qkv.shape[1] // LANES
    give_late = call(
        weight_back_kernel,
        "weight_back",
        (steps, 2),
        [grad_block] * 3 + [patch_block, whole(gw_part.shape)],
        whole((columns, width, LANES)),
        jax.ShapeDtypeStruct((columns, width, LANES), BF16),
        [pltpu.VMEM((width, columns * LANES), F32)],
        flops=2 * steps * rows * width * 3 * width,
        moved=steps * rows * width * 8,
    )(dq, dk, dv, n1.reshape(steps, 2, patches, width), gw_part)

    direct = Direct(mesh_shape, columns * width // 16)
    full_shape = (2, direct.padded, LANES)
    late_all_shape = (2, direct.peers, 16, LANES)
    grad_own, grad_got, late_sum, late_all = call(
        functools.partial(tail_kernel, direct, len(dx_got)),
        "tail",
        (steps, 2),
        [whole((2, direct.half, LANES)), step_block, step_block, whole(mod.shape), scalars()]
        + [patch_block]
        + [grad_block] * 3
        + [whole(w_qkv.shape)]
        + [patch_block] * len(dx_got),
        [step_block, hbm, hbm, hbm],
        [
            jax.ShapeDtypeStruct((steps, patches, width), BF16),
            jax.ShapeDtypeStruct((steps, patches, width), BF16),
            jax.ShapeDtypeStruct(full_shape, BF16),
            jax.ShapeDtypeStruct(late_all_shape, BF16),
        ],
        [
            pltpu.VMEM((16, LANES), F32),
            pltpu.VMEM((steps, patches, width), BF16),
            pltpu.VMEM((steps, patches, width), BF16),
            pltpu.VMEM((direct.padded, LANES), BF16),
            pltpu.VMEM((direct.half, LANES), BF16),
            pltpu.VMEM((direct.peers, direct.piece, LANES), BF16),
            pltpu.VMEM(full_shape, BF16),
            pltpu.VMEM(late_all_shape, BF16),
            pltpu.SemaphoreType.DMA((6,)),
            pltpu.SemaphoreType.DMA((2, direct.peers)),
            pltpu.SemaphoreType.DMA((2, direct.peers)),
            pltpu.SemaphoreType.DMA((2, direct.peers)),
            pltpu.SemaphoreType.DMA((2, steps)),
            pltpu.SemaphoreType.DMA((3,)),
        ],
        flops=2 * steps * rows * width * 3 * width,
        collective=3,
    )(
        give_late.reshape(2, direct.half, LANES),
        own_x,
        sib_x,
        mod,
        lead_steps,
        gm,
        dq,
        dk,
        dv,
        w_qkv,
        *dx_got,
    )

    early_all = early_all.reshape(-1, width)
    late_all = late_all.reshape(-1, LANES)
    small = [early_all, late_all, emb_table, w_ada, *early_sums, late_sum]
    out_shapes = [(slots * items, patches, width)] * 2 + [emb_table.shape, w_ada.shape]
    out_shapes += [(1, 6 * width), w_qkv.shape, w_out.shape, w_fc1.shape, w_fc2.shape]
    outs = call(
        functools.partial(final_kernel, early, direct),
        "final",
        (),
        [whole(value.shape) for value in small] + [whole((steps, patches, width))] * 4,
        [hbm] * 2 + [whole(emb_table.shape), hbm, whole((1, 6 * width))] + [hbm] * 4,
        [
            jax.ShapeDtypeStruct(shape, BF16 if index < 2 else F32)
            for index, shape in enumerate(out_shapes)
        ],
        [pltpu.VMEM(w.shape, F32) for w in (w_ada, w_qkv, w_out, w_fc1, w_fc2)]
        + [pltpu.SemaphoreType.DMA((4 * 2 + 5,))],
        flops=2 * early_all.shape[0] * width * 6 * width,
        moved=6 * w_ada.size,
    )(*small, final_own, final_got, grad_own, grad_got)
    outputs, grad_inputs, g_emb, g_ada, g_bada, g_qkv, g_out, g_fc1, g_fc2 = outs
    return (
        outputs.reshape(inputs.shape),
        grad_inputs.reshape(inputs.shape),
        g_emb,
        g_ada,
        g_bada.reshape(-1),
        g_qkv,
        g_out,
        g_fc1,
        g_fc2,
    )


def solution(mesh):
    tokens = P(None, "dp", "seq", None)
    return jax.shard_map(
        functools.partial(local, dict(mesh.shape)),
        mesh=mesh,
        in_specs=(tokens, tokens, P("dp"), P("dp", None)) + (P(),) * 7,
        out_specs=(tokens, tokens) + (P(),) * 7,
        check_vma=False,
    )
```

```python
import functools

import jax
import jax.numpy as jnp
from jax import lax
from jax.experimental import pallas as pl
from jax.experimental.pallas import tpu as pltpu
from jax.sharding import PartitionSpec as P

HD = 64
LANES = 128
EPSILON = 1e-06
LOG2E = 1.4426950408889634
NN = (((1,), (0,)), ((), ()))
NT = (((1,), (1,)), ((), ()))
TN = (((0,), (0,)), ((), ()))
F32 = jnp.float32
BF16 = jnp.bfloat16
VMEM_BYTES = 56 * 1024 * 1024


def dot(a, b, dims=NN):
    return lax.dot_general(a, b, dims, preferred_element_type=F32)


def call(
    body,
    name,
    grid,
    in_specs,
    out_specs,
    out_shape,
    scratch=(),
    flops=0,
    moved=0,
    exps=0,
    collective=None,
    aliases=None,
):
    return pl.pallas_call(
        body,
        name=name,
        grid=grid,
        in_specs=in_specs,
        out_specs=out_specs,
        out_shape=out_shape,
        scratch_shapes=list(scratch),
        input_output_aliases=aliases or {},
        cost_estimate=pl.CostEstimate(flops=flops, bytes_accessed=moved, transcendentals=exps),
        compiler_params=pltpu.CompilerParams(
            vmem_limit_bytes=VMEM_BYTES,
            collective_id=collective,
            has_side_effects=collective is not None,
        ),
    )


def whole(shape):
    return pl.BlockSpec(shape, lambda *_: (0,) * len(shape))


def scalars():
    return pl.BlockSpec(memory_space=pltpu.SMEM)


def lane_index(shape):
    return lax.broadcasted_iota(jnp.int32, shape, 1)


def first_step(steps):
    return lax.rem(lax.axis_index("seq"), 2) * steps


def normalize(values):
    center = values - jnp.mean(values, axis=-1, keepdims=True)
    spread = jnp.mean(center * center, axis=-1, keepdims=True)
    inverse = lax.rsqrt(spread + EPSILON)
    return center * inverse, inverse


def norm_back(grad, xhat, inverse):
    first = jnp.mean(grad, axis=-1, keepdims=True)
    second = jnp.mean(grad * xhat, axis=-1, keepdims=True)
    return inverse * (grad - first - xhat * second)


def pick(refs, which):
    value = refs[0][0]
    for index in range(1, len(refs)):
        value = jnp.where(which == index, refs[index][0], value)
    return value


class Exchange:
    def __init__(self, mesh_shape, row_tiles, turn=0):
        bits = {"seq": [], "dp": []}
        for axis in bits:
            bit = 1
            while bit < mesh_shape[axis]:
                bits[axis].append((axis, bit))
                bit *= 2
        turned = bits["dp"][turn:] + bits["dp"][:turn]
        self.bits = bits["seq"][:1] + turned + bits["seq"][1:]
        self.all_levels = len(self.bits)
        self.levels = 1 + len(turned)
        self.even = 0
        while self.even < self.levels and row_tiles % 2 == 0:
            row_tiles //= 2
            self.even += 1
        unit = 2 ** (self.levels - self.even)
        self.groups = 2**self.even
        self.real = row_tiles * 16
        self.padded = -(-row_tiles // unit) * unit * 16
        self.shard = self.padded // unit

    def sizes(self, level):
        if level < self.even:
            return (self.groups >> (level + 1), self.real)
        return (1, self.padded >> (level - self.even + 1))

    def receive_scratch(self, width):
        last = self.levels - 1
        return [
            pltpu.VMEM(self.sizes(min(level, last)) + (width,), BF16)
            for level in range(self.all_levels)
        ]

    def place(self, level):
        axis, bit = self.bits[level]
        here = lax.axis_index(axis)
        value = (here // bit) % 2
        return value, {axis: here + bit * (1 - 2 * value)}

    def spot(self, level, first, flip):
        group, row = 0, 0
        for index in range(first, level + 1):
            value, _ = self.place(index)
            if flip and index == level:
                value = 1 - value
            if index < self.even:
                group = group + value * (self.groups >> (index + 1))
            else:
                row = row + value * (self.padded >> (index - self.even + 1))
        if level >= self.even:
            row = pl.multiple_of(row, 16)
        count, rows = self.sizes(level)
        return pl.ds(group, count), pl.ds(row, rows)

    def barrier(self):
        semaphore = pltpu.get_barrier_semaphore()
        for level in range(self.all_levels):
            _, partner = self.place(level)
            pl.semaphore_signal(
                semaphore, inc=1, device_id=partner, device_id_type=pl.DeviceIdType.MESH
            )
        pl.semaphore_wait(semaphore, self.all_levels)

    def copy(self, source, target, sends, recvs, level):
        _, partner = self.place(level)
        return pltpu.make_async_remote_copy(
            src_ref=source,
            dst_ref=target,
            send_sem=sends.at[level],
            recv_sem=recvs.at[level],
            device_id=partner,
            device_id_type=pl.DeviceIdType.MESH,
        )

    def reduce_copy(self, level, start_ref, acc_ref, got, sends, recvs):
        if level >= self.levels:
            return self.copy(self.own_shard(acc_ref, 1), got[level], sends, recvs, level)
        groups, rows = self.spot(level, min(level, 1), True)
        source = start_ref if level == 0 else acc_ref
        return self.copy(source.at[groups, rows], got[level], sends, recvs, level)

    def reduce_start(self, level, *refs):
        self.reduce_copy(level, *refs).start()

    def reduce_finish(self, level, start_ref, acc_ref, got, sends, recvs):
        self.reduce_copy(level, start_ref, acc_ref, got, sends, recvs).wait()
        if level >= self.levels:
            own = self.own_shard(acc_ref, 1)
            own[...] = (own[...].astype(F32) + got[level][...].astype(F32)).astype(BF16)
            return
        count, rows = self.sizes(level)
        groups, spots = self.spot(level, min(level, 1), False)
        if level == 0:
            target_groups, target_rows = pl.ds(0, count), pl.ds(0, rows)
            if self.padded > self.real:
                acc_ref[:, self.real :, :] = jnp.zeros_like(acc_ref[:, self.real :, :])
        else:
            target_groups, target_rows = groups, spots
        source = start_ref if level == 0 else acc_ref

        def add(index, carry):
            one = pl.ds(groups.start + index, 1)
            to = pl.ds(target_groups.start + index, 1)
            value = source[one, spots, :].astype(F32) + got[level][pl.ds(index, 1)].astype(F32)
            acc_ref[to, target_rows, :] = value.astype(BF16)
            return carry

        lax.fori_loop(0, count, add, 0)

    def own_shard(self, ref, first):
        if self.levels > self.even:
            return ref.at[self.spot(self.levels - 1, first, False)]
        groups, _ = self.spot(self.levels - 1, first, False)
        return ref.at[groups, pl.ds(0, self.shard)]

    def gather_copy(self, level, full_ref, sends, recvs):
        piece = full_ref.at[self.spot(level, 0, False)]
        return self.copy(piece, piece, sends, recvs, level)

    def gather_start(self, level, *refs):
        self.gather_copy(level, *refs).start()

    def gather_finish(self, level, *refs):
        self.gather_copy(level, *refs).wait()


def modulation(lead_ref, emb_ref, ada_ref, bias_ref):
    shape = (16, emb_ref.shape[0])
    rows = lax.broadcasted_iota(jnp.int32, shape, 0)
    columns = lane_index(shape)
    onehot = jnp.zeros(shape, F32)
    for step in range(2):
        lead = lead_ref[0, first_step(2) + step]
        onehot = jnp.where((rows == step) & (columns == lead), 1.0, onehot)
    condition = dot(onehot.astype(BF16), emb_ref[...])
    active = (condition * jax.nn.sigmoid(condition)).astype(BF16)
    return dot(active, ada_ref[...]) + bias_ref[...].astype(F32)


def project(x_refs, mod_ref, step, w_ref, normed_ref, head_refs):
    width = w_ref.shape[0]
    patches = x_refs[0].shape[1]
    shift = mod_ref[pl.ds(step, 1), 0:width]
    scale = mod_ref[pl.ds(step, 1), width : 2 * width]
    queries = len(head_refs) == 3
    for index, x_ref in enumerate(x_refs):
        at = slice(index * patches, (index + 1) * patches)
        xhat, _ = normalize(x_ref[0].astype(F32))
        normed = (xhat * (1.0 + scale) + shift).astype(BF16)
        normed_ref[0, at, :] = normed
        for part, head_ref in enumerate(head_refs):
            start = (part + (0 if queries else 1)) * width
            projected = dot(normed, w_ref[:, start : start + width])
            if queries and part == 0:
                projected = projected.astype(BF16).astype(F32) * HD**-0.5
            projected = projected.astype(BF16)
            for pair in range(width // LANES):
                head_ref[0, pair, at, :] = projected[:, pair * LANES : (pair + 1) * LANES]


def with_ones(values):
    low = lane_index(values.shape) < HD
    one = jnp.ones_like(values)
    return jnp.where(low, values, one), jnp.where(low, one, values)


def exponentials(query, keys_ref, pair, width=256):
    count = keys_ref.shape[2]
    width = min(width, count)
    return jnp.concatenate(
        [
            jnp.exp(dot(query, keys_ref[0, pair, start : start + width, :], NT)).astype(BF16)
            for start in range(0, count, width)
        ],
        axis=-1,
    )


def masked(values):
    low = lane_index(values.shape) < HD
    zero = jnp.zeros_like(values)
    return jnp.where(low, values, zero), jnp.where(low, zero, values)


def near_kernel(rows, *refs):
    lead_ref, emb_ref, ada_ref, bias_ref, own_x, sib_x, w_ref = refs[:7]
    mod_ref, normed_ref, q_ref, k_ref, v_ref, acc_ref, ext_ref = refs[7:]
    step, pair = pl.program_id(0), pl.program_id(1)

    @pl.when((step == 0) & (pair == 0))
    def _():
        mod_ref[...] = modulation(lead_ref, emb_ref, ada_ref, bias_ref)

    @pl.when(pair == 0)
    def _():
        project([own_x, sib_x], mod_ref, step, w_ref, normed_ref, [q_ref, k_ref, v_ref])

    ext_ref[0], ext_ref[1] = with_ones(v_ref[0, pair])
    for start in range(0, q_ref.shape[2], rows):
        at = slice(start, start + rows)
        for head, query in enumerate(masked(q_ref[0, pair, at, :])):
            acc_ref[0, 0, head, at, :] = dot(exponentials(query, k_ref, pair), ext_ref[head])


def far_kernel(rows, step, sources, *refs):
    x_refs, refs = refs[:sources], refs[sources:]
    mod_ref, w_ref, q_ref, k_ref, v_ref, acc_ref = refs[:6]
    normed_ref, kr_ref, vr_ref, o_ref, qe_ref, ext_ref, total_ref = refs[-7:]
    pair = pl.program_id(0)

    @pl.when(pair == 0)
    def _():
        project(x_refs, mod_ref, step, w_ref, normed_ref, [kr_ref, vr_ref])

    ext_ref[0], ext_ref[1] = with_ones(vr_ref[0, pair])
    def finish(at, query, first, second, top_first, top_second):
        lane = lane_index(query.shape)
        low = lane < HD
        swapped = jnp.where(low, second, first)
        total = pltpu.roll(swapped, HD, 1)
        o_ref[0, 0, at, :] = jnp.where(low, first, second) / total
        log_total = jnp.log(swapped) + jnp.where(low, top_second, top_first)
        high = log_total.astype(BF16).astype(F32)
        middle = (log_total - high).astype(BF16).astype(F32)
        rest = log_total - high - middle
        spot = lane % HD
        extra = jnp.where(spot == 0, -high, jnp.where(spot == 1, -middle, -rest))
        extra = jnp.where(spot < 3, extra, 0.0).astype(BF16)
        qe_ref[0, 0, 0, at, :] = jnp.where(low, query, extra)
        qe_ref[0, 0, 1, at, :] = jnp.where(low, extra, query)
        return total

    for start in range(0, q_ref.shape[2], rows):
        at = slice(start, start + rows)
        query = q_ref[0, 0, at, :]
        sums = []
        for head, own in enumerate(masked(query)):
            more = dot(exponentials(own, kr_ref, pair), ext_ref[head])
            sums.append(acc_ref[0, 0, head, at, :] + more)
        total_ref[at, :] = finish(at, query, sums[0], sums[1], 0.0, 0.0)

    total = total_ref[...]
    bad = jnp.sum(jnp.where((total > 1e-25) & (total < 1e25), 0.0, 1.0))

    @pl.when(bad > 0.0)
    def _():
        own_ext = with_ones(v_ref[0, 0])

        again_rows = min(256, q_ref.shape[2])

        def again(index, carry):
            at = pl.ds(pl.multiple_of(index * again_rows, again_rows), again_rows)
            query = q_ref[0, 0, at, :]
            sums, tops = [], []
            for head, own in enumerate(masked(query)):
                scores = dot(own, k_ref[0, 0], NT)
                others = dot(own, kr_ref[0, pair], NT)
                top = jnp.maximum(
                    jnp.max(scores, axis=-1, keepdims=True),
                    jnp.max(others, axis=-1, keepdims=True),
                )
                sums.append(
                    dot(jnp.exp(scores - top).astype(BF16), own_ext[head])
                    + dot(jnp.exp(others - top).astype(BF16), ext_ref[head])
                )
                tops.append(top)
            finish(at, query, sums[0], sums[1], tops[0], tops[1])
            return carry

        lax.fori_loop(0, q_ref.shape[2] // again_rows, again, 0)


def gelu_parts(values):
    cumulative = 0.5 * lax.erf(values * 0.7071067811865476) + 0.5
    bell = jnp.exp2(values * values * (-0.5 * LOG2E))
    return values * cumulative, cumulative + values * bell * 0.3989422804014327


def patch_kernel(
    rows,
    chunk,
    counts_ref,
    lead_ref,
    own_x,
    sib_x,
    own_ct,
    sib_ct,
    mod_ref,
    o_ref,
    out_w,
    fc1_w,
    fc2_w,
    final_own,
    final_sib,
    gm_ref,
    ge_ref,
    sums_ref,
    stack_one,
    stack_two,
    hidden_s,
    gpre_s,
    n2_s,
    g2_s,
    g1_s,
    mixed_s,
    gout_s,
    gfc1_s,
    gfc2_s,
    sums_s,
):
    step, half = pl.program_id(0), pl.program_id(1)
    width, hidden_width = fc1_w.shape
    patches = own_x.shape[1]
    slot = first_step(pl.num_programs(0)) + step
    active = (slot < counts_ref[0]).astype(F32)

    def piece(index):
        return mod_ref[pl.ds(step, 1), index * width : (index + 1) * width]

    gate1, shift2, scale2, gate2 = piece(2), piece(3), piece(4), piece(5)

    @pl.when((step == 0) & (half == 0))
    def _():
        sums_s[...] = jnp.zeros_like(sums_s)
        gout_s[...] = jnp.zeros_like(gout_s)
        gfc1_s[...] = jnp.zeros_like(gfc1_s)
        gfc2_s[...] = jnp.zeros_like(gfc2_s)

    def block(index, carry):
        at = pl.ds(pl.multiple_of(index * rows, rows), rows)
        x = jnp.where(half == 0, own_x[0, at, :], sib_x[0, at, :]).astype(F32)
        final_grad = jnp.where(half == 0, own_ct[0, at, :], sib_ct[0, at, :]).astype(F32) * active
        outs = [o_ref[0, pair, at, :] for pair in range(width // LANES)]
        mixed = jnp.concatenate([o.astype(BF16) for o in outs], axis=-1)
        mixed_s[at, :] = mixed
        branch_one = dot(mixed, out_w[...])
        middle = x + gate1 * branch_one
        xhat, inverse = normalize(middle)
        n2 = (xhat * (1.0 + scale2) + shift2).astype(BF16)
        n2_s[at, :] = n2
        g2 = (gate2 * final_grad).astype(BF16)
        g2_s[at, :] = g2
        branch_two = jnp.zeros((rows, width), F32)
        gy = jnp.zeros((rows, width), F32)
        for start in range(0, hidden_width, chunk):
            columns = slice(start, start + chunk)
            pre = dot(n2, fc1_w[:, columns])
            grad_hidden = dot(g2, fc2_w[columns, :], NT)
            hidden, slope = gelu_parts(pre)
            hidden = hidden.astype(BF16)
            grad_pre = (slope * grad_hidden).astype(BF16)
            hidden_s[at, columns] = hidden
            gpre_s[at, columns] = grad_pre
            branch_two += dot(hidden, fc2_w[columns, :])
            gy += dot(grad_pre, fc1_w[:, columns], NT)
        final = ((middle + gate2 * branch_two) * active).astype(BF16)

        @pl.when(half == 0)
        def _():
            final_own[0, at, :] = final

        @pl.when(half == 1)
        def _():
            final_sib[0, at, :] = final

        gm = final_grad + norm_back(gy * (1.0 + scale2), xhat, inverse)
        gm_ref[0, 0, at, :] = gm
        g1 = (gate1 * gm).astype(BF16)
        g1_s[at, :] = g1
        sums = [branch_one * gm, gy, gy * xhat, branch_two * final_grad]
        for row, value in enumerate(sums):
            place = pl.ds(2 * row + step, 1)
            sums_s[place, :] += jnp.sum(value, axis=0, keepdims=True)
        grad_mixed = dot(g1, out_w[...], NT).astype(BF16)
        lane = lane_index((rows, LANES))
        low = lane < HD
        spot = lane % HD
        for pair, o in enumerate(outs):
            grad = grad_mixed[:, pair * LANES : (pair + 1) * LANES]
            product = grad.astype(F32) * o
            first = jnp.sum(jnp.where(low, product, 0.0), axis=-1, keepdims=True)
            second = jnp.sum(jnp.where(low, 0.0, product), axis=-1, keepdims=True)
            inner = jnp.where(low, second, first)
            high = inner.astype(BF16).astype(F32)
            mid = (inner - high).astype(BF16).astype(F32)
            extra = jnp.where(spot == 0, -high, jnp.where(spot == 1, -mid, high + mid - inner))
            extra = jnp.where(spot < 3, extra, 0.0).astype(BF16)
            ge_ref[0, pair, 0, at, :] = jnp.where(low, grad, extra)
            ge_ref[0, pair, 1, at, :] = jnp.where(low, extra, grad)
        return carry

    lax.fori_loop(0, patches // rows, block, 0)
    gout_s[...] += dot(mixed_s[...], g1_s[...], TN)
    gfc1_s[...] += dot(n2_s[...], gpre_s[...], TN)
    gfc2_s[...] += dot(g2_s[...], hidden_s[...], TN)

    @pl.when((step == pl.num_programs(0) - 1) & (half == pl.num_programs(1) - 1))
    def _():
        for index in range(2):
            lead = lead_ref[0, first_step(2) + index]
            sums_s[12 + index : 13 + index, :] = jnp.where(lane_index((1, width)) == lead, 1.0, 0.0)
        sums_ref[...] = sums_s[...].astype(BF16)
        blocks = hidden_width // width
        for index in range(blocks):
            columns = slice(index * width, (index + 1) * width)
            stack_one[index] = gfc1_s[:, columns].astype(BF16)
            stack_two[index] = gfc2_s[:, columns].T.astype(BF16)
        stack_two[blocks] = gout_s[...].astype(BF16)


def attend_back_kernel(rows, first_pass, exchanges, grid_steps, *refs):
    count = len(exchanges)
    qe_ref, ge_ref, k_ref, v_ref = refs[:4]
    refs = refs[4:]
    if first_pass:
        gives, sums_ref, refs = refs[:count], refs[count], refs[count + 1 :]
        dq_ref, dk_ref, dv_ref = refs[:3]
        shards, all_ref, refs = refs[3 : 3 + count], refs[3 + count], refs[4 + count :]
        all_s, all_sends, all_recvs = refs[-3:]
    else:
        dq_in, shards, refs = refs[0], refs[1 : 1 + count], refs[1 + count :]
        dq_ref, dk_ref, dv_ref = refs[:3]
        fulls, refs = refs[3 : 3 + count], refs[3 + count :]
    dq_s, refs = refs[0], refs[1:]
    states = []
    for index, exchange in enumerate(exchanges):
        sends, recvs = refs[1], refs[2]
        if first_pass:
            got = refs[3 : 3 + exchange.all_levels]
            states.append((gives[index], refs[0], got, sends, recvs))
            refs = refs[3 + exchange.all_levels :]
        else:
            states.append((refs[0], sends, recvs))
            refs = refs[3:]
    per_step = k_ref.shape[2] // rows
    static_slots = grid_steps * per_step
    first_slot = (pl.program_id(0) * pl.num_programs(1) + pl.program_id(1)) * per_step
    levels = exchanges[0].all_levels if first_pass else exchanges[0].levels

    def all_copy(level):
        index = 0
        for lower in range(len(exchanges[0].bits)):
            index = index + exchanges[0].place(lower)[0] * (1 << lower)
        if level < 0:
            return all_s.at[pl.ds(index, 1)]
        size = 1 << level
        piece = all_s.at[pl.ds((index // size) * size, size)]
        return exchanges[0].copy(piece, piece, all_sends, all_recvs, level)

    def reduce_action(order):
        if order == 0:
            exchanges[0].barrier()
            own = all_copy(-1)
            own[...] = sums_ref[...][None]
        else:
            all_copy(order - 1).wait()
        if order < levels:
            all_copy(order).start()
        else:
            all_ref[...] = all_s[...]
        for exchange, state, shard in zip(exchanges, states, shards):
            if order > 0:
                exchange.reduce_finish(order - 1, *state)
            if order < levels:
                exchange.reduce_start(order, *state)
            else:
                shard[...] = exchange.own_shard(state[1], 1)[...][0]

    def gather_action(order):
        if order == 0:
            exchanges[0].barrier()
        for exchange, state, shard in zip(exchanges, states, shards):
            if order == 0:
                exchange.own_shard(state[0], 0)[...] = shard[...][None]
            else:
                exchange.gather_finish(levels - order, *state)
            if order < levels:
                exchange.gather_start(levels - 1 - order, *state)
        if order == levels:
            copies = [
                pltpu.make_async_copy(state[0], full, refs[index])
                for index, (state, full) in enumerate(zip(states, fulls))
            ]
            for copy in copies:
                copy.start()
            for copy in copies:
                copy.wait()

    action = reduce_action if first_pass else gather_action
    weights = [5.0, 10.0, 9.0, 6.0] + [4.0] * levels
    weights = weights[:levels] if first_pass else weights[:levels][::-1]
    marks, total = [0], 0.0
    for weight in weights:
        total += weight
        marks.append(total)
    last = static_slots - (2 if first_pass else 1)
    marks = [min(int(mark * last / total + 0.5), last) for mark in marks]

    dq_s[...] = jnp.zeros_like(dq_s) if first_pass else dq_in[0, 0].T

    def block(index, carry):
        for order, mark in enumerate(marks[:-1]):
            pl.when(first_slot + index == mark)(functools.partial(action, order))
        at = pl.ds(pl.multiple_of(index * rows, rows), rows)
        keys = k_ref[0, 0, at, :]
        values = v_ref[0, 0, at, :]
        lane = lane_index(keys.shape)
        low = lane < HD
        ones = jnp.where(lane % HD < 3, 1.0, 0.0).astype(BF16)
        zero = jnp.zeros_like(keys)
        grads = []
        for head in range(2):
            own = low if head == 0 else jnp.logical_not(low)
            query = qe_ref[0, 0, head]
            grad = ge_ref[0, 0, head]
            probs = jnp.exp(dot(jnp.where(own, keys, ones), query, NT))
            grad_probs = dot(jnp.where(own, values, ones), grad, NT)
            grad_scores = (probs * grad_probs).astype(BF16)
            grads.append((dot(grad_scores, query), dot(probs.astype(BF16), grad)))
            dq_s[...] += dot(jnp.where(own, keys, zero), grad_scores, TN)
        dk_ref[0, 0, at, :] = jnp.where(low, grads[0][0], grads[1][0]).astype(BF16)
        dv_ref[0, 0, at, :] = jnp.where(low, grads[0][1], grads[1][1]).astype(BF16)
        return carry

    lax.fori_loop(0, per_step, block, 0)
    if first_pass:
        dq_ref[0, 0] = dq_s[...].T
    else:
        dq_ref[0, 0] = (dq_s[...].T * HD**-0.5).astype(BF16)
    pl.when(first_slot + per_step == static_slots)(functools.partial(action, levels))


def project_back_far_kernel(dk_ref, dv_ref, normed_ref, w_ref, dx_ref, gw_ref):
    width = w_ref.shape[0]
    joined = join_heads(dk_ref, dv_ref)
    dx_ref[0, 0] = dot(joined, w_ref[:, width:], NT).astype(BF16)

    @pl.when((pl.program_id(0) == 0) & (pl.program_id(1) == 0))
    def _():
        gw_ref[...] = jnp.zeros_like(gw_ref)

    gw_ref[...] += dot(normed_ref[0, 0], joined, TN)


def weight_back_kernel(dq_ref, dk_ref, dv_ref, normed_ref, far_ref, gw_ref, gw_s):
    step, which = pl.program_id(0), pl.program_id(1)
    width = normed_ref.shape[3]

    @pl.when((step == 0) & (which == 0))
    def _():
        gw_s[:, :width] = jnp.zeros_like(gw_s[:, :width])
        gw_s[:, width:] = far_ref[...]

    gw_s[...] += dot(normed_ref[0, 0], join_heads(dq_ref, dk_ref, dv_ref), TN)

    @pl.when((step == pl.num_programs(0) - 1) & (which == pl.num_programs(1) - 1))
    def _():
        for block in range(gw_ref.shape[0]):
            gw_ref[block] = gw_s[:, block * LANES : (block + 1) * LANES].astype(BF16)


def join_heads(*grads):
    return jnp.concatenate([ref[0, pair] for ref in grads for pair in range(ref.shape[1])], axis=-1)


class Direct:
    def __init__(self, mesh_shape, row_tiles):
        self.chips = mesh_shape["seq"] // 2
        self.peers = mesh_shape["dp"] * self.chips
        self.half = row_tiles * 8
        self.piece = -(-row_tiles // (2 * self.peers)) * 16
        self.padded = self.piece * self.peers

    def me(self):
        return lax.axis_index("dp") * self.chips + lax.axis_index("seq") // 2

    def core(self):
        return lax.axis_index("seq") % 2

    def sibling(self):
        return {"seq": lax.axis_index("seq") + 1 - 2 * self.core()}

    def peer(self, shift):
        other = (self.me() + shift) % self.peers
        device = {"dp": other // self.chips, "seq": (other % self.chips) * 2 + self.core()}
        return other, device

    def rows(self, index):
        return pl.ds(pl.multiple_of(index * self.piece, 16), self.piece)

    def barrier(self):
        semaphore = pltpu.get_barrier_semaphore()

        def signal(device):
            pl.semaphore_signal(semaphore, 1, device_id=device, device_id_type=pl.DeviceIdType.MESH)

        signal(self.sibling())

        def greet(shift, carry):
            signal(self.peer(shift)[1])
            return carry

        lax.fori_loop(1, self.peers, greet, 0)
        pl.semaphore_wait(semaphore, self.peers)

    def copy(self, source, target, send, recv, device):
        return pltpu.make_async_remote_copy(
            src_ref=source,
            dst_ref=target,
            send_sem=send,
            recv_sem=recv,
            device_id=device,
            device_id_type=pl.DeviceIdType.MESH,
        )

    def each_peer(self, do):
        def one(shift, carry):
            do(shift)
            return carry

        lax.fori_loop(1, self.peers, one, 0)


def tail_kernel(direct, remote, *refs):
    give_ref, own_x, sib_x, mod_ref, lead_ref, gm_ref, dq_ref, dk_ref, dv_ref, w_ref = refs[:10]
    others = refs[10 : 10 + remote]
    grad_ref, got_ref, full_ref, all_ref = refs[10 + remote : 14 + remote]
    sums_s, other_s, got_s, sum_s, core_s, pieces_s, full_s, all_s = refs[14 + remote : 22 + remote]
    core_sems, piece_sems, back_sems, all_sems, grad_sems, local_sem = refs[22 + remote :]
    step, half = pl.program_id(0), pl.program_id(1)
    width = own_x.shape[2]
    core, me = direct.core(), direct.me()

    core_copy = direct.copy(
        give_ref.at[1 - core], core_s, core_sems.at[0], core_sems.at[1], direct.sibling()
    )

    def piece_copy(shift):
        other, device = direct.peer(shift)
        return direct.copy(
            sum_s.at[direct.rows(other)],
            pieces_s.at[shift],
            piece_sems.at[0, shift],
            piece_sems.at[1, shift],
            device,
        )

    def full_copy(shift, arriving):
        _, device = direct.peer(shift)
        owner = (me + direct.peers - shift) % direct.peers if arriving else me
        place = full_s.at[core, direct.rows(owner)]
        return direct.copy(place, place, back_sems.at[0, shift], back_sems.at[1, shift], device)

    def sums_copy(shift, arriving):
        _, device = direct.peer(shift)
        owner = (me + direct.peers - shift) % direct.peers if arriving else me
        place = all_s.at[core, owner]
        return direct.copy(place, place, all_sems.at[0, shift], all_sems.at[1, shift], device)

    def side_copy(values, which, side):
        place = values.at[side]
        return direct.copy(
            place, place, core_sems.at[which], core_sems.at[which + 1], direct.sibling()
        )

    def grad_copy(index):
        return direct.copy(
            other_s.at[index],
            got_s.at[index],
            grad_sems.at[0, index],
            grad_sems.at[1, index],
            direct.sibling(),
        )

    @pl.when((step == 0) & (half == 0))
    def _():
        direct.barrier()
        core_copy.start()
        sums_s[...] = jnp.zeros_like(sums_s)

    @pl.when((step == 0) & (half == 1))
    def _():
        core_copy.wait()
        real = core_s.shape[0]
        sum_s[:real] = (give_ref[core].astype(F32) + core_s[...].astype(F32)).astype(BF16)
        if direct.padded > real:
            sum_s[real:] = jnp.zeros_like(sum_s[real:])
        direct.each_peer(lambda shift: piece_copy(shift).start())

    x = jnp.where(half == 0, own_x[0], sib_x[0]).astype(F32)
    scale = mod_ref[pl.ds(step, 1), width : 2 * width]
    xhat, inverse = normalize(x)
    gy = dot(join_heads(dq_ref, dk_ref, dv_ref), w_ref[...], NT)
    for other in others:
        gy = gy + other[0, 0].astype(F32)
    grad = (gm_ref[0, 0] + norm_back(gy * (1.0 + scale), xhat, inverse)).astype(BF16)

    @pl.when(half == 0)
    def _():
        grad_ref[0] = grad

    @pl.when(half == 1)
    def _():
        other_s[step] = grad
        grad_copy(step).start()

    for kind, value in enumerate((gy, gy * xhat)):
        total = jnp.sum(value, axis=0, keepdims=True)
        for index in range(width // LANES):
            place = pl.ds((kind * 2 + step) * (width // LANES) + index, 1)
            sums_s[place, :] += total[:, index * LANES : (index + 1) * LANES]

    @pl.when((step == 1) & (half == 1))
    def _():
        for index in range(2):
            chosen = lane_index((1, LANES)) == lead_ref[0, first_step(2) + index]
            sums_s[12 + index : 13 + index, :] = jnp.where(chosen, 1.0, 0.0)
        all_s[core, me] = sums_s[...].astype(BF16)
        direct.each_peer(lambda shift: sums_copy(shift, False).start())
        direct.each_peer(lambda shift: piece_copy(shift).wait())

        def add(shift, total):
            return total + pieces_s[shift].astype(F32)

        total = lax.fori_loop(1, direct.peers, add, sum_s[direct.rows(me)].astype(F32))
        full_s[core, direct.rows(me)] = total.astype(BF16)
        direct.each_peer(lambda shift: full_copy(shift, False).start())

        def arrived(shift):
            full_copy(shift, False).wait_send()
            full_copy(shift, True).wait_recv()
            sums_copy(shift, False).wait_send()
            sums_copy(shift, True).wait_recv()

        direct.each_peer(arrived)
        side_copy(full_s, 2, core).start()
        side_copy(all_s, 4, core).start()
        for index in range(2):
            grad_copy(index).wait()
        side_copy(full_s, 2, core).wait_send()
        side_copy(full_s, 2, 1 - core).wait_recv()
        side_copy(all_s, 4, core).wait_send()
        side_copy(all_s, 4, 1 - core).wait_recv()
        outs = [(got_s, got_ref), (full_s, full_ref), (all_s, all_ref)]
        copies = [
            pltpu.make_async_copy(source, target, local_sem.at[index])
            for index, (source, target) in enumerate(outs)
        ]
        for copy in copies:
            copy.start()
        for copy in copies:
            copy.wait()


def unstack(at, full_ref, targets, rows):
    row, end = 0, rows * len(targets)
    while row < end:
        group, inside, left = at(row)
        block, place = divmod(row, rows)
        count = min(left, rows - place)
        target, first_row, first_column = targets[block]
        columns = slice(first_column, first_column + full_ref.shape[2])
        value = full_ref[group, inside : inside + count, :].astype(F32)
        target[first_row + place : first_row + place + count, columns] = value
        row += count


def spread_leads(grads, step_of, table_rows):
    count = grads.shape[0]
    part = min(count, 512)
    row = lax.broadcasted_iota(jnp.int32, (part, part), 0)
    column = lane_index((part, part))
    chosen = (row // 16 == column // 16) & (row % 16 == 12 + step_of(column % 16))
    spread = jnp.where(chosen, 1.0, 0.0).astype(BF16)
    leads = [
        dot(grads[start : start + part, :LANES], spread, TN)[:table_rows]
        for start in range(0, count, part)
    ]
    return jnp.concatenate(leads, axis=-1)


def final_kernel(early, direct, *refs):
    early_sums, late_sums, emb_ref, ada_ref = refs[:4]
    stacks, moved, outs = refs[4:7], refs[7:11], refs[11:20]
    gada_s, gqkv_s, gout_s, gfc1_s, gfc2_s, one_ref, two_ref, late_ref, *held = refs[20:32]
    load_sems, sems = refs[32:]
    final_out, grad_out, gemb_ref, gada_out, gbada_ref, gqkv_out, gout_out, gfc1_out, gfc2_out = outs
    size = gout_s.shape[0]
    blocks = gfc1_s.shape[1] // size
    copies = []
    loads = [
        pltpu.make_async_copy(source, target, load_sems.at[index])
        for index, (source, target) in enumerate(
            zip([*stacks, *moved], [one_ref, two_ref, late_ref, *held])
        )
    ]
    for load in loads:
        load.start()

    def start(source, target):
        copy = pltpu.make_async_copy(source, target, sems.at[len(copies)])
        copy.start()
        copies.append(copy)

    def grouped(exchange):
        def at(row):
            group, inside = divmod(row, exchange.real)
            return group, inside, exchange.real - inside

        return at

    def halved(row):
        group, inside = divmod(row, direct.half)
        return group, inside, direct.half - inside

    loads[0].wait()
    unstack(grouped(early[0]), one_ref, [(gfc1_s, 0, block * size) for block in range(blocks)], size)
    start(gfc1_s, gfc1_out)
    rest = [(gfc2_s, block * size, 0) for block in range(blocks)] + [(gout_s, 0, 0)]
    loads[1].wait()
    unstack(grouped(early[1]), two_ref, rest, size)
    start(gfc2_s, gfc2_out)
    start(gout_s, gout_out)
    columns = gqkv_s.shape[1] // LANES
    loads[2].wait()
    unstack(halved, late_ref, [(gqkv_s, 0, block * LANES) for block in range(columns)], size)
    start(gqkv_s, gqkv_out)
    mine = first_step(2)
    for index in range(4):
        loads[3 + index].wait()
        first = mine if index % 2 == 0 else 2 - mine
        start(held[index], (final_out if index < 2 else grad_out).at[pl.ds(first, 2)])

    table_rows = emb_ref.shape[0]
    table = emb_ref[...].astype(F32)
    gate = jax.nn.sigmoid(table)
    slope = gate * (1.0 + table * (1.0 - gate))
    table_act = (table * gate).astype(BF16)
    total = jnp.zeros((table_rows, size), F32)

    def one_piece(grads, leads, place, first):
        chosen = jnp.where(place, leads, 0.0).astype(BF16)
        acts = dot(table_act, chosen, TN).astype(BF16)
        where = slice(first, first + grads.shape[1])
        gada_s[:, where] = dot(acts, grads)
        by_lead = dot(chosen, grads)
        gbada_ref[where] = jnp.sum(by_lead, axis=0)
        high = by_lead.astype(BF16)
        low = (by_lead - high.astype(F32)).astype(BF16)
        return dot(high, ada_ref[:, where], NT) + dot(low, ada_ref[:, where], NT)

    grads = early_sums[...]
    leads = spread_leads(grads, lambda row: row % 2, table_rows)
    row = lane_index((1, grads.shape[0])) % 16
    for index in range(4):
        total += one_piece(grads, leads, row // 2 == index, (2 + index) * size)
    grads = late_sums[...]
    parts = size // LANES
    leads = spread_leads(grads, lambda row: (row // parts) % 2, table_rows)
    row = lane_index((1, grads.shape[0])) % 16
    for index in range(2):
        for part in range(parts):
            place = (row // (2 * parts) == index) & (row % parts == part)
            total += one_piece(grads, leads, place, index * size + part * LANES)
    gemb_ref[...] = total * slope
    start(gada_s, gada_out)
    for copy in copies:
        copy.wait()


def local(
    mesh_shape, inputs, cotangent, counts, lead_steps, emb_table, w_ada, b_ada, w_qkv, w_out, w_fc1, w_fc2
):
    slots, items, patches, width = inputs.shape
    chips = mesh_shape["seq"] // 2
    blocks = w_fc1.shape[1] // w_fc1.shape[0]
    steps = slots * items // 2
    hidden_width = w_fc1.shape[1]
    pairs = width // LANES
    rows = 2 * patches
    remote = 2 * (chips - 1)
    far_rows = remote * patches
    spot = lax.axis_index("seq")
    core = lax.rem(spot, 2)
    devices = 2 * chips

    def send(values, shift, cross):
        pairs_list = []
        for source in range(devices):
            chip, side = source // 2, source % 2
            pairs_list.append((source, ((chip + shift) % chips) * 2 + (1 - side if cross else side)))
        return lax.ppermute(values, "seq", pairs_list)

    x_steps = inputs.reshape(2, steps, patches, width)
    ct_steps = cotangent.reshape(2, steps, patches, width)
    own_x = lax.dynamic_index_in_dim(x_steps, core, 0, keepdims=False)
    other_x = lax.dynamic_index_in_dim(x_steps, 1 - core, 0, keepdims=False)
    own_ct = lax.dynamic_index_in_dim(ct_steps, core, 0, keepdims=False)
    other_ct = lax.dynamic_index_in_dim(ct_steps, 1 - core, 0, keepdims=False)
    sib_x = send(other_x, 0, True)
    far_x = []
    for step in range(steps):
        some = slice(step, step + 1)
        for shift in range(1, chips):
            far_x.append(send(own_x[some], shift, False))
            far_x.append(send(other_x[some], shift, True))
    sib_ct = send(other_ct, 0, True)

    step_block = pl.BlockSpec((1, patches, width), lambda j, i: (j, 0, 0))
    patch_block = pl.BlockSpec((1, 1, patches, width), lambda j, i: (j, i, 0, 0))

    def head_rows(count):
        return pl.BlockSpec((1, 1, count, LANES), lambda j, p: (j, p, 0, 0))

    def of_step(*shape):
        return pl.BlockSpec((1,) + shape, lambda j, p: (j,) + (0,) * len(shape))

    both_heads = pl.BlockSpec((1, 1, 2, rows, LANES), lambda j, p: (j, p, 0, 0, 0))
    piece = min(256, rows)
    near_work = 4 * steps * pairs * 2 * rows * LANES * rows
    near_heads = jax.ShapeDtypeStruct((steps, pairs, rows, LANES), BF16)
    mod, n1, q, k, v, acc = call(
        functools.partial(near_kernel, piece),
        "near",
        (steps, pairs),
        [scalars(), whole(emb_table.shape), whole(w_ada.shape), whole((1, 6 * width))]
        + [step_block] * 2
        + [whole(w_qkv.shape)],
        [whole((16, 6 * width)), of_step(rows, width)]
        + [of_step(pairs, rows, LANES)] * 3
        + [both_heads],
        [
            jax.ShapeDtypeStruct((16, 6 * width), F32),
            jax.ShapeDtypeStruct((steps, rows, width), BF16),
            near_heads,
            near_heads,
            near_heads,
            jax.ShapeDtypeStruct((steps, pairs, 2, rows, LANES), F32),
        ],
        [pltpu.VMEM((2, rows, LANES), BF16)],
        flops=near_work + 6 * steps * rows * width * width,
        exps=steps * pairs * 2 * rows * rows,
    )(lead_steps, emb_table, w_ada, b_ada.reshape(1, -1), own_x, sib_x, w_qkv)

    def far(step, before):
        some_x = far_x[step * remote : (step + 1) * remote]

        def at_step(*shape):
            return pl.BlockSpec((1,) + shape, lambda p: (step,) + (0,) * len(shape))

        def at_pair(*shape):
            return pl.BlockSpec((1, 1) + shape, lambda p: (step, p) + (0,) * len(shape))

        operands = [*some_x, mod, w_qkv, q, k, v, acc]
        return call(
            functools.partial(far_kernel, piece, step, remote),
            "far",
            (pairs,),
            [whole((1, patches, width))] * remote
            + [whole(mod.shape), whole(w_qkv.shape)]
            + [at_pair(rows, LANES)] * 3
            + [at_pair(2, rows, LANES)]
            + [pl.BlockSpec(memory_space=pl.ANY)] * len(before),
            [at_step(far_rows, width)]
            + [at_step(pairs, far_rows, LANES)] * 2
            + [at_pair(rows, LANES), at_pair(2, rows, LANES)],
            [
                jax.ShapeDtypeStruct((steps, far_rows, width), BF16),
                jax.ShapeDtypeStruct((steps, pairs, far_rows, LANES), BF16),
                jax.ShapeDtypeStruct((steps, pairs, far_rows, LANES), BF16),
                jax.ShapeDtypeStruct((steps, pairs, rows, LANES), F32),
                jax.ShapeDtypeStruct((steps, pairs, 2, rows, LANES), BF16),
            ],
            [pltpu.VMEM((2, far_rows, LANES), BF16), pltpu.VMEM((rows, LANES), F32)],
            flops=near_work // 2,
            exps=pairs * 2 * rows * far_rows,
            aliases={len(operands) + index: index for index in range(len(before))},
        )(*operands, *before)

    far_results = []
    for step in range(steps):
        far_results = far(step, far_results)
    n1r, kr, vr, o, qe = far_results

    block_rows = min(256, patches)
    outs = call(
        functools.partial(patch_kernel, block_rows, hidden_width),
        "patchwise",
        (steps, 2),
        [scalars()] * 2
        + [step_block] * 4
        + [
            whole(mod.shape),
            pl.BlockSpec((1, pairs, patches, LANES), lambda j, i: (j, 0, i, 0)),
            whole(w_out.shape),
            whole(w_fc1.shape),
            whole(w_fc2.shape),
        ],
        [
            step_block,
            step_block,
            patch_block,
            pl.BlockSpec((1, pairs, 2, patches, LANES), lambda j, i: (j, 0, 0, i, 0)),
            whole((16, width)),
            whole((blocks, width, width)),
            whole((blocks + 1, width, width)),
        ],
        [
            jax.ShapeDtypeStruct((steps, patches, width), BF16),
            jax.ShapeDtypeStruct((steps, patches, width), BF16),
            jax.ShapeDtypeStruct((steps, 2, patches, width), F32),
            jax.ShapeDtypeStruct((steps, pairs, 2, rows, LANES), BF16),
            jax.ShapeDtypeStruct((16, width), BF16),
            jax.ShapeDtypeStruct((blocks, width, width), BF16),
            jax.ShapeDtypeStruct((blocks + 1, width, width), BF16),
        ],
        [pltpu.VMEM((patches, hidden_width), BF16)] * 2
        + [pltpu.VMEM((patches, width), BF16)] * 4
        + [
            pltpu.VMEM((width, width), F32),
            pltpu.VMEM((width, hidden_width), F32),
            pltpu.VMEM((width, hidden_width), F32),
            pltpu.VMEM((16, width), F32),
        ],
        flops=6 * steps * rows * width * (2 * hidden_width + width),
        moved=steps * rows * width * 20,
        exps=2 * steps * rows * hidden_width,
    )(counts, lead_steps, own_x, sib_x, own_ct, sib_ct, mod, o, w_out, w_fc1, w_fc2)
    final_own, final_sib, gm, ge, sums, stack_one, stack_two = outs
    final_got = send(final_sib, 0, True)
    early = [Exchange(mesh_shape, blocks * width // 16, 0), Exchange(mesh_shape, (blocks + 1) * width // 16, 1)]
    gives = [g.reshape(e.groups, e.real, width) for e, g in zip(early, (stack_one, stack_two))]

    def attend_back(keys, values, extra, first, name):
        count = keys.shape[2]
        in_specs = [both_heads] * 2 + [head_rows(count)] * 2
        out_specs = [head_rows(rows), head_rows(count), head_rows(count)]
        out_shape = [
            jax.ShapeDtypeStruct((steps, pairs, rows, LANES), F32 if first else BF16),
            jax.ShapeDtypeStruct((steps, pairs, count, LANES), BF16),
            jax.ShapeDtypeStruct((steps, pairs, count, LANES), BF16),
        ]
        scratch = [pltpu.VMEM((LANES, rows), F32)]
        if not first:
            in_specs += [head_rows(rows)]
        for exchange in early:
            shape = (exchange.groups, exchange.padded, width)
            shard = (exchange.shard, width)
            sems = [pltpu.SemaphoreType.DMA((exchange.all_levels,))] * 2
            if first:
                in_specs += [whole((exchange.groups, exchange.real, width))]
                out_specs += [whole(shard)]
                out_shape += [jax.ShapeDtypeStruct(shard, BF16)]
                half = (exchange.groups // 2, exchange.padded, width)
                scratch += [pltpu.VMEM(half, BF16)] + sems + exchange.receive_scratch(width)
            else:
                in_specs += [whole(shard)]
                out_specs += [pl.BlockSpec(memory_space=pl.ANY)]
                out_shape += [jax.ShapeDtypeStruct(shape, BF16)]
                scratch += [pltpu.VMEM(shape, BF16)] + sems
        if first:
            every = (mesh_shape["dp"] * mesh_shape["seq"], 16, width)
            in_specs += [whole(sums.shape)]
            out_specs += [whole(every)]
            out_shape += [jax.ShapeDtypeStruct(every, BF16)]
            sems = [pltpu.SemaphoreType.DMA((early[0].all_levels,))] * 2
            scratch += [pltpu.VMEM(every, BF16)] + sems
        else:
            scratch += [pltpu.SemaphoreType.DMA] * len(early)
        return call(
            functools.partial(attend_back_kernel, min(512, count), first, early, steps * pairs),
            name,
            (steps, pairs),
            in_specs,
            out_specs,
            out_shape,
            scratch,
            flops=10 * steps * pairs * 2 * rows * count * LANES,
            exps=steps * pairs * 2 * rows * count,
            collective=1 if first else 2,
        )(qe, ge, keys, values, *extra)

    grad_block = pl.BlockSpec((1, pairs, patches, LANES), lambda j, i: (j, 0, i, 0))
    hbm = pl.BlockSpec(memory_space=pl.ANY)

    dq_part, dkr, dvr, shard_one, shard_two, early_all = attend_back(
        kr, vr, [*gives, sums], True, "attend_back_far"
    )
    dx_far, gw_part = call(
        project_back_far_kernel,
        "project_back_far",
        (steps, remote),
        [grad_block] * 2 + [patch_block, whole(w_qkv.shape)],
        [patch_block, whole((width, 2 * width))],
        [
            jax.ShapeDtypeStruct((steps, remote, patches, width), BF16),
            jax.ShapeDtypeStruct((width, 2 * width), F32),
        ],
        flops=4 * steps * far_rows * width * 2 * width,
        moved=steps * far_rows * width * 8,
    )(dkr, dvr, n1r.reshape(steps, remote, patches, width), w_qkv)
    dx_got = [send(dx_far[:, 2 * r - 2 : 2 * r], -r, False) for r in range(1, chips)]
    dq, dk, dv, *early_sums = attend_back(
        k, v, [dq_part, shard_one, shard_two], False, "attend_back_near"
    )
    columns = w_qkv.shape[1] // LANES
    give_late = call(
        weight_back_kernel,
        "weight_back",
        (steps, 2),
        [grad_block] * 3 + [patch_block, whole(gw_part.shape)],
        whole((columns, width, LANES)),
        jax.ShapeDtypeStruct((columns, width, LANES), BF16),
        [pltpu.VMEM((width, columns * LANES), F32)],
        flops=2 * steps * rows * width * 3 * width,
        moved=steps * rows * width * 8,
    )(dq, dk, dv, n1.reshape(steps, 2, patches, width), gw_part)

    direct = Direct(mesh_shape, columns * width // 16)
    full_shape = (2, direct.padded, LANES)
    late_all_shape = (2, direct.peers, 16, LANES)
    grad_own, grad_got, late_sum, late_all = call(
        functools.partial(tail_kernel, direct, len(dx_got)),
        "tail",
        (steps, 2),
        [whole((2, direct.half, LANES)), step_block, step_block, whole(mod.shape), scalars()]
        + [patch_block]
        + [grad_block] * 3
        + [whole(w_qkv.shape)]
        + [patch_block] * len(dx_got),
        [step_block, hbm, hbm, hbm],
        [
            jax.ShapeDtypeStruct((steps, patches, width), BF16),
            jax.ShapeDtypeStruct((steps, patches, width), BF16),
            jax.ShapeDtypeStruct(full_shape, BF16),
            jax.ShapeDtypeStruct(late_all_shape, BF16),
        ],
        [
            pltpu.VMEM((16, LANES), F32),
            pltpu.VMEM((steps, patches, width), BF16),
            pltpu.VMEM((steps, patches, width), BF16),
            pltpu.VMEM((direct.padded, LANES), BF16),
            pltpu.VMEM((direct.half, LANES), BF16),
            pltpu.VMEM((direct.peers, direct.piece, LANES), BF16),
            pltpu.VMEM(full_shape, BF16),
            pltpu.VMEM(late_all_shape, BF16),
            pltpu.SemaphoreType.DMA((6,)),
            pltpu.SemaphoreType.DMA((2, direct.peers)),
            pltpu.SemaphoreType.DMA((2, direct.peers)),
            pltpu.SemaphoreType.DMA((2, direct.peers)),
            pltpu.SemaphoreType.DMA((2, steps)),
            pltpu.SemaphoreType.DMA((3,)),
        ],
        flops=2 * steps * rows * width * 3 * width,
        collective=3,
    )(
        give_late.reshape(2, direct.half, LANES),
        own_x,
        sib_x,
        mod,
        lead_steps,
        gm,
        dq,
        dk,
        dv,
        w_qkv,
        *dx_got,
    )

    early_all = early_all.reshape(-1, width)
    late_all = late_all.reshape(-1, LANES)
    small = [early_all, late_all, emb_table, w_ada]
    large = [*early_sums, late_sum, final_own, final_got, grad_own, grad_got]
    out_shapes = [(slots * items, patches, width)] * 2 + [emb_table.shape, w_ada.shape]
    out_shapes += [b_ada.shape, w_qkv.shape, w_out.shape, w_fc1.shape, w_fc2.shape]
    outs = call(
        functools.partial(final_kernel, early, direct),
        "final",
        (),
        [whole(value.shape) for value in small] + [hbm] * len(large),
        [hbm] * 2 + [whole(emb_table.shape), hbm, whole(b_ada.shape)] + [hbm] * 4,
        [
            jax.ShapeDtypeStruct(shape, BF16 if index < 2 else F32)
            for index, shape in enumerate(out_shapes)
        ],
        [pltpu.VMEM(w.shape, F32) for w in (w_ada, w_qkv, w_out, w_fc1, w_fc2)]
        + [pltpu.VMEM(value.shape, BF16) for value in large]
        + [pltpu.SemaphoreType.DMA((len(large),)), pltpu.SemaphoreType.DMA((4 + 5,))],
        flops=2 * early_all.shape[0] * width * 6 * width,
        moved=6 * w_ada.size,
    )(*small, *large)
    outputs, grad_inputs, g_emb, g_ada, g_bada, g_qkv, g_out, g_fc1, g_fc2 = outs
    return (
        outputs.reshape(inputs.shape),
        grad_inputs.reshape(inputs.shape),
        g_emb,
        g_ada,
        g_bada,
        g_qkv,
        g_out,
        g_fc1,
        g_fc2,
    )


def solution(mesh):
    tokens = P(None, "dp", "seq", None)
    return jax.shard_map(
        functools.partial(local, dict(mesh.shape)),
        mesh=mesh,
        in_specs=(tokens, tokens, P("dp"), P("dp", None)) + (P(),) * 7,
        out_specs=(tokens, tokens) + (P(),) * 7,
        check_vma=False,
    )
```

```python
import functools

import jax
import jax.numpy as jnp
from jax import lax
from jax.experimental import pallas as pl
from jax.experimental.pallas import tpu as pltpu
from jax.sharding import PartitionSpec as P

HD = 64
LANES = 128
EPSILON = 1e-06
LOG2E = 1.4426950408889634
NN = (((1,), (0,)), ((), ()))
NT = (((1,), (1,)), ((), ()))
TN = (((0,), (0,)), ((), ()))
F32 = jnp.float32
BF16 = jnp.bfloat16
VMEM_BYTES = 56 * 1024 * 1024


def dot(a, b, dims=NN):
    return lax.dot_general(a, b, dims, preferred_element_type=F32)


def call(
    body,
    name,
    grid,
    in_specs,
    out_specs,
    out_shape,
    scratch=(),
    flops=0,
    moved=0,
    exps=0,
    collective=None,
    aliases=None,
):
    return pl.pallas_call(
        body,
        name=name,
        grid=grid,
        in_specs=in_specs,
        out_specs=out_specs,
        out_shape=out_shape,
        scratch_shapes=list(scratch),
        input_output_aliases=aliases or {},
        cost_estimate=pl.CostEstimate(flops=flops, bytes_accessed=moved, transcendentals=exps),
        compiler_params=pltpu.CompilerParams(
            vmem_limit_bytes=VMEM_BYTES,
            collective_id=collective,
            has_side_effects=collective is not None,
        ),
    )


def whole(shape):
    return pl.BlockSpec(shape, lambda *_: (0,) * len(shape))


def scalars():
    return pl.BlockSpec(memory_space=pltpu.SMEM)


def lane_index(shape):
    return lax.broadcasted_iota(jnp.int32, shape, 1)


def first_step(steps):
    return lax.rem(lax.axis_index("seq"), 2) * steps


def normalize(values):
    center = values - jnp.mean(values, axis=-1, keepdims=True)
    spread = jnp.mean(center * center, axis=-1, keepdims=True)
    inverse = lax.rsqrt(spread + EPSILON)
    return center * inverse, inverse


def norm_back(grad, xhat, inverse):
    first = jnp.mean(grad, axis=-1, keepdims=True)
    second = jnp.mean(grad * xhat, axis=-1, keepdims=True)
    return inverse * (grad - first - xhat * second)


def pick(refs, which):
    value = refs[0][0]
    for index in range(1, len(refs)):
        value = jnp.where(which == index, refs[index][0], value)
    return value


class Exchange:
    def __init__(self, mesh_shape, row_tiles, turn=0):
        bits = {"seq": [], "dp": []}
        for axis in bits:
            bit = 1
            while bit < mesh_shape[axis]:
                bits[axis].append((axis, bit))
                bit *= 2
        turned = bits["dp"][turn:] + bits["dp"][:turn]
        self.bits = bits["seq"][:1] + turned + bits["seq"][1:]
        self.all_levels = len(self.bits)
        self.levels = 1 + len(turned)
        self.even = 0
        while self.even < self.levels and row_tiles % 2 == 0:
            row_tiles //= 2
            self.even += 1
        unit = 2 ** (self.levels - self.even)
        self.groups = 2**self.even
        self.real = row_tiles * 16
        self.padded = -(-row_tiles // unit) * unit * 16
        self.shard = self.padded // unit

    def sizes(self, level):
        if level < self.even:
            return (self.groups >> (level + 1), self.real)
        return (1, self.padded >> (level - self.even + 1))

    def receive_scratch(self, width):
        last = self.levels - 1
        return [
            pltpu.VMEM(self.sizes(min(level, last)) + (width,), BF16)
            for level in range(self.all_levels)
        ]

    def place(self, level):
        axis, bit = self.bits[level]
        here = lax.axis_index(axis)
        value = (here // bit) % 2
        return value, {axis: here + bit * (1 - 2 * value)}

    def spot(self, level, first, flip):
        group, row = 0, 0
        for index in range(first, level + 1):
            value, _ = self.place(index)
            if flip and index == level:
                value = 1 - value
            if index < self.even:
                group = group + value * (self.groups >> (index + 1))
            else:
                row = row + value * (self.padded >> (index - self.even + 1))
        if level >= self.even:
            row = pl.multiple_of(row, 16)
        count, rows = self.sizes(level)
        return pl.ds(group, count), pl.ds(row, rows)

    def barrier(self):
        semaphore = pltpu.get_barrier_semaphore()
        for level in range(self.all_levels):
            _, partner = self.place(level)
            pl.semaphore_signal(
                semaphore, inc=1, device_id=partner, device_id_type=pl.DeviceIdType.MESH
            )
        pl.semaphore_wait(semaphore, self.all_levels)

    def copy(self, source, target, sends, recvs, level):
        _, partner = self.place(level)
        return pltpu.make_async_remote_copy(
            src_ref=source,
            dst_ref=target,
            send_sem=sends.at[level],
            recv_sem=recvs.at[level],
            device_id=partner,
            device_id_type=pl.DeviceIdType.MESH,
        )

    def reduce_copy(self, level, start_ref, acc_ref, got, sends, recvs):
        if level >= self.levels:
            return self.copy(self.own_shard(acc_ref, 1), got[level], sends, recvs, level)
        groups, rows = self.spot(level, min(level, 1), True)
        source = start_ref if level == 0 else acc_ref
        return self.copy(source.at[groups, rows], got[level], sends, recvs, level)

    def reduce_start(self, level, *refs):
        self.reduce_copy(level, *refs).start()

    def reduce_finish(self, level, start_ref, acc_ref, got, sends, recvs):
        self.reduce_copy(level, start_ref, acc_ref, got, sends, recvs).wait()
        if level >= self.levels:
            own = self.own_shard(acc_ref, 1)
            own[...] = (own[...].astype(F32) + got[level][...].astype(F32)).astype(BF16)
            return
        count, rows = self.sizes(level)
        groups, spots = self.spot(level, min(level, 1), False)
        if level == 0:
            target_groups, target_rows = pl.ds(0, count), pl.ds(0, rows)
            if self.padded > self.real:
                acc_ref[:, self.real :, :] = jnp.zeros_like(acc_ref[:, self.real :, :])
        else:
            target_groups, target_rows = groups, spots
        source = start_ref if level == 0 else acc_ref

        def add(index, carry):
            one = pl.ds(groups.start + index, 1)
            to = pl.ds(target_groups.start + index, 1)
            value = source[one, spots, :].astype(F32) + got[level][pl.ds(index, 1)].astype(F32)
            acc_ref[to, target_rows, :] = value.astype(BF16)
            return carry

        lax.fori_loop(0, count, add, 0)

    def own_shard(self, ref, first):
        if self.levels > self.even:
            return ref.at[self.spot(self.levels - 1, first, False)]
        groups, _ = self.spot(self.levels - 1, first, False)
        return ref.at[groups, pl.ds(0, self.shard)]

    def gather_copy(self, level, full_ref, sends, recvs):
        piece = full_ref.at[self.spot(level, 0, False)]
        return self.copy(piece, piece, sends, recvs, level)

    def gather_start(self, level, *refs):
        self.gather_copy(level, *refs).start()

    def gather_finish(self, level, *refs):
        self.gather_copy(level, *refs).wait()


def modulation(lead_ref, emb_ref, ada_ref, bias_ref):
    shape = (16, emb_ref.shape[0])
    rows = lax.broadcasted_iota(jnp.int32, shape, 0)
    columns = lane_index(shape)
    onehot = jnp.zeros(shape, F32)
    for step in range(2):
        lead = lead_ref[0, first_step(2) + step]
        onehot = jnp.where((rows == step) & (columns == lead), 1.0, onehot)
    condition = dot(onehot.astype(BF16), emb_ref[...])
    active = (condition * jax.nn.sigmoid(condition)).astype(BF16)
    return dot(active, ada_ref[...]) + bias_ref[...].astype(F32)


def project(x_refs, mod_ref, step, w_ref, normed_ref, head_refs):
    width = w_ref.shape[0]
    patches = x_refs[0].shape[1]
    rows = min(256, patches)
    shift = mod_ref[pl.ds(step, 1), 0:width]
    scale = mod_ref[pl.ds(step, 1), width : 2 * width]
    queries = len(head_refs) == 3
    for index, x_ref in enumerate(x_refs):

        def block(count, carry):
            start = pl.multiple_of(count * rows, rows)
            at = pl.ds(pl.multiple_of(index * patches + start, rows), rows)
            xhat, _ = normalize(x_ref[0, pl.ds(start, rows), :].astype(F32))
            normed = (xhat * (1.0 + scale) + shift).astype(BF16)
            normed_ref[0, :, at] = normed.T
            for part, head_ref in enumerate(head_refs):
                first = (part + (0 if queries else 1)) * width
                projected = dot(normed, w_ref[:, first : first + width])
                if queries and part == 0:
                    projected = projected.astype(BF16).astype(F32) * HD**-0.5
                projected = projected.astype(BF16)
                for pair in range(width // LANES):
                    head_ref[0, pair, at, :] = projected[:, pair * LANES : (pair + 1) * LANES]
            return carry

        lax.fori_loop(0, patches // rows, block, 0)


def with_ones(values):
    low = lane_index(values.shape) < HD
    one = jnp.ones_like(values)
    return jnp.where(low, values, one), jnp.where(low, one, values)


def exponentials(query, keys_ref, pair, width=256):
    count = keys_ref.shape[2]
    width = min(width, count)
    return jnp.concatenate(
        [
            jnp.exp(dot(query, keys_ref[0, pair, start : start + width, :], NT)).astype(BF16)
            for start in range(0, count, width)
        ],
        axis=-1,
    )


def masked(values):
    low = lane_index(values.shape) < HD
    zero = jnp.zeros_like(values)
    return jnp.where(low, values, zero), jnp.where(low, zero, values)


def near_kernel(rows, *refs):
    lead_ref, emb_ref, ada_ref, bias_ref, own_x, sib_x, w_ref = refs[:7]
    mod_ref, normed_ref, q_ref, k_ref, v_ref, acc_ref, ext_ref = refs[7:]
    step, pair = pl.program_id(0), pl.program_id(1)

    @pl.when((step == 0) & (pair == 0))
    def _():
        mod_ref[...] = modulation(lead_ref, emb_ref, ada_ref, bias_ref)

    @pl.when(pair == 0)
    def _():
        project([own_x, sib_x], mod_ref, step, w_ref, normed_ref, [q_ref, k_ref, v_ref])

    ext_ref[0], ext_ref[1] = with_ones(v_ref[0, pair])

    def block(index, carry):
        at = pl.ds(pl.multiple_of(index * rows, rows), rows)
        for head, query in enumerate(masked(q_ref[0, pair, at, :])):
            acc_ref[0, 0, head, at, :] = dot(exponentials(query, k_ref, pair), ext_ref[head])
        return carry

    lax.fori_loop(0, q_ref.shape[2] // rows, block, 0, unroll=2)


def far_kernel(rows, step, sources, *refs):
    x_refs, refs = refs[:sources], refs[sources:]
    mod_ref, w_ref, q_ref, k_ref, v_ref, acc_ref = refs[:6]
    normed_ref, kr_ref, vr_ref, o_ref, qe_ref, ext_ref, total_ref = refs[-7:]
    pair = pl.program_id(0)

    @pl.when(pair == 0)
    def _():
        project(x_refs, mod_ref, step, w_ref, normed_ref, [kr_ref, vr_ref])

    ext_ref[0], ext_ref[1] = with_ones(vr_ref[0, pair])
    def finish(at, query, first, second, top_first, top_second):
        lane = lane_index(query.shape)
        low = lane < HD
        swapped = jnp.where(low, second, first)
        total = pltpu.roll(swapped, HD, 1)
        o_ref[0, 0, at, :] = jnp.where(low, first, second) / total
        log_total = jnp.log(swapped) + jnp.where(low, top_second, top_first)
        high = log_total.astype(BF16).astype(F32)
        middle = (log_total - high).astype(BF16).astype(F32)
        rest = log_total - high - middle
        spot = lane % HD
        extra = jnp.where(spot == 0, -high, jnp.where(spot == 1, -middle, -rest))
        extra = jnp.where(spot < 3, extra, 0.0).astype(BF16)
        qe_ref[0, 0, 0, at, :] = jnp.where(low, query, extra)
        qe_ref[0, 0, 1, at, :] = jnp.where(low, extra, query)
        return total

    def block(index, carry):
        at = pl.ds(pl.multiple_of(index * rows, rows), rows)
        query = q_ref[0, 0, at, :]
        sums = []
        for head, own in enumerate(masked(query)):
            more = dot(exponentials(own, kr_ref, pair), ext_ref[head])
            sums.append(acc_ref[0, 0, head, at, :] + more)
        total_ref[at, :] = finish(at, query, sums[0], sums[1], 0.0, 0.0)
        return carry

    lax.fori_loop(0, q_ref.shape[2] // rows, block, 0, unroll=2)
    total = total_ref[...]
    bad = jnp.sum(jnp.where((total > 1e-25) & (total < 1e25), 0.0, 1.0))

    @pl.when(bad > 0.0)
    def _():
        own_ext = with_ones(v_ref[0, 0])

        again_rows = min(256, q_ref.shape[2])

        def again(index, carry):
            at = pl.ds(pl.multiple_of(index * again_rows, again_rows), again_rows)
            query = q_ref[0, 0, at, :]
            sums, tops = [], []
            for head, own in enumerate(masked(query)):
                scores = dot(own, k_ref[0, 0], NT)
                others = dot(own, kr_ref[0, pair], NT)
                top = jnp.maximum(
                    jnp.max(scores, axis=-1, keepdims=True),
                    jnp.max(others, axis=-1, keepdims=True),
                )
                sums.append(
                    dot(jnp.exp(scores - top).astype(BF16), own_ext[head])
                    + dot(jnp.exp(others - top).astype(BF16), ext_ref[head])
                )
                tops.append(top)
            finish(at, query, sums[0], sums[1], tops[0], tops[1])
            return carry

        lax.fori_loop(0, q_ref.shape[2] // again_rows, again, 0)


def gelu_parts(values):
    cumulative = 0.5 * lax.erf(values * 0.7071067811865476) + 0.5
    bell = jnp.exp2(values * values * (-0.5 * LOG2E))
    return values * cumulative, cumulative + values * bell * 0.3989422804014327


def patch_kernel(
    rows,
    chunk,
    counts_ref,
    lead_ref,
    own_x,
    sib_x,
    own_ct,
    sib_ct,
    mod_ref,
    o_ref,
    out_w,
    fc1_w,
    fc2_w,
    final_own,
    final_sib,
    gm_ref,
    ge_ref,
    sums_ref,
    stack_one,
    stack_two,
    hidden_s,
    gpre_s,
    n2_s,
    g2_s,
    g1_s,
    mixed_s,
    gout_s,
    gfc1_s,
    gfc2_s,
    sums_s,
):
    step, half = pl.program_id(0), pl.program_id(1)
    width, hidden_width = fc1_w.shape
    patches = own_x.shape[1]
    slot = first_step(pl.num_programs(0)) + step
    active = (slot < counts_ref[0]).astype(F32)

    def piece(index):
        return mod_ref[pl.ds(step, 1), index * width : (index + 1) * width]

    gate1, shift2, scale2, gate2 = piece(2), piece(3), piece(4), piece(5)

    @pl.when((step == 0) & (half == 0))
    def _():
        sums_s[...] = jnp.zeros_like(sums_s)
        gout_s[...] = jnp.zeros_like(gout_s)
        gfc1_s[...] = jnp.zeros_like(gfc1_s)
        gfc2_s[...] = jnp.zeros_like(gfc2_s)

    def block(index, carry):
        at = pl.ds(pl.multiple_of(index * rows, rows), rows)
        x = jnp.where(half == 0, own_x[0, at, :], sib_x[0, at, :]).astype(F32)
        final_grad = jnp.where(half == 0, own_ct[0, at, :], sib_ct[0, at, :]).astype(F32) * active
        outs = [o_ref[0, pair, at, :] for pair in range(width // LANES)]
        mixed = jnp.concatenate([o.astype(BF16) for o in outs], axis=-1)
        mixed_s[at, :] = mixed
        branch_one = dot(mixed, out_w[...])
        middle = x + gate1 * branch_one
        xhat, inverse = normalize(middle)
        n2 = (xhat * (1.0 + scale2) + shift2).astype(BF16)
        n2_s[at, :] = n2
        g2 = (gate2 * final_grad).astype(BF16)
        g2_s[at, :] = g2
        branch_two = jnp.zeros((rows, width), F32)
        gy = jnp.zeros((rows, width), F32)
        for start in range(0, hidden_width, chunk):
            columns = slice(start, start + chunk)
            pre = dot(n2, fc1_w[:, columns])
            grad_hidden = dot(g2, fc2_w[columns, :], NT)
            hidden, slope = gelu_parts(pre)
            hidden = hidden.astype(BF16)
            grad_pre = (slope * grad_hidden).astype(BF16)
            hidden_s[at, columns] = hidden
            gpre_s[at, columns] = grad_pre
            branch_two += dot(hidden, fc2_w[columns, :])
            gy += dot(grad_pre, fc1_w[:, columns], NT)
        final = ((middle + gate2 * branch_two) * active).astype(BF16)

        @pl.when(half == 0)
        def _():
            final_own[0, at, :] = final

        @pl.when(half == 1)
        def _():
            final_sib[0, at, :] = final

        gm = final_grad + norm_back(gy * (1.0 + scale2), xhat, inverse)
        gm_ref[0, 0, at, :] = gm
        g1 = (gate1 * gm).astype(BF16)
        g1_s[at, :] = g1
        sums = [branch_one * gm, gy, gy * xhat, branch_two * final_grad]
        for row, value in enumerate(sums):
            place = pl.ds(2 * row + step, 1)
            sums_s[place, :] += jnp.sum(value, axis=0, keepdims=True)
        grad_mixed = dot(g1, out_w[...], NT).astype(BF16)
        lane = lane_index((rows, LANES))
        low = lane < HD
        spot = lane % HD
        for pair, o in enumerate(outs):
            grad = grad_mixed[:, pair * LANES : (pair + 1) * LANES]
            product = grad.astype(F32) * o
            first = jnp.sum(jnp.where(low, product, 0.0), axis=-1, keepdims=True)
            second = jnp.sum(jnp.where(low, 0.0, product), axis=-1, keepdims=True)
            inner = jnp.where(low, second, first)
            high = inner.astype(BF16).astype(F32)
            mid = (inner - high).astype(BF16).astype(F32)
            extra = jnp.where(spot == 0, -high, jnp.where(spot == 1, -mid, high + mid - inner))
            extra = jnp.where(spot < 3, extra, 0.0).astype(BF16)
            ge_ref[0, pair, 0, at, :] = jnp.where(low, grad, extra)
            ge_ref[0, pair, 1, at, :] = jnp.where(low, extra, grad)
        return carry

    lax.fori_loop(0, patches // rows, block, 0)
    gout_s[...] += dot(mixed_s[...], g1_s[...], TN)
    gfc1_s[...] += dot(n2_s[...], gpre_s[...], TN)
    gfc2_s[...] += dot(g2_s[...], hidden_s[...], TN)

    @pl.when((step == pl.num_programs(0) - 1) & (half == pl.num_programs(1) - 1))
    def _():
        for index in range(2):
            lead = lead_ref[0, first_step(2) + index]
            sums_s[12 + index : 13 + index, :] = jnp.where(lane_index((1, width)) == lead, 1.0, 0.0)
        sums_ref[...] = sums_s[...].astype(BF16)
        blocks = hidden_width // width
        for index in range(blocks):
            columns = slice(index * width, (index + 1) * width)
            stack_one[index] = gfc1_s[:, columns].astype(BF16)
            stack_two[index] = gfc2_s[:, columns].T.astype(BF16)
        stack_two[blocks] = gout_s[...].astype(BF16)


def back_block(qe_ref, ge_ref, keys, values, dq_ref):
    lane = lane_index(keys.shape)
    low = lane < HD
    ones = jnp.where(lane % HD < 3, 1.0, 0.0).astype(BF16)
    zero = jnp.zeros_like(keys)
    grads = []
    for head in range(2):
        own = low if head == 0 else jnp.logical_not(low)
        query = qe_ref[0, 0, head]
        grad = ge_ref[0, 0, head]
        probs = jnp.exp(dot(jnp.where(own, keys, ones), query, NT))
        grad_probs = dot(jnp.where(own, values, ones), grad, NT)
        grad_scores = (probs * grad_probs).astype(BF16)
        grads.append((dot(grad_scores, query), dot(probs.astype(BF16), grad)))
        dq_ref[...] += dot(jnp.where(own, keys, zero), grad_scores, TN)
    return [
        jnp.where(low, first, second).astype(BF16) for first, second in zip(grads[0], grads[1])
    ]


def level_marks(levels, last, turned):
    weights = ([5.0, 10.0, 9.0, 6.0] + [4.0] * levels)[:levels]
    marks, total = [], 0.0
    for weight in weights[::-1] if turned else weights:
        marks.append(total)
        total += weight
    return [min(int(mark * last / total + 0.5), last) for mark in marks]


def back_far_kernel(rows, exchanges, direct, chips, grid, *refs):
    count = len(exchanges)
    qe_ref, ge_ref, k_ref, v_ref, normed_ref, w_ref, sums_ref = refs[:7]
    gives, refs = refs[7 : 7 + count], refs[7 + count :]
    dq_ref, gw_ref, all_ref, got_ref, dx_ref = refs[:5]
    shards, refs = refs[5 : 5 + count], refs[5 + count :]
    kv_s, dx_s, got_s, all_s, dx_sems, all_sends, all_recvs, local_sem = refs[:8]
    refs = refs[8:]
    states = []
    for index, exchange in enumerate(exchanges):
        got = refs[3 : 3 + exchange.all_levels]
        states.append((gives[index], refs[0], got, refs[1], refs[2]))
        refs = refs[3 + exchange.all_levels :]
    step, pair = pl.program_id(0), pl.program_id(1)
    pairs = grid[1]
    per_step = k_ref.shape[2] // rows
    slots = grid[0] * pairs * per_step
    first_slot = (step * pairs + pair) * per_step
    levels = exchanges[0].all_levels
    width = w_ref.shape[0]
    chip_rows = got_s.shape[1]

    def all_copy(level):
        index = 0
        for lower in range(levels):
            index = index + exchanges[0].place(lower)[0] * (1 << lower)
        if level < 0:
            return all_s.at[pl.ds(index, 1)]
        size = 1 << level
        piece = all_s.at[pl.ds((index // size) * size, size)]
        return exchanges[0].copy(piece, piece, all_sends, all_recvs, level)

    def dx_copy(shift):
        chip = (lax.axis_index("seq") // 2 + chips - shift) % chips
        return direct.copy(
            dx_s.at[(shift - 1) * chip_rows : shift * chip_rows],
            got_s.at[shift - 1],
            dx_sems.at[0, shift - 1],
            dx_sems.at[1, shift - 1],
            {"seq": chip * 2 + direct.core()},
        )

    def action(order):
        if order == 0:
            direct.barrier()
            all_copy(-1)[...] = sums_ref[...][None]
        else:
            all_copy(order - 1).wait()
        if order < levels:
            all_copy(order).start()
        else:
            all_ref[...] = all_s[...]
        for exchange, state, shard in zip(exchanges, states, shards):
            if order > 0:
                exchange.reduce_finish(order - 1, *state)
            if order < levels:
                exchange.reduce_start(order, *state)
            else:
                shard[...] = exchange.own_shard(state[1], 1)[...][0]

    marks = level_marks(levels, slots - 2, False)
    dq_ref[...] = jnp.zeros_like(dq_ref)

    def block(index, carry):
        for order, mark in enumerate(marks):
            pl.when(first_slot + index == mark)(functools.partial(action, order))
        at = pl.ds(pl.multiple_of(index * rows, rows), rows)
        grads = back_block(qe_ref, ge_ref, k_ref[0, 0, at, :], v_ref[0, 0, at, :], dq_ref.at[0, 0])
        kv_s[pair, at, :] = grads[0]
        kv_s[pairs + pair, at, :] = grads[1]
        return carry

    lax.fori_loop(0, per_step, block, 0)

    @pl.when((step == 0) & (pair == 0))
    def _():
        gw_ref[...] = jnp.zeros_like(gw_ref)

    @pl.when(pair == pairs - 1)
    def _():
        def through(index, carry):
            at = pl.ds(pl.multiple_of(index * rows, rows), rows)
            joined = jnp.concatenate([kv_s[part, at, :] for part in range(2 * pairs)], axis=-1)
            dx = dot(joined, w_ref[:, width:], NT).astype(BF16)

            @pl.when(step == 0)
            def _():
                dx_s[at, :] = dx

            @pl.when(step == 1)
            def _():
                dx_ref[at, :] = dx

            gw_ref[...] += dot(normed_ref[0, :, at], joined)
            return carry

        lax.fori_loop(0, per_step, through, 0)

        @pl.when(step == 0)
        def _():
            for shift in range(1, chips):
                dx_copy(shift).start()

    @pl.when((step == grid[0] - 1) & (pair == pairs - 1))
    def _():
        action(levels)
        for shift in range(1, chips):
            dx_copy(shift).wait()
        copy = pltpu.make_async_copy(got_s, got_ref, local_sem)
        copy.start()
        copy.wait()


def back_near_kernel(rows, exchanges, direct, grid, *refs):
    count = len(exchanges)
    qe_ref, ge_ref, k_ref, v_ref, dq_in, normed_ref, far_ref = refs[:7]
    shards, refs = refs[7 : 7 + count], refs[7 + count :]
    dq_ref, dk_ref, dv_ref, give_ref = refs[:4]
    fulls, refs = refs[4 : 4 + count], refs[4 + count :]
    late = grid[0] - 1
    late_fulls, refs = refs[:late], refs[late:]
    dq_s, gw_s, local_sems = refs[:3]
    refs = refs[3:]
    states = []
    for index in range(count):
        states.append(refs[:3])
        refs = refs[3:]
    sums = []
    for index in range(late):
        sums.append(LateSum(direct, *refs[:8]))
        refs = refs[8:]
    pair, step = pl.program_id(0), pl.program_id(1)
    per_step = k_ref.shape[2] // rows
    per_pair = grid[1] * per_step
    slots = grid[0] * per_pair
    first_slot = (pair * grid[1] + step) * per_step
    levels = exchanges[0].levels
    width = normed_ref.shape[1]
    parts = width // LANES

    def action(order):
        if order == 0:
            direct.barrier()
        for exchange, state, shard in zip(exchanges, states, shards):
            if order == 0:
                exchange.own_shard(state[0], 0)[...] = shard[...][None]
            else:
                exchange.gather_finish(levels - order, *state)
            if order < levels:
                exchange.gather_start(levels - 1 - order, *state)

    marks = level_marks(levels, slots - 1, True)
    actions = [(mark, functools.partial(action, order)) for order, mark in enumerate(marks)]
    for index, one in enumerate(sums):
        first = (index + 1) * per_pair
        for phase in range(4):
            mark = first + phase * (slots - first) // 4
            actions.append((mark, one.phases()[phase]))

    dq_s[...] = dq_in[0, 0]

    def block(index, carry):
        for mark, act in actions:
            pl.when(first_slot + index == mark)(act)
        at = pl.ds(pl.multiple_of(index * rows, rows), rows)
        grads = back_block(qe_ref, ge_ref, k_ref[0, 0, at, :], v_ref[0, 0, at, :], dq_s)
        dk_ref[0, 0, at, :] = grads[0]
        dv_ref[0, 0, at, :] = grads[1]
        return carry

    lax.fori_loop(0, per_step, block, 0)
    dq_ref[0, 0] = (dq_s[...].T * HD**-0.5).astype(BF16)

    @pl.when(step == 0)
    def _():
        gw_s[:, :LANES] = jnp.zeros_like(gw_s[:, :LANES])
        for some in range(parts):

            @pl.when(pair == some)
            def _():
                for part in range(2):
                    start = part * width + some * LANES
                    target = slice((part + 1) * LANES, (part + 2) * LANES)
                    gw_s[:, target] = far_ref[:, start : start + LANES]

    joined = jnp.concatenate([dq_ref[0, 0], dk_ref[0, 0], dv_ref[0, 0]], axis=-1)
    gw_s[...] += dot(normed_ref[0], joined)

    @pl.when(step == grid[1] - 1)
    def _():
        for some in range(late + 1):
            target = give_ref if some == late else sums[some].give

            @pl.when(pair == some)
            def _():
                for part in range(3):
                    value = gw_s[:, part * LANES : (part + 1) * LANES].astype(BF16)
                    row, done = part * width, 0
                    while done < width:
                        half, inside = divmod(row + done, direct.half)
                        size = min(width - done, direct.half - inside)
                        target[half, inside : inside + size, :] = value[done : done + size]
                        done += size

    @pl.when((pair == late) & (step == grid[1] - 1))
    def _():
        action(levels)
        for one in sums:
            one.phases()[4]()
        pieces = list(zip([state[0] for state in states] + [one.full for one in sums], [*fulls, *late_fulls]))
        copies = [
            pltpu.make_async_copy(source, target, local_sems.at[index])
            for index, (source, target) in enumerate(pieces)
        ]
        for copy in copies:
            copy.start()
        for copy in copies:
            copy.wait()


def join_heads(*grads):
    return jnp.concatenate([ref[0, pair] for ref in grads for pair in range(ref.shape[1])], axis=-1)


class Direct:
    def __init__(self, mesh_shape, row_tiles):
        self.chips = mesh_shape["seq"] // 2
        self.peers = mesh_shape["dp"] * self.chips
        self.half = row_tiles * 8
        self.piece = -(-row_tiles // (2 * self.peers)) * 16
        self.padded = self.piece * self.peers

    def me(self):
        return lax.axis_index("dp") * self.chips + lax.axis_index("seq") // 2

    def core(self):
        return lax.axis_index("seq") % 2

    def sibling(self):
        return {"seq": lax.axis_index("seq") + 1 - 2 * self.core()}

    def peer(self, shift):
        other = (self.me() + shift) % self.peers
        device = {"dp": other // self.chips, "seq": (other % self.chips) * 2 + self.core()}
        return other, device

    def rows(self, index):
        return pl.ds(pl.multiple_of(index * self.piece, 16), self.piece)

    def barrier(self):
        semaphore = pltpu.get_barrier_semaphore()

        def signal(device):
            pl.semaphore_signal(semaphore, 1, device_id=device, device_id_type=pl.DeviceIdType.MESH)

        signal(self.sibling())

        def greet(shift, carry):
            signal(self.peer(shift)[1])
            return carry

        lax.fori_loop(1, self.peers, greet, 0)
        pl.semaphore_wait(semaphore, self.peers)

    def copy(self, source, target, send, recv, device):
        return pltpu.make_async_remote_copy(
            src_ref=source,
            dst_ref=target,
            send_sem=send,
            recv_sem=recv,
            device_id=device,
            device_id_type=pl.DeviceIdType.MESH,
        )

    def each_peer(self, do):
        def one(shift, carry):
            do(shift)
            return carry

        lax.fori_loop(1, self.peers, one, 0)


class LateSum:
    def __init__(self, direct, give, core_s, sum_s, pieces_s, full, core_sems, piece_sems, back_sems):
        self.direct, self.give, self.full = direct, give, full
        self.core_s, self.sum_s, self.pieces_s = core_s, sum_s, pieces_s
        self.core_sems, self.piece_sems, self.back_sems = core_sems, piece_sems, back_sems

    @staticmethod
    def scratch(direct):
        return [
            pltpu.VMEM((direct.half, LANES), BF16),
            pltpu.VMEM((direct.padded, LANES), BF16),
            pltpu.VMEM((direct.peers, direct.piece, LANES), BF16),
            pltpu.VMEM((2, direct.padded, LANES), BF16),
            pltpu.SemaphoreType.DMA((4,)),
            pltpu.SemaphoreType.DMA((2, direct.peers)),
            pltpu.SemaphoreType.DMA((2, direct.peers)),
        ]

    def core_copy(self):
        direct = self.direct
        source = self.give.at[1 - direct.core()]
        sems = self.core_sems
        return direct.copy(source, self.core_s, sems.at[0], sems.at[1], direct.sibling())

    def piece_copy(self, shift):
        other, device = self.direct.peer(shift)
        sems = self.piece_sems
        source = self.sum_s.at[self.direct.rows(other)]
        return self.direct.copy(
            source, self.pieces_s.at[shift], sems.at[0, shift], sems.at[1, shift], device
        )

    def full_copy(self, shift, arriving):
        direct = self.direct
        _, device = direct.peer(shift)
        owner = (direct.me() + direct.peers - shift) % direct.peers if arriving else direct.me()
        place = self.full.at[direct.core(), direct.rows(owner)]
        sems = self.back_sems
        return direct.copy(place, place, sems.at[0, shift], sems.at[1, shift], device)

    def side_copy(self, side):
        direct = self.direct
        place = self.full.at[side]
        sems = self.core_sems
        return direct.copy(place, place, sems.at[2], sems.at[3], direct.sibling())

    def phases(self):
        direct = self.direct

        def to_core():
            self.core_copy().start()

        def to_peers():
            self.core_copy().wait()
            real = direct.half
            own = self.give[direct.core()].astype(F32)
            self.sum_s[:real] = (own + self.core_s[...].astype(F32)).astype(BF16)
            if direct.padded > real:
                self.sum_s[real:] = jnp.zeros_like(self.sum_s[real:])
            direct.each_peer(lambda shift: self.piece_copy(shift).start())

        def from_peers():
            direct.each_peer(lambda shift: self.piece_copy(shift).wait())

            def add(shift, total):
                return total + self.pieces_s[shift].astype(F32)

            mine = direct.rows(direct.me())
            total = lax.fori_loop(1, direct.peers, add, self.sum_s[mine].astype(F32))
            self.full[direct.core(), mine] = total.astype(BF16)
            direct.each_peer(lambda shift: self.full_copy(shift, False).start())

        def arrived(shift):
            self.full_copy(shift, False).wait_send()
            self.full_copy(shift, True).wait_recv()

        def to_side():
            direct.each_peer(arrived)
            self.side_copy(direct.core()).start()

        def done():
            self.side_copy(direct.core()).wait_send()
            self.side_copy(1 - direct.core()).wait_recv()

        return [to_core, to_peers, from_peers, to_side, done]


def tail_kernel(direct, remote, *refs):
    give_ref, own_x, sib_x, mod_ref, lead_ref, gm_ref, dq_ref, dk_ref, dv_ref, w_ref = refs[:10]
    others = refs[10 : 10 + remote]
    grad_ref, got_ref, full_ref, all_ref = refs[10 + remote : 14 + remote]
    sums_s, other_s, got_s, all_s, all_sems, side_sems, grad_sems, local_sem = refs[14 + remote : 22 + remote]
    late = LateSum(direct, give_ref, *refs[22 + remote :])
    step, half = pl.program_id(0), pl.program_id(1)
    width = own_x.shape[2]
    core, me = direct.core(), direct.me()
    phases = late.phases()

    def sums_copy(shift, arriving):
        _, device = direct.peer(shift)
        owner = (me + direct.peers - shift) % direct.peers if arriving else me
        place = all_s.at[core, owner]
        return direct.copy(place, place, all_sems.at[0, shift], all_sems.at[1, shift], device)

    def side_copy(side):
        place = all_s.at[side]
        return direct.copy(place, place, side_sems.at[0], side_sems.at[1], direct.sibling())

    def grad_copy(index):
        return direct.copy(
            other_s.at[index],
            got_s.at[index],
            grad_sems.at[0, index],
            grad_sems.at[1, index],
            direct.sibling(),
        )

    @pl.when((step == 0) & (half == 0))
    def _():
        direct.barrier()
        phases[0]()
        sums_s[...] = jnp.zeros_like(sums_s)

    @pl.when((step == 0) & (half == 1))
    def _():
        phases[1]()

    @pl.when((step == 1) & (half == 1))
    def _():
        phases[2]()

    x = jnp.where(half == 0, own_x[0], sib_x[0]).astype(F32)
    scale = mod_ref[pl.ds(step, 1), width : 2 * width]
    xhat, inverse = normalize(x)
    gy = dot(join_heads(dq_ref, dk_ref, dv_ref), w_ref[...], NT)
    for index in range(remote // 2):
        first, second = others[2 * index], others[2 * index + 1]
        gy = gy + jnp.where(step == 0, first[0], second[0]).astype(F32)
    grad = (gm_ref[0, 0] + norm_back(gy * (1.0 + scale), xhat, inverse)).astype(BF16)

    @pl.when(half == 0)
    def _():
        grad_ref[0] = grad

    @pl.when(half == 1)
    def _():
        other_s[step] = grad
        grad_copy(step).start()

    for kind, value in enumerate((gy, gy * xhat)):
        total = jnp.sum(value, axis=0, keepdims=True)
        for index in range(width // LANES):
            place = pl.ds((kind * 2 + step) * (width // LANES) + index, 1)
            sums_s[place, :] += total[:, index * LANES : (index + 1) * LANES]

    @pl.when((step == 1) & (half == 1))
    def _():
        for index in range(2):
            chosen = lane_index((1, LANES)) == lead_ref[0, first_step(2) + index]
            sums_s[12 + index : 13 + index, :] = jnp.where(chosen, 1.0, 0.0)
        all_s[core, me] = sums_s[...].astype(BF16)
        direct.each_peer(lambda shift: sums_copy(shift, False).start())
        phases[3]()

        def arrived(shift):
            sums_copy(shift, False).wait_send()
            sums_copy(shift, True).wait_recv()

        direct.each_peer(arrived)
        side_copy(core).start()
        for index in range(2):
            grad_copy(index).wait()
        phases[4]()
        side_copy(core).wait_send()
        side_copy(1 - core).wait_recv()
        outs = [(got_s, got_ref), (late.full, full_ref), (all_s, all_ref)]
        copies = [
            pltpu.make_async_copy(source, target, local_sem.at[index])
            for index, (source, target) in enumerate(outs)
        ]
        for copy in copies:
            copy.start()
        for copy in copies:
            copy.wait()


def unstack(at, full_ref, targets, rows):
    row, end = 0, rows * len(targets)
    while row < end:
        group, inside, left = at(row)
        block, place = divmod(row, rows)
        count = min(left, rows - place)
        target, first_row, first_column = targets[block]
        columns = slice(first_column, first_column + full_ref.shape[2])
        value = full_ref[group, inside : inside + count, :].astype(F32)
        target[first_row + place : first_row + place + count, columns] = value
        row += count


def spread_leads(grads, step_of, table_rows):
    count = grads.shape[0]
    part = min(count, 512)
    row = lax.broadcasted_iota(jnp.int32, (part, part), 0)
    column = lane_index((part, part))
    chosen = (row // 16 == column // 16) & (row % 16 == 12 + step_of(column % 16))
    spread = jnp.where(chosen, 1.0, 0.0).astype(BF16)
    leads = [
        dot(grads[start : start + part, :LANES], spread, TN)[:table_rows]
        for start in range(0, count, part)
    ]
    return jnp.concatenate(leads, axis=-1)


def final_kernel(early, direct, late, *refs):
    early_sums, late_sums, emb_ref, ada_ref = refs[:4]
    moved, stacks, outs = refs[4:8], refs[8 : 10 + late], refs[10 + late : 19 + late]
    refs = refs[19 + late :]
    gada_s, gqkv_s, gout_s, gfc1_s, gfc2_s = refs[:5]
    held, (one_ref, two_ref, *late_refs) = refs[5:9], refs[9 : 11 + late]
    load_sems, sems = refs[11 + late :]
    final_out, grad_out, gemb_ref, gada_out, gbada_ref, gqkv_out, gout_out, gfc1_out, gfc2_out = outs
    size = gout_s.shape[0]
    blocks = gfc1_s.shape[1] // size
    copies = []
    loads = [
        pltpu.make_async_copy(source, target, load_sems.at[index])
        for index, (source, target) in enumerate(
            zip([*stacks, *moved], [one_ref, two_ref, *late_refs, *held])
        )
    ]
    for load in loads:
        load.start()

    def start(source, target):
        copy = pltpu.make_async_copy(source, target, sems.at[len(copies)])
        copy.start()
        copies.append(copy)

    def grouped(exchange):
        def at(row):
            group, inside = divmod(row, exchange.real)
            return group, inside, exchange.real - inside

        return at

    def halved(row):
        group, inside = divmod(row, direct.half)
        return group, inside, direct.half - inside

    loads[0].wait()
    unstack(grouped(early[0]), one_ref, [(gfc1_s, 0, block * size) for block in range(blocks)], size)
    start(gfc1_s, gfc1_out)
    rest = [(gfc2_s, block * size, 0) for block in range(blocks)] + [(gout_s, 0, 0)]
    loads[1].wait()
    unstack(grouped(early[1]), two_ref, rest, size)
    start(gfc2_s, gfc2_out)
    start(gout_s, gout_out)
    for pair, late_ref in enumerate(late_refs):
        loads[2 + pair].wait()
        unstack(halved, late_ref, [(gqkv_s, 0, part * size + pair * LANES) for part in range(3)], size)
    start(gqkv_s, gqkv_out)
    mine = first_step(2)
    for index in range(4):
        loads[2 + late + index].wait()
        first = mine if index % 2 == 0 else 2 - mine
        start(held[index], (final_out if index < 2 else grad_out).at[pl.ds(first, 2)])

    table_rows = emb_ref.shape[0]
    table = emb_ref[...].astype(F32)
    gate = jax.nn.sigmoid(table)
    slope = gate * (1.0 + table * (1.0 - gate))
    table_act = (table * gate).astype(BF16)
    total = jnp.zeros((table_rows, size), F32)

    def one_piece(grads, leads, place, first):
        chosen = jnp.where(place, leads, 0.0).astype(BF16)
        acts = dot(table_act, chosen, TN).astype(BF16)
        where = slice(first, first + grads.shape[1])
        gada_s[:, where] = dot(acts, grads)
        by_lead = dot(chosen, grads)
        gbada_ref[where] = jnp.sum(by_lead, axis=0)
        high = by_lead.astype(BF16)
        low = (by_lead - high.astype(F32)).astype(BF16)
        return dot(high, ada_ref[:, where], NT) + dot(low, ada_ref[:, where], NT)

    grads = early_sums[...]
    leads = spread_leads(grads, lambda row: row % 2, table_rows)
    row = lane_index((1, grads.shape[0])) % 16
    for index in range(4):
        total += one_piece(grads, leads, row // 2 == index, (2 + index) * size)
    grads = late_sums[...]
    parts = size // LANES
    leads = spread_leads(grads, lambda row: (row // parts) % 2, table_rows)
    row = lane_index((1, grads.shape[0])) % 16
    for index in range(2):
        for part in range(parts):
            place = (row // (2 * parts) == index) & (row % parts == part)
            total += one_piece(grads, leads, place, index * size + part * LANES)
    gemb_ref[...] = total * slope
    start(gada_s, gada_out)
    for copy in copies:
        copy.wait()


def local(
    mesh_shape, inputs, cotangent, counts, lead_steps, emb_table, w_ada, b_ada, w_qkv, w_out, w_fc1, w_fc2
):
    slots, items, patches, width = inputs.shape
    chips = mesh_shape["seq"] // 2
    blocks = w_fc1.shape[1] // w_fc1.shape[0]
    steps = slots * items // 2
    hidden_width = w_fc1.shape[1]
    pairs = width // LANES
    rows = 2 * patches
    remote = 2 * (chips - 1)
    far_rows = remote * patches
    spot = lax.axis_index("seq")
    core = lax.rem(spot, 2)
    devices = 2 * chips

    def send(values, shift, cross):
        pairs_list = []
        for source in range(devices):
            chip, side = source // 2, source % 2
            pairs_list.append((source, ((chip + shift) % chips) * 2 + (1 - side if cross else side)))
        return lax.ppermute(values, "seq", pairs_list)

    x_steps = inputs.reshape(2, steps, patches, width)
    ct_steps = cotangent.reshape(2, steps, patches, width)
    own_x = lax.dynamic_index_in_dim(x_steps, core, 0, keepdims=False)
    other_x = lax.dynamic_index_in_dim(x_steps, 1 - core, 0, keepdims=False)
    own_ct = lax.dynamic_index_in_dim(ct_steps, core, 0, keepdims=False)
    other_ct = lax.dynamic_index_in_dim(ct_steps, 1 - core, 0, keepdims=False)
    sib_x = send(other_x, 0, True)
    far_x = []
    for step in range(steps):
        some = slice(step, step + 1)
        for shift in range(1, chips):
            far_x.append(send(own_x[some], shift, False))
            far_x.append(send(other_x[some], shift, True))
    sib_ct = send(other_ct, 0, True)

    step_block = pl.BlockSpec((1, patches, width), lambda j, i: (j, 0, 0))
    patch_block = pl.BlockSpec((1, 1, patches, width), lambda j, i: (j, i, 0, 0))

    def head_rows(count):
        return pl.BlockSpec((1, 1, count, LANES), lambda j, p: (j, p, 0, 0))

    def of_step(*shape):
        return pl.BlockSpec((1,) + shape, lambda j, p: (j,) + (0,) * len(shape))

    both_heads = pl.BlockSpec((1, 1, 2, rows, LANES), lambda j, p: (j, p, 0, 0, 0))
    piece = min(256, rows)
    near_work = 4 * steps * pairs * 2 * rows * LANES * rows
    near_heads = jax.ShapeDtypeStruct((steps, pairs, rows, LANES), BF16)
    mod, n1, q, k, v, acc = call(
        functools.partial(near_kernel, piece),
        "near",
        (steps, pairs),
        [scalars(), whole(emb_table.shape), whole(w_ada.shape), whole((1, 6 * width))]
        + [step_block] * 2
        + [whole(w_qkv.shape)],
        [whole((16, 6 * width)), of_step(width, rows)]
        + [of_step(pairs, rows, LANES)] * 3
        + [both_heads],
        [
            jax.ShapeDtypeStruct((16, 6 * width), F32),
            jax.ShapeDtypeStruct((steps, width, rows), BF16),
            near_heads,
            near_heads,
            near_heads,
            jax.ShapeDtypeStruct((steps, pairs, 2, rows, LANES), F32),
        ],
        [pltpu.VMEM((2, rows, LANES), BF16)],
        flops=near_work + 6 * steps * rows * width * width,
        exps=steps * pairs * 2 * rows * rows,
    )(lead_steps, emb_table, w_ada, b_ada.reshape(1, -1), own_x, sib_x, w_qkv)

    def far(step, before):
        some_x = far_x[step * remote : (step + 1) * remote]

        def at_step(*shape):
            return pl.BlockSpec((1,) + shape, lambda p: (step,) + (0,) * len(shape))

        def at_pair(*shape):
            return pl.BlockSpec((1, 1) + shape, lambda p: (step, p) + (0,) * len(shape))

        operands = [*some_x, mod, w_qkv, q, k, v, acc]
        return call(
            functools.partial(far_kernel, piece, step, remote),
            "far",
            (pairs,),
            [whole((1, patches, width))] * remote
            + [whole(mod.shape), whole(w_qkv.shape)]
            + [at_pair(rows, LANES)] * 3
            + [at_pair(2, rows, LANES)]
            + [pl.BlockSpec(memory_space=pl.ANY)] * len(before),
            [at_step(width, far_rows)]
            + [at_step(pairs, far_rows, LANES)] * 2
            + [at_pair(rows, LANES), at_pair(2, rows, LANES)],
            [
                jax.ShapeDtypeStruct((steps, width, far_rows), BF16),
                jax.ShapeDtypeStruct((steps, pairs, far_rows, LANES), BF16),
                jax.ShapeDtypeStruct((steps, pairs, far_rows, LANES), BF16),
                jax.ShapeDtypeStruct((steps, pairs, rows, LANES), F32),
                jax.ShapeDtypeStruct((steps, pairs, 2, rows, LANES), BF16),
            ],
            [pltpu.VMEM((2, far_rows, LANES), BF16), pltpu.VMEM((rows, LANES), F32)],
            flops=near_work // 2,
            exps=pairs * 2 * rows * far_rows,
            aliases={len(operands) + index: index for index in range(len(before))},
        )(*operands, *before)

    far_results = []
    for step in range(steps):
        far_results = far(step, far_results)
    n1r, kr, vr, o, qe = far_results

    block_rows = min(256, patches)
    outs = call(
        functools.partial(patch_kernel, block_rows, hidden_width),
        "patchwise",
        (steps, 2),
        [scalars()] * 2
        + [step_block] * 4
        + [
            whole(mod.shape),
            pl.BlockSpec((1, pairs, patches, LANES), lambda j, i: (j, 0, i, 0)),
            whole(w_out.shape),
            whole(w_fc1.shape),
            whole(w_fc2.shape),
        ],
        [
            step_block,
            step_block,
            patch_block,
            pl.BlockSpec((1, pairs, 2, patches, LANES), lambda j, i: (j, 0, 0, i, 0)),
            whole((16, width)),
            whole((blocks, width, width)),
            whole((blocks + 1, width, width)),
        ],
        [
            jax.ShapeDtypeStruct((steps, patches, width), BF16),
            jax.ShapeDtypeStruct((steps, patches, width), BF16),
            jax.ShapeDtypeStruct((steps, 2, patches, width), F32),
            jax.ShapeDtypeStruct((steps, pairs, 2, rows, LANES), BF16),
            jax.ShapeDtypeStruct((16, width), BF16),
            jax.ShapeDtypeStruct((blocks, width, width), BF16),
            jax.ShapeDtypeStruct((blocks + 1, width, width), BF16),
        ],
        [pltpu.VMEM((patches, hidden_width), BF16)] * 2
        + [pltpu.VMEM((patches, width), BF16)] * 4
        + [
            pltpu.VMEM((width, width), F32),
            pltpu.VMEM((width, hidden_width), F32),
            pltpu.VMEM((width, hidden_width), F32),
            pltpu.VMEM((16, width), F32),
        ],
        flops=6 * steps * rows * width * (2 * hidden_width + width),
        moved=steps * rows * width * 20,
        exps=2 * steps * rows * hidden_width,
    )(counts, lead_steps, own_x, sib_x, own_ct, sib_ct, mod, o, w_out, w_fc1, w_fc2)
    final_own, final_sib, gm, ge, sums, stack_one, stack_two = outs
    final_got = send(final_sib, 0, True)
    early = [Exchange(mesh_shape, blocks * width // 16, 0), Exchange(mesh_shape, (blocks + 1) * width // 16, 1)]
    gives = [g.reshape(e.groups, e.real, width) for e, g in zip(early, (stack_one, stack_two))]

    grad_block = pl.BlockSpec((1, pairs, patches, LANES), lambda j, i: (j, 0, i, 0))
    hbm = pl.BlockSpec(memory_space=pl.ANY)
    direct = Direct(mesh_shape, 3 * width // 16)
    every = (mesh_shape["dp"] * mesh_shape["seq"], 16, width)
    shard_shapes = [(exchange.shard, width) for exchange in early]
    scratch = [
        pltpu.VMEM((2 * pairs, far_rows, LANES), BF16),
        pltpu.VMEM((far_rows, width), BF16),
        pltpu.VMEM((chips - 1, rows, width), BF16),
        pltpu.VMEM(every, BF16),
        pltpu.SemaphoreType.DMA((2, chips - 1)),
        pltpu.SemaphoreType.DMA((early[0].all_levels,)),
        pltpu.SemaphoreType.DMA((early[0].all_levels,)),
        pltpu.SemaphoreType.DMA,
    ]
    for exchange in early:
        scratch += [pltpu.VMEM((exchange.groups // 2, exchange.padded, width), BF16)]
        scratch += [pltpu.SemaphoreType.DMA((exchange.all_levels,))] * 2
        scratch += exchange.receive_scratch(width)
    dq_turned = pl.BlockSpec((1, 1, LANES, rows), lambda j, p: (j, p, 0, 0))
    dq_part, gw_part, early_all, dx_first, dx_second, *shards = call(
        functools.partial(
            back_far_kernel, min(512, far_rows), early, direct, chips, (steps, pairs)
        ),
        "back_far",
        (steps, pairs),
        [both_heads] * 2
        + [head_rows(far_rows)] * 2
        + [of_step(width, far_rows), whole(w_qkv.shape), whole(sums.shape)]
        + [whole(give.shape) for give in gives],
        [dq_turned, whole((width, 2 * width)), whole(every), hbm, whole((far_rows, width))]
        + [whole(shape) for shape in shard_shapes],
        [
            jax.ShapeDtypeStruct((steps, pairs, LANES, rows), F32),
            jax.ShapeDtypeStruct((width, 2 * width), F32),
            jax.ShapeDtypeStruct(every, BF16),
            jax.ShapeDtypeStruct((chips - 1, rows, width), BF16),
            jax.ShapeDtypeStruct((far_rows, width), BF16),
        ]
        + [jax.ShapeDtypeStruct(shape, BF16) for shape in shard_shapes],
        scratch,
        flops=10 * steps * pairs * 2 * rows * far_rows * LANES,
        exps=steps * pairs * 2 * rows * far_rows,
        collective=1,
    )(qe, ge, kr, vr, n1r, w_qkv, sums, *gives)
    others = []
    for shift in range(1, chips):
        second = send(dx_second[(shift - 1) * rows : shift * rows], -shift, False)
        others += [dx_first[shift - 1].reshape(2, patches, width), second.reshape(2, patches, width)]

    def turned(*shape):
        return pl.BlockSpec((1, 1) + shape, lambda p, j: (j, p) + (0,) * len(shape))

    late = pairs - 1
    late_shape = (2, direct.padded, LANES)
    give_shape = (2, direct.half, LANES)
    full_shapes = [(e.groups, e.padded, width) for e in early]
    scratch = [
        pltpu.VMEM((LANES, rows), F32),
        pltpu.VMEM((width, 3 * LANES), F32),
        pltpu.SemaphoreType.DMA((late + 2,)),
    ]
    for exchange, shape in zip(early, full_shapes):
        scratch += [pltpu.VMEM(shape, BF16)]
        scratch += [pltpu.SemaphoreType.DMA((exchange.levels,))] * 2
    for _ in range(late):
        scratch += [pltpu.VMEM(give_shape, BF16)] + LateSum.scratch(direct)
    results = call(
        functools.partial(back_near_kernel, min(512, rows), early, direct, (pairs, steps)),
        "back_near",
        (pairs, steps),
        [turned(2, rows, LANES)] * 2
        + [turned(rows, LANES)] * 2
        + [turned(LANES, rows), pl.BlockSpec((1, width, rows), lambda p, j: (j, 0, 0))]
        + [whole(gw_part.shape)]
        + [whole(shape) for shape in shard_shapes],
        [turned(rows, LANES)] * 3 + [whole(give_shape)] + [hbm] * (2 + late),
        [jax.ShapeDtypeStruct((steps, pairs, rows, LANES), BF16)] * 3
        + [jax.ShapeDtypeStruct(give_shape, BF16)]
        + [jax.ShapeDtypeStruct(shape, BF16) for shape in full_shapes + [late_shape] * late],
        scratch,
        flops=10 * steps * pairs * 2 * rows * rows * LANES,
        exps=steps * pairs * 2 * rows * rows,
        collective=2,
    )(qe, ge, k, v, dq_part, n1, gw_part, *shards)
    dq, dk, dv, give_last = results[:4]
    early_sums, late_sums = results[4:6], results[6:]

    late_all_shape = (2, direct.peers, 16, LANES)
    half_block = pl.BlockSpec((1, patches, width), lambda j, i: (i, 0, 0))
    grad_own, grad_got, late_last, late_all = call(
        functools.partial(tail_kernel, direct, len(others)),
        "tail",
        (steps, 2),
        [whole(give_shape), step_block, step_block, whole(mod.shape), scalars()]
        + [patch_block]
        + [grad_block] * 3
        + [whole(w_qkv.shape)]
        + [half_block] * len(others),
        [step_block, hbm, hbm, hbm],
        [
            jax.ShapeDtypeStruct((steps, patches, width), BF16),
            jax.ShapeDtypeStruct((steps, patches, width), BF16),
            jax.ShapeDtypeStruct(late_shape, BF16),
            jax.ShapeDtypeStruct(late_all_shape, BF16),
        ],
        [
            pltpu.VMEM((16, LANES), F32),
            pltpu.VMEM((steps, patches, width), BF16),
            pltpu.VMEM((steps, patches, width), BF16),
            pltpu.VMEM(late_all_shape, BF16),
            pltpu.SemaphoreType.DMA((2, direct.peers)),
            pltpu.SemaphoreType.DMA((2,)),
            pltpu.SemaphoreType.DMA((2, steps)),
            pltpu.SemaphoreType.DMA((3,)),
        ]
        + LateSum.scratch(direct),
        flops=2 * steps * rows * width * 3 * width,
        collective=3,
    )(give_last, own_x, sib_x, mod, lead_steps, gm, dq, dk, dv, w_qkv, *others)

    early_all = early_all.reshape(-1, width)
    late_all = late_all.reshape(-1, LANES)
    small = [early_all, late_all, emb_table, w_ada]
    moved = [final_own, final_got, grad_own, grad_got]
    stacks = [*early_sums, *late_sums, late_last]
    large = moved + stacks
    out_shapes = [(slots * items, patches, width)] * 2 + [emb_table.shape, w_ada.shape]
    out_shapes += [b_ada.shape, w_qkv.shape, w_out.shape, w_fc1.shape, w_fc2.shape]
    outs = call(
        functools.partial(final_kernel, early, direct, pairs),
        "final",
        (),
        [whole(value.shape) for value in small] + [hbm] * len(large),
        [hbm] * 2 + [whole(emb_table.shape), hbm, whole(b_ada.shape)] + [hbm] * 4,
        [
            jax.ShapeDtypeStruct(shape, BF16 if index < 2 else F32)
            for index, shape in enumerate(out_shapes)
        ],
        [pltpu.VMEM(w.shape, F32) for w in (w_ada, w_qkv, w_out, w_fc1, w_fc2)]
        + [pltpu.VMEM(value.shape, BF16) for value in large]
        + [pltpu.SemaphoreType.DMA((len(large),)), pltpu.SemaphoreType.DMA((4 + 5,))],
        flops=2 * early_all.shape[0] * width * 6 * width,
        moved=6 * w_ada.size,
    )(*small, *large)
    outputs, grad_inputs, g_emb, g_ada, g_bada, g_qkv, g_out, g_fc1, g_fc2 = outs
    return (
        outputs.reshape(inputs.shape),
        grad_inputs.reshape(inputs.shape),
        g_emb,
        g_ada,
        g_bada,
        g_qkv,
        g_out,
        g_fc1,
        g_fc2,
    )


def solution(mesh):
    tokens = P(None, "dp", "seq", None)
    return jax.shard_map(
        functools.partial(local, dict(mesh.shape)),
        mesh=mesh,
        in_specs=(tokens, tokens, P("dp"), P("dp", None)) + (P(),) * 7,
        out_specs=(tokens, tokens) + (P(),) * 7,
        check_vma=False,
    )
```

```python
import functools

import jax
import jax.numpy as jnp
from jax import lax
from jax.experimental import pallas as pl
from jax.experimental.pallas import tpu as pltpu
from jax.sharding import PartitionSpec as P

HD = 64
LANES = 128
EPSILON = 1e-06
LOG2E = 1.4426950408889634
NN = (((1,), (0,)), ((), ()))
NT = (((1,), (1,)), ((), ()))
TN = (((0,), (0,)), ((), ()))
F32 = jnp.float32
BF16 = jnp.bfloat16
VMEM_BYTES = 56 * 1024 * 1024


def dot(a, b, dims=NN):
    return lax.dot_general(a, b, dims, preferred_element_type=F32)


def call(
    body,
    name,
    grid,
    in_specs,
    out_specs,
    out_shape,
    scratch=(),
    flops=0,
    moved=0,
    exps=0,
    collective=None,
    aliases=None,
):
    return pl.pallas_call(
        body,
        name=name,
        grid=grid,
        in_specs=in_specs,
        out_specs=out_specs,
        out_shape=out_shape,
        scratch_shapes=list(scratch),
        input_output_aliases=aliases or {},
        cost_estimate=pl.CostEstimate(flops=flops, bytes_accessed=moved, transcendentals=exps),
        compiler_params=pltpu.CompilerParams(
            vmem_limit_bytes=VMEM_BYTES,
            collective_id=collective,
            has_side_effects=collective is not None,
        ),
    )


def whole(shape):
    return pl.BlockSpec(shape, lambda *_: (0,) * len(shape))


def scalars():
    return pl.BlockSpec(memory_space=pltpu.SMEM)


def lane_index(shape):
    return lax.broadcasted_iota(jnp.int32, shape, 1)


def first_step(steps):
    return lax.rem(lax.axis_index("seq"), 2) * steps


def normalize(values):
    center = values - jnp.mean(values, axis=-1, keepdims=True)
    spread = jnp.mean(center * center, axis=-1, keepdims=True)
    inverse = lax.rsqrt(spread + EPSILON)
    return center * inverse, inverse


def norm_back(grad, xhat, inverse):
    first = jnp.mean(grad, axis=-1, keepdims=True)
    second = jnp.mean(grad * xhat, axis=-1, keepdims=True)
    return inverse * (grad - first - xhat * second)


def pick(refs, which):
    value = refs[0][0]
    for index in range(1, len(refs)):
        value = jnp.where(which == index, refs[index][0], value)
    return value


class Exchange:
    def __init__(self, mesh_shape, row_tiles, turn=0):
        bits = {"seq": [], "dp": []}
        for axis in bits:
            bit = 1
            while bit < mesh_shape[axis]:
                bits[axis].append((axis, bit))
                bit *= 2
        turned = bits["dp"][turn:] + bits["dp"][:turn]
        self.bits = bits["seq"][:1] + turned + bits["seq"][1:]
        self.all_levels = len(self.bits)
        self.levels = 1 + len(turned)
        self.even = 0
        while self.even < self.levels and row_tiles % 2 == 0:
            row_tiles //= 2
            self.even += 1
        unit = 2 ** (self.levels - self.even)
        self.groups = 2**self.even
        self.real = row_tiles * 16
        self.padded = -(-row_tiles // unit) * unit * 16
        self.shard = self.padded // unit

    def sizes(self, level):
        if level < self.even:
            return (self.groups >> (level + 1), self.real)
        return (1, self.padded >> (level - self.even + 1))

    def receive_scratch(self, width):
        last = self.levels - 1
        return [
            pltpu.VMEM(self.sizes(min(level, last)) + (width,), BF16)
            for level in range(self.all_levels)
        ]

    def place(self, level):
        axis, bit = self.bits[level]
        here = lax.axis_index(axis)
        value = (here // bit) % 2
        return value, {axis: here + bit * (1 - 2 * value)}

    def spot(self, level, first, flip):
        group, row = 0, 0
        for index in range(first, level + 1):
            value, _ = self.place(index)
            if flip and index == level:
                value = 1 - value
            if index < self.even:
                group = group + value * (self.groups >> (index + 1))
            else:
                row = row + value * (self.padded >> (index - self.even + 1))
        if level >= self.even:
            row = pl.multiple_of(row, 16)
        count, rows = self.sizes(level)
        return pl.ds(group, count), pl.ds(row, rows)

    def barrier(self):
        semaphore = pltpu.get_barrier_semaphore()
        for level in range(self.all_levels):
            _, partner = self.place(level)
            pl.semaphore_signal(
                semaphore, inc=1, device_id=partner, device_id_type=pl.DeviceIdType.MESH
            )
        pl.semaphore_wait(semaphore, self.all_levels)

    def copy(self, source, target, sends, recvs, level):
        _, partner = self.place(level)
        return pltpu.make_async_remote_copy(
            src_ref=source,
            dst_ref=target,
            send_sem=sends.at[level],
            recv_sem=recvs.at[level],
            device_id=partner,
            device_id_type=pl.DeviceIdType.MESH,
        )

    def reduce_copy(self, level, start_ref, acc_ref, got, sends, recvs):
        if level >= self.levels:
            return self.copy(self.own_shard(acc_ref, 1), got[level], sends, recvs, level)
        groups, rows = self.spot(level, min(level, 1), True)
        source = start_ref if level == 0 else acc_ref
        return self.copy(source.at[groups, rows], got[level], sends, recvs, level)

    def reduce_start(self, level, *refs):
        self.reduce_copy(level, *refs).start()

    def reduce_finish(self, level, start_ref, acc_ref, got, sends, recvs):
        self.reduce_copy(level, start_ref, acc_ref, got, sends, recvs).wait()
        if level >= self.levels:
            own = self.own_shard(acc_ref, 1)
            own[...] = (own[...].astype(F32) + got[level][...].astype(F32)).astype(BF16)
            return
        count, rows = self.sizes(level)
        groups, spots = self.spot(level, min(level, 1), False)
        if level == 0:
            target_groups, target_rows = pl.ds(0, count), pl.ds(0, rows)
            if self.padded > self.real:
                acc_ref[:, self.real :, :] = jnp.zeros_like(acc_ref[:, self.real :, :])
        else:
            target_groups, target_rows = groups, spots
        source = start_ref if level == 0 else acc_ref

        def add(index, carry):
            one = pl.ds(groups.start + index, 1)
            to = pl.ds(target_groups.start + index, 1)
            value = source[one, spots, :].astype(F32) + got[level][pl.ds(index, 1)].astype(F32)
            acc_ref[to, target_rows, :] = value.astype(BF16)
            return carry

        lax.fori_loop(0, count, add, 0)

    def own_shard(self, ref, first):
        if self.levels > self.even:
            return ref.at[self.spot(self.levels - 1, first, False)]
        groups, _ = self.spot(self.levels - 1, first, False)
        return ref.at[groups, pl.ds(0, self.shard)]

    def gather_copy(self, level, full_ref, sends, recvs):
        piece = full_ref.at[self.spot(level, 0, False)]
        return self.copy(piece, piece, sends, recvs, level)

    def gather_start(self, level, *refs):
        self.gather_copy(level, *refs).start()

    def gather_finish(self, level, *refs):
        self.gather_copy(level, *refs).wait()


def modulation(lead_ref, emb_ref, ada_ref, bias_ref):
    shape = (16, emb_ref.shape[0])
    rows = lax.broadcasted_iota(jnp.int32, shape, 0)
    columns = lane_index(shape)
    onehot = jnp.zeros(shape, F32)
    for step in range(2):
        lead = lead_ref[0, first_step(2) + step]
        onehot = jnp.where((rows == step) & (columns == lead), 1.0, onehot)
    condition = dot(onehot.astype(BF16), emb_ref[...])
    active = (condition * jax.nn.sigmoid(condition)).astype(BF16)
    return dot(active, ada_ref[...]) + bias_ref[...].astype(F32)


def project(x_refs, mod_ref, step, w_ref, normed_ref, head_refs):
    width = w_ref.shape[0]
    patches = x_refs[0].shape[1]
    rows = min(256, patches)
    shift = mod_ref[pl.ds(step, 1), 0:width]
    scale = mod_ref[pl.ds(step, 1), width : 2 * width]
    queries = len(head_refs) == 3
    for index, x_ref in enumerate(x_refs):

        def block(count, carry):
            start = pl.multiple_of(count * rows, rows)
            at = pl.ds(pl.multiple_of(index * patches + start, rows), rows)
            xhat, _ = normalize(x_ref[0, pl.ds(start, rows), :].astype(F32))
            normed = (xhat * (1.0 + scale) + shift).astype(BF16)
            normed_ref[0, at, :] = normed
            for part, head_ref in enumerate(head_refs):
                first = (part + (0 if queries else 1)) * width
                projected = dot(normed, w_ref[:, first : first + width])
                if queries and part == 0:
                    projected = projected.astype(BF16).astype(F32) * HD**-0.5
                projected = projected.astype(BF16)
                for pair in range(width // LANES):
                    head_ref[0, pair, at, :] = projected[:, pair * LANES : (pair + 1) * LANES]
            return carry

        lax.fori_loop(0, patches // rows, block, 0)


def with_ones(values):
    low = lane_index(values.shape) < HD
    one = jnp.ones_like(values)
    return jnp.where(low, values, one), jnp.where(low, one, values)


def exponentials(query, keys_ref, pair, width=256):
    count = keys_ref.shape[2]
    width = min(width, count)
    return jnp.concatenate(
        [
            jnp.exp(dot(query, keys_ref[0, pair, start : start + width, :], NT)).astype(BF16)
            for start in range(0, count, width)
        ],
        axis=-1,
    )


def masked(values):
    low = lane_index(values.shape) < HD
    zero = jnp.zeros_like(values)
    return jnp.where(low, values, zero), jnp.where(low, zero, values)


def near_kernel(rows, *refs):
    lead_ref, emb_ref, ada_ref, bias_ref, own_x, sib_x, w_ref = refs[:7]
    mod_ref, normed_ref, q_ref, k_ref, v_ref, acc_ref, ext_ref = refs[7:]
    step, pair = pl.program_id(0), pl.program_id(1)

    @pl.when((step == 0) & (pair == 0))
    def _():
        mod_ref[...] = modulation(lead_ref, emb_ref, ada_ref, bias_ref)

    @pl.when(pair == 0)
    def _():
        project([own_x, sib_x], mod_ref, step, w_ref, normed_ref, [q_ref, k_ref, v_ref])

    ext_ref[0], ext_ref[1] = with_ones(v_ref[0, pair])
    for start in range(0, q_ref.shape[2], rows):
        at = slice(start, start + rows)
        for head, query in enumerate(masked(q_ref[0, pair, at, :])):
            acc_ref[0, 0, head, at, :] = dot(exponentials(query, k_ref, pair), ext_ref[head])


def far_kernel(rows, step, sources, *refs):
    x_refs, refs = refs[:sources], refs[sources:]
    mod_ref, w_ref, q_ref, k_ref, v_ref, acc_ref = refs[:6]
    normed_ref, kr_ref, vr_ref, o_ref, qe_ref, ext_ref, total_ref = refs[-7:]
    pair = pl.program_id(0)

    @pl.when(pair == 0)
    def _():
        project(x_refs, mod_ref, step, w_ref, normed_ref, [kr_ref, vr_ref])

    ext_ref[0], ext_ref[1] = with_ones(vr_ref[0, pair])
    def finish(at, query, first, second, top_first, top_second):
        lane = lane_index(query.shape)
        low = lane < HD
        swapped = jnp.where(low, second, first)
        total = pltpu.roll(swapped, HD, 1)
        o_ref[0, 0, at, :] = jnp.where(low, first, second) / total
        log_total = jnp.log(swapped) + jnp.where(low, top_second, top_first)
        high = log_total.astype(BF16).astype(F32)
        middle = (log_total - high).astype(BF16).astype(F32)
        rest = log_total - high - middle
        spot = lane % HD
        extra = jnp.where(spot == 0, -high, jnp.where(spot == 1, -middle, -rest))
        extra = jnp.where(spot < 3, extra, 0.0).astype(BF16)
        qe_ref[0, 0, 0, at, :] = jnp.where(low, query, extra)
        qe_ref[0, 0, 1, at, :] = jnp.where(low, extra, query)
        return total

    def block(index, carry):
        at = pl.ds(pl.multiple_of(index * rows, rows), rows)
        query = q_ref[0, 0, at, :]
        sums = []
        for head, own in enumerate(masked(query)):
            more = dot(exponentials(own, kr_ref, pair), ext_ref[head])
            sums.append(acc_ref[0, 0, head, at, :] + more)
        total_ref[at, :] = finish(at, query, sums[0], sums[1], 0.0, 0.0)
        return carry

    lax.fori_loop(0, q_ref.shape[2] // rows, block, 0, unroll=2)
    total = total_ref[...]
    bad = jnp.sum(jnp.where((total > 1e-25) & (total < 1e25), 0.0, 1.0))

    @pl.when(bad > 0.0)
    def _():
        own_ext = with_ones(v_ref[0, 0])

        again_rows = min(64, q_ref.shape[2])

        def again(index, carry):
            at = pl.ds(pl.multiple_of(index * again_rows, again_rows), again_rows)
            query = q_ref[0, 0, at, :]
            sums, tops = [], []
            for head, own in enumerate(masked(query)):
                scores = dot(own, k_ref[0, 0], NT)
                others = dot(own, kr_ref[0, pair], NT)
                top = jnp.maximum(
                    jnp.max(scores, axis=-1, keepdims=True),
                    jnp.max(others, axis=-1, keepdims=True),
                )
                sums.append(
                    dot(jnp.exp(scores - top).astype(BF16), own_ext[head])
                    + dot(jnp.exp(others - top).astype(BF16), ext_ref[head])
                )
                tops.append(top)
            finish(at, query, sums[0], sums[1], tops[0], tops[1])
            return carry

        lax.fori_loop(0, q_ref.shape[2] // again_rows, again, 0)


def gelu_parts(values):
    base = 1.0 + jnp.abs(values) * (0.3275911 * 0.7071067811865476)
    t = pl.reciprocal(base, approx=True)
    t = t * (2.0 - base * t)
    t = t * (2.0 - base * t)
    bell = jnp.exp2(values * values * (-0.5 * LOG2E))
    series = 0.5 * 1.061405429
    for coefficient in (-1.453152027, 1.421413741, -0.284496736, 0.254829592):
        series = series * t + 0.5 * coefficient
    tail = series * t * bell
    cumulative = jnp.where(values < 0.0, tail, 1.0 - tail)
    return values * cumulative, cumulative + values * bell * 0.3989422804014327


def patch_kernel(
    rows,
    chunk,
    counts_ref,
    lead_ref,
    own_x,
    sib_x,
    own_ct,
    sib_ct,
    mod_ref,
    o_ref,
    out_w,
    fc1_w,
    fc2_w,
    final_own,
    final_sib,
    gm_ref,
    ge_ref,
    sums_ref,
    stack_one,
    stack_two,
    hidden_s,
    gpre_s,
    n2_s,
    g2_s,
    g1_s,
    mixed_s,
    gout_s,
    gfc1_s,
    gfc2_s,
    sums_s,
):
    step, half = pl.program_id(0), pl.program_id(1)
    width, hidden_width = fc1_w.shape
    patches = own_x.shape[1]
    slot = first_step(pl.num_programs(0)) + step
    active = (slot < counts_ref[0]).astype(F32)

    def piece(index):
        return mod_ref[pl.ds(step, 1), index * width : (index + 1) * width]

    gate1, shift2, scale2, gate2 = piece(2), piece(3), piece(4), piece(5)

    @pl.when((step == 0) & (half == 0))
    def _():
        sums_s[...] = jnp.zeros_like(sums_s)
        gout_s[...] = jnp.zeros_like(gout_s)
        gfc1_s[...] = jnp.zeros_like(gfc1_s)
        gfc2_s[...] = jnp.zeros_like(gfc2_s)

    def block(index, carry):
        at = pl.ds(pl.multiple_of(index * rows, rows), rows)
        x = jnp.where(half == 0, own_x[0, at, :], sib_x[0, at, :]).astype(F32)
        final_grad = jnp.where(half == 0, own_ct[0, at, :], sib_ct[0, at, :]).astype(F32) * active
        outs = [o_ref[0, pair, at, :] for pair in range(width // LANES)]
        mixed = jnp.concatenate([o.astype(BF16) for o in outs], axis=-1)
        mixed_s[at, :] = mixed
        branch_one = dot(mixed, out_w[...])
        middle = x + gate1 * branch_one
        xhat, inverse = normalize(middle)
        n2 = (xhat * (1.0 + scale2) + shift2).astype(BF16)
        n2_s[at, :] = n2
        g2 = (gate2 * final_grad).astype(BF16)
        g2_s[at, :] = g2
        branch_two = jnp.zeros((rows, width), F32)
        gy = jnp.zeros((rows, width), F32)
        for start in range(0, hidden_width, chunk):
            columns = slice(start, start + chunk)
            pre = dot(n2, fc1_w[:, columns])
            grad_hidden = dot(g2, fc2_w[columns, :], NT)
            hidden, slope = gelu_parts(pre)
            hidden = hidden.astype(BF16)
            grad_pre = (slope * grad_hidden).astype(BF16)
            hidden_s[at, columns] = hidden
            gpre_s[at, columns] = grad_pre
            branch_two += dot(hidden, fc2_w[columns, :])
            gy += dot(grad_pre, fc1_w[:, columns], NT)
        final = ((middle + gate2 * branch_two) * active).astype(BF16)

        @pl.when(half == 0)
        def _():
            final_own[0, at, :] = final

        @pl.when(half == 1)
        def _():
            final_sib[0, at, :] = final

        gm = final_grad + norm_back(gy * (1.0 + scale2), xhat, inverse)
        gm_ref[0, 0, at, :] = gm
        g1 = (gate1 * gm).astype(BF16)
        g1_s[at, :] = g1
        sums = [branch_one * gm, gy, gy * xhat, branch_two * final_grad]
        for row, value in enumerate(sums):
            place = pl.ds(2 * row + step, 1)
            sums_s[place, :] += jnp.sum(value, axis=0, keepdims=True)
        grad_mixed = dot(g1, out_w[...], NT).astype(BF16)
        lane = lane_index((rows, LANES))
        low = lane < HD
        spot = lane % HD
        for pair, o in enumerate(outs):
            grad = grad_mixed[:, pair * LANES : (pair + 1) * LANES]
            product = grad.astype(F32) * o
            first = jnp.sum(jnp.where(low, product, 0.0), axis=-1, keepdims=True)
            second = jnp.sum(jnp.where(low, 0.0, product), axis=-1, keepdims=True)
            inner = jnp.where(low, second, first)
            high = inner.astype(BF16).astype(F32)
            mid = (inner - high).astype(BF16).astype(F32)
            extra = jnp.where(spot == 0, -high, jnp.where(spot == 1, -mid, high + mid - inner))
            extra = jnp.where(spot < 3, extra, 0.0).astype(BF16)
            ge_ref[0, pair, 0, at, :] = jnp.where(low, grad, extra)
            ge_ref[0, pair, 1, at, :] = jnp.where(low, extra, grad)
        return carry

    lax.fori_loop(0, patches // rows, block, 0)
    gout_s[...] += dot(mixed_s[...], g1_s[...], TN)
    gfc1_s[...] += dot(n2_s[...], gpre_s[...], TN)
    gfc2_s[...] += dot(g2_s[...], hidden_s[...], TN)

    @pl.when((step == pl.num_programs(0) - 1) & (half == pl.num_programs(1) - 1))
    def _():
        for index in range(2):
            lead = lead_ref[0, first_step(2) + index]
            sums_s[12 + index : 13 + index, :] = jnp.where(lane_index((1, width)) == lead, 1.0, 0.0)
        sums_ref[...] = sums_s[...].astype(BF16)
        blocks = hidden_width // width
        for index in range(blocks):
            columns = slice(index * width, (index + 1) * width)
            stack_one[index] = gfc1_s[:, columns].astype(BF16)
            stack_two[index] = gfc2_s[:, columns].T.astype(BF16)
        stack_two[blocks] = gout_s[...].astype(BF16)


def attend_back_kernel(rows, first_pass, exchanges, grid_steps, *refs):
    count = len(exchanges)
    qe_ref, ge_ref, k_ref, v_ref = refs[:4]
    refs = refs[4:]
    if first_pass:
        gives, sums_ref, refs = refs[:count], refs[count], refs[count + 1 :]
        dq_ref, dk_ref, dv_ref = refs[:3]
        shards, all_ref, refs = refs[3 : 3 + count], refs[3 + count], refs[4 + count :]
        all_s, all_sends, all_recvs = refs[-3:]
    else:
        dq_in, shards, refs = refs[0], refs[1 : 1 + count], refs[1 + count :]
        dq_ref, dk_ref, dv_ref = refs[:3]
        fulls, refs = refs[3 : 3 + count], refs[3 + count :]
    dq_s, refs = refs[0], refs[1:]
    states = []
    for index, exchange in enumerate(exchanges):
        sends, recvs = refs[1], refs[2]
        if first_pass:
            got = refs[3 : 3 + exchange.all_levels]
            states.append((gives[index], refs[0], got, sends, recvs))
            refs = refs[3 + exchange.all_levels :]
        else:
            states.append((refs[0], sends, recvs))
            refs = refs[3:]
    per_step = k_ref.shape[2] // rows
    static_slots = grid_steps * per_step
    first_slot = (pl.program_id(0) * pl.num_programs(1) + pl.program_id(1)) * per_step
    levels = exchanges[0].all_levels if first_pass else exchanges[0].levels

    def all_copy(level):
        index = 0
        for lower in range(len(exchanges[0].bits)):
            index = index + exchanges[0].place(lower)[0] * (1 << lower)
        if level < 0:
            return all_s.at[pl.ds(index, 1)]
        size = 1 << level
        piece = all_s.at[pl.ds((index // size) * size, size)]
        return exchanges[0].copy(piece, piece, all_sends, all_recvs, level)

    def reduce_action(order):
        if order == 0:
            exchanges[0].barrier()
            own = all_copy(-1)
            own[...] = sums_ref[...][None]
        else:
            all_copy(order - 1).wait()
        if order < levels:
            all_copy(order).start()
        else:
            all_ref[...] = all_s[...]
        for exchange, state, shard in zip(exchanges, states, shards):
            if order > 0:
                exchange.reduce_finish(order - 1, *state)
            if order < levels:
                exchange.reduce_start(order, *state)
            else:
                shard[...] = exchange.own_shard(state[1], 1)[...][0]

    def gather_action(order):
        if order == 0:
            exchanges[0].barrier()
        for exchange, state, shard in zip(exchanges, states, shards):
            if order == 0:
                exchange.own_shard(state[0], 0)[...] = shard[...][None]
            else:
                exchange.gather_finish(levels - order, *state)
            if order < levels:
                exchange.gather_start(levels - 1 - order, *state)
        if order == levels:
            copies = [
                pltpu.make_async_copy(state[0], full, refs[index])
                for index, (state, full) in enumerate(zip(states, fulls))
            ]
            for copy in copies:
                copy.start()
            for copy in copies:
                copy.wait()

    action = reduce_action if first_pass else gather_action
    weights = [5.0, 10.0, 9.0, 6.0] + [4.0] * levels
    weights = weights[:levels] if first_pass else weights[:levels][::-1]
    marks, total = [0], 0.0
    for weight in weights:
        total += weight
        marks.append(total)
    last = static_slots - (2 if first_pass else 1)
    marks = [min(int(mark * last / total + 0.5), last) for mark in marks]

    dq_s[...] = jnp.zeros_like(dq_s) if first_pass else dq_in[0, 0].T

    def block(index, carry):
        for order, mark in enumerate(marks[:-1]):
            pl.when(first_slot + index == mark)(functools.partial(action, order))
        at = pl.ds(pl.multiple_of(index * rows, rows), rows)
        keys = k_ref[0, 0, at, :]
        values = v_ref[0, 0, at, :]
        lane = lane_index(keys.shape)
        low = lane < HD
        ones = jnp.where(lane % HD < 3, 1.0, 0.0).astype(BF16)
        zero = jnp.zeros_like(keys)
        grads = []
        for head in range(2):
            own = low if head == 0 else jnp.logical_not(low)
            query = qe_ref[0, 0, head]
            grad = ge_ref[0, 0, head]
            probs = jnp.exp(dot(jnp.where(own, keys, ones), query, NT))
            grad_probs = dot(jnp.where(own, values, ones), grad, NT)
            grad_scores = (probs * grad_probs).astype(BF16)
            grads.append((dot(grad_scores, query), dot(probs.astype(BF16), grad)))
            dq_s[...] += dot(jnp.where(own, keys, zero), grad_scores, TN)
        dk_ref[0, 0, at, :] = jnp.where(low, grads[0][0], grads[1][0]).astype(BF16)
        dv_ref[0, 0, at, :] = jnp.where(low, grads[0][1], grads[1][1]).astype(BF16)
        return carry

    lax.fori_loop(0, per_step, block, 0)
    if first_pass:
        dq_ref[0, 0] = dq_s[...].T
    else:
        dq_ref[0, 0] = (dq_s[...].T * HD**-0.5).astype(BF16)
    pl.when(first_slot + per_step == static_slots)(functools.partial(action, levels))


def joining(at, read, write, wait, own_ref, got_ref, out_ref, own_s, got_s, sems):
    mine = first_step(2)
    reads = [
        pltpu.make_async_copy(own_ref, own_s, sems.at[0]),
        pltpu.make_async_copy(got_ref, got_s, sems.at[1]),
    ]
    writes = [
        pltpu.make_async_copy(own_s, out_ref.at[pl.ds(mine, 2)], sems.at[2]),
        pltpu.make_async_copy(got_s, out_ref.at[pl.ds(2 - mine, 2)], sems.at[3]),
    ]

    @pl.when(at == read)
    def _():
        for copy in reads:
            copy.start()

    @pl.when(at == write)
    def _():
        for copy in reads:
            copy.wait()
        for copy in writes:
            copy.start()

    @pl.when(at == wait)
    def _():
        for copy in writes:
            copy.wait()


def project_back_far_kernel(
    dk_ref, dv_ref, normed_ref, w_ref, own_ref, got_ref, dx_ref, gw_ref, out_ref, own_s, got_s, sems
):
    width = w_ref.shape[0]
    at = pl.program_id(0) * pl.num_programs(1) + pl.program_id(1)
    joining(at, 0, 1, 3, own_ref, got_ref, out_ref, own_s, got_s, sems)
    joined = join_heads(dk_ref, dv_ref)
    dx_ref[0, 0] = dot(joined, w_ref[:, width:], NT).astype(BF16)

    @pl.when((pl.program_id(0) == 0) & (pl.program_id(1) == 0))
    def _():
        gw_ref[...] = jnp.zeros_like(gw_ref)

    gw_ref[...] += dot(normed_ref[0, 0], joined, TN)


def weight_back_kernel(early, *refs):
    dq_ref, dk_ref, dv_ref, normed_ref, far_ref, one_ref, two_ref = refs[:7]
    gw_ref, gfc1_ref, gfc2_ref, gout_ref = refs[7:11]
    gw_s, one_s, two_s, gfc1_s, gfc2_s, gout_s, sems = refs[11:]
    at = pl.program_id(0) * pl.num_programs(1) + pl.program_id(1)
    size = gout_s.shape[0]
    blocks = gfc1_s.shape[1] // size
    reads = [
        pltpu.make_async_copy(one_ref, one_s, sems.at[0]),
        pltpu.make_async_copy(two_ref, two_s, sems.at[1]),
    ]
    writes = [
        pltpu.make_async_copy(gfc1_s, gfc1_ref, sems.at[2]),
        pltpu.make_async_copy(gfc2_s, gfc2_ref, sems.at[3]),
        pltpu.make_async_copy(gout_s, gout_ref, sems.at[4]),
    ]

    @pl.when(at == 0)
    def _():
        for copy in reads:
            copy.start()

    @pl.when(at == 1)
    def _():
        reads[0].wait()
        unstack(
            grouped(early[0]), one_s, [(gfc1_s, 0, block * size) for block in range(blocks)], size
        )
        writes[0].start()

    @pl.when(at == 2)
    def _():
        reads[1].wait()
        rest = [(gfc2_s, block * size, 0) for block in range(blocks)] + [(gout_s, 0, 0)]
        unstack(grouped(early[1]), two_s, rest, size)
        writes[1].start()
        writes[2].start()

    @pl.when(at == pl.num_programs(0) * pl.num_programs(1) - 1)
    def _():
        for copy in writes:
            copy.wait()

    step, which = pl.program_id(0), pl.program_id(1)
    width = normed_ref.shape[3]

    @pl.when((step == 0) & (which == 0))
    def _():
        gw_s[:, :width] = jnp.zeros_like(gw_s[:, :width])
        gw_s[:, width:] = far_ref[...]

    gw_s[...] += dot(normed_ref[0, 0], join_heads(dq_ref, dk_ref, dv_ref), TN)

    @pl.when((step == pl.num_programs(0) - 1) & (which == pl.num_programs(1) - 1))
    def _():
        for block in range(gw_ref.shape[0]):
            gw_ref[block] = gw_s[:, block * LANES : (block + 1) * LANES].astype(BF16)


def join_heads(*grads):
    return jnp.concatenate([ref[0, pair] for ref in grads for pair in range(ref.shape[1])], axis=-1)


class Direct:
    def __init__(self, mesh_shape, row_tiles):
        self.chips = mesh_shape["seq"] // 2
        self.peers = mesh_shape["dp"] * self.chips
        self.half = row_tiles * 8
        self.piece = -(-row_tiles // (2 * self.peers)) * 16
        self.padded = self.piece * self.peers

    def me(self):
        return lax.axis_index("dp") * self.chips + lax.axis_index("seq") // 2

    def core(self):
        return lax.axis_index("seq") % 2

    def sibling(self):
        return {"seq": lax.axis_index("seq") + 1 - 2 * self.core()}

    def peer(self, shift):
        other = (self.me() + shift) % self.peers
        device = {"dp": other // self.chips, "seq": (other % self.chips) * 2 + self.core()}
        return other, device

    def rows(self, index):
        return pl.ds(pl.multiple_of(index * self.piece, 16), self.piece)

    def barrier(self):
        semaphore = pltpu.get_barrier_semaphore()

        def signal(device):
            pl.semaphore_signal(semaphore, 1, device_id=device, device_id_type=pl.DeviceIdType.MESH)

        signal(self.sibling())

        def greet(shift, carry):
            signal(self.peer(shift)[1])
            return carry

        lax.fori_loop(1, self.peers, greet, 0)
        pl.semaphore_wait(semaphore, self.peers)

    def copy(self, source, target, send, recv, device):
        return pltpu.make_async_remote_copy(
            src_ref=source,
            dst_ref=target,
            send_sem=send,
            recv_sem=recv,
            device_id=device,
            device_id_type=pl.DeviceIdType.MESH,
        )

    def each_peer(self, do):
        def one(shift, carry):
            do(shift)
            return carry

        lax.fori_loop(1, self.peers, one, 0)


def tail_kernel(direct, remote, *refs):
    give_ref, own_x, sib_x, mod_ref, lead_ref, gm_ref, dq_ref, dk_ref, dv_ref, w_ref = refs[:10]
    others = refs[10 : 10 + remote]
    grad_ref, got_ref, full_ref, all_ref = refs[10 + remote : 14 + remote]
    sums_s, other_s, got_s, sum_s, core_s, pieces_s, full_s, all_s = refs[14 + remote : 22 + remote]
    core_sems, piece_sems, back_sems, all_sems, grad_sems, local_sem = refs[22 + remote :]
    step, half = pl.program_id(0), pl.program_id(1)
    width = own_x.shape[2]
    core, me = direct.core(), direct.me()

    core_copy = direct.copy(
        give_ref.at[1 - core], core_s, core_sems.at[0], core_sems.at[1], direct.sibling()
    )

    def piece_copy(shift):
        other, device = direct.peer(shift)
        return direct.copy(
            sum_s.at[direct.rows(other)],
            pieces_s.at[shift],
            piece_sems.at[0, shift],
            piece_sems.at[1, shift],
            device,
        )

    def full_copy(shift, arriving):
        _, device = direct.peer(shift)
        owner = (me + direct.peers - shift) % direct.peers if arriving else me
        place = full_s.at[core, direct.rows(owner)]
        return direct.copy(place, place, back_sems.at[0, shift], back_sems.at[1, shift], device)

    def sums_copy(shift, arriving):
        _, device = direct.peer(shift)
        owner = (me + direct.peers - shift) % direct.peers if arriving else me
        place = all_s.at[core, owner]
        return direct.copy(place, place, all_sems.at[0, shift], all_sems.at[1, shift], device)

    def side_copy(values, which, side):
        place = values.at[side]
        return direct.copy(
            place, place, core_sems.at[which], core_sems.at[which + 1], direct.sibling()
        )

    def grad_copy(index):
        return direct.copy(
            other_s.at[index],
            got_s.at[index],
            grad_sems.at[0, index],
            grad_sems.at[1, index],
            direct.sibling(),
        )

    @pl.when((step == 0) & (half == 0))
    def _():
        direct.barrier()
        core_copy.start()
        sums_s[...] = jnp.zeros_like(sums_s)

    @pl.when((step == 0) & (half == 1))
    def _():
        core_copy.wait()
        real = core_s.shape[0]
        sum_s[:real] = (give_ref[core].astype(F32) + core_s[...].astype(F32)).astype(BF16)
        if direct.padded > real:
            sum_s[real:] = jnp.zeros_like(sum_s[real:])
        direct.each_peer(lambda shift: piece_copy(shift).start())

    x = jnp.where(half == 0, own_x[0], sib_x[0]).astype(F32)
    scale = mod_ref[pl.ds(step, 1), width : 2 * width]
    xhat, inverse = normalize(x)
    gy = dot(join_heads(dq_ref, dk_ref, dv_ref), w_ref[...], NT)
    for other in others:
        gy = gy + other[0, 0].astype(F32)
    grad = (gm_ref[0, 0] + norm_back(gy * (1.0 + scale), xhat, inverse)).astype(BF16)

    @pl.when(half == 0)
    def _():
        grad_ref[0] = grad

    @pl.when(half == 1)
    def _():
        other_s[step] = grad
        grad_copy(step).start()

    for kind, value in enumerate((gy, gy * xhat)):
        total = jnp.sum(value, axis=0, keepdims=True)
        for index in range(width // LANES):
            place = pl.ds((kind * 2 + step) * (width // LANES) + index, 1)
            sums_s[place, :] += total[:, index * LANES : (index + 1) * LANES]

    @pl.when((step == 1) & (half == 1))
    def _():
        for index in range(2):
            chosen = lane_index((1, LANES)) == lead_ref[0, first_step(2) + index]
            sums_s[12 + index : 13 + index, :] = jnp.where(chosen, 1.0, 0.0)
        all_s[core, me] = sums_s[...].astype(BF16)
        direct.each_peer(lambda shift: sums_copy(shift, False).start())
        direct.each_peer(lambda shift: piece_copy(shift).wait())

        def add(shift, total):
            return total + pieces_s[shift].astype(F32)

        total = lax.fori_loop(1, direct.peers, add, sum_s[direct.rows(me)].astype(F32))
        full_s[core, direct.rows(me)] = total.astype(BF16)
        direct.each_peer(lambda shift: full_copy(shift, False).start())

        def arrived(shift):
            full_copy(shift, False).wait_send()
            full_copy(shift, True).wait_recv()
            sums_copy(shift, False).wait_send()
            sums_copy(shift, True).wait_recv()

        direct.each_peer(arrived)
        side_copy(full_s, 2, core).start()
        side_copy(all_s, 4, core).start()
        for index in range(2):
            grad_copy(index).wait()
        side_copy(full_s, 2, core).wait_send()
        side_copy(full_s, 2, 1 - core).wait_recv()
        side_copy(all_s, 4, core).wait_send()
        side_copy(all_s, 4, 1 - core).wait_recv()
        outs = [(got_s, got_ref), (full_s, full_ref), (all_s, all_ref)]
        copies = [
            pltpu.make_async_copy(source, target, local_sem.at[index])
            for index, (source, target) in enumerate(outs)
        ]
        for copy in copies:
            copy.start()
        for copy in copies:
            copy.wait()


def unstack(at, full_ref, targets, rows):
    row, end = 0, rows * len(targets)
    while row < end:
        group, inside, left = at(row)
        block, place = divmod(row, rows)
        count = min(left, rows - place)
        target, first_row, first_column = targets[block]
        columns = slice(first_column, first_column + full_ref.shape[2])
        value = full_ref[group, inside : inside + count, :].astype(F32)
        target[first_row + place : first_row + place + count, columns] = value
        row += count


def grouped(exchange):
    def at(row):
        group, inside = divmod(row, exchange.real)
        return group, inside, exchange.real - inside

    return at


def spread_leads(grads, step_of, table_rows):
    count = grads.shape[0]
    part = min(count, 512)
    row = lax.broadcasted_iota(jnp.int32, (part, part), 0)
    column = lane_index((part, part))
    chosen = (row // 16 == column // 16) & (row % 16 == 12 + step_of(column % 16))
    spread = jnp.where(chosen, 1.0, 0.0).astype(BF16)
    leads = [
        dot(grads[start : start + part, :LANES], spread, TN)[:table_rows]
        for start in range(0, count, part)
    ]
    return jnp.concatenate(leads, axis=-1)


def final_kernel(direct, *refs):
    early_sums, late_sums, emb_ref, ada_ref, late_ref, own_ref, got_ref = refs[:7]
    grad_out, gemb_ref, gada_out, gbada_ref, gqkv_out = refs[7:12]
    gada_s, gqkv_s, late_s, own_s, got_s, sems = refs[12:]
    size = emb_ref.shape[1]
    mine = first_step(2)
    pairs = [(late_ref, late_s), (own_ref, own_s), (got_ref, got_s)]
    reads = [
        pltpu.make_async_copy(source, target, sems.at[index])
        for index, (source, target) in enumerate(pairs)
    ]
    for read in reads:
        read.start()
    copies = []

    def start(source, target):
        copy = pltpu.make_async_copy(source, target, sems.at[3 + len(copies)])
        copy.start()
        copies.append(copy)

    def halved(row):
        group, inside = divmod(row, direct.half)
        return group, inside, direct.half - inside

    columns = gqkv_s.shape[1] // LANES
    reads[0].wait()
    unstack(halved, late_s, [(gqkv_s, 0, block * LANES) for block in range(columns)], size)
    start(gqkv_s, gqkv_out)
    reads[1].wait()
    start(own_s, grad_out.at[pl.ds(mine, 2)])
    reads[2].wait()
    start(got_s, grad_out.at[pl.ds(2 - mine, 2)])

    table_rows = emb_ref.shape[0]
    table = emb_ref[...].astype(F32)
    gate = jax.nn.sigmoid(table)
    slope = gate * (1.0 + table * (1.0 - gate))
    table_act = (table * gate).astype(BF16)
    total = jnp.zeros((table_rows, size), F32)

    def one_piece(grads, leads, place, first):
        chosen = jnp.where(place, leads, 0.0).astype(BF16)
        acts = dot(table_act, chosen, TN).astype(BF16)
        where = slice(first, first + grads.shape[1])
        gada_s[:, where] = dot(acts, grads)
        by_lead = dot(chosen, grads)
        gbada_ref[where] = jnp.sum(by_lead, axis=0)
        high = by_lead.astype(BF16)
        low = (by_lead - high.astype(F32)).astype(BF16)
        return dot(high, ada_ref[:, where], NT) + dot(low, ada_ref[:, where], NT)

    grads = early_sums[...]
    leads = spread_leads(grads, lambda row: row % 2, table_rows)
    row = lane_index((1, grads.shape[0])) % 16
    for index in range(4):
        total += one_piece(grads, leads, row // 2 == index, (2 + index) * size)
    grads = late_sums[...]
    parts = size // LANES
    leads = spread_leads(grads, lambda row: (row // parts) % 2, table_rows)
    row = lane_index((1, grads.shape[0])) % 16
    for index in range(2):
        for part in range(parts):
            place = (row // (2 * parts) == index) & (row % parts == part)
            total += one_piece(grads, leads, place, index * size + part * LANES)
    gemb_ref[...] = total * slope
    start(gada_s, gada_out)
    for copy in copies:
        copy.wait()


def local(
    mesh_shape, inputs, cotangent, counts, lead_steps, emb_table, w_ada, b_ada, w_qkv, w_out, w_fc1, w_fc2
):
    slots, items, patches, width = inputs.shape
    chips = mesh_shape["seq"] // 2
    blocks = w_fc1.shape[1] // w_fc1.shape[0]
    steps = slots * items // 2
    hidden_width = w_fc1.shape[1]
    pairs = width // LANES
    rows = 2 * patches
    remote = 2 * (chips - 1)
    far_rows = remote * patches
    spot = lax.axis_index("seq")
    core = lax.rem(spot, 2)
    devices = 2 * chips

    def send(values, shift, cross):
        pairs_list = []
        for source in range(devices):
            chip, side = source // 2, source % 2
            pairs_list.append((source, ((chip + shift) % chips) * 2 + (1 - side if cross else side)))
        return lax.ppermute(values, "seq", pairs_list)

    x_steps = inputs.reshape(2, steps, patches, width)
    ct_steps = cotangent.reshape(2, steps, patches, width)
    own_x = lax.dynamic_index_in_dim(x_steps, core, 0, keepdims=False)
    other_x = lax.dynamic_index_in_dim(x_steps, 1 - core, 0, keepdims=False)
    own_ct = lax.dynamic_index_in_dim(ct_steps, core, 0, keepdims=False)
    other_ct = lax.dynamic_index_in_dim(ct_steps, 1 - core, 0, keepdims=False)
    sib_x = send(other_x, 0, True)
    far_x = []
    for step in range(steps):
        some = slice(step, step + 1)
        for shift in range(1, chips):
            far_x.append(send(own_x[some], shift, False))
            far_x.append(send(other_x[some], shift, True))
    sib_ct = send(other_ct, 0, True)

    step_block = pl.BlockSpec((1, patches, width), lambda j, i: (j, 0, 0))
    patch_block = pl.BlockSpec((1, 1, patches, width), lambda j, i: (j, i, 0, 0))

    def head_rows(count):
        return pl.BlockSpec((1, 1, count, LANES), lambda j, p: (j, p, 0, 0))

    def of_step(*shape):
        return pl.BlockSpec((1,) + shape, lambda j, p: (j,) + (0,) * len(shape))

    both_heads = pl.BlockSpec((1, 1, 2, rows, LANES), lambda j, p: (j, p, 0, 0, 0))
    piece = min(256, rows)
    near_work = 4 * steps * pairs * 2 * rows * LANES * rows
    near_heads = jax.ShapeDtypeStruct((steps, pairs, rows, LANES), BF16)
    mod, n1, q, k, v, acc = call(
        functools.partial(near_kernel, piece),
        "near",
        (steps, pairs),
        [scalars(), whole(emb_table.shape), whole(w_ada.shape), whole((1, 6 * width))]
        + [step_block] * 2
        + [whole(w_qkv.shape)],
        [whole((16, 6 * width)), of_step(rows, width)]
        + [of_step(pairs, rows, LANES)] * 3
        + [both_heads],
        [
            jax.ShapeDtypeStruct((16, 6 * width), F32),
            jax.ShapeDtypeStruct((steps, rows, width), BF16),
            near_heads,
            near_heads,
            near_heads,
            jax.ShapeDtypeStruct((steps, pairs, 2, rows, LANES), F32),
        ],
        [pltpu.VMEM((2, rows, LANES), BF16)],
        flops=near_work + 6 * steps * rows * width * width,
        exps=steps * pairs * 2 * rows * rows,
    )(lead_steps, emb_table, w_ada, b_ada.reshape(1, -1), own_x, sib_x, w_qkv)

    def far(step, before):
        some_x = far_x[step * remote : (step + 1) * remote]

        def at_step(*shape):
            return pl.BlockSpec((1,) + shape, lambda p: (step,) + (0,) * len(shape))

        def at_pair(*shape):
            return pl.BlockSpec((1, 1) + shape, lambda p: (step, p) + (0,) * len(shape))

        operands = [*some_x, mod, w_qkv, q, k, v, acc]
        return call(
            functools.partial(far_kernel, piece, step, remote),
            "far",
            (pairs,),
            [whole((1, patches, width))] * remote
            + [whole(mod.shape), whole(w_qkv.shape)]
            + [at_pair(rows, LANES)] * 3
            + [at_pair(2, rows, LANES)]
            + [pl.BlockSpec(memory_space=pl.ANY)] * len(before),
            [at_step(far_rows, width)]
            + [at_step(pairs, far_rows, LANES)] * 2
            + [at_pair(rows, LANES), at_pair(2, rows, LANES)],
            [
                jax.ShapeDtypeStruct((steps, far_rows, width), BF16),
                jax.ShapeDtypeStruct((steps, pairs, far_rows, LANES), BF16),
                jax.ShapeDtypeStruct((steps, pairs, far_rows, LANES), BF16),
                jax.ShapeDtypeStruct((steps, pairs, rows, LANES), F32),
                jax.ShapeDtypeStruct((steps, pairs, 2, rows, LANES), BF16),
            ],
            [pltpu.VMEM((2, far_rows, LANES), BF16), pltpu.VMEM((rows, LANES), F32)],
            flops=near_work // 2,
            exps=pairs * 2 * rows * far_rows,
            aliases={len(operands) + index: index for index in range(len(before))},
        )(*operands, *before)

    far_results = []
    for step in range(steps):
        far_results = far(step, far_results)
    n1r, kr, vr, o, qe = far_results

    block_rows = min(256, patches)
    outs = call(
        functools.partial(patch_kernel, block_rows, hidden_width),
        "patchwise",
        (steps, 2),
        [scalars()] * 2
        + [step_block] * 4
        + [
            whole(mod.shape),
            pl.BlockSpec((1, pairs, patches, LANES), lambda j, i: (j, 0, i, 0)),
            whole(w_out.shape),
            whole(w_fc1.shape),
            whole(w_fc2.shape),
        ],
        [
            step_block,
            step_block,
            patch_block,
            pl.BlockSpec((1, pairs, 2, patches, LANES), lambda j, i: (j, 0, 0, i, 0)),
            whole((16, width)),
            whole((blocks, width, width)),
            whole((blocks + 1, width, width)),
        ],
        [
            jax.ShapeDtypeStruct((steps, patches, width), BF16),
            jax.ShapeDtypeStruct((steps, patches, width), BF16),
            jax.ShapeDtypeStruct((steps, 2, patches, width), F32),
            jax.ShapeDtypeStruct((steps, pairs, 2, rows, LANES), BF16),
            jax.ShapeDtypeStruct((16, width), BF16),
            jax.ShapeDtypeStruct((blocks, width, width), BF16),
            jax.ShapeDtypeStruct((blocks + 1, width, width), BF16),
        ],
        [pltpu.VMEM((patches, hidden_width), BF16)] * 2
        + [pltpu.VMEM((patches, width), BF16)] * 4
        + [
            pltpu.VMEM((width, width), F32),
            pltpu.VMEM((width, hidden_width), F32),
            pltpu.VMEM((width, hidden_width), F32),
            pltpu.VMEM((16, width), F32),
        ],
        flops=6 * steps * rows * width * (2 * hidden_width + width),
        moved=steps * rows * width * 20,
        exps=2 * steps * rows * hidden_width,
    )(counts, lead_steps, own_x, sib_x, own_ct, sib_ct, mod, o, w_out, w_fc1, w_fc2)
    final_own, final_sib, gm, ge, sums, stack_one, stack_two = outs
    final_got = send(final_sib, 0, True)
    early = [Exchange(mesh_shape, blocks * width // 16, 0), Exchange(mesh_shape, (blocks + 1) * width // 16, 1)]
    gives = [g.reshape(e.groups, e.real, width) for e, g in zip(early, (stack_one, stack_two))]

    def attend_back(keys, values, extra, first, name):
        count = keys.shape[2]
        in_specs = [both_heads] * 2 + [head_rows(count)] * 2
        out_specs = [head_rows(rows), head_rows(count), head_rows(count)]
        out_shape = [
            jax.ShapeDtypeStruct((steps, pairs, rows, LANES), F32 if first else BF16),
            jax.ShapeDtypeStruct((steps, pairs, count, LANES), BF16),
            jax.ShapeDtypeStruct((steps, pairs, count, LANES), BF16),
        ]
        scratch = [pltpu.VMEM((LANES, rows), F32)]
        if not first:
            in_specs += [head_rows(rows)]
        for exchange in early:
            shape = (exchange.groups, exchange.padded, width)
            shard = (exchange.shard, width)
            sems = [pltpu.SemaphoreType.DMA((exchange.all_levels,))] * 2
            if first:
                in_specs += [whole((exchange.groups, exchange.real, width))]
                out_specs += [whole(shard)]
                out_shape += [jax.ShapeDtypeStruct(shard, BF16)]
                half = (exchange.groups // 2, exchange.padded, width)
                scratch += [pltpu.VMEM(half, BF16)] + sems + exchange.receive_scratch(width)
            else:
                in_specs += [whole(shard)]
                out_specs += [pl.BlockSpec(memory_space=pl.ANY)]
                out_shape += [jax.ShapeDtypeStruct(shape, BF16)]
                scratch += [pltpu.VMEM(shape, BF16)] + sems
        if first:
            every = (mesh_shape["dp"] * mesh_shape["seq"], 16, width)
            in_specs += [whole(sums.shape)]
            out_specs += [whole(every)]
            out_shape += [jax.ShapeDtypeStruct(every, BF16)]
            sems = [pltpu.SemaphoreType.DMA((early[0].all_levels,))] * 2
            scratch += [pltpu.VMEM(every, BF16)] + sems
        else:
            scratch += [pltpu.SemaphoreType.DMA] * len(early)
        return call(
            functools.partial(attend_back_kernel, min(512, count), first, early, steps * pairs),
            name,
            (steps, pairs),
            in_specs,
            out_specs,
            out_shape,
            scratch,
            flops=10 * steps * pairs * 2 * rows * count * LANES,
            exps=steps * pairs * 2 * rows * count,
            collective=1 if first else 2,
        )(qe, ge, keys, values, *extra)

    grad_block = pl.BlockSpec((1, pairs, patches, LANES), lambda j, i: (j, 0, i, 0))
    hbm = pl.BlockSpec(memory_space=pl.ANY)

    dq_part, dkr, dvr, shard_one, shard_two, early_all = attend_back(
        kr, vr, [*gives, sums], True, "attend_back_far"
    )
    dx_far, gw_part, outputs = call(
        project_back_far_kernel,
        "project_back_far",
        (steps, remote),
        [grad_block] * 2 + [patch_block, whole(w_qkv.shape), hbm, hbm],
        [patch_block, whole((width, 2 * width)), hbm],
        [
            jax.ShapeDtypeStruct((steps, remote, patches, width), BF16),
            jax.ShapeDtypeStruct((width, 2 * width), F32),
            jax.ShapeDtypeStruct((2 * steps, patches, width), BF16),
        ],
        [pltpu.VMEM((steps, patches, width), BF16)] * 2 + [pltpu.SemaphoreType.DMA((4,))],
        flops=4 * steps * far_rows * width * 2 * width,
        moved=steps * far_rows * width * 8,
    )(dkr, dvr, n1r.reshape(steps, remote, patches, width), w_qkv, final_own, final_got)
    dx_got = [send(dx_far[:, 2 * r - 2 : 2 * r], -r, False) for r in range(1, chips)]
    dq, dk, dv, *early_sums = attend_back(
        k, v, [dq_part, shard_one, shard_two], False, "attend_back_near"
    )
    columns = w_qkv.shape[1] // LANES
    early_weights = (w_fc1, w_fc2, w_out)
    give_late, g_fc1, g_fc2, g_out = call(
        functools.partial(weight_back_kernel, early),
        "weight_back",
        (steps, 2),
        [grad_block] * 3 + [patch_block, whole(gw_part.shape), hbm, hbm],
        [whole((columns, width, LANES))] + [hbm] * 3,
        [jax.ShapeDtypeStruct((columns, width, LANES), BF16)]
        + [jax.ShapeDtypeStruct(w.shape, F32) for w in early_weights],
        [pltpu.VMEM((width, columns * LANES), F32)]
        + [pltpu.VMEM(value.shape, BF16) for value in early_sums]
        + [pltpu.VMEM(w.shape, F32) for w in early_weights]
        + [pltpu.SemaphoreType.DMA((5,))],
        flops=2 * steps * rows * width * 3 * width,
        moved=steps * rows * width * 8,
    )(dq, dk, dv, n1.reshape(steps, 2, patches, width), gw_part, *early_sums)

    direct = Direct(mesh_shape, columns * width // 16)
    full_shape = (2, direct.padded, LANES)
    late_all_shape = (2, direct.peers, 16, LANES)
    grad_own, grad_got, late_sum, late_all = call(
        functools.partial(tail_kernel, direct, len(dx_got)),
        "tail",
        (steps, 2),
        [whole((2, direct.half, LANES)), step_block, step_block, whole(mod.shape), scalars()]
        + [patch_block]
        + [grad_block] * 3
        + [whole(w_qkv.shape)]
        + [patch_block] * len(dx_got),
        [step_block, hbm, hbm, hbm],
        [
            jax.ShapeDtypeStruct((steps, patches, width), BF16),
            jax.ShapeDtypeStruct((steps, patches, width), BF16),
            jax.ShapeDtypeStruct(full_shape, BF16),
            jax.ShapeDtypeStruct(late_all_shape, BF16),
        ],
        [
            pltpu.VMEM((16, LANES), F32),
            pltpu.VMEM((steps, patches, width), BF16),
            pltpu.VMEM((steps, patches, width), BF16),
            pltpu.VMEM((direct.padded, LANES), BF16),
            pltpu.VMEM((direct.half, LANES), BF16),
            pltpu.VMEM((direct.peers, direct.piece, LANES), BF16),
            pltpu.VMEM(full_shape, BF16),
            pltpu.VMEM(late_all_shape, BF16),
            pltpu.SemaphoreType.DMA((6,)),
            pltpu.SemaphoreType.DMA((2, direct.peers)),
            pltpu.SemaphoreType.DMA((2, direct.peers)),
            pltpu.SemaphoreType.DMA((2, direct.peers)),
            pltpu.SemaphoreType.DMA((2, steps)),
            pltpu.SemaphoreType.DMA((3,)),
        ],
        flops=2 * steps * rows * width * 3 * width,
        collective=3,
    )(
        give_late.reshape(2, direct.half, LANES),
        own_x,
        sib_x,
        mod,
        lead_steps,
        gm,
        dq,
        dk,
        dv,
        w_qkv,
        *dx_got,
    )

    early_all = early_all.reshape(-1, width)
    late_all = late_all.reshape(-1, LANES)
    small = [early_all, late_all, emb_table, w_ada]
    large = [late_sum, grad_own, grad_got]
    out_shapes = [(slots * items, patches, width), emb_table.shape, w_ada.shape, b_ada.shape, w_qkv.shape]
    grad_inputs, g_emb, g_ada, g_bada, g_qkv = call(
        functools.partial(final_kernel, direct),
        "final",
        (),
        [whole(value.shape) for value in small] + [hbm] * len(large),
        [hbm, whole(emb_table.shape), hbm, whole(b_ada.shape), hbm],
        [
            jax.ShapeDtypeStruct(shape, F32 if index else BF16)
            for index, shape in enumerate(out_shapes)
        ],
        [pltpu.VMEM(w.shape, F32) for w in (w_ada, w_qkv)]
        + [pltpu.VMEM(value.shape, BF16) for value in large]
        + [pltpu.SemaphoreType.DMA((7,))],
        flops=2 * early_all.shape[0] * width * 6 * width,
        moved=6 * w_ada.size,
    )(*small, *large)
    return (
        outputs.reshape(inputs.shape),
        grad_inputs.reshape(inputs.shape),
        g_emb,
        g_ada,
        g_bada,
        g_qkv,
        g_out,
        g_fc1,
        g_fc2,
    )


def solution(mesh):
    tokens = P(None, "dp", "seq", None)
    return jax.shard_map(
        functools.partial(local, dict(mesh.shape)),
        mesh=mesh,
        in_specs=(tokens, tokens, P("dp"), P("dp", None)) + (P(),) * 7,
        out_specs=(tokens, tokens) + (P(),) * 7,
        check_vma=False,
    )
```

```python
import functools

import jax
import jax.numpy as jnp
from jax import lax
from jax.experimental import pallas as pl
from jax.experimental.pallas import tpu as pltpu
from jax.sharding import PartitionSpec as P

HD = 64
LANES = 128
EPSILON = 1e-06
LOG2E = 1.4426950408889634
NN = (((1,), (0,)), ((), ()))
NT = (((1,), (1,)), ((), ()))
TN = (((0,), (0,)), ((), ()))
F32 = jnp.float32
BF16 = jnp.bfloat16
VMEM_BYTES = 24 * 1024 * 1024


def dot(a, b, dims=NN):
    return lax.dot_general(a, b, dims, preferred_element_type=F32)


def call(
    body,
    name,
    grid,
    in_specs,
    out_specs,
    out_shape,
    scratch=(),
    flops=0,
    moved=0,
    exps=0,
    collective=None,
    aliases=None,
):
    return pl.pallas_call(
        body,
        name=name,
        grid=grid,
        in_specs=in_specs,
        out_specs=out_specs,
        out_shape=out_shape,
        scratch_shapes=list(scratch),
        input_output_aliases=aliases or {},
        cost_estimate=pl.CostEstimate(flops=flops, bytes_accessed=moved, transcendentals=exps),
        compiler_params=pltpu.CompilerParams(
            vmem_limit_bytes=VMEM_BYTES,
            collective_id=collective,
            has_side_effects=collective is not None,
        ),
    )


def whole(shape):
    return pl.BlockSpec(shape, lambda *_: (0,) * len(shape))


def scalars():
    return pl.BlockSpec(memory_space=pltpu.SMEM)


def lane_index(shape):
    return lax.broadcasted_iota(jnp.int32, shape, 1)


def first_step(steps):
    return lax.rem(lax.axis_index("seq"), 2) * steps


def normalize(values):
    center = values - jnp.mean(values, axis=-1, keepdims=True)
    spread = jnp.mean(center * center, axis=-1, keepdims=True)
    inverse = lax.rsqrt(spread + EPSILON)
    return center * inverse, inverse


def norm_back(grad, xhat, inverse):
    first = jnp.mean(grad, axis=-1, keepdims=True)
    second = jnp.mean(grad * xhat, axis=-1, keepdims=True)
    return inverse * (grad - first - xhat * second)


def pick(refs, which):
    value = refs[0][0]
    for index in range(1, len(refs)):
        value = jnp.where(which == index, refs[index][0], value)
    return value


class Exchange:
    def __init__(self, mesh_shape, row_tiles, turn=0):
        bits = {"seq": [], "dp": []}
        for axis in bits:
            bit = 1
            while bit < mesh_shape[axis]:
                bits[axis].append((axis, bit))
                bit *= 2
        turned = bits["dp"][turn:] + bits["dp"][:turn]
        self.bits = bits["seq"][:1] + turned + bits["seq"][1:]
        self.all_levels = len(self.bits)
        self.levels = 1 + len(turned)
        self.even = 0
        while self.even < self.levels and row_tiles % 2 == 0:
            row_tiles //= 2
            self.even += 1
        unit = 2 ** (self.levels - self.even)
        self.groups = 2**self.even
        self.real = row_tiles * 16
        self.padded = -(-row_tiles // unit) * unit * 16
        self.shard = self.padded // unit

    def sizes(self, level):
        if level < self.even:
            return (self.groups >> (level + 1), self.real)
        return (1, self.padded >> (level - self.even + 1))

    def receive_scratch(self, width):
        last = self.levels - 1
        return [
            pltpu.VMEM(self.sizes(min(level, last)) + (width,), BF16)
            for level in range(self.all_levels)
        ]

    def place(self, level):
        axis, bit = self.bits[level]
        here = lax.axis_index(axis)
        value = (here // bit) % 2
        return value, {axis: here + bit * (1 - 2 * value)}

    def spot(self, level, first, flip):
        group, row = 0, 0
        for index in range(first, level + 1):
            value, _ = self.place(index)
            if flip and index == level:
                value = 1 - value
            if index < self.even:
                group = group + value * (self.groups >> (index + 1))
            else:
                row = row + value * (self.padded >> (index - self.even + 1))
        if level >= self.even:
            row = pl.multiple_of(row, 16)
        count, rows = self.sizes(level)
        return pl.ds(group, count), pl.ds(row, rows)

    def barrier(self):
        semaphore = pltpu.get_barrier_semaphore()
        for level in range(self.all_levels):
            _, partner = self.place(level)
            pl.semaphore_signal(
                semaphore, inc=1, device_id=partner, device_id_type=pl.DeviceIdType.MESH
            )
        pl.semaphore_wait(semaphore, self.all_levels)

    def copy(self, source, target, sends, recvs, level):
        _, partner = self.place(level)
        return pltpu.make_async_remote_copy(
            src_ref=source,
            dst_ref=target,
            send_sem=sends.at[level],
            recv_sem=recvs.at[level],
            device_id=partner,
            device_id_type=pl.DeviceIdType.MESH,
        )

    def reduce_copy(self, level, start_ref, acc_ref, got, sends, recvs):
        if level >= self.levels:
            return self.copy(self.own_shard(acc_ref, 1), got[level], sends, recvs, level)
        groups, rows = self.spot(level, min(level, 1), True)
        source = start_ref if level == 0 else acc_ref
        return self.copy(source.at[groups, rows], got[level], sends, recvs, level)

    def reduce_start(self, level, *refs):
        self.reduce_copy(level, *refs).start()

    def reduce_finish(self, level, start_ref, acc_ref, got, sends, recvs):
        self.reduce_copy(level, start_ref, acc_ref, got, sends, recvs).wait()
        if level >= self.levels:
            own = self.own_shard(acc_ref, 1)
            own[...] = (own[...].astype(F32) + got[level][...].astype(F32)).astype(BF16)
            return
        count, rows = self.sizes(level)
        groups, spots = self.spot(level, min(level, 1), False)
        if level == 0:
            target_groups, target_rows = pl.ds(0, count), pl.ds(0, rows)
            if self.padded > self.real:
                acc_ref[:, self.real :, :] = jnp.zeros_like(acc_ref[:, self.real :, :])
        else:
            target_groups, target_rows = groups, spots
        source = start_ref if level == 0 else acc_ref

        def add(index, carry):
            one = pl.ds(groups.start + index, 1)
            to = pl.ds(target_groups.start + index, 1)
            value = source[one, spots, :].astype(F32) + got[level][pl.ds(index, 1)].astype(F32)
            acc_ref[to, target_rows, :] = value.astype(BF16)
            return carry

        lax.fori_loop(0, count, add, 0)

    def own_shard(self, ref, first):
        if self.levels > self.even:
            return ref.at[self.spot(self.levels - 1, first, False)]
        groups, _ = self.spot(self.levels - 1, first, False)
        return ref.at[groups, pl.ds(0, self.shard)]

    def gather_copy(self, level, full_ref, sends, recvs):
        piece = full_ref.at[self.spot(level, 0, False)]
        return self.copy(piece, piece, sends, recvs, level)

    def gather_start(self, level, *refs):
        self.gather_copy(level, *refs).start()

    def gather_finish(self, level, *refs):
        self.gather_copy(level, *refs).wait()


def modulation(lead_ref, emb_ref, ada_ref, bias_ref):
    shape = (16, emb_ref.shape[0])
    rows = lax.broadcasted_iota(jnp.int32, shape, 0)
    columns = lane_index(shape)
    onehot = jnp.zeros(shape, F32)
    for step in range(2):
        lead = lead_ref[0, first_step(2) + step]
        onehot = jnp.where((rows == step) & (columns == lead), 1.0, onehot)
    condition = dot(onehot.astype(BF16), emb_ref[...])
    active = (condition * jax.nn.sigmoid(condition)).astype(BF16)
    return dot(active, ada_ref[...]) + bias_ref[...].astype(F32)


def project(x_refs, mod_ref, step, w_ref, normed_ref, head_refs):
    width = w_ref.shape[0]
    patches = x_refs[0].shape[1]
    rows = min(256, patches)
    shift = mod_ref[pl.ds(step, 1), 0:width]
    scale = mod_ref[pl.ds(step, 1), width : 2 * width]
    queries = len(head_refs) == 3
    for index, x_ref in enumerate(x_refs):

        def block(count, carry):
            start = pl.multiple_of(count * rows, rows)
            at = pl.ds(pl.multiple_of(index * patches + start, rows), rows)
            xhat, _ = normalize(x_ref[0, pl.ds(start, rows), :].astype(F32))
            normed = (xhat * (1.0 + scale) + shift).astype(BF16)
            normed_ref[0, at, :] = normed
            for part, head_ref in enumerate(head_refs):
                first = (part + (0 if queries else 1)) * width
                projected = dot(normed, w_ref[:, first : first + width])
                if queries and part == 0:
                    projected = projected.astype(BF16).astype(F32) * HD**-0.5
                projected = projected.astype(BF16)
                for pair in range(width // LANES):
                    head_ref[0, pair, at, :] = projected[:, pair * LANES : (pair + 1) * LANES]
            return carry

        lax.fori_loop(0, patches // rows, block, 0, unroll=True)


def with_ones(values):
    low = lane_index(values.shape) < HD
    one = jnp.ones_like(values)
    return jnp.where(low, values, one), jnp.where(low, one, values)


def exponentials(query, keys_ref, pair, width=256):
    count = keys_ref.shape[2]
    width = min(width, count)
    return jnp.concatenate(
        [
            jnp.exp(dot(query, keys_ref[0, pair, start : start + width, :], NT)).astype(BF16)
            for start in range(0, count, width)
        ],
        axis=-1,
    )


def masked(values):
    low = lane_index(values.shape) < HD
    zero = jnp.zeros_like(values)
    return jnp.where(low, values, zero), jnp.where(low, zero, values)


def near_kernel(rows, *refs):
    lead_ref, emb_ref, ada_ref, bias_ref, own_x, sib_x, w_ref = refs[:7]
    mod_ref, normed_ref, q_ref, k_ref, v_ref, acc_ref, ext_ref = refs[7:]
    step, pair = pl.program_id(0), pl.program_id(1)

    @pl.when((step == 0) & (pair == 0))
    def _():
        mod_ref[...] = modulation(lead_ref, emb_ref, ada_ref, bias_ref)

    @pl.when(pair == 0)
    def _():
        project([own_x, sib_x], mod_ref, step, w_ref, normed_ref, [q_ref, k_ref, v_ref])

    ext_ref[0], ext_ref[1] = with_ones(v_ref[0, pair])
    for start in range(0, q_ref.shape[2], rows):
        at = slice(start, start + rows)
        for head, query in enumerate(masked(q_ref[0, pair, at, :])):
            acc_ref[0, 0, head, at, :] = dot(exponentials(query, k_ref, pair), ext_ref[head])


def far_kernel(rows, step, sources, *refs):
    x_refs, refs = refs[:sources], refs[sources:]
    mod_ref, w_ref, q_ref, k_ref, v_ref, acc_ref = refs[:6]
    normed_ref, kr_ref, vr_ref, o_ref, qe_ref, ext_ref, total_ref = refs[-7:]
    pair = pl.program_id(0)

    @pl.when(pair == 0)
    def _():
        project(x_refs, mod_ref, step, w_ref, normed_ref, [kr_ref, vr_ref])

    ext_ref[0], ext_ref[1] = with_ones(vr_ref[0, pair])
    def finish(at, query, first, second, top_first, top_second):
        lane = lane_index(query.shape)
        low = lane < HD
        swapped = jnp.where(low, second, first)
        total = pltpu.roll(swapped, HD, 1)
        o_ref[0, 0, at, :] = jnp.where(low, first, second) / total
        log_total = jnp.log(swapped) + jnp.where(low, top_second, top_first)
        high = log_total.astype(BF16).astype(F32)
        middle = (log_total - high).astype(BF16).astype(F32)
        rest = log_total - high - middle
        spot = lane % HD
        extra = jnp.where(spot == 0, -high, jnp.where(spot == 1, -middle, -rest))
        extra = jnp.where(spot < 3, extra, 0.0).astype(BF16)
        qe_ref[0, 0, 0, at, :] = jnp.where(low, query, extra)
        qe_ref[0, 0, 1, at, :] = jnp.where(low, extra, query)
        return total

    def block(index, carry):
        at = pl.ds(pl.multiple_of(index * rows, rows), rows)
        query = q_ref[0, 0, at, :]
        sums = []
        for head, own in enumerate(masked(query)):
            more = dot(exponentials(own, kr_ref, pair), ext_ref[head])
            sums.append(acc_ref[0, 0, head, at, :] + more)
        total_ref[at, :] = finish(at, query, sums[0], sums[1], 0.0, 0.0)
        return carry

    lax.fori_loop(0, q_ref.shape[2] // rows, block, 0, unroll=True)
    total = total_ref[...]
    bad = jnp.sum(jnp.where((total > 1e-25) & (total < 1e25), 0.0, 1.0))

    @pl.when(bad > 0.0)
    def _():
        own_ext = with_ones(v_ref[0, 0])

        again_rows = min(32, q_ref.shape[2])

        def again(index, carry):
            at = pl.ds(pl.multiple_of(index * again_rows, again_rows), again_rows)
            query = q_ref[0, 0, at, :]
            sums, tops = [], []
            for head, own in enumerate(masked(query)):
                scores = dot(own, k_ref[0, 0], NT)
                others = dot(own, kr_ref[0, pair], NT)
                top = jnp.maximum(
                    jnp.max(scores, axis=-1, keepdims=True),
                    jnp.max(others, axis=-1, keepdims=True),
                )
                sums.append(
                    dot(jnp.exp(scores - top).astype(BF16), own_ext[head])
                    + dot(jnp.exp(others - top).astype(BF16), ext_ref[head])
                )
                tops.append(top)
            finish(at, query, sums[0], sums[1], tops[0], tops[1])
            return carry

        lax.fori_loop(0, q_ref.shape[2] // again_rows, again, 0)


def gelu_parts(values):
    cumulative = 0.5 * lax.erf(values * 0.7071067811865476) + 0.5
    bell = jnp.exp2(values * values * (-0.5 * LOG2E))
    return values * cumulative, cumulative + values * bell * 0.3989422804014327


def patch_kernel(
    rows,
    chunk,
    counts_ref,
    lead_ref,
    own_x,
    sib_x,
    own_ct,
    sib_ct,
    mod_ref,
    o_ref,
    out_w,
    fc1_w,
    fc2_w,
    final_own,
    final_sib,
    gm_ref,
    ge_ref,
    sums_ref,
    stack_one,
    stack_two,
    hidden_s,
    gpre_s,
    n2_s,
    g2_s,
    g1_s,
    mixed_s,
    gout_s,
    gfc1_s,
    gfc2_s,
    sums_s,
):
    step, half = pl.program_id(0), pl.program_id(1)
    width, hidden_width = fc1_w.shape
    patches = own_x.shape[1]
    slot = first_step(pl.num_programs(0)) + step
    active = (slot < counts_ref[0]).astype(F32)

    def piece(index):
        return mod_ref[pl.ds(step, 1), index * width : (index + 1) * width]

    gate1, shift2, scale2, gate2 = piece(2), piece(3), piece(4), piece(5)

    @pl.when((step == 0) & (half == 0))
    def _():
        sums_s[...] = jnp.zeros_like(sums_s)
        gout_s[...] = jnp.zeros_like(gout_s)
        gfc1_s[...] = jnp.zeros_like(gfc1_s)
        gfc2_s[...] = jnp.zeros_like(gfc2_s)

    def block(index, carry):
        at = pl.ds(pl.multiple_of(index * rows, rows), rows)
        x = jnp.where(half == 0, own_x[0, at, :], sib_x[0, at, :]).astype(F32)
        final_grad = jnp.where(half == 0, own_ct[0, at, :], sib_ct[0, at, :]).astype(F32) * active
        outs = [o_ref[0, pair, at, :] for pair in range(width // LANES)]
        mixed = jnp.concatenate([o.astype(BF16) for o in outs], axis=-1)
        mixed_s[at, :] = mixed
        branch_one = dot(mixed, out_w[...])
        middle = x + gate1 * branch_one
        xhat, inverse = normalize(middle)
        n2 = (xhat * (1.0 + scale2) + shift2).astype(BF16)
        n2_s[at, :] = n2
        g2 = (gate2 * final_grad).astype(BF16)
        g2_s[at, :] = g2
        branch_two = jnp.zeros((rows, width), F32)
        gy = jnp.zeros((rows, width), F32)
        for start in range(0, hidden_width, chunk):
            columns = slice(start, start + chunk)
            pre = dot(n2, fc1_w[:, columns])
            grad_hidden = dot(g2, fc2_w[columns, :], NT)
            hidden, slope = gelu_parts(pre)
            hidden = hidden.astype(BF16)
            grad_pre = (slope * grad_hidden).astype(BF16)
            hidden_s[at, columns] = hidden
            gpre_s[at, columns] = grad_pre
            branch_two += dot(hidden, fc2_w[columns, :])
            gy += dot(grad_pre, fc1_w[:, columns], NT)
        final = ((middle + gate2 * branch_two) * active).astype(BF16)

        @pl.when(half == 0)
        def _():
            final_own[0, at, :] = final

        @pl.when(half == 1)
        def _():
            final_sib[0, at, :] = final

        gm = final_grad + norm_back(gy * (1.0 + scale2), xhat, inverse)
        gm_ref[0, 0, at, :] = gm
        g1 = (gate1 * gm).astype(BF16)
        g1_s[at, :] = g1
        sums = [branch_one * gm, gy, gy * xhat, branch_two * final_grad]
        for row, value in enumerate(sums):
            place = pl.ds(2 * row + step, 1)
            sums_s[place, :] += jnp.sum(value, axis=0, keepdims=True)
        grad_mixed = dot(g1, out_w[...], NT).astype(BF16)
        lane = lane_index((rows, LANES))
        low = lane < HD
        spot = lane % HD
        for pair, o in enumerate(outs):
            grad = grad_mixed[:, pair * LANES : (pair + 1) * LANES]
            product = grad.astype(F32) * o
            first = jnp.sum(jnp.where(low, product, 0.0), axis=-1, keepdims=True)
            second = jnp.sum(jnp.where(low, 0.0, product), axis=-1, keepdims=True)
            inner = jnp.where(low, second, first)
            high = inner.astype(BF16).astype(F32)
            mid = (inner - high).astype(BF16).astype(F32)
            extra = jnp.where(spot == 0, -high, jnp.where(spot == 1, -mid, high + mid - inner))
            extra = jnp.where(spot < 3, extra, 0.0).astype(BF16)
            ge_ref[0, pair, 0, at, :] = jnp.where(low, grad, extra)
            ge_ref[0, pair, 1, at, :] = jnp.where(low, extra, grad)
        return carry

    lax.fori_loop(0, patches // rows, block, 0)
    gout_s[...] += dot(mixed_s[...], g1_s[...], TN)
    gfc1_s[...] += dot(n2_s[...], gpre_s[...], TN)
    gfc2_s[...] += dot(g2_s[...], hidden_s[...], TN)

    @pl.when((step == pl.num_programs(0) - 1) & (half == pl.num_programs(1) - 1))
    def _():
        for index in range(2):
            lead = lead_ref[0, first_step(2) + index]
            sums_s[12 + index : 13 + index, :] = jnp.where(lane_index((1, width)) == lead, 1.0, 0.0)
        sums_ref[...] = sums_s[...].astype(BF16)
        blocks = hidden_width // width
        for index in range(blocks):
            columns = slice(index * width, (index + 1) * width)
            stack_one[index] = gfc1_s[:, columns].astype(BF16)
            stack_two[index] = gfc2_s[:, columns].T.astype(BF16)
        stack_two[blocks] = gout_s[...].astype(BF16)


def attend_back_kernel(rows, first_pass, exchanges, grid_steps, *refs):
    count = len(exchanges)
    qe_ref, ge_ref, k_ref, v_ref = refs[:4]
    refs = refs[4:]
    if first_pass:
        gives, sums_ref, refs = refs[:count], refs[count], refs[count + 1 :]
        dq_ref, dk_ref, dv_ref = refs[:3]
        shards, all_ref, refs = refs[3 : 3 + count], refs[3 + count], refs[4 + count :]
        all_s, all_sends, all_recvs = refs[-3:]
    else:
        dq_in, shards, refs = refs[0], refs[1 : 1 + count], refs[1 + count :]
        dq_ref, dk_ref, dv_ref = refs[:3]
        fulls, refs = refs[3 : 3 + count], refs[3 + count :]
    dq_s, refs = refs[0], refs[1:]
    states = []
    for index, exchange in enumerate(exchanges):
        sends, recvs = refs[1], refs[2]
        if first_pass:
            got = refs[3 : 3 + exchange.all_levels]
            states.append((gives[index], refs[0], got, sends, recvs))
            refs = refs[3 + exchange.all_levels :]
        else:
            states.append((refs[0], sends, recvs))
            refs = refs[3:]
    per_step = k_ref.shape[2] // rows
    static_slots = grid_steps * per_step
    first_slot = (pl.program_id(0) * pl.num_programs(1) + pl.program_id(1)) * per_step
    levels = exchanges[0].all_levels if first_pass else exchanges[0].levels

    def all_copy(level):
        index = 0
        for lower in range(len(exchanges[0].bits)):
            index = index + exchanges[0].place(lower)[0] * (1 << lower)
        if level < 0:
            return all_s.at[pl.ds(index, 1)]
        size = 1 << level
        piece = all_s.at[pl.ds((index // size) * size, size)]
        return exchanges[0].copy(piece, piece, all_sends, all_recvs, level)

    def reduce_action(order):
        if order == 0:
            exchanges[0].barrier()
            own = all_copy(-1)
            own[...] = sums_ref[...][None]
        else:
            all_copy(order - 1).wait()
        if order < levels:
            all_copy(order).start()
        else:
            all_ref[...] = all_s[...]
        for exchange, state, shard in zip(exchanges, states, shards):
            if order > 0:
                exchange.reduce_finish(order - 1, *state)
            if order < levels:
                exchange.reduce_start(order, *state)
            else:
                shard[...] = exchange.own_shard(state[1], 1)[...][0]

    def gather_action(order):
        if order == 0:
            exchanges[0].barrier()
        for exchange, state, shard in zip(exchanges, states, shards):
            if order == 0:
                exchange.own_shard(state[0], 0)[...] = shard[...][None]
            else:
                exchange.gather_finish(levels - order, *state)
            if order < levels:
                exchange.gather_start(levels - 1 - order, *state)
        if order == levels:
            copies = [
                pltpu.make_async_copy(state[0], full, refs[index])
                for index, (state, full) in enumerate(zip(states, fulls))
            ]
            for copy in copies:
                copy.start()
            for copy in copies:
                copy.wait()

    action = reduce_action if first_pass else gather_action
    weights = [5.0, 10.0, 9.0, 6.0] + [4.0] * levels
    weights = weights[:levels] if first_pass else weights[:levels][::-1]
    marks, total = [0], 0.0
    for weight in weights:
        total += weight
        marks.append(total)
    last = static_slots - (2 if first_pass else 1)
    marks = [min(int(mark * last / total + 0.5), last) for mark in marks]

    dq_s[...] = jnp.zeros_like(dq_s) if first_pass else dq_in[0, 0].T

    def block(index, carry):
        for order, mark in enumerate(marks[:-1]):
            pl.when(first_slot + index == mark)(functools.partial(action, order))
        at = pl.ds(pl.multiple_of(index * rows, rows), rows)
        keys = k_ref[0, 0, at, :]
        values = v_ref[0, 0, at, :]
        lane = lane_index(keys.shape)
        low = lane < HD
        ones = jnp.where(lane % HD < 3, 1.0, 0.0).astype(BF16)
        zero = jnp.zeros_like(keys)
        grads = []
        for head in range(2):
            own = low if head == 0 else jnp.logical_not(low)
            query = qe_ref[0, 0, head]
            grad = ge_ref[0, 0, head]
            probs = jnp.exp(dot(jnp.where(own, keys, ones), query, NT))
            grad_probs = dot(jnp.where(own, values, ones), grad, NT)
            grad_scores = (probs * grad_probs).astype(BF16)
            grads.append((dot(grad_scores, query), dot(probs.astype(BF16), grad)))
            dq_s[...] += dot(jnp.where(own, keys, zero), grad_scores, TN)
        dk_ref[0, 0, at, :] = jnp.where(low, grads[0][0], grads[1][0]).astype(BF16)
        dv_ref[0, 0, at, :] = jnp.where(low, grads[0][1], grads[1][1]).astype(BF16)
        return carry

    lax.fori_loop(0, per_step, block, 0)
    if first_pass:
        dq_ref[0, 0] = dq_s[...].T
    else:
        dq_ref[0, 0] = (dq_s[...].T * HD**-0.5).astype(BF16)
    pl.when(first_slot + per_step == static_slots)(functools.partial(action, levels))


def joining(at, read, write, wait, own_ref, got_ref, out_ref, own_s, got_s, sems):
    mine = first_step(2)
    reads = [
        pltpu.make_async_copy(own_ref, own_s, sems.at[0]),
        pltpu.make_async_copy(got_ref, got_s, sems.at[1]),
    ]
    writes = [
        pltpu.make_async_copy(own_s, out_ref.at[pl.ds(mine, 2)], sems.at[2]),
        pltpu.make_async_copy(got_s, out_ref.at[pl.ds(2 - mine, 2)], sems.at[3]),
    ]

    @pl.when(at == read)
    def _():
        for copy in reads:
            copy.start()

    @pl.when(at == write)
    def _():
        for copy in reads:
            copy.wait()
        for copy in writes:
            copy.start()

    @pl.when(at == wait)
    def _():
        for copy in writes:
            copy.wait()


def project_back_far_kernel(
    dk_ref, dv_ref, normed_ref, w_ref, own_ref, got_ref, dx_ref, gw_ref, out_ref, own_s, got_s, sems
):
    width = w_ref.shape[0]
    at = pl.program_id(0) * pl.num_programs(1) + pl.program_id(1)
    joining(at, 0, 1, 3, own_ref, got_ref, out_ref, own_s, got_s, sems)
    joined = join_heads(dk_ref, dv_ref)
    dx_ref[0, 0] = dot(joined, w_ref[:, width:], NT).astype(BF16)

    @pl.when((pl.program_id(0) == 0) & (pl.program_id(1) == 0))
    def _():
        gw_ref[...] = jnp.zeros_like(gw_ref)

    gw_ref[...] += dot(normed_ref[0, 0], joined, TN)


def weight_back_kernel(early, *refs):
    dq_ref, dk_ref, dv_ref, normed_ref, far_ref, one_ref, two_ref = refs[:7]
    gw_ref, gfc1_ref, gfc2_ref, gout_ref = refs[7:11]
    gw_s, one_s, two_s, gfc1_s, gfc2_s, gout_s, sems = refs[11:]
    at = pl.program_id(0) * pl.num_programs(1) + pl.program_id(1)
    size = gout_s.shape[0]
    blocks = gfc1_s.shape[1] // size
    reads = [
        pltpu.make_async_copy(one_ref, one_s, sems.at[0]),
        pltpu.make_async_copy(two_ref, two_s, sems.at[1]),
    ]
    writes = [
        pltpu.make_async_copy(gfc1_s, gfc1_ref, sems.at[2]),
        pltpu.make_async_copy(gfc2_s, gfc2_ref, sems.at[3]),
        pltpu.make_async_copy(gout_s, gout_ref, sems.at[4]),
    ]

    @pl.when(at == 0)
    def _():
        for copy in reads:
            copy.start()

    @pl.when(at == 1)
    def _():
        reads[0].wait()
        unstack(
            grouped(early[0]), one_s, [(gfc1_s, 0, block * size) for block in range(blocks)], size
        )
        writes[0].start()

    @pl.when(at == 2)
    def _():
        reads[1].wait()
        rest = [(gfc2_s, block * size, 0) for block in range(blocks)] + [(gout_s, 0, 0)]
        unstack(grouped(early[1]), two_s, rest, size)
        writes[1].start()
        writes[2].start()

    @pl.when(at == pl.num_programs(0) * pl.num_programs(1) - 1)
    def _():
        for copy in writes:
            copy.wait()

    step, which = pl.program_id(0), pl.program_id(1)
    width = normed_ref.shape[3]

    @pl.when((step == 0) & (which == 0))
    def _():
        gw_s[:, :width] = jnp.zeros_like(gw_s[:, :width])
        gw_s[:, width:] = far_ref[...]

    gw_s[...] += dot(normed_ref[0, 0], join_heads(dq_ref, dk_ref, dv_ref), TN)

    @pl.when((step == pl.num_programs(0) - 1) & (which == pl.num_programs(1) - 1))
    def _():
        for block in range(gw_ref.shape[0]):
            gw_ref[block] = gw_s[:, block * LANES : (block + 1) * LANES].astype(BF16)


def join_heads(*grads):
    return jnp.concatenate([ref[0, pair] for ref in grads for pair in range(ref.shape[1])], axis=-1)


class Direct:
    def __init__(self, mesh_shape, row_tiles):
        self.chips = mesh_shape["seq"] // 2
        self.peers = mesh_shape["dp"] * self.chips
        self.half = row_tiles * 8
        self.piece = -(-row_tiles // (2 * self.peers)) * 16
        self.padded = self.piece * self.peers

    def me(self):
        return lax.axis_index("dp") * self.chips + lax.axis_index("seq") // 2

    def core(self):
        return lax.axis_index("seq") % 2

    def sibling(self):
        return {"seq": lax.axis_index("seq") + 1 - 2 * self.core()}

    def peer(self, shift):
        other = (self.me() + shift) % self.peers
        device = {"dp": other // self.chips, "seq": (other % self.chips) * 2 + self.core()}
        return other, device

    def rows(self, index):
        return pl.ds(pl.multiple_of(index * self.piece, 16), self.piece)

    def barrier(self):
        semaphore = pltpu.get_barrier_semaphore()

        def signal(device):
            pl.semaphore_signal(semaphore, 1, device_id=device, device_id_type=pl.DeviceIdType.MESH)

        signal(self.sibling())

        def greet(shift, carry):
            signal(self.peer(shift)[1])
            return carry

        lax.fori_loop(1, self.peers, greet, 0)
        pl.semaphore_wait(semaphore, self.peers)

    def copy(self, source, target, send, recv, device):
        return pltpu.make_async_remote_copy(
            src_ref=source,
            dst_ref=target,
            send_sem=send,
            recv_sem=recv,
            device_id=device,
            device_id_type=pl.DeviceIdType.MESH,
        )

    def each_peer(self, do):
        def one(shift, carry):
            do(shift)
            return carry

        lax.fori_loop(1, self.peers, one, 0)


def tail_kernel(direct, remote, *refs):
    give_ref, own_x, sib_x, mod_ref, lead_ref, gm_ref, dq_ref, dk_ref, dv_ref, w_ref = refs[:10]
    others = refs[10 : 10 + remote]
    grad_ref, got_ref, full_ref, all_ref = refs[10 + remote : 14 + remote]
    sums_s, other_s, got_s, sum_s, core_s, pieces_s, full_s, all_s = refs[14 + remote : 22 + remote]
    core_sems, piece_sems, back_sems, all_sems, grad_sems, local_sem = refs[22 + remote :]
    step, half = pl.program_id(0), pl.program_id(1)
    width = own_x.shape[2]
    core, me = direct.core(), direct.me()

    core_copy = direct.copy(
        give_ref.at[1 - core], core_s, core_sems.at[0], core_sems.at[1], direct.sibling()
    )

    def piece_copy(shift):
        other, device = direct.peer(shift)
        return direct.copy(
            sum_s.at[direct.rows(other)],
            pieces_s.at[shift],
            piece_sems.at[0, shift],
            piece_sems.at[1, shift],
            device,
        )

    def full_copy(shift, arriving):
        _, device = direct.peer(shift)
        owner = (me + direct.peers - shift) % direct.peers if arriving else me
        place = full_s.at[core, direct.rows(owner)]
        return direct.copy(place, place, back_sems.at[0, shift], back_sems.at[1, shift], device)

    def sums_copy(shift, arriving):
        _, device = direct.peer(shift)
        owner = (me + direct.peers - shift) % direct.peers if arriving else me
        place = all_s.at[core, owner]
        return direct.copy(place, place, all_sems.at[0, shift], all_sems.at[1, shift], device)

    def side_copy(values, which, side):
        place = values.at[side]
        return direct.copy(
            place, place, core_sems.at[which], core_sems.at[which + 1], direct.sibling()
        )

    def grad_copy(index):
        return direct.copy(
            other_s.at[index],
            got_s.at[index],
            grad_sems.at[0, index],
            grad_sems.at[1, index],
            direct.sibling(),
        )

    @pl.when((step == 0) & (half == 0))
    def _():
        direct.barrier()
        core_copy.start()
        sums_s[...] = jnp.zeros_like(sums_s)

    @pl.when((step == 0) & (half == 1))
    def _():
        core_copy.wait()
        real = core_s.shape[0]
        sum_s[:real] = (give_ref[core].astype(F32) + core_s[...].astype(F32)).astype(BF16)
        if direct.padded > real:
            sum_s[real:] = jnp.zeros_like(sum_s[real:])
        direct.each_peer(lambda shift: piece_copy(shift).start())

    x = jnp.where(half == 0, own_x[0], sib_x[0]).astype(F32)
    scale = mod_ref[pl.ds(step, 1), width : 2 * width]
    xhat, inverse = normalize(x)
    gy = dot(join_heads(dq_ref, dk_ref, dv_ref), w_ref[...], NT)
    for other in others:
        gy = gy + other[0, 0].astype(F32)
    grad = (gm_ref[0, 0] + norm_back(gy * (1.0 + scale), xhat, inverse)).astype(BF16)

    @pl.when(half == 0)
    def _():
        grad_ref[0] = grad

    @pl.when(half == 1)
    def _():
        other_s[step] = grad
        grad_copy(step).start()

    for kind, value in enumerate((gy, gy * xhat)):
        total = jnp.sum(value, axis=0, keepdims=True)
        for index in range(width // LANES):
            place = pl.ds((kind * 2 + step) * (width // LANES) + index, 1)
            sums_s[place, :] += total[:, index * LANES : (index + 1) * LANES]

    @pl.when((step == 1) & (half == 1))
    def _():
        for index in range(2):
            chosen = lane_index((1, LANES)) == lead_ref[0, first_step(2) + index]
            sums_s[12 + index : 13 + index, :] = jnp.where(chosen, 1.0, 0.0)
        all_s[core, me] = sums_s[...].astype(BF16)
        direct.each_peer(lambda shift: sums_copy(shift, False).start())
        direct.each_peer(lambda shift: piece_copy(shift).wait())

        def add(shift, total):
            return total + pieces_s[shift].astype(F32)

        total = lax.fori_loop(1, direct.peers, add, sum_s[direct.rows(me)].astype(F32))
        full_s[core, direct.rows(me)] = total.astype(BF16)
        direct.each_peer(lambda shift: full_copy(shift, False).start())

        def arrived(shift):
            full_copy(shift, False).wait_send()
            full_copy(shift, True).wait_recv()
            sums_copy(shift, False).wait_send()
            sums_copy(shift, True).wait_recv()

        direct.each_peer(arrived)
        side_copy(full_s, 2, core).start()
        side_copy(all_s, 4, core).start()
        for index in range(2):
            grad_copy(index).wait()
        side_copy(full_s, 2, core).wait_send()
        side_copy(full_s, 2, 1 - core).wait_recv()
        side_copy(all_s, 4, core).wait_send()
        side_copy(all_s, 4, 1 - core).wait_recv()
        outs = [(got_s, got_ref), (full_s, full_ref), (all_s, all_ref)]
        copies = [
            pltpu.make_async_copy(source, target, local_sem.at[index])
            for index, (source, target) in enumerate(outs)
        ]
        for copy in copies:
            copy.start()
        for copy in copies:
            copy.wait()


def unstack(at, full_ref, targets, rows):
    row, end = 0, rows * len(targets)
    while row < end:
        group, inside, left = at(row)
        block, place = divmod(row, rows)
        count = min(left, rows - place)
        target, first_row, first_column = targets[block]
        columns = slice(first_column, first_column + full_ref.shape[2])
        value = full_ref[group, inside : inside + count, :].astype(F32)
        target[first_row + place : first_row + place + count, columns] = value
        row += count


def grouped(exchange):
    def at(row):
        group, inside = divmod(row, exchange.real)
        return group, inside, exchange.real - inside

    return at


def spread_leads(grads, step_of, table_rows):
    count = grads.shape[0]
    part = min(count, 512)
    row = lax.broadcasted_iota(jnp.int32, (part, part), 0)
    column = lane_index((part, part))
    chosen = (row // 16 == column // 16) & (row % 16 == 12 + step_of(column % 16))
    spread = jnp.where(chosen, 1.0, 0.0).astype(BF16)
    leads = [
        dot(grads[start : start + part, :LANES], spread, TN)[:table_rows]
        for start in range(0, count, part)
    ]
    return jnp.concatenate(leads, axis=-1)


def final_kernel(direct, *refs):
    early_sums, late_sums, emb_ref, ada_ref, late_ref, own_ref, got_ref = refs[:7]
    grad_out, gemb_ref, gada_out, gbada_ref, gqkv_out = refs[7:12]
    gada_s, gqkv_s, late_s, own_s, got_s, sems = refs[12:]
    size = emb_ref.shape[1]
    mine = first_step(2)
    pairs = [(late_ref, late_s), (own_ref, own_s), (got_ref, got_s)]
    reads = [
        pltpu.make_async_copy(source, target, sems.at[index])
        for index, (source, target) in enumerate(pairs)
    ]
    for read in reads:
        read.start()
    copies = []

    def start(source, target):
        copy = pltpu.make_async_copy(source, target, sems.at[3 + len(copies)])
        copy.start()
        copies.append(copy)

    def halved(row):
        group, inside = divmod(row, direct.half)
        return group, inside, direct.half - inside

    columns = gqkv_s.shape[1] // LANES
    reads[0].wait()
    unstack(halved, late_s, [(gqkv_s, 0, block * LANES) for block in range(columns)], size)
    start(gqkv_s, gqkv_out)
    reads[1].wait()
    start(own_s, grad_out.at[pl.ds(mine, 2)])
    reads[2].wait()
    start(got_s, grad_out.at[pl.ds(2 - mine, 2)])

    table_rows = emb_ref.shape[0]
    table = emb_ref[...].astype(F32)
    gate = jax.nn.sigmoid(table)
    slope = gate * (1.0 + table * (1.0 - gate))
    table_act = (table * gate).astype(BF16)
    total = jnp.zeros((table_rows, size), F32)

    def one_piece(grads, leads, place, first):
        chosen = jnp.where(place, leads, 0.0).astype(BF16)
        acts = dot(table_act, chosen, TN).astype(BF16)
        where = slice(first, first + grads.shape[1])
        gada_s[:, where] = dot(acts, grads)
        by_lead = dot(chosen, grads)
        gbada_ref[where] = jnp.sum(by_lead, axis=0)
        high = by_lead.astype(BF16)
        low = (by_lead - high.astype(F32)).astype(BF16)
        return dot(high, ada_ref[:, where], NT) + dot(low, ada_ref[:, where], NT)

    grads = early_sums[...]
    leads = spread_leads(grads, lambda row: row % 2, table_rows)
    row = lane_index((1, grads.shape[0])) % 16
    for index in range(4):
        total += one_piece(grads, leads, row // 2 == index, (2 + index) * size)
    grads = late_sums[...]
    parts = size // LANES
    leads = spread_leads(grads, lambda row: (row // parts) % 2, table_rows)
    row = lane_index((1, grads.shape[0])) % 16
    for index in range(2):
        for part in range(parts):
            place = (row // (2 * parts) == index) & (row % parts == part)
            total += one_piece(grads, leads, place, index * size + part * LANES)
    gemb_ref[...] = total * slope
    start(gada_s, gada_out)
    for copy in copies:
        copy.wait()


def local(
    mesh_shape, inputs, cotangent, counts, lead_steps, emb_table, w_ada, b_ada, w_qkv, w_out, w_fc1, w_fc2
):
    slots, items, patches, width = inputs.shape
    chips = mesh_shape["seq"] // 2
    blocks = w_fc1.shape[1] // w_fc1.shape[0]
    steps = slots * items // 2
    hidden_width = w_fc1.shape[1]
    pairs = width // LANES
    rows = 2 * patches
    remote = 2 * (chips - 1)
    far_rows = remote * patches
    spot = lax.axis_index("seq")
    core = lax.rem(spot, 2)
    devices = 2 * chips

    def send(values, shift, cross):
        pairs_list = []
        for source in range(devices):
            chip, side = source // 2, source % 2
            pairs_list.append((source, ((chip + shift) % chips) * 2 + (1 - side if cross else side)))
        return lax.ppermute(values, "seq", pairs_list)

    x_steps = inputs.reshape(2, steps, patches, width)
    ct_steps = cotangent.reshape(2, steps, patches, width)
    own_x = lax.dynamic_index_in_dim(x_steps, core, 0, keepdims=False)
    other_x = lax.dynamic_index_in_dim(x_steps, 1 - core, 0, keepdims=False)
    own_ct = lax.dynamic_index_in_dim(ct_steps, core, 0, keepdims=False)
    other_ct = lax.dynamic_index_in_dim(ct_steps, 1 - core, 0, keepdims=False)
    sib_x = send(other_x, 0, True)
    far_x = []
    for step in range(steps):
        some = slice(step, step + 1)
        for shift in range(1, chips):
            far_x.append(send(own_x[some], shift, False))
            far_x.append(send(other_x[some], shift, True))
    sib_ct = send(other_ct, 0, True)

    step_block = pl.BlockSpec((1, patches, width), lambda j, i: (j, 0, 0))
    patch_block = pl.BlockSpec((1, 1, patches, width), lambda j, i: (j, i, 0, 0))

    def head_rows(count):
        return pl.BlockSpec((1, 1, count, LANES), lambda j, p: (j, p, 0, 0))

    def of_step(*shape):
        return pl.BlockSpec((1,) + shape, lambda j, p: (j,) + (0,) * len(shape))

    both_heads = pl.BlockSpec((1, 1, 2, rows, LANES), lambda j, p: (j, p, 0, 0, 0))
    piece = min(256, rows)
    near_work = 4 * steps * pairs * 2 * rows * LANES * rows
    near_heads = jax.ShapeDtypeStruct((steps, pairs, rows, LANES), BF16)
    mod, n1, q, k, v, acc = call(
        functools.partial(near_kernel, piece),
        "near",
        (steps, pairs),
        [scalars(), whole(emb_table.shape), whole(w_ada.shape), whole((1, 6 * width))]
        + [step_block] * 2
        + [whole(w_qkv.shape)],
        [whole((16, 6 * width)), of_step(rows, width)]
        + [of_step(pairs, rows, LANES)] * 3
        + [both_heads],
        [
            jax.ShapeDtypeStruct((16, 6 * width), F32),
            jax.ShapeDtypeStruct((steps, rows, width), BF16),
            near_heads,
            near_heads,
            near_heads,
            jax.ShapeDtypeStruct((steps, pairs, 2, rows, LANES), F32),
        ],
        [pltpu.VMEM((2, rows, LANES), BF16)],
        flops=near_work + 6 * steps * rows * width * width,
        exps=steps * pairs * 2 * rows * rows,
    )(lead_steps, emb_table, w_ada, b_ada.reshape(1, -1), own_x, sib_x, w_qkv)

    def far(step, before):
        some_x = far_x[step * remote : (step + 1) * remote]

        def at_step(*shape):
            return pl.BlockSpec((1,) + shape, lambda p: (step,) + (0,) * len(shape))

        def at_pair(*shape):
            return pl.BlockSpec((1, 1) + shape, lambda p: (step, p) + (0,) * len(shape))

        operands = [*some_x, mod, w_qkv, q, k, v, acc]
        return call(
            functools.partial(far_kernel, piece, step, remote),
            "far",
            (pairs,),
            [whole((1, patches, width))] * remote
            + [whole(mod.shape), whole(w_qkv.shape)]
            + [at_pair(rows, LANES)] * 3
            + [at_pair(2, rows, LANES)]
            + [pl.BlockSpec(memory_space=pl.ANY)] * len(before),
            [at_step(far_rows, width)]
            + [at_step(pairs, far_rows, LANES)] * 2
            + [at_pair(rows, LANES), at_pair(2, rows, LANES)],
            [
                jax.ShapeDtypeStruct((steps, far_rows, width), BF16),
                jax.ShapeDtypeStruct((steps, pairs, far_rows, LANES), BF16),
                jax.ShapeDtypeStruct((steps, pairs, far_rows, LANES), BF16),
                jax.ShapeDtypeStruct((steps, pairs, rows, LANES), F32),
                jax.ShapeDtypeStruct((steps, pairs, 2, rows, LANES), BF16),
            ],
            [pltpu.VMEM((2, far_rows, LANES), BF16), pltpu.VMEM((rows, LANES), F32)],
            flops=near_work // 2,
            exps=pairs * 2 * rows * far_rows,
            aliases={len(operands) + index: index for index in range(len(before))},
        )(*operands, *before)

    far_results = []
    for step in range(steps):
        far_results = far(step, far_results)
    n1r, kr, vr, o, qe = far_results

    block_rows = min(256, patches)
    outs = call(
        functools.partial(patch_kernel, block_rows, hidden_width),
        "patchwise",
        (steps, 2),
        [scalars()] * 2
        + [step_block] * 4
        + [
            whole(mod.shape),
            pl.BlockSpec((1, pairs, patches, LANES), lambda j, i: (j, 0, i, 0)),
            whole(w_out.shape),
            whole(w_fc1.shape),
            whole(w_fc2.shape),
        ],
        [
            step_block,
            step_block,
            patch_block,
            pl.BlockSpec((1, pairs, 2, patches, LANES), lambda j, i: (j, 0, 0, i, 0)),
            whole((16, width)),
            whole((blocks, width, width)),
            whole((blocks + 1, width, width)),
        ],
        [
            jax.ShapeDtypeStruct((steps, patches, width), BF16),
            jax.ShapeDtypeStruct((steps, patches, width), BF16),
            jax.ShapeDtypeStruct((steps, 2, patches, width), F32),
            jax.ShapeDtypeStruct((steps, pairs, 2, rows, LANES), BF16),
            jax.ShapeDtypeStruct((16, width), BF16),
            jax.ShapeDtypeStruct((blocks, width, width), BF16),
            jax.ShapeDtypeStruct((blocks + 1, width, width), BF16),
        ],
        [pltpu.VMEM((patches, hidden_width), BF16)] * 2
        + [pltpu.VMEM((patches, width), BF16)] * 4
        + [
            pltpu.VMEM((width, width), F32),
            pltpu.VMEM((width, hidden_width), F32),
            pltpu.VMEM((width, hidden_width), F32),
            pltpu.VMEM((16, width), F32),
        ],
        flops=6 * steps * rows * width * (2 * hidden_width + width),
        moved=steps * rows * width * 20,
        exps=2 * steps * rows * hidden_width,
    )(counts, lead_steps, own_x, sib_x, own_ct, sib_ct, mod, o, w_out, w_fc1, w_fc2)
    final_own, final_sib, gm, ge, sums, stack_one, stack_two = outs
    final_got = send(final_sib, 0, True)
    early = [Exchange(mesh_shape, blocks * width // 16, 0), Exchange(mesh_shape, (blocks + 1) * width // 16, 1)]
    gives = [g.reshape(e.groups, e.real, width) for e, g in zip(early, (stack_one, stack_two))]

    def attend_back(keys, values, extra, first, name):
        count = keys.shape[2]
        in_specs = [both_heads] * 2 + [head_rows(count)] * 2
        out_specs = [head_rows(rows), head_rows(count), head_rows(count)]
        out_shape = [
            jax.ShapeDtypeStruct((steps, pairs, rows, LANES), F32 if first else BF16),
            jax.ShapeDtypeStruct((steps, pairs, count, LANES), BF16),
            jax.ShapeDtypeStruct((steps, pairs, count, LANES), BF16),
        ]
        scratch = [pltpu.VMEM((LANES, rows), F32)]
        if not first:
            in_specs += [head_rows(rows)]
        for exchange in early:
            shape = (exchange.groups, exchange.padded, width)
            shard = (exchange.shard, width)
            sems = [pltpu.SemaphoreType.DMA((exchange.all_levels,))] * 2
            if first:
                in_specs += [whole((exchange.groups, exchange.real, width))]
                out_specs += [whole(shard)]
                out_shape += [jax.ShapeDtypeStruct(shard, BF16)]
                half = (exchange.groups // 2, exchange.padded, width)
                scratch += [pltpu.VMEM(half, BF16)] + sems + exchange.receive_scratch(width)
            else:
                in_specs += [whole(shard)]
                out_specs += [pl.BlockSpec(memory_space=pl.ANY)]
                out_shape += [jax.ShapeDtypeStruct(shape, BF16)]
                scratch += [pltpu.VMEM(shape, BF16)] + sems
        if first:
            every = (mesh_shape["dp"] * mesh_shape["seq"], 16, width)
            in_specs += [whole(sums.shape)]
            out_specs += [whole(every)]
            out_shape += [jax.ShapeDtypeStruct(every, BF16)]
            sems = [pltpu.SemaphoreType.DMA((early[0].all_levels,))] * 2
            scratch += [pltpu.VMEM(every, BF16)] + sems
        else:
            scratch += [pltpu.SemaphoreType.DMA] * len(early)
        return call(
            functools.partial(attend_back_kernel, min(512, count), first, early, steps * pairs),
            name,
            (steps, pairs),
            in_specs,
            out_specs,
            out_shape,
            scratch,
            flops=10 * steps * pairs * 2 * rows * count * LANES,
            exps=steps * pairs * 2 * rows * count,
            collective=1 if first else 2,
        )(qe, ge, keys, values, *extra)

    grad_block = pl.BlockSpec((1, pairs, patches, LANES), lambda j, i: (j, 0, i, 0))
    hbm = pl.BlockSpec(memory_space=pl.ANY)

    dq_part, dkr, dvr, shard_one, shard_two, early_all = attend_back(
        kr, vr, [*gives, sums], True, "attend_back_far"
    )
    dx_far, gw_part, outputs = call(
        project_back_far_kernel,
        "project_back_far",
        (steps, remote),
        [grad_block] * 2 + [patch_block, whole(w_qkv.shape), hbm, hbm],
        [patch_block, whole((width, 2 * width)), hbm],
        [
            jax.ShapeDtypeStruct((steps, remote, patches, width), BF16),
            jax.ShapeDtypeStruct((width, 2 * width), F32),
            jax.ShapeDtypeStruct((2 * steps, patches, width), BF16),
        ],
        [pltpu.VMEM((steps, patches, width), BF16)] * 2 + [pltpu.SemaphoreType.DMA((4,))],
        flops=4 * steps * far_rows * width * 2 * width,
        moved=steps * far_rows * width * 8,
    )(dkr, dvr, n1r.reshape(steps, remote, patches, width), w_qkv, final_own, final_got)
    dx_got = [send(dx_far[:, 2 * r - 2 : 2 * r], -r, False) for r in range(1, chips)]
    dq, dk, dv, *early_sums = attend_back(
        k, v, [dq_part, shard_one, shard_two], False, "attend_back_near"
    )
    columns = w_qkv.shape[1] // LANES
    early_weights = (w_fc1, w_fc2, w_out)
    give_late, g_fc1, g_fc2, g_out = call(
        functools.partial(weight_back_kernel, early),
        "weight_back",
        (steps, 2),
        [grad_block] * 3 + [patch_block, whole(gw_part.shape), hbm, hbm],
        [whole((columns, width, LANES))] + [hbm] * 3,
        [jax.ShapeDtypeStruct((columns, width, LANES), BF16)]
        + [jax.ShapeDtypeStruct(w.shape, F32) for w in early_weights],
        [pltpu.VMEM((width, columns * LANES), F32)]
        + [pltpu.VMEM(value.shape, BF16) for value in early_sums]
        + [pltpu.VMEM(w.shape, F32) for w in early_weights]
        + [pltpu.SemaphoreType.DMA((5,))],
        flops=2 * steps * rows * width * 3 * width,
        moved=steps * rows * width * 8,
    )(dq, dk, dv, n1.reshape(steps, 2, patches, width), gw_part, *early_sums)

    direct = Direct(mesh_shape, columns * width // 16)
    full_shape = (2, direct.padded, LANES)
    late_all_shape = (2, direct.peers, 16, LANES)
    grad_own, grad_got, late_sum, late_all = call(
        functools.partial(tail_kernel, direct, len(dx_got)),
        "tail",
        (steps, 2),
        [whole((2, direct.half, LANES)), step_block, step_block, whole(mod.shape), scalars()]
        + [patch_block]
        + [grad_block] * 3
        + [whole(w_qkv.shape)]
        + [patch_block] * len(dx_got),
        [step_block, hbm, hbm, hbm],
        [
            jax.ShapeDtypeStruct((steps, patches, width), BF16),
            jax.ShapeDtypeStruct((steps, patches, width), BF16),
            jax.ShapeDtypeStruct(full_shape, BF16),
            jax.ShapeDtypeStruct(late_all_shape, BF16),
        ],
        [
            pltpu.VMEM((16, LANES), F32),
            pltpu.VMEM((steps, patches, width), BF16),
            pltpu.VMEM((steps, patches, width), BF16),
            pltpu.VMEM((direct.padded, LANES), BF16),
            pltpu.VMEM((direct.half, LANES), BF16),
            pltpu.VMEM((direct.peers, direct.piece, LANES), BF16),
            pltpu.VMEM(full_shape, BF16),
            pltpu.VMEM(late_all_shape, BF16),
            pltpu.SemaphoreType.DMA((6,)),
            pltpu.SemaphoreType.DMA((2, direct.peers)),
            pltpu.SemaphoreType.DMA((2, direct.peers)),
            pltpu.SemaphoreType.DMA((2, direct.peers)),
            pltpu.SemaphoreType.DMA((2, steps)),
            pltpu.SemaphoreType.DMA((3,)),
        ],
        flops=2 * steps * rows * width * 3 * width,
        collective=3,
    )(
        give_late.reshape(2, direct.half, LANES),
        own_x,
        sib_x,
        mod,
        lead_steps,
        gm,
        dq,
        dk,
        dv,
        w_qkv,
        *dx_got,
    )

    early_all = early_all.reshape(-1, width)
    late_all = late_all.reshape(-1, LANES)
    small = [early_all, late_all, emb_table, w_ada]
    large = [late_sum, grad_own, grad_got]
    out_shapes = [(slots * items, patches, width), emb_table.shape, w_ada.shape, b_ada.shape, w_qkv.shape]
    grad_inputs, g_emb, g_ada, g_bada, g_qkv = call(
        functools.partial(final_kernel, direct),
        "final",
        (),
        [whole(value.shape) for value in small] + [hbm] * len(large),
        [hbm, whole(emb_table.shape), hbm, whole(b_ada.shape), hbm],
        [
            jax.ShapeDtypeStruct(shape, F32 if index else BF16)
            for index, shape in enumerate(out_shapes)
        ],
        [pltpu.VMEM(w.shape, F32) for w in (w_ada, w_qkv)]
        + [pltpu.VMEM(value.shape, BF16) for value in large]
        + [pltpu.SemaphoreType.DMA((7,))],
        flops=2 * early_all.shape[0] * width * 6 * width,
        moved=6 * w_ada.size,
    )(*small, *large)
    return (
        outputs.reshape(inputs.shape),
        grad_inputs.reshape(inputs.shape),
        g_emb,
        g_ada,
        g_bada,
        g_qkv,
        g_out,
        g_fc1,
        g_fc2,
    )


def solution(mesh):
    tokens = P(None, "dp", "seq", None)
    return jax.shard_map(
        functools.partial(local, dict(mesh.shape)),
        mesh=mesh,
        in_specs=(tokens, tokens, P("dp"), P("dp", None)) + (P(),) * 7,
        out_specs=(tokens, tokens) + (P(),) * 7,
        check_vma=False,
    )
```

```python
import functools

import jax
import jax.numpy as jnp
from jax import lax
from jax.experimental import pallas as pl
from jax.experimental.pallas import tpu as pltpu
from jax.sharding import PartitionSpec as P

HD = 64
LANES = 128
EPSILON = 1e-06
LOG2E = 1.4426950408889634
NN = (((1,), (0,)), ((), ()))
NT = (((1,), (1,)), ((), ()))
TN = (((0,), (0,)), ((), ()))
F32 = jnp.float32
BF16 = jnp.bfloat16
VMEM_BYTES = 24 * 1024 * 1024


def dot(a, b, dims=NN):
    return lax.dot_general(a, b, dims, preferred_element_type=F32)


def call(
    body,
    name,
    grid,
    in_specs,
    out_specs,
    out_shape,
    scratch=(),
    flops=0,
    moved=0,
    exps=0,
    collective=None,
    aliases=None,
):
    return pl.pallas_call(
        body,
        name=name,
        grid=grid,
        in_specs=in_specs,
        out_specs=out_specs,
        out_shape=out_shape,
        scratch_shapes=list(scratch),
        input_output_aliases=aliases or {},
        cost_estimate=pl.CostEstimate(flops=flops, bytes_accessed=moved, transcendentals=exps),
        compiler_params=pltpu.CompilerParams(
            vmem_limit_bytes=VMEM_BYTES,
            collective_id=collective,
            has_side_effects=collective is not None,
        ),
    )


def whole(shape):
    return pl.BlockSpec(shape, lambda *_: (0,) * len(shape))


def scalars():
    return pl.BlockSpec(memory_space=pltpu.SMEM)


def lane_index(shape):
    return lax.broadcasted_iota(jnp.int32, shape, 1)


def first_step(steps):
    return lax.rem(lax.axis_index("seq"), 2) * steps


def normalize(values):
    center = values - jnp.mean(values, axis=-1, keepdims=True)
    spread = jnp.mean(center * center, axis=-1, keepdims=True)
    inverse = lax.rsqrt(spread + EPSILON)
    return center * inverse, inverse


def norm_back(grad, xhat, inverse):
    first = jnp.mean(grad, axis=-1, keepdims=True)
    second = jnp.mean(grad * xhat, axis=-1, keepdims=True)
    return inverse * (grad - first - xhat * second)


def pick(refs, which):
    value = refs[0][0]
    for index in range(1, len(refs)):
        value = jnp.where(which == index, refs[index][0], value)
    return value


class Exchange:
    def __init__(self, mesh_shape, row_tiles, turn=0):
        bits = {"seq": [], "dp": []}
        for axis in bits:
            bit = 1
            while bit < mesh_shape[axis]:
                bits[axis].append((axis, bit))
                bit *= 2
        turned = bits["dp"][turn:] + bits["dp"][:turn]
        self.bits = bits["seq"][:1] + turned + bits["seq"][1:]
        self.all_levels = len(self.bits)
        self.levels = 1 + len(turned)
        self.even = 0
        while self.even < self.levels and row_tiles % 2 == 0:
            row_tiles //= 2
            self.even += 1
        unit = 2 ** (self.levels - self.even)
        self.groups = 2**self.even
        self.real = row_tiles * 16
        self.padded = -(-row_tiles // unit) * unit * 16
        self.shard = self.padded // unit

    def sizes(self, level):
        if level < self.even:
            return (self.groups >> (level + 1), self.real)
        return (1, self.padded >> (level - self.even + 1))

    def receive_scratch(self, width):
        last = self.levels - 1
        return [
            pltpu.VMEM(self.sizes(min(level, last)) + (width,), BF16)
            for level in range(self.all_levels)
        ]

    def place(self, level):
        axis, bit = self.bits[level]
        here = lax.axis_index(axis)
        value = (here // bit) % 2
        return value, {axis: here + bit * (1 - 2 * value)}

    def spot(self, level, first, flip):
        group, row = 0, 0
        for index in range(first, level + 1):
            value, _ = self.place(index)
            if flip and index == level:
                value = 1 - value
            if index < self.even:
                group = group + value * (self.groups >> (index + 1))
            else:
                row = row + value * (self.padded >> (index - self.even + 1))
        if level >= self.even:
            row = pl.multiple_of(row, 16)
        count, rows = self.sizes(level)
        return pl.ds(group, count), pl.ds(row, rows)

    def barrier(self):
        semaphore = pltpu.get_barrier_semaphore()
        for level in range(self.all_levels):
            _, partner = self.place(level)
            pl.semaphore_signal(
                semaphore, inc=1, device_id=partner, device_id_type=pl.DeviceIdType.MESH
            )
        pl.semaphore_wait(semaphore, self.all_levels)

    def copy(self, source, target, sends, recvs, level):
        _, partner = self.place(level)
        return pltpu.make_async_remote_copy(
            src_ref=source,
            dst_ref=target,
            send_sem=sends.at[level],
            recv_sem=recvs.at[level],
            device_id=partner,
            device_id_type=pl.DeviceIdType.MESH,
        )

    def reduce_copy(self, level, start_ref, acc_ref, got, sends, recvs):
        if level >= self.levels:
            return self.copy(self.own_shard(acc_ref, 1), got[level], sends, recvs, level)
        groups, rows = self.spot(level, min(level, 1), True)
        source = start_ref if level == 0 else acc_ref
        return self.copy(source.at[groups, rows], got[level], sends, recvs, level)

    def reduce_start(self, level, *refs):
        self.reduce_copy(level, *refs).start()

    def reduce_finish(self, level, start_ref, acc_ref, got, sends, recvs):
        self.reduce_copy(level, start_ref, acc_ref, got, sends, recvs).wait()
        if level >= self.levels:
            own = self.own_shard(acc_ref, 1)
            own[...] = (own[...].astype(F32) + got[level][...].astype(F32)).astype(BF16)
            return
        count, rows = self.sizes(level)
        groups, spots = self.spot(level, min(level, 1), False)
        if level == 0:
            target_groups, target_rows = pl.ds(0, count), pl.ds(0, rows)
            if self.padded > self.real:
                acc_ref[:, self.real :, :] = jnp.zeros_like(acc_ref[:, self.real :, :])
        else:
            target_groups, target_rows = groups, spots
        source = start_ref if level == 0 else acc_ref

        def add(index, carry):
            one = pl.ds(groups.start + index, 1)
            to = pl.ds(target_groups.start + index, 1)
            value = source[one, spots, :].astype(F32) + got[level][pl.ds(index, 1)].astype(F32)
            acc_ref[to, target_rows, :] = value.astype(BF16)
            return carry

        lax.fori_loop(0, count, add, 0)

    def own_shard(self, ref, first):
        if self.levels > self.even:
            return ref.at[self.spot(self.levels - 1, first, False)]
        groups, _ = self.spot(self.levels - 1, first, False)
        return ref.at[groups, pl.ds(0, self.shard)]

    def gather_copy(self, level, full_ref, sends, recvs):
        piece = full_ref.at[self.spot(level, 0, False)]
        return self.copy(piece, piece, sends, recvs, level)

    def gather_start(self, level, *refs):
        self.gather_copy(level, *refs).start()

    def gather_finish(self, level, *refs):
        self.gather_copy(level, *refs).wait()


def modulation(lead_ref, emb_ref, ada_ref, bias_ref):
    shape = (16, emb_ref.shape[0])
    rows = lax.broadcasted_iota(jnp.int32, shape, 0)
    columns = lane_index(shape)
    onehot = jnp.zeros(shape, F32)
    for step in range(2):
        lead = lead_ref[0, first_step(2) + step]
        onehot = jnp.where((rows == step) & (columns == lead), 1.0, onehot)
    condition = dot(onehot.astype(BF16), emb_ref[...])
    active = (condition * jax.nn.sigmoid(condition)).astype(BF16)
    return dot(active, ada_ref[...]) + bias_ref[...].astype(F32)


def project(x_refs, mod_ref, step, w_ref, normed_ref, head_refs):
    width = w_ref.shape[0]
    patches = x_refs[0].shape[1]
    rows = min(256, patches)
    shift = mod_ref[pl.ds(step, 1), 0:width]
    scale = mod_ref[pl.ds(step, 1), width : 2 * width]
    queries = len(head_refs) == 3
    for index, x_ref in enumerate(x_refs):

        def block(count, carry):
            start = pl.multiple_of(count * rows, rows)
            at = pl.ds(pl.multiple_of(index * patches + start, rows), rows)
            xhat, _ = normalize(x_ref[0, pl.ds(start, rows), :].astype(F32))
            normed = (xhat * (1.0 + scale) + shift).astype(BF16)
            normed_ref[0, at, :] = normed
            for part, head_ref in enumerate(head_refs):
                first = (part + (0 if queries else 1)) * width
                projected = dot(normed, w_ref[:, first : first + width])
                if queries and part == 0:
                    projected = projected.astype(BF16).astype(F32) * HD**-0.5
                projected = projected.astype(BF16)
                for pair in range(width // LANES):
                    head_ref[0, pair, at, :] = projected[:, pair * LANES : (pair + 1) * LANES]
            return carry

        lax.fori_loop(0, patches // rows, block, 0, unroll=True)


def with_ones(values):
    low = lane_index(values.shape) < HD
    one = jnp.ones_like(values)
    return jnp.where(low, values, one), jnp.where(low, one, values)


def exponentials(query, keys_ref, pair, width):
    count = keys_ref.shape[2]
    width = min(width, count)
    return jnp.concatenate(
        [
            jnp.exp(dot(query, keys_ref[0, pair, start : start + width, :], NT)).astype(BF16)
            for start in range(0, count, width)
        ],
        axis=-1,
    )


def masked(values):
    low = lane_index(values.shape) < HD
    zero = jnp.zeros_like(values)
    return jnp.where(low, values, zero), jnp.where(low, zero, values)


def near_kernel(rows, *refs):
    lead_ref, emb_ref, ada_ref, bias_ref, own_x, sib_x, w_ref = refs[:7]
    mod_ref, normed_ref, q_ref, k_ref, v_ref, acc_ref, ext_ref = refs[7:]
    step, pair = pl.program_id(0), pl.program_id(1)

    @pl.when((step == 0) & (pair == 0))
    def _():
        mod_ref[...] = modulation(lead_ref, emb_ref, ada_ref, bias_ref)

    @pl.when(pair == 0)
    def _():
        project([own_x, sib_x], mod_ref, step, w_ref, normed_ref, [q_ref, k_ref, v_ref])

    ext_ref[0], ext_ref[1] = with_ones(v_ref[0, pair])
    for start in range(0, q_ref.shape[2], rows):
        at = slice(start, start + rows)
        for head, query in enumerate(masked(q_ref[0, pair, at, :])):
            acc_ref[0, 0, head, at, :] = dot(exponentials(query, k_ref, pair, 256), ext_ref[head])


def far_kernel(rows, step, sources, *refs):
    x_refs, refs = refs[:sources], refs[sources:]
    mod_ref, w_ref, q_ref, k_ref, v_ref, acc_ref = refs[:6]
    normed_ref, kr_ref, vr_ref, o_ref, qe_ref, ext_ref, total_ref = refs[-7:]
    pair = pl.program_id(0)

    @pl.when(pair == 0)
    def _():
        project(x_refs, mod_ref, step, w_ref, normed_ref, [kr_ref, vr_ref])

    ext_ref[0], ext_ref[1] = with_ones(vr_ref[0, pair])
    def finish(at, query, first, second, top_first, top_second):
        lane = lane_index(query.shape)
        low = lane < HD
        swapped = jnp.where(low, second, first)
        total = pltpu.roll(swapped, HD, 1)
        o_ref[0, 0, at, :] = jnp.where(low, first, second) / total
        log_total = jnp.log(swapped) + jnp.where(low, top_second, top_first)
        high = log_total.astype(BF16).astype(F32)
        middle = (log_total - high).astype(BF16).astype(F32)
        rest = log_total - high - middle
        spot = lane % HD
        extra = jnp.where(spot == 0, -high, jnp.where(spot == 1, -middle, -rest))
        extra = jnp.where(spot < 3, extra, 0.0).astype(BF16)
        qe_ref[0, 0, 0, at, :] = jnp.where(low, query, extra)
        qe_ref[0, 0, 1, at, :] = jnp.where(low, extra, query)
        return total

    def block(index, carry):
        at = pl.ds(pl.multiple_of(index * rows, rows), rows)
        query = q_ref[0, 0, at, :]
        sums = []
        for head, own in enumerate(masked(query)):
            more = dot(exponentials(own, kr_ref, pair, 512), ext_ref[head])
            sums.append(acc_ref[0, 0, head, at, :] + more)
        total_ref[at, :] = finish(at, query, sums[0], sums[1], 0.0, 0.0)
        return carry

    lax.fori_loop(0, q_ref.shape[2] // rows, block, 0, unroll=True)
    total = total_ref[...]
    bad = jnp.sum(jnp.where((total > 1e-25) & (total < 1e25), 0.0, 1.0))

    @pl.when(bad > 0.0)
    def _():
        own_ext = with_ones(v_ref[0, 0])

        again_rows = min(32, q_ref.shape[2])

        def again(index, carry):
            at = pl.ds(pl.multiple_of(index * again_rows, again_rows), again_rows)
            query = q_ref[0, 0, at, :]
            sums, tops = [], []
            for head, own in enumerate(masked(query)):
                scores = dot(own, k_ref[0, 0], NT)
                others = dot(own, kr_ref[0, pair], NT)
                top = jnp.maximum(
                    jnp.max(scores, axis=-1, keepdims=True),
                    jnp.max(others, axis=-1, keepdims=True),
                )
                sums.append(
                    dot(jnp.exp(scores - top).astype(BF16), own_ext[head])
                    + dot(jnp.exp(others - top).astype(BF16), ext_ref[head])
                )
                tops.append(top)
            finish(at, query, sums[0], sums[1], tops[0], tops[1])
            return carry

        lax.fori_loop(0, q_ref.shape[2] // again_rows, again, 0)


def gelu_parts(values):
    cumulative = 0.5 * lax.erf(values * 0.7071067811865476) + 0.5
    bell = jnp.exp2(values * values * (-0.5 * LOG2E))
    return values * cumulative, cumulative + values * bell * 0.3989422804014327


def patch_kernel(
    rows,
    chunk,
    counts_ref,
    lead_ref,
    own_x,
    sib_x,
    own_ct,
    sib_ct,
    mod_ref,
    o_ref,
    out_w,
    fc1_w,
    fc2_w,
    final_own,
    final_sib,
    gm_ref,
    ge_ref,
    sums_ref,
    stack_one,
    stack_two,
    hidden_s,
    gpre_s,
    n2_s,
    g2_s,
    g1_s,
    mixed_s,
    gout_s,
    gfc1_s,
    gfc2_s,
    sums_s,
):
    step, half = pl.program_id(0), pl.program_id(1)
    width, hidden_width = fc1_w.shape
    patches = own_x.shape[1]
    slot = first_step(pl.num_programs(0)) + step
    active = (slot < counts_ref[0]).astype(F32)

    def piece(index):
        return mod_ref[pl.ds(step, 1), index * width : (index + 1) * width]

    gate1, shift2, scale2, gate2 = piece(2), piece(3), piece(4), piece(5)

    @pl.when((step == 0) & (half == 0))
    def _():
        sums_s[...] = jnp.zeros_like(sums_s)
        gout_s[...] = jnp.zeros_like(gout_s)
        gfc1_s[...] = jnp.zeros_like(gfc1_s)
        gfc2_s[...] = jnp.zeros_like(gfc2_s)

    def block(index, carry):
        at = pl.ds(pl.multiple_of(index * rows, rows), rows)
        x = jnp.where(half == 0, own_x[0, at, :], sib_x[0, at, :]).astype(F32)
        final_grad = jnp.where(half == 0, own_ct[0, at, :], sib_ct[0, at, :]).astype(F32) * active
        outs = [o_ref[0, pair, at, :] for pair in range(width // LANES)]
        mixed = jnp.concatenate([o.astype(BF16) for o in outs], axis=-1)
        mixed_s[at, :] = mixed
        branch_one = dot(mixed, out_w[...])
        middle = x + gate1 * branch_one
        xhat, inverse = normalize(middle)
        n2 = (xhat * (1.0 + scale2) + shift2).astype(BF16)
        n2_s[at, :] = n2
        g2 = (gate2 * final_grad).astype(BF16)
        g2_s[at, :] = g2
        branch_two = jnp.zeros((rows, width), F32)
        gy = jnp.zeros((rows, width), F32)
        for start in range(0, hidden_width, chunk):
            columns = slice(start, start + chunk)
            pre = dot(n2, fc1_w[:, columns])
            grad_hidden = dot(g2, fc2_w[columns, :], NT)
            hidden, slope = gelu_parts(pre)
            hidden = hidden.astype(BF16)
            grad_pre = (slope * grad_hidden).astype(BF16)
            hidden_s[at, columns] = hidden
            gpre_s[at, columns] = grad_pre
            branch_two += dot(hidden, fc2_w[columns, :])
            gy += dot(grad_pre, fc1_w[:, columns], NT)
        final = ((middle + gate2 * branch_two) * active).astype(BF16)

        @pl.when(half == 0)
        def _():
            final_own[0, at, :] = final

        @pl.when(half == 1)
        def _():
            final_sib[0, at, :] = final

        gm = final_grad + norm_back(gy * (1.0 + scale2), xhat, inverse)
        gm_ref[0, 0, at, :] = gm
        g1 = (gate1 * gm).astype(BF16)
        g1_s[at, :] = g1
        sums = [branch_one * gm, gy, gy * xhat, branch_two * final_grad]
        for row, value in enumerate(sums):
            place = pl.ds(2 * row + step, 1)
            sums_s[place, :] += jnp.sum(value, axis=0, keepdims=True)
        grad_mixed = dot(g1, out_w[...], NT).astype(BF16)
        lane = lane_index((rows, LANES))
        low = lane < HD
        spot = lane % HD
        for pair, o in enumerate(outs):
            grad = grad_mixed[:, pair * LANES : (pair + 1) * LANES]
            product = grad.astype(F32) * o
            first = jnp.sum(jnp.where(low, product, 0.0), axis=-1, keepdims=True)
            second = jnp.sum(jnp.where(low, 0.0, product), axis=-1, keepdims=True)
            inner = jnp.where(low, second, first)
            high = inner.astype(BF16).astype(F32)
            mid = (inner - high).astype(BF16).astype(F32)
            extra = jnp.where(spot == 0, -high, jnp.where(spot == 1, -mid, high + mid - inner))
            extra = jnp.where(spot < 3, extra, 0.0).astype(BF16)
            ge_ref[0, pair, 0, at, :] = jnp.where(low, grad, extra)
            ge_ref[0, pair, 1, at, :] = jnp.where(low, extra, grad)
        return carry

    lax.fori_loop(0, patches // rows, block, 0)
    gout_s[...] += dot(mixed_s[...], g1_s[...], TN)
    gfc1_s[...] += dot(n2_s[...], gpre_s[...], TN)
    gfc2_s[...] += dot(g2_s[...], hidden_s[...], TN)

    @pl.when((step == pl.num_programs(0) - 1) & (half == pl.num_programs(1) - 1))
    def _():
        for index in range(2):
            lead = lead_ref[0, first_step(2) + index]
            sums_s[12 + index : 13 + index, :] = jnp.where(lane_index((1, width)) == lead, 1.0, 0.0)
        sums_ref[...] = sums_s[...].astype(BF16)
        blocks = hidden_width // width
        for index in range(blocks):
            columns = slice(index * width, (index + 1) * width)
            stack_one[index] = gfc1_s[:, columns].astype(BF16)
            stack_two[index] = gfc2_s[:, columns].T.astype(BF16)
        stack_two[blocks] = gout_s[...].astype(BF16)


def attend_back_kernel(rows, first_pass, exchanges, grid_steps, *refs):
    count = len(exchanges)
    qe_ref, ge_ref, k_ref, v_ref = refs[:4]
    refs = refs[4:]
    if first_pass:
        gives, sums_ref, refs = refs[:count], refs[count], refs[count + 1 :]
        dq_ref, dk_ref, dv_ref = refs[:3]
        shards, all_ref, refs = refs[3 : 3 + count], refs[3 + count], refs[4 + count :]
        all_s, all_sends, all_recvs = refs[-3:]
    else:
        dq_in, shards, refs = refs[0], refs[1 : 1 + count], refs[1 + count :]
        dq_ref, dk_ref, dv_ref = refs[:3]
        fulls, refs = refs[3 : 3 + count], refs[3 + count :]
    dq_s, refs = refs[0], refs[1:]
    states = []
    for index, exchange in enumerate(exchanges):
        sends, recvs = refs[1], refs[2]
        if first_pass:
            got = refs[3 : 3 + exchange.all_levels]
            states.append((gives[index], refs[0], got, sends, recvs))
            refs = refs[3 + exchange.all_levels :]
        else:
            states.append((refs[0], sends, recvs))
            refs = refs[3:]
    per_step = k_ref.shape[2] // rows
    static_slots = grid_steps * per_step
    first_slot = (pl.program_id(0) * pl.num_programs(1) + pl.program_id(1)) * per_step
    levels = exchanges[0].all_levels if first_pass else exchanges[0].levels

    def all_copy(level):
        index = 0
        for lower in range(len(exchanges[0].bits)):
            index = index + exchanges[0].place(lower)[0] * (1 << lower)
        if level < 0:
            return all_s.at[pl.ds(index, 1)]
        size = 1 << level
        piece = all_s.at[pl.ds((index // size) * size, size)]
        return exchanges[0].copy(piece, piece, all_sends, all_recvs, level)

    def reduce_action(order):
        if order == 0:
            exchanges[0].barrier()
            own = all_copy(-1)
            own[...] = sums_ref[...][None]
        else:
            all_copy(order - 1).wait()
        if order < levels:
            all_copy(order).start()
        else:
            all_ref[...] = all_s[...]
        for exchange, state, shard in zip(exchanges, states, shards):
            if order > 0:
                exchange.reduce_finish(order - 1, *state)
            if order < levels:
                exchange.reduce_start(order, *state)
            else:
                shard[...] = exchange.own_shard(state[1], 1)[...][0]

    def gather_action(order):
        if order == 0:
            exchanges[0].barrier()
        for exchange, state, shard in zip(exchanges, states, shards):
            if order == 0:
                exchange.own_shard(state[0], 0)[...] = shard[...][None]
            else:
                exchange.gather_finish(levels - order, *state)
            if order < levels:
                exchange.gather_start(levels - 1 - order, *state)
        if order == levels:
            copies = [
                pltpu.make_async_copy(state[0], full, refs[index])
                for index, (state, full) in enumerate(zip(states, fulls))
            ]
            for copy in copies:
                copy.start()
            for copy in copies:
                copy.wait()

    action = reduce_action if first_pass else gather_action
    weights = [5.0, 10.0, 9.0, 6.0] + [4.0] * levels
    weights = weights[:levels] if first_pass else weights[:levels][::-1]
    marks, total = [0], 0.0
    for weight in weights:
        total += weight
        marks.append(total)
    last = static_slots - (4 if first_pass else 1)
    marks = [min(int(mark * last / total + 0.5), last) for mark in marks]

    dq_s[...] = jnp.zeros_like(dq_s) if first_pass else dq_in[0, 0].T

    def block(index, carry):
        for order, mark in enumerate(marks[:-1]):
            pl.when(first_slot + index == mark)(functools.partial(action, order))
        at = pl.ds(pl.multiple_of(index * rows, rows), rows)
        keys = k_ref[0, 0, at, :]
        values = v_ref[0, 0, at, :]
        lane = lane_index(keys.shape)
        low = lane < HD
        ones = jnp.where(lane % HD < 3, 1.0, 0.0).astype(BF16)
        zero = jnp.zeros_like(keys)
        grads = []
        for head in range(2):
            own = low if head == 0 else jnp.logical_not(low)
            query = qe_ref[0, 0, head]
            grad = ge_ref[0, 0, head]
            probs = jnp.exp(dot(jnp.where(own, keys, ones), query, NT))
            grad_probs = dot(jnp.where(own, values, ones), grad, NT)
            grad_scores = (probs * grad_probs).astype(BF16)
            grads.append((dot(grad_scores, query), dot(probs.astype(BF16), grad)))
            dq_s[...] += dot(jnp.where(own, keys, zero), grad_scores, TN)
        dk_ref[0, 0, at, :] = jnp.where(low, grads[0][0], grads[1][0]).astype(BF16)
        dv_ref[0, 0, at, :] = jnp.where(low, grads[0][1], grads[1][1]).astype(BF16)
        return carry

    lax.fori_loop(0, per_step, block, 0)
    if first_pass:
        dq_ref[0, 0] = dq_s[...].T
    else:
        dq_ref[0, 0] = (dq_s[...].T * HD**-0.5).astype(BF16)
    pl.when(first_slot + per_step == static_slots)(functools.partial(action, levels))


def joining(at, read, write, wait, own_ref, got_ref, out_ref, own_s, got_s, sems):
    mine = first_step(2)
    reads = [
        pltpu.make_async_copy(own_ref, own_s, sems.at[0]),
        pltpu.make_async_copy(got_ref, got_s, sems.at[1]),
    ]
    writes = [
        pltpu.make_async_copy(own_s, out_ref.at[pl.ds(mine, 2)], sems.at[2]),
        pltpu.make_async_copy(got_s, out_ref.at[pl.ds(2 - mine, 2)], sems.at[3]),
    ]

    @pl.when(at == read)
    def _():
        for copy in reads:
            copy.start()

    @pl.when(at == write)
    def _():
        for copy in reads:
            copy.wait()
        for copy in writes:
            copy.start()

    @pl.when(at == wait)
    def _():
        for copy in writes:
            copy.wait()


def project_back_far_kernel(
    dk_ref, dv_ref, normed_ref, w_ref, own_ref, got_ref, dx_ref, gw_ref, out_ref, own_s, got_s, sems
):
    width = w_ref.shape[0]
    at = pl.program_id(0) * pl.num_programs(1) + pl.program_id(1)
    joining(at, 0, 1, 3, own_ref, got_ref, out_ref, own_s, got_s, sems)
    joined = join_heads(dk_ref, dv_ref)
    dx_ref[0, 0] = dot(joined, w_ref[:, width:], NT).astype(BF16)

    @pl.when((pl.program_id(0) == 0) & (pl.program_id(1) == 0))
    def _():
        gw_ref[...] = jnp.zeros_like(gw_ref)

    gw_ref[...] += dot(normed_ref[0, 0], joined, TN)


def weight_back_kernel(early, *refs):
    dq_ref, dk_ref, dv_ref, normed_ref, far_ref, one_ref, two_ref = refs[:7]
    gw_ref, gfc1_ref, gfc2_ref, gout_ref = refs[7:11]
    gw_s, one_s, two_s, gfc1_s, gfc2_s, gout_s, sems = refs[11:]
    at = pl.program_id(0) * pl.num_programs(1) + pl.program_id(1)
    size = gout_s.shape[0]
    blocks = gfc1_s.shape[1] // size
    reads = [
        pltpu.make_async_copy(one_ref, one_s, sems.at[0]),
        pltpu.make_async_copy(two_ref, two_s, sems.at[1]),
    ]
    writes = [
        pltpu.make_async_copy(gfc1_s, gfc1_ref, sems.at[2]),
        pltpu.make_async_copy(gfc2_s, gfc2_ref, sems.at[3]),
        pltpu.make_async_copy(gout_s, gout_ref, sems.at[4]),
    ]

    @pl.when(at == 0)
    def _():
        for copy in reads:
            copy.start()

    @pl.when(at == 1)
    def _():
        reads[0].wait()
        unstack(
            grouped(early[0]), one_s, [(gfc1_s, 0, block * size) for block in range(blocks)], size
        )
        writes[0].start()

    @pl.when(at == 2)
    def _():
        reads[1].wait()
        rest = [(gfc2_s, block * size, 0) for block in range(blocks)] + [(gout_s, 0, 0)]
        unstack(grouped(early[1]), two_s, rest, size)
        writes[1].start()
        writes[2].start()

    @pl.when(at == pl.num_programs(0) * pl.num_programs(1) - 1)
    def _():
        for copy in writes:
            copy.wait()

    step, which = pl.program_id(0), pl.program_id(1)
    width = normed_ref.shape[3]

    @pl.when((step == 0) & (which == 0))
    def _():
        gw_s[:, :width] = jnp.zeros_like(gw_s[:, :width])
        gw_s[:, width:] = far_ref[...]

    gw_s[...] += dot(normed_ref[0, 0], join_heads(dq_ref, dk_ref, dv_ref), TN)

    @pl.when((step == pl.num_programs(0) - 1) & (which == pl.num_programs(1) - 1))
    def _():
        for block in range(gw_ref.shape[0]):
            gw_ref[block] = gw_s[:, block * LANES : (block + 1) * LANES].astype(BF16)


def join_heads(*grads):
    return jnp.concatenate([ref[0, pair] for ref in grads for pair in range(ref.shape[1])], axis=-1)


class Direct:
    def __init__(self, mesh_shape, row_tiles):
        self.chips = mesh_shape["seq"] // 2
        self.peers = mesh_shape["dp"] * self.chips
        self.half = row_tiles * 8
        self.piece = -(-row_tiles // (2 * self.peers)) * 16
        self.padded = self.piece * self.peers

    def me(self):
        return lax.axis_index("dp") * self.chips + lax.axis_index("seq") // 2

    def core(self):
        return lax.axis_index("seq") % 2

    def sibling(self):
        return {"seq": lax.axis_index("seq") + 1 - 2 * self.core()}

    def peer(self, shift):
        other = (self.me() + shift) % self.peers
        device = {"dp": other // self.chips, "seq": (other % self.chips) * 2 + self.core()}
        return other, device

    def rows(self, index):
        return pl.ds(pl.multiple_of(index * self.piece, 16), self.piece)

    def barrier(self):
        semaphore = pltpu.get_barrier_semaphore()

        def signal(device):
            pl.semaphore_signal(semaphore, 1, device_id=device, device_id_type=pl.DeviceIdType.MESH)

        signal(self.sibling())

        def greet(shift, carry):
            signal(self.peer(shift)[1])
            return carry

        lax.fori_loop(1, self.peers, greet, 0)
        pl.semaphore_wait(semaphore, self.peers)

    def copy(self, source, target, send, recv, device):
        return pltpu.make_async_remote_copy(
            src_ref=source,
            dst_ref=target,
            send_sem=send,
            recv_sem=recv,
            device_id=device,
            device_id_type=pl.DeviceIdType.MESH,
        )

    def each_peer(self, do):
        def one(shift, carry):
            do(shift)
            return carry

        lax.fori_loop(1, self.peers, one, 0)


def tail_kernel(direct, remote, *refs):
    give_ref, own_x, sib_x, mod_ref, lead_ref, gm_ref, dq_ref, dk_ref, dv_ref, w_ref = refs[:10]
    others = refs[10 : 10 + remote]
    grad_ref, got_ref, full_ref, all_ref = refs[10 + remote : 14 + remote]
    sums_s, other_s, got_s, sum_s, core_s, pieces_s, full_s, all_s = refs[14 + remote : 22 + remote]
    core_sems, piece_sems, back_sems, all_sems, grad_sems, local_sem = refs[22 + remote :]
    step, half = pl.program_id(0), pl.program_id(1)
    width = own_x.shape[2]
    core, me = direct.core(), direct.me()

    core_copy = direct.copy(
        give_ref.at[1 - core], core_s, core_sems.at[0], core_sems.at[1], direct.sibling()
    )

    def piece_copy(shift):
        other, device = direct.peer(shift)
        return direct.copy(
            sum_s.at[direct.rows(other)],
            pieces_s.at[shift],
            piece_sems.at[0, shift],
            piece_sems.at[1, shift],
            device,
        )

    def full_copy(shift, arriving):
        _, device = direct.peer(shift)
        owner = (me + direct.peers - shift) % direct.peers if arriving else me
        place = full_s.at[core, direct.rows(owner)]
        return direct.copy(place, place, back_sems.at[0, shift], back_sems.at[1, shift], device)

    def sums_copy(shift, arriving):
        _, device = direct.peer(shift)
        owner = (me + direct.peers - shift) % direct.peers if arriving else me
        place = all_s.at[core, owner]
        return direct.copy(place, place, all_sems.at[0, shift], all_sems.at[1, shift], device)

    def side_copy(values, which, side):
        place = values.at[side]
        return direct.copy(
            place, place, core_sems.at[which], core_sems.at[which + 1], direct.sibling()
        )

    def grad_copy(index):
        return direct.copy(
            other_s.at[index],
            got_s.at[index],
            grad_sems.at[0, index],
            grad_sems.at[1, index],
            direct.sibling(),
        )

    @pl.when((step == 0) & (half == 0))
    def _():
        direct.barrier()
        core_copy.start()
        sums_s[...] = jnp.zeros_like(sums_s)

    @pl.when((step == 0) & (half == 1))
    def _():
        core_copy.wait()
        real = core_s.shape[0]
        sum_s[:real] = (give_ref[core].astype(F32) + core_s[...].astype(F32)).astype(BF16)
        if direct.padded > real:
            sum_s[real:] = jnp.zeros_like(sum_s[real:])
        direct.each_peer(lambda shift: piece_copy(shift).start())

    x = jnp.where(half == 0, own_x[0], sib_x[0]).astype(F32)
    scale = mod_ref[pl.ds(step, 1), width : 2 * width]
    xhat, inverse = normalize(x)
    gy = dot(join_heads(dq_ref, dk_ref, dv_ref), w_ref[...], NT)
    for other in others:
        gy = gy + other[0, 0].astype(F32)
    grad = (gm_ref[0, 0] + norm_back(gy * (1.0 + scale), xhat, inverse)).astype(BF16)

    @pl.when(half == 0)
    def _():
        grad_ref[0] = grad

    @pl.when(half == 1)
    def _():
        other_s[step] = grad
        grad_copy(step).start()

    for kind, value in enumerate((gy, gy * xhat)):
        total = jnp.sum(value, axis=0, keepdims=True)
        for index in range(width // LANES):
            place = pl.ds((kind * 2 + step) * (width // LANES) + index, 1)
            sums_s[place, :] += total[:, index * LANES : (index + 1) * LANES]

    @pl.when((step == 1) & (half == 1))
    def _():
        for index in range(2):
            chosen = lane_index((1, LANES)) == lead_ref[0, first_step(2) + index]
            sums_s[12 + index : 13 + index, :] = jnp.where(chosen, 1.0, 0.0)
        all_s[core, me] = sums_s[...].astype(BF16)
        direct.each_peer(lambda shift: sums_copy(shift, False).start())
        direct.each_peer(lambda shift: piece_copy(shift).wait())

        def add(shift, total):
            return total + pieces_s[shift].astype(F32)

        total = lax.fori_loop(1, direct.peers, add, sum_s[direct.rows(me)].astype(F32))
        full_s[core, direct.rows(me)] = total.astype(BF16)
        direct.each_peer(lambda shift: full_copy(shift, False).start())

        def arrived(shift):
            full_copy(shift, False).wait_send()
            full_copy(shift, True).wait_recv()
            sums_copy(shift, False).wait_send()
            sums_copy(shift, True).wait_recv()

        direct.each_peer(arrived)
        side_copy(full_s, 2, core).start()
        side_copy(all_s, 4, core).start()
        for index in range(2):
            grad_copy(index).wait()
        side_copy(full_s, 2, core).wait_send()
        side_copy(full_s, 2, 1 - core).wait_recv()
        side_copy(all_s, 4, core).wait_send()
        side_copy(all_s, 4, 1 - core).wait_recv()
        outs = [(got_s, got_ref), (full_s, full_ref), (all_s, all_ref)]
        copies = [
            pltpu.make_async_copy(source, target, local_sem.at[index])
            for index, (source, target) in enumerate(outs)
        ]
        for copy in copies:
            copy.start()
        for copy in copies:
            copy.wait()


def unstack(at, full_ref, targets, rows):
    row, end = 0, rows * len(targets)
    while row < end:
        group, inside, left = at(row)
        block, place = divmod(row, rows)
        count = min(left, rows - place)
        target, first_row, first_column = targets[block]
        columns = slice(first_column, first_column + full_ref.shape[2])
        value = full_ref[group, inside : inside + count, :].astype(F32)
        target[first_row + place : first_row + place + count, columns] = value
        row += count


def grouped(exchange):
    def at(row):
        group, inside = divmod(row, exchange.real)
        return group, inside, exchange.real - inside

    return at


def spread_leads(grads, step_of, table_rows):
    count = grads.shape[0]
    part = min(count, 512)
    row = lax.broadcasted_iota(jnp.int32, (part, part), 0)
    column = lane_index((part, part))
    chosen = (row // 16 == column // 16) & (row % 16 == 12 + step_of(column % 16))
    spread = jnp.where(chosen, 1.0, 0.0).astype(BF16)
    leads = [
        dot(grads[start : start + part, :LANES], spread, TN)[:table_rows]
        for start in range(0, count, part)
    ]
    return jnp.concatenate(leads, axis=-1)


def final_kernel(direct, *refs):
    early_sums, late_sums, emb_ref, ada_ref, late_ref, own_ref, got_ref = refs[:7]
    grad_out, gemb_ref, gada_out, gbada_ref, gqkv_out = refs[7:12]
    gada_s, gqkv_s, late_s, own_s, got_s, sems = refs[12:]
    size = emb_ref.shape[1]
    mine = first_step(2)
    pairs = [(late_ref, late_s), (own_ref, own_s), (got_ref, got_s)]
    reads = [
        pltpu.make_async_copy(source, target, sems.at[index])
        for index, (source, target) in enumerate(pairs)
    ]
    for read in reads:
        read.start()
    copies = []

    def start(source, target):
        copy = pltpu.make_async_copy(source, target, sems.at[3 + len(copies)])
        copy.start()
        copies.append(copy)

    def halved(row):
        group, inside = divmod(row, direct.half)
        return group, inside, direct.half - inside

    columns = gqkv_s.shape[1] // LANES
    reads[0].wait()
    unstack(halved, late_s, [(gqkv_s, 0, block * LANES) for block in range(columns)], size)
    start(gqkv_s, gqkv_out)
    reads[1].wait()
    start(own_s, grad_out.at[pl.ds(mine, 2)])
    reads[2].wait()
    start(got_s, grad_out.at[pl.ds(2 - mine, 2)])

    table_rows = emb_ref.shape[0]
    table = emb_ref[...].astype(F32)
    gate = jax.nn.sigmoid(table)
    slope = gate * (1.0 + table * (1.0 - gate))
    table_act = (table * gate).astype(BF16)
    total = jnp.zeros((table_rows, size), F32)

    def one_piece(grads, leads, place, first):
        chosen = jnp.where(place, leads, 0.0).astype(BF16)
        acts = dot(table_act, chosen, TN).astype(BF16)
        where = slice(first, first + grads.shape[1])
        gada_s[:, where] = dot(acts, grads)
        by_lead = dot(chosen, grads)
        gbada_ref[where] = jnp.sum(by_lead, axis=0)
        high = by_lead.astype(BF16)
        low = (by_lead - high.astype(F32)).astype(BF16)
        return dot(high, ada_ref[:, where], NT) + dot(low, ada_ref[:, where], NT)

    grads = early_sums[...]
    leads = spread_leads(grads, lambda row: row % 2, table_rows)
    row = lane_index((1, grads.shape[0])) % 16
    for index in range(4):
        total += one_piece(grads, leads, row // 2 == index, (2 + index) * size)
    grads = late_sums[...]
    parts = size // LANES
    leads = spread_leads(grads, lambda row: (row // parts) % 2, table_rows)
    row = lane_index((1, grads.shape[0])) % 16
    for index in range(2):
        for part in range(parts):
            place = (row // (2 * parts) == index) & (row % parts == part)
            total += one_piece(grads, leads, place, index * size + part * LANES)
    gemb_ref[...] = total * slope
    start(gada_s, gada_out)
    for copy in copies:
        copy.wait()


def local(
    mesh_shape, inputs, cotangent, counts, lead_steps, emb_table, w_ada, b_ada, w_qkv, w_out, w_fc1, w_fc2
):
    slots, items, patches, width = inputs.shape
    chips = mesh_shape["seq"] // 2
    blocks = w_fc1.shape[1] // w_fc1.shape[0]
    steps = slots * items // 2
    hidden_width = w_fc1.shape[1]
    pairs = width // LANES
    rows = 2 * patches
    remote = 2 * (chips - 1)
    far_rows = remote * patches
    spot = lax.axis_index("seq")
    core = lax.rem(spot, 2)
    devices = 2 * chips

    def send(values, shift, cross):
        pairs_list = []
        for source in range(devices):
            chip, side = source // 2, source % 2
            pairs_list.append((source, ((chip + shift) % chips) * 2 + (1 - side if cross else side)))
        return lax.ppermute(values, "seq", pairs_list)

    x_steps = inputs.reshape(2, steps, patches, width)
    ct_steps = cotangent.reshape(2, steps, patches, width)
    own_x = lax.dynamic_index_in_dim(x_steps, core, 0, keepdims=False)
    other_x = lax.dynamic_index_in_dim(x_steps, 1 - core, 0, keepdims=False)
    own_ct = lax.dynamic_index_in_dim(ct_steps, core, 0, keepdims=False)
    other_ct = lax.dynamic_index_in_dim(ct_steps, 1 - core, 0, keepdims=False)
    sib_x = send(other_x, 0, True)
    far_x = []
    for step in range(steps):
        some = slice(step, step + 1)
        for shift in range(1, chips):
            far_x.append(send(own_x[some], shift, False))
            far_x.append(send(other_x[some], shift, True))
    sib_ct = send(other_ct, 0, True)

    step_block = pl.BlockSpec((1, patches, width), lambda j, i: (j, 0, 0))
    patch_block = pl.BlockSpec((1, 1, patches, width), lambda j, i: (j, i, 0, 0))

    def head_rows(count):
        return pl.BlockSpec((1, 1, count, LANES), lambda j, p: (j, p, 0, 0))

    def of_step(*shape):
        return pl.BlockSpec((1,) + shape, lambda j, p: (j,) + (0,) * len(shape))

    both_heads = pl.BlockSpec((1, 1, 2, rows, LANES), lambda j, p: (j, p, 0, 0, 0))
    piece = min(256, rows)
    near_work = 4 * steps * pairs * 2 * rows * LANES * rows
    near_heads = jax.ShapeDtypeStruct((steps, pairs, rows, LANES), BF16)
    mod, n1, q, k, v, acc = call(
        functools.partial(near_kernel, min(512, rows)),
        "near",
        (steps, pairs),
        [scalars(), whole(emb_table.shape), whole(w_ada.shape), whole((1, 6 * width))]
        + [step_block] * 2
        + [whole(w_qkv.shape)],
        [whole((16, 6 * width)), of_step(rows, width)]
        + [of_step(pairs, rows, LANES)] * 3
        + [both_heads],
        [
            jax.ShapeDtypeStruct((16, 6 * width), F32),
            jax.ShapeDtypeStruct((steps, rows, width), BF16),
            near_heads,
            near_heads,
            near_heads,
            jax.ShapeDtypeStruct((steps, pairs, 2, rows, LANES), F32),
        ],
        [pltpu.VMEM((2, rows, LANES), BF16)],
        flops=near_work + 6 * steps * rows * width * width,
        exps=steps * pairs * 2 * rows * rows,
    )(lead_steps, emb_table, w_ada, b_ada.reshape(1, -1), own_x, sib_x, w_qkv)

    def far(step, before):
        some_x = far_x[step * remote : (step + 1) * remote]

        def at_step(*shape):
            return pl.BlockSpec((1,) + shape, lambda p: (step,) + (0,) * len(shape))

        def at_pair(*shape):
            return pl.BlockSpec((1, 1) + shape, lambda p: (step, p) + (0,) * len(shape))

        operands = [*some_x, mod, w_qkv, q, k, v, acc]
        return call(
            functools.partial(far_kernel, piece, step, remote),
            "far",
            (pairs,),
            [whole((1, patches, width))] * remote
            + [whole(mod.shape), whole(w_qkv.shape)]
            + [at_pair(rows, LANES)] * 3
            + [at_pair(2, rows, LANES)]
            + [pl.BlockSpec(memory_space=pl.ANY)] * len(before),
            [at_step(far_rows, width)]
            + [at_step(pairs, far_rows, LANES)] * 2
            + [at_pair(rows, LANES), at_pair(2, rows, LANES)],
            [
                jax.ShapeDtypeStruct((steps, far_rows, width), BF16),
                jax.ShapeDtypeStruct((steps, pairs, far_rows, LANES), BF16),
                jax.ShapeDtypeStruct((steps, pairs, far_rows, LANES), BF16),
                jax.ShapeDtypeStruct((steps, pairs, rows, LANES), F32),
                jax.ShapeDtypeStruct((steps, pairs, 2, rows, LANES), BF16),
            ],
            [pltpu.VMEM((2, far_rows, LANES), BF16), pltpu.VMEM((rows, LANES), F32)],
            flops=near_work // 2,
            exps=pairs * 2 * rows * far_rows,
            aliases={len(operands) + index: index for index in range(len(before))},
        )(*operands, *before)

    far_results = []
    for step in range(steps):
        far_results = far(step, far_results)
    n1r, kr, vr, o, qe = far_results

    block_rows = min(256, patches)
    outs = call(
        functools.partial(patch_kernel, block_rows, 512),
        "patchwise",
        (steps, 2),
        [scalars()] * 2
        + [step_block] * 4
        + [
            whole(mod.shape),
            pl.BlockSpec((1, pairs, patches, LANES), lambda j, i: (j, 0, i, 0)),
            whole(w_out.shape),
            whole(w_fc1.shape),
            whole(w_fc2.shape),
        ],
        [
            step_block,
            step_block,
            patch_block,
            pl.BlockSpec((1, pairs, 2, patches, LANES), lambda j, i: (j, 0, 0, i, 0)),
            whole((16, width)),
            whole((blocks, width, width)),
            whole((blocks + 1, width, width)),
        ],
        [
            jax.ShapeDtypeStruct((steps, patches, width), BF16),
            jax.ShapeDtypeStruct((steps, patches, width), BF16),
            jax.ShapeDtypeStruct((steps, 2, patches, width), F32),
            jax.ShapeDtypeStruct((steps, pairs, 2, rows, LANES), BF16),
            jax.ShapeDtypeStruct((16, width), BF16),
            jax.ShapeDtypeStruct((blocks, width, width), BF16),
            jax.ShapeDtypeStruct((blocks + 1, width, width), BF16),
        ],
        [pltpu.VMEM((patches, hidden_width), BF16)] * 2
        + [pltpu.VMEM((patches, width), BF16)] * 4
        + [
            pltpu.VMEM((width, width), F32),
            pltpu.VMEM((width, hidden_width), F32),
            pltpu.VMEM((width, hidden_width), F32),
            pltpu.VMEM((16, width), F32),
        ],
        flops=6 * steps * rows * width * (2 * hidden_width + width),
        moved=steps * rows * width * 20,
        exps=2 * steps * rows * hidden_width,
    )(counts, lead_steps, own_x, sib_x, own_ct, sib_ct, mod, o, w_out, w_fc1, w_fc2)
    final_own, final_sib, gm, ge, sums, stack_one, stack_two = outs
    final_got = send(final_sib, 0, True)
    early = [Exchange(mesh_shape, blocks * width // 16, 0), Exchange(mesh_shape, (blocks + 1) * width // 16, 1)]
    gives = [g.reshape(e.groups, e.real, width) for e, g in zip(early, (stack_one, stack_two))]

    def attend_back(keys, values, extra, first, name):
        count = keys.shape[2]
        in_specs = [both_heads] * 2 + [head_rows(count)] * 2
        out_specs = [head_rows(rows), head_rows(count), head_rows(count)]
        out_shape = [
            jax.ShapeDtypeStruct((steps, pairs, rows, LANES), F32 if first else BF16),
            jax.ShapeDtypeStruct((steps, pairs, count, LANES), BF16),
            jax.ShapeDtypeStruct((steps, pairs, count, LANES), BF16),
        ]
        scratch = [pltpu.VMEM((LANES, rows), F32)]
        if not first:
            in_specs += [head_rows(rows)]
        for exchange in early:
            shape = (exchange.groups, exchange.padded, width)
            shard = (exchange.shard, width)
            sems = [pltpu.SemaphoreType.DMA((exchange.all_levels,))] * 2
            if first:
                in_specs += [whole((exchange.groups, exchange.real, width))]
                out_specs += [whole(shard)]
                out_shape += [jax.ShapeDtypeStruct(shard, BF16)]
                half = (exchange.groups // 2, exchange.padded, width)
                scratch += [pltpu.VMEM(half, BF16)] + sems + exchange.receive_scratch(width)
            else:
                in_specs += [whole(shard)]
                out_specs += [pl.BlockSpec(memory_space=pl.ANY)]
                out_shape += [jax.ShapeDtypeStruct(shape, BF16)]
                scratch += [pltpu.VMEM(shape, BF16)] + sems
        if first:
            every = (mesh_shape["dp"] * mesh_shape["seq"], 16, width)
            in_specs += [whole(sums.shape)]
            out_specs += [whole(every)]
            out_shape += [jax.ShapeDtypeStruct(every, BF16)]
            sems = [pltpu.SemaphoreType.DMA((early[0].all_levels,))] * 2
            scratch += [pltpu.VMEM(every, BF16)] + sems
        else:
            scratch += [pltpu.SemaphoreType.DMA] * len(early)
        return call(
            functools.partial(
                attend_back_kernel, min(512 if first else 1024, count), first, early, steps * pairs
            ),
            name,
            (steps, pairs),
            in_specs,
            out_specs,
            out_shape,
            scratch,
            flops=10 * steps * pairs * 2 * rows * count * LANES,
            exps=steps * pairs * 2 * rows * count,
            collective=1 if first else 2,
        )(qe, ge, keys, values, *extra)

    grad_block = pl.BlockSpec((1, pairs, patches, LANES), lambda j, i: (j, 0, i, 0))
    hbm = pl.BlockSpec(memory_space=pl.ANY)

    dq_part, dkr, dvr, shard_one, shard_two, early_all = attend_back(
        kr, vr, [*gives, sums], True, "attend_back_far"
    )
    dx_far, gw_part, outputs = call(
        project_back_far_kernel,
        "project_back_far",
        (steps, remote),
        [grad_block] * 2 + [patch_block, whole(w_qkv.shape), hbm, hbm],
        [patch_block, whole((width, 2 * width)), hbm],
        [
            jax.ShapeDtypeStruct((steps, remote, patches, width), BF16),
            jax.ShapeDtypeStruct((width, 2 * width), F32),
            jax.ShapeDtypeStruct((2 * steps, patches, width), BF16),
        ],
        [pltpu.VMEM((steps, patches, width), BF16)] * 2 + [pltpu.SemaphoreType.DMA((4,))],
        flops=4 * steps * far_rows * width * 2 * width,
        moved=steps * far_rows * width * 8,
    )(dkr, dvr, n1r.reshape(steps, remote, patches, width), w_qkv, final_own, final_got)
    dx_got = [send(dx_far[:, 2 * r - 2 : 2 * r], -r, False) for r in range(1, chips)]
    dq, dk, dv, *early_sums = attend_back(
        k, v, [dq_part, shard_one, shard_two], False, "attend_back_near"
    )
    columns = w_qkv.shape[1] // LANES
    early_weights = (w_fc1, w_fc2, w_out)
    give_late, g_fc1, g_fc2, g_out = call(
        functools.partial(weight_back_kernel, early),
        "weight_back",
        (steps, 2),
        [grad_block] * 3 + [patch_block, whole(gw_part.shape), hbm, hbm],
        [whole((columns, width, LANES))] + [hbm] * 3,
        [jax.ShapeDtypeStruct((columns, width, LANES), BF16)]
        + [jax.ShapeDtypeStruct(w.shape, F32) for w in early_weights],
        [pltpu.VMEM((width, columns * LANES), F32)]
        + [pltpu.VMEM(value.shape, BF16) for value in early_sums]
        + [pltpu.VMEM(w.shape, F32) for w in early_weights]
        + [pltpu.SemaphoreType.DMA((5,))],
        flops=2 * steps * rows * width * 3 * width,
        moved=steps * rows * width * 8,
    )(dq, dk, dv, n1.reshape(steps, 2, patches, width), gw_part, *early_sums)

    direct = Direct(mesh_shape, columns * width // 16)
    full_shape = (2, direct.padded, LANES)
    late_all_shape = (2, direct.peers, 16, LANES)
    grad_own, grad_got, late_sum, late_all = call(
        functools.partial(tail_kernel, direct, len(dx_got)),
        "tail",
        (steps, 2),
        [whole((2, direct.half, LANES)), step_block, step_block, whole(mod.shape), scalars()]
        + [patch_block]
        + [grad_block] * 3
        + [whole(w_qkv.shape)]
        + [patch_block] * len(dx_got),
        [step_block, hbm, hbm, hbm],
        [
            jax.ShapeDtypeStruct((steps, patches, width), BF16),
            jax.ShapeDtypeStruct((steps, patches, width), BF16),
            jax.ShapeDtypeStruct(full_shape, BF16),
            jax.ShapeDtypeStruct(late_all_shape, BF16),
        ],
        [
            pltpu.VMEM((16, LANES), F32),
            pltpu.VMEM((steps, patches, width), BF16),
            pltpu.VMEM((steps, patches, width), BF16),
            pltpu.VMEM((direct.padded, LANES), BF16),
            pltpu.VMEM((direct.half, LANES), BF16),
            pltpu.VMEM((direct.peers, direct.piece, LANES), BF16),
            pltpu.VMEM(full_shape, BF16),
            pltpu.VMEM(late_all_shape, BF16),
            pltpu.SemaphoreType.DMA((6,)),
            pltpu.SemaphoreType.DMA((2, direct.peers)),
            pltpu.SemaphoreType.DMA((2, direct.peers)),
            pltpu.SemaphoreType.DMA((2, direct.peers)),
            pltpu.SemaphoreType.DMA((2, steps)),
            pltpu.SemaphoreType.DMA((3,)),
        ],
        flops=2 * steps * rows * width * 3 * width,
        collective=3,
    )(
        give_late.reshape(2, direct.half, LANES),
        own_x,
        sib_x,
        mod,
        lead_steps,
        gm,
        dq,
        dk,
        dv,
        w_qkv,
        *dx_got,
    )

    early_all = early_all.reshape(-1, width)
    late_all = late_all.reshape(-1, LANES)
    small = [early_all, late_all, emb_table, w_ada]
    large = [late_sum, grad_own, grad_got]
    out_shapes = [(slots * items, patches, width), emb_table.shape, w_ada.shape, b_ada.shape, w_qkv.shape]
    grad_inputs, g_emb, g_ada, g_bada, g_qkv = call(
        functools.partial(final_kernel, direct),
        "final",
        (),
        [whole(value.shape) for value in small] + [hbm] * len(large),
        [hbm, whole(emb_table.shape), hbm, whole(b_ada.shape), hbm],
        [
            jax.ShapeDtypeStruct(shape, F32 if index else BF16)
            for index, shape in enumerate(out_shapes)
        ],
        [pltpu.VMEM(w.shape, F32) for w in (w_ada, w_qkv)]
        + [pltpu.VMEM(value.shape, BF16) for value in large]
        + [pltpu.SemaphoreType.DMA((7,))],
        flops=2 * early_all.shape[0] * width * 6 * width,
        moved=6 * w_ada.size,
    )(*small, *large)
    return (
        outputs.reshape(inputs.shape),
        grad_inputs.reshape(inputs.shape),
        g_emb,
        g_ada,
        g_bada,
        g_qkv,
        g_out,
        g_fc1,
        g_fc2,
    )


def solution(mesh):
    tokens = P(None, "dp", "seq", None)
    return jax.shard_map(
        functools.partial(local, dict(mesh.shape)),
        mesh=mesh,
        in_specs=(tokens, tokens, P("dp"), P("dp", None)) + (P(),) * 7,
        out_specs=(tokens, tokens) + (P(),) * 7,
        check_vma=False,
    )
```

```python
import functools

import jax
import jax.numpy as jnp
from jax import lax
from jax.experimental import pallas as pl
from jax.experimental.pallas import tpu as pltpu
from jax.sharding import PartitionSpec as P

HD = 64
LANES = 128
EPSILON = 1e-06
LOG2E = 1.4426950408889634
NN = (((1,), (0,)), ((), ()))
NT = (((1,), (1,)), ((), ()))
TN = (((0,), (0,)), ((), ()))
F32 = jnp.float32
BF16 = jnp.bfloat16
VMEM_BYTES = 24 * 1024 * 1024


def dot(a, b, dims=NN):
    return lax.dot_general(a, b, dims, preferred_element_type=F32)


def call(
    body,
    name,
    grid,
    in_specs,
    out_specs,
    out_shape,
    scratch=(),
    flops=0,
    moved=0,
    exps=0,
    collective=None,
    aliases=None,
):
    return pl.pallas_call(
        body,
        name=name,
        grid=grid,
        in_specs=in_specs,
        out_specs=out_specs,
        out_shape=out_shape,
        scratch_shapes=list(scratch),
        input_output_aliases=aliases or {},
        cost_estimate=pl.CostEstimate(flops=flops, bytes_accessed=moved, transcendentals=exps),
        compiler_params=pltpu.CompilerParams(
            vmem_limit_bytes=VMEM_BYTES,
            collective_id=collective,
            has_side_effects=collective is not None,
        ),
    )


def whole(shape):
    return pl.BlockSpec(shape, lambda *_: (0,) * len(shape))


def scalars():
    return pl.BlockSpec(memory_space=pltpu.SMEM)


def lane_index(shape):
    return lax.broadcasted_iota(jnp.int32, shape, 1)


def first_step(steps):
    return lax.rem(lax.axis_index("seq"), 2) * steps


def normalize(values):
    center = values - jnp.mean(values, axis=-1, keepdims=True)
    spread = jnp.mean(center * center, axis=-1, keepdims=True)
    inverse = lax.rsqrt(spread + EPSILON)
    return center * inverse, inverse


def norm_back(grad, xhat, inverse):
    first = jnp.mean(grad, axis=-1, keepdims=True)
    second = jnp.mean(grad * xhat, axis=-1, keepdims=True)
    return inverse * (grad - first - xhat * second)


def pick(refs, which):
    value = refs[0][0]
    for index in range(1, len(refs)):
        value = jnp.where(which == index, refs[index][0], value)
    return value


class Exchange:
    def __init__(self, mesh_shape, row_tiles, turn=0):
        bits = {"seq": [], "dp": []}
        for axis in bits:
            bit = 1
            while bit < mesh_shape[axis]:
                bits[axis].append((axis, bit))
                bit *= 2
        turned = bits["dp"][turn:] + bits["dp"][:turn]
        self.bits = bits["seq"][:1] + turned + bits["seq"][1:]
        self.all_levels = len(self.bits)
        self.levels = 1 + len(turned)
        self.even = 0
        while self.even < self.levels and row_tiles % 2 == 0:
            row_tiles //= 2
            self.even += 1
        unit = 2 ** (self.levels - self.even)
        self.groups = 2**self.even
        self.real = row_tiles * 16
        self.padded = -(-row_tiles // unit) * unit * 16
        self.shard = self.padded // unit

    def sizes(self, level):
        if level < self.even:
            return (self.groups >> (level + 1), self.real)
        return (1, self.padded >> (level - self.even + 1))

    def receive_scratch(self, width):
        last = self.levels - 1
        return [
            pltpu.VMEM(self.sizes(min(level, last)) + (width,), BF16)
            for level in range(self.all_levels)
        ]

    def place(self, level):
        axis, bit = self.bits[level]
        here = lax.axis_index(axis)
        value = (here // bit) % 2
        return value, {axis: here + bit * (1 - 2 * value)}

    def spot(self, level, first, flip):
        group, row = 0, 0
        for index in range(first, level + 1):
            value, _ = self.place(index)
            if flip and index == level:
                value = 1 - value
            if index < self.even:
                group = group + value * (self.groups >> (index + 1))
            else:
                row = row + value * (self.padded >> (index - self.even + 1))
        if level >= self.even:
            row = pl.multiple_of(row, 16)
        count, rows = self.sizes(level)
        return pl.ds(group, count), pl.ds(row, rows)

    def barrier(self):
        semaphore = pltpu.get_barrier_semaphore()
        for level in range(self.all_levels):
            _, partner = self.place(level)
            pl.semaphore_signal(
                semaphore, inc=1, device_id=partner, device_id_type=pl.DeviceIdType.MESH
            )
        pl.semaphore_wait(semaphore, self.all_levels)

    def copy(self, source, target, sends, recvs, level):
        _, partner = self.place(level)
        return pltpu.make_async_remote_copy(
            src_ref=source,
            dst_ref=target,
            send_sem=sends.at[level],
            recv_sem=recvs.at[level],
            device_id=partner,
            device_id_type=pl.DeviceIdType.MESH,
        )

    def reduce_copy(self, level, start_ref, acc_ref, got, sends, recvs):
        if level >= self.levels:
            return self.copy(self.own_shard(acc_ref, 1), got[level], sends, recvs, level)
        groups, rows = self.spot(level, min(level, 1), True)
        source = start_ref if level == 0 else acc_ref
        return self.copy(source.at[groups, rows], got[level], sends, recvs, level)

    def reduce_start(self, level, *refs):
        self.reduce_copy(level, *refs).start()

    def reduce_finish(self, level, start_ref, acc_ref, got, sends, recvs):
        self.reduce_copy(level, start_ref, acc_ref, got, sends, recvs).wait()
        if level >= self.levels:
            own = self.own_shard(acc_ref, 1)
            own[...] = (own[...].astype(F32) + got[level][...].astype(F32)).astype(BF16)
            return
        count, rows = self.sizes(level)
        groups, spots = self.spot(level, min(level, 1), False)
        if level == 0:
            target_groups, target_rows = pl.ds(0, count), pl.ds(0, rows)
            if self.padded > self.real:
                acc_ref[:, self.real :, :] = jnp.zeros_like(acc_ref[:, self.real :, :])
        else:
            target_groups, target_rows = groups, spots
        source = start_ref if level == 0 else acc_ref

        def add(index, carry):
            one = pl.ds(groups.start + index, 1)
            to = pl.ds(target_groups.start + index, 1)
            value = source[one, spots, :].astype(F32) + got[level][pl.ds(index, 1)].astype(F32)
            acc_ref[to, target_rows, :] = value.astype(BF16)
            return carry

        lax.fori_loop(0, count, add, 0)

    def own_shard(self, ref, first):
        if self.levels > self.even:
            return ref.at[self.spot(self.levels - 1, first, False)]
        groups, _ = self.spot(self.levels - 1, first, False)
        return ref.at[groups, pl.ds(0, self.shard)]

    def gather_copy(self, level, full_ref, sends, recvs):
        piece = full_ref.at[self.spot(level, 0, False)]
        return self.copy(piece, piece, sends, recvs, level)

    def gather_start(self, level, *refs):
        self.gather_copy(level, *refs).start()

    def gather_finish(self, level, *refs):
        self.gather_copy(level, *refs).wait()


def modulation(lead_ref, emb_ref, ada_ref, bias_ref):
    shape = (16, emb_ref.shape[0])
    rows = lax.broadcasted_iota(jnp.int32, shape, 0)
    columns = lane_index(shape)
    onehot = jnp.zeros(shape, F32)
    for step in range(2):
        lead = lead_ref[0, first_step(2) + step]
        onehot = jnp.where((rows == step) & (columns == lead), 1.0, onehot)
    condition = dot(onehot.astype(BF16), emb_ref[...])
    active = (condition * jax.nn.sigmoid(condition)).astype(BF16)
    return dot(active, ada_ref[...]) + bias_ref[...].astype(F32)


def project(x_refs, mod_ref, step, w_ref, normed_ref, head_refs):
    width = w_ref.shape[0]
    patches = x_refs[0].shape[1]
    rows = min(256, patches)
    shift = mod_ref[pl.ds(step, 1), 0:width]
    scale = mod_ref[pl.ds(step, 1), width : 2 * width]
    queries = len(head_refs) == 3
    for index, x_ref in enumerate(x_refs):

        def block(count, carry):
            start = pl.multiple_of(count * rows, rows)
            at = pl.ds(pl.multiple_of(index * patches + start, rows), rows)
            xhat, _ = normalize(x_ref[0, pl.ds(start, rows), :].astype(F32))
            normed = (xhat * (1.0 + scale) + shift).astype(BF16)
            normed_ref[0, at, :] = normed
            for part, head_ref in enumerate(head_refs):
                first = (part + (0 if queries else 1)) * width
                projected = dot(normed, w_ref[:, first : first + width])
                if queries and part == 0:
                    projected = projected.astype(BF16).astype(F32) * HD**-0.5
                projected = projected.astype(BF16)
                for pair in range(width // LANES):
                    head_ref[0, pair, at, :] = projected[:, pair * LANES : (pair + 1) * LANES]
            return carry

        lax.fori_loop(0, patches // rows, block, 0, unroll=True)


def with_ones(values):
    low = lane_index(values.shape) < HD
    one = jnp.ones_like(values)
    return jnp.where(low, values, one), jnp.where(low, one, values)


def exponentials(query, keys_ref, pair, width=256):
    count = keys_ref.shape[2]
    width = min(width, count)
    return jnp.concatenate(
        [
            jnp.exp(dot(query, keys_ref[0, pair, start : start + width, :], NT)).astype(BF16)
            for start in range(0, count, width)
        ],
        axis=-1,
    )


def masked(values):
    low = lane_index(values.shape) < HD
    zero = jnp.zeros_like(values)
    return jnp.where(low, values, zero), jnp.where(low, zero, values)


def near_kernel(rows, *refs):
    lead_ref, emb_ref, ada_ref, bias_ref, own_x, sib_x, w_ref = refs[:7]
    mod_ref, normed_ref, q_ref, k_ref, v_ref, acc_ref, ext_ref = refs[7:]
    step, pair = pl.program_id(0), pl.program_id(1)

    @pl.when((step == 0) & (pair == 0))
    def _():
        mod_ref[...] = modulation(lead_ref, emb_ref, ada_ref, bias_ref)

    @pl.when(pair == 0)
    def _():
        project([own_x, sib_x], mod_ref, step, w_ref, normed_ref, [q_ref, k_ref, v_ref])

    ext_ref[0], ext_ref[1] = with_ones(v_ref[0, pair])
    for start in range(0, q_ref.shape[2], rows):
        at = slice(start, start + rows)
        for head, query in enumerate(masked(q_ref[0, pair, at, :])):
            acc_ref[0, 0, head, at, :] = dot(exponentials(query, k_ref, pair), ext_ref[head])


def far_kernel(rows, step, sources, *refs):
    x_refs, refs = refs[:sources], refs[sources:]
    mod_ref, w_ref, q_ref, k_ref, v_ref, acc_ref = refs[:6]
    normed_ref, kr_ref, vr_ref, o_ref, qe_ref, ext_ref, total_ref = refs[-7:]
    pair = pl.program_id(0)

    @pl.when(pair == 0)
    def _():
        project(x_refs, mod_ref, step, w_ref, normed_ref, [kr_ref, vr_ref])

    ext_ref[0], ext_ref[1] = with_ones(vr_ref[0, pair])
    def finish(at, query, first, second, top_first, top_second):
        lane = lane_index(query.shape)
        low = lane < HD
        swapped = jnp.where(low, second, first)
        total = pltpu.roll(swapped, HD, 1)
        o_ref[0, 0, at, :] = jnp.where(low, first, second) / total
        log_total = jnp.log(swapped) + jnp.where(low, top_second, top_first)
        high = log_total.astype(BF16).astype(F32)
        middle = (log_total - high).astype(BF16).astype(F32)
        rest = log_total - high - middle
        spot = lane % HD
        extra = jnp.where(spot == 0, -high, jnp.where(spot == 1, -middle, -rest))
        extra = jnp.where(spot < 3, extra, 0.0).astype(BF16)
        qe_ref[0, 0, 0, at, :] = jnp.where(low, query, extra)
        qe_ref[0, 0, 1, at, :] = jnp.where(low, extra, query)
        return total

    def block(index, carry):
        at = pl.ds(pl.multiple_of(index * rows, rows), rows)
        query = q_ref[0, 0, at, :]
        sums = []
        for head, own in enumerate(masked(query)):
            more = dot(exponentials(own, kr_ref, pair), ext_ref[head])
            sums.append(acc_ref[0, 0, head, at, :] + more)
        total_ref[at, :] = finish(at, query, sums[0], sums[1], 0.0, 0.0)
        return carry

    lax.fori_loop(0, q_ref.shape[2] // rows, block, 0, unroll=True)
    total = total_ref[...]
    bad = jnp.sum(jnp.where((total > 1e-25) & (total < 1e25), 0.0, 1.0))

    @pl.when(bad > 0.0)
    def _():
        own_ext = with_ones(v_ref[0, 0])

        again_rows = min(32, q_ref.shape[2])

        def again(index, carry):
            at = pl.ds(pl.multiple_of(index * again_rows, again_rows), again_rows)
            query = q_ref[0, 0, at, :]
            sums, tops = [], []
            for head, own in enumerate(masked(query)):
                scores = dot(own, k_ref[0, 0], NT)
                others = dot(own, kr_ref[0, pair], NT)
                top = jnp.maximum(
                    jnp.max(scores, axis=-1, keepdims=True),
                    jnp.max(others, axis=-1, keepdims=True),
                )
                sums.append(
                    dot(jnp.exp(scores - top).astype(BF16), own_ext[head])
                    + dot(jnp.exp(others - top).astype(BF16), ext_ref[head])
                )
                tops.append(top)
            finish(at, query, sums[0], sums[1], tops[0], tops[1])
            return carry

        lax.fori_loop(0, q_ref.shape[2] // again_rows, again, 0)


def gelu_parts(values):
    cumulative = 0.5 * lax.erf(values * 0.7071067811865476) + 0.5
    bell = jnp.exp2(values * values * (-0.5 * LOG2E))
    return values * cumulative, cumulative + values * bell * 0.3989422804014327


def patch_kernel(
    rows,
    chunk,
    counts_ref,
    lead_ref,
    own_x,
    sib_x,
    own_ct,
    sib_ct,
    mod_ref,
    o_ref,
    out_w,
    fc1_w,
    fc2_w,
    final_own,
    final_sib,
    gm_ref,
    ge_ref,
    sums_ref,
    stack_one,
    stack_two,
    hidden_s,
    gpre_s,
    n2_s,
    g2_s,
    g1_s,
    mixed_s,
    gout_s,
    gfc1_s,
    gfc2_s,
    sums_s,
):
    step, half = pl.program_id(0), pl.program_id(1)
    width, hidden_width = fc1_w.shape
    patches = own_x.shape[1]
    slot = first_step(pl.num_programs(0)) + step
    active = (slot < counts_ref[0]).astype(F32)

    def piece(index):
        return mod_ref[pl.ds(step, 1), index * width : (index + 1) * width]

    gate1, shift2, scale2, gate2 = piece(2), piece(3), piece(4), piece(5)

    @pl.when((step == 0) & (half == 0))
    def _():
        sums_s[...] = jnp.zeros_like(sums_s)
        gout_s[...] = jnp.zeros_like(gout_s)
        gfc1_s[...] = jnp.zeros_like(gfc1_s)
        gfc2_s[...] = jnp.zeros_like(gfc2_s)

    def block(index, carry):
        at = pl.ds(pl.multiple_of(index * rows, rows), rows)
        x = jnp.where(half == 0, own_x[0, at, :], sib_x[0, at, :]).astype(F32)
        final_grad = jnp.where(half == 0, own_ct[0, at, :], sib_ct[0, at, :]).astype(F32) * active
        outs = [o_ref[0, pair, at, :] for pair in range(width // LANES)]
        mixed = jnp.concatenate([o.astype(BF16) for o in outs], axis=-1)
        mixed_s[at, :] = mixed
        branch_one = dot(mixed, out_w[...])
        middle = x + gate1 * branch_one
        xhat, inverse = normalize(middle)
        n2 = (xhat * (1.0 + scale2) + shift2).astype(BF16)
        n2_s[at, :] = n2
        g2 = (gate2 * final_grad).astype(BF16)
        g2_s[at, :] = g2
        branch_two = jnp.zeros((rows, width), F32)
        gy = jnp.zeros((rows, width), F32)
        for start in range(0, hidden_width, chunk):
            columns = slice(start, start + chunk)
            pre = dot(n2, fc1_w[:, columns])
            grad_hidden = dot(g2, fc2_w[columns, :], NT)
            hidden, slope = gelu_parts(pre)
            hidden = hidden.astype(BF16)
            grad_pre = (slope * grad_hidden).astype(BF16)
            hidden_s[at, columns] = hidden
            gpre_s[at, columns] = grad_pre
            branch_two += dot(hidden, fc2_w[columns, :])
            gy += dot(grad_pre, fc1_w[:, columns], NT)
        final = ((middle + gate2 * branch_two) * active).astype(BF16)

        @pl.when(half == 0)
        def _():
            final_own[0, at, :] = final

        @pl.when(half == 1)
        def _():
            final_sib[0, at, :] = final

        gm = final_grad + norm_back(gy * (1.0 + scale2), xhat, inverse)
        gm_ref[0, 0, at, :] = gm
        g1 = (gate1 * gm).astype(BF16)
        g1_s[at, :] = g1
        sums = [branch_one * gm, gy, gy * xhat, branch_two * final_grad]
        for row, value in enumerate(sums):
            place = pl.ds(2 * row + step, 1)
            sums_s[place, :] += jnp.sum(value, axis=0, keepdims=True)
        grad_mixed = dot(g1, out_w[...], NT).astype(BF16)
        lane = lane_index((rows, LANES))
        low = lane < HD
        spot = lane % HD
        for pair, o in enumerate(outs):
            grad = grad_mixed[:, pair * LANES : (pair + 1) * LANES]
            product = grad.astype(F32) * o
            first = jnp.sum(jnp.where(low, product, 0.0), axis=-1, keepdims=True)
            second = jnp.sum(jnp.where(low, 0.0, product), axis=-1, keepdims=True)
            inner = jnp.where(low, second, first)
            high = inner.astype(BF16).astype(F32)
            mid = (inner - high).astype(BF16).astype(F32)
            extra = jnp.where(spot == 0, -high, jnp.where(spot == 1, -mid, high + mid - inner))
            extra = jnp.where(spot < 3, extra, 0.0).astype(BF16)
            ge_ref[0, pair, 0, at, :] = jnp.where(low, grad, extra)
            ge_ref[0, pair, 1, at, :] = jnp.where(low, extra, grad)
        return carry

    lax.fori_loop(0, patches // rows, block, 0)
    gout_s[...] += dot(mixed_s[...], g1_s[...], TN)
    gfc1_s[...] += dot(n2_s[...], gpre_s[...], TN)
    gfc2_s[...] += dot(g2_s[...], hidden_s[...], TN)

    @pl.when((step == pl.num_programs(0) - 1) & (half == pl.num_programs(1) - 1))
    def _():
        for index in range(2):
            lead = lead_ref[0, first_step(2) + index]
            sums_s[12 + index : 13 + index, :] = jnp.where(lane_index((1, width)) == lead, 1.0, 0.0)
        sums_ref[...] = sums_s[...].astype(BF16)
        blocks = hidden_width // width
        for index in range(blocks):
            columns = slice(index * width, (index + 1) * width)
            stack_one[index] = gfc1_s[:, columns].astype(BF16)
            stack_two[index] = gfc2_s[:, columns].T.astype(BF16)
        stack_two[blocks] = gout_s[...].astype(BF16)


def attend_back_kernel(rows, first_pass, exchanges, grid_steps, *refs):
    count = len(exchanges)
    qe_ref, ge_ref, k_ref, v_ref = refs[:4]
    refs = refs[4:]
    if first_pass:
        gives, sums_ref, refs = refs[:count], refs[count], refs[count + 1 :]
        dq_ref, dk_ref, dv_ref = refs[:3]
        shards, all_ref, refs = refs[3 : 3 + count], refs[3 + count], refs[4 + count :]
        all_s, all_sends, all_recvs = refs[-3:]
    else:
        dq_in, shards, refs = refs[0], refs[1 : 1 + count], refs[1 + count :]
        dq_ref, dk_ref, dv_ref = refs[:3]
        fulls, refs = refs[3 : 3 + count], refs[3 + count :]
    dq_s, refs = refs[0], refs[1:]
    states = []
    for index, exchange in enumerate(exchanges):
        sends, recvs = refs[1], refs[2]
        if first_pass:
            got = refs[3 : 3 + exchange.all_levels]
            states.append((gives[index], refs[0], got, sends, recvs))
            refs = refs[3 + exchange.all_levels :]
        else:
            states.append((refs[0], sends, recvs))
            refs = refs[3:]
    per_step = k_ref.shape[2] // rows
    static_slots = grid_steps * per_step
    first_slot = (pl.program_id(0) * pl.num_programs(1) + pl.program_id(1)) * per_step
    levels = exchanges[0].all_levels if first_pass else exchanges[0].levels

    def all_copy(level):
        index = 0
        for lower in range(len(exchanges[0].bits)):
            index = index + exchanges[0].place(lower)[0] * (1 << lower)
        if level < 0:
            return all_s.at[pl.ds(index, 1)]
        size = 1 << level
        piece = all_s.at[pl.ds((index // size) * size, size)]
        return exchanges[0].copy(piece, piece, all_sends, all_recvs, level)

    def reduce_action(order):
        if order == 0:
            exchanges[0].barrier()
            own = all_copy(-1)
            own[...] = sums_ref[...][None]
        else:
            all_copy(order - 1).wait()
        if order < levels:
            all_copy(order).start()
        else:
            all_ref[...] = all_s[...]
        for exchange, state, shard in zip(exchanges, states, shards):
            if order > 0:
                exchange.reduce_finish(order - 1, *state)
            if order < levels:
                exchange.reduce_start(order, *state)
            else:
                shard[...] = exchange.own_shard(state[1], 1)[...][0]

    def gather_action(order):
        if order == 0:
            exchanges[0].barrier()
        for exchange, state, shard in zip(exchanges, states, shards):
            if order == 0:
                exchange.own_shard(state[0], 0)[...] = shard[...][None]
            else:
                exchange.gather_finish(levels - order, *state)
            if order < levels:
                exchange.gather_start(levels - 1 - order, *state)
        if order == levels:
            copies = [
                pltpu.make_async_copy(state[0], full, refs[index])
                for index, (state, full) in enumerate(zip(states, fulls))
            ]
            for copy in copies:
                copy.start()
            for copy in copies:
                copy.wait()

    action = reduce_action if first_pass else gather_action
    weights = [5.0, 10.0, 9.0, 6.0] + [4.0] * levels
    weights = weights[:levels] if first_pass else weights[:levels][::-1]
    marks, total = [0], 0.0
    for weight in weights:
        total += weight
        marks.append(total)
    last = static_slots - 1
    marks = [min(int(mark * last / total + 0.5), last) for mark in marks]

    dq_s[...] = jnp.zeros_like(dq_s) if first_pass else dq_in[0, 0].T

    def block(index, carry):
        for order, mark in enumerate(marks[:-1]):
            pl.when(first_slot + index == mark)(functools.partial(action, order))
        at = pl.ds(pl.multiple_of(index * rows, rows), rows)
        keys = k_ref[0, 0, at, :]
        values = v_ref[0, 0, at, :]
        lane = lane_index(keys.shape)
        low = lane < HD
        ones = jnp.where(lane % HD < 3, 1.0, 0.0).astype(BF16)
        zero = jnp.zeros_like(keys)
        grads = []
        for head in range(2):
            own = low if head == 0 else jnp.logical_not(low)
            query = qe_ref[0, 0, head]
            grad = ge_ref[0, 0, head]
            probs = jnp.exp(dot(jnp.where(own, keys, ones), query, NT))
            grad_probs = dot(jnp.where(own, values, ones), grad, NT)
            grad_scores = (probs * grad_probs).astype(BF16)
            grads.append((dot(grad_scores, query), dot(probs.astype(BF16), grad)))
            dq_s[...] += dot(jnp.where(own, keys, zero), grad_scores, TN)
        dk_ref[0, 0, at, :] = jnp.where(low, grads[0][0], grads[1][0]).astype(BF16)
        dv_ref[0, 0, at, :] = jnp.where(low, grads[0][1], grads[1][1]).astype(BF16)
        return carry

    lax.fori_loop(0, per_step, block, 0)
    if first_pass:
        dq_ref[0, 0] = dq_s[...].T
    else:
        dq_ref[0, 0] = (dq_s[...].T * HD**-0.5).astype(BF16)
    pl.when(first_slot + per_step == static_slots)(functools.partial(action, levels))


def joining(at, read, write, wait, own_ref, got_ref, out_ref, own_s, got_s, sems):
    mine = first_step(2)
    reads = [
        pltpu.make_async_copy(own_ref, own_s, sems.at[0]),
        pltpu.make_async_copy(got_ref, got_s, sems.at[1]),
    ]
    writes = [
        pltpu.make_async_copy(own_s, out_ref.at[pl.ds(mine, 2)], sems.at[2]),
        pltpu.make_async_copy(got_s, out_ref.at[pl.ds(2 - mine, 2)], sems.at[3]),
    ]

    @pl.when(at == read)
    def _():
        for copy in reads:
            copy.start()

    @pl.when(at == write)
    def _():
        for copy in reads:
            copy.wait()
        for copy in writes:
            copy.start()

    @pl.when(at == wait)
    def _():
        for copy in writes:
            copy.wait()


def project_back_far_kernel(
    dk_ref, dv_ref, normed_ref, w_ref, own_ref, got_ref, dx_ref, gw_ref, out_ref, own_s, got_s, sems
):
    width = w_ref.shape[0]
    at = pl.program_id(0) * pl.num_programs(1) + pl.program_id(1)
    joining(at, 0, 1, 3, own_ref, got_ref, out_ref, own_s, got_s, sems)
    joined = join_heads(dk_ref, dv_ref)
    dx_ref[0, 0] = dot(joined, w_ref[:, width:], NT).astype(BF16)

    @pl.when((pl.program_id(0) == 0) & (pl.program_id(1) == 0))
    def _():
        gw_ref[...] = jnp.zeros_like(gw_ref)

    gw_ref[...] += dot(normed_ref[0, 0], joined, TN)


def weight_back_kernel(early, *refs):
    dq_ref, dk_ref, dv_ref, normed_ref, far_ref, one_ref, two_ref = refs[:7]
    gw_ref, gfc1_ref, gfc2_ref, gout_ref = refs[7:11]
    gw_s, one_s, two_s, gfc1_s, gfc2_s, gout_s, sems = refs[11:]
    at = pl.program_id(0) * pl.num_programs(1) + pl.program_id(1)
    size = gout_s.shape[0]
    blocks = gfc1_s.shape[1] // size
    reads = [
        pltpu.make_async_copy(one_ref, one_s, sems.at[0]),
        pltpu.make_async_copy(two_ref, two_s, sems.at[1]),
    ]
    writes = [
        pltpu.make_async_copy(gfc1_s, gfc1_ref, sems.at[2]),
        pltpu.make_async_copy(gfc2_s, gfc2_ref, sems.at[3]),
        pltpu.make_async_copy(gout_s, gout_ref, sems.at[4]),
    ]

    @pl.when(at == 0)
    def _():
        for copy in reads:
            copy.start()

    @pl.when(at == 1)
    def _():
        reads[0].wait()
        unstack(
            grouped(early[0]), one_s, [(gfc1_s, 0, block * size) for block in range(blocks)], size
        )
        writes[0].start()

    @pl.when(at == 2)
    def _():
        reads[1].wait()
        rest = [(gfc2_s, block * size, 0) for block in range(blocks)] + [(gout_s, 0, 0)]
        unstack(grouped(early[1]), two_s, rest, size)
        writes[1].start()
        writes[2].start()

    @pl.when(at == pl.num_programs(0) * pl.num_programs(1) - 1)
    def _():
        for copy in writes:
            copy.wait()

    step, which = pl.program_id(0), pl.program_id(1)
    width = normed_ref.shape[3]

    @pl.when((step == 0) & (which == 0))
    def _():
        gw_s[:, :width] = jnp.zeros_like(gw_s[:, :width])
        gw_s[:, width:] = far_ref[...]

    gw_s[...] += dot(normed_ref[0, 0], join_heads(dq_ref, dk_ref, dv_ref), TN)

    @pl.when((step == pl.num_programs(0) - 1) & (which == pl.num_programs(1) - 1))
    def _():
        for block in range(gw_ref.shape[0]):
            gw_ref[block] = gw_s[:, block * LANES : (block + 1) * LANES].astype(BF16)


def join_heads(*grads):
    return jnp.concatenate([ref[0, pair] for ref in grads for pair in range(ref.shape[1])], axis=-1)


class Direct:
    def __init__(self, mesh_shape, row_tiles):
        self.chips = mesh_shape["seq"] // 2
        self.peers = mesh_shape["dp"] * self.chips
        self.half = row_tiles * 8
        self.piece = -(-row_tiles // (2 * self.peers)) * 16
        self.padded = self.piece * self.peers

    def me(self):
        return lax.axis_index("dp") * self.chips + lax.axis_index("seq") // 2

    def core(self):
        return lax.axis_index("seq") % 2

    def sibling(self):
        return {"seq": lax.axis_index("seq") + 1 - 2 * self.core()}

    def peer(self, shift):
        other = (self.me() + shift) % self.peers
        device = {"dp": other // self.chips, "seq": (other % self.chips) * 2 + self.core()}
        return other, device

    def rows(self, index):
        return pl.ds(pl.multiple_of(index * self.piece, 16), self.piece)

    def barrier(self):
        semaphore = pltpu.get_barrier_semaphore()

        def signal(device):
            pl.semaphore_signal(semaphore, 1, device_id=device, device_id_type=pl.DeviceIdType.MESH)

        signal(self.sibling())

        def greet(shift, carry):
            signal(self.peer(shift)[1])
            return carry

        lax.fori_loop(1, self.peers, greet, 0)
        pl.semaphore_wait(semaphore, self.peers)

    def copy(self, source, target, send, recv, device):
        return pltpu.make_async_remote_copy(
            src_ref=source,
            dst_ref=target,
            send_sem=send,
            recv_sem=recv,
            device_id=device,
            device_id_type=pl.DeviceIdType.MESH,
        )

    def each_peer(self, do):
        def one(shift, carry):
            do(shift)
            return carry

        lax.fori_loop(1, self.peers, one, 0)


def spread_leads(grads, step_of, table_rows):
    count = grads.shape[0]
    part = min(count, 512)
    row = lax.broadcasted_iota(jnp.int32, (part, part), 0)
    column = lane_index((part, part))
    chosen = (row // 16 == column // 16) & (row % 16 == 12 + step_of(column % 16))
    spread = jnp.where(chosen, 1.0, 0.0).astype(BF16)
    leads = [
        dot(grads[start : start + part, :LANES], spread, TN)[:table_rows]
        for start in range(0, count, part)
    ]
    return jnp.concatenate(leads, axis=-1)


def lead_grads(emb_ref, ada_ref, grads, leads, place, columns, gada_ref, gbada_ref, target):
    table = emb_ref[...].astype(F32)
    table_act = (table * jax.nn.sigmoid(table)).astype(BF16)
    chosen = jnp.where(place, leads, 0.0).astype(BF16)
    acts = dot(table_act, chosen, TN).astype(BF16)
    gada_ref[:, target] = dot(acts, grads)
    by_lead = dot(chosen, grads)
    gbada_ref[:, target] = jnp.sum(by_lead, axis=0, keepdims=True)
    high = by_lead.astype(BF16)
    low = (by_lead - high.astype(F32)).astype(BF16)
    return dot(high, ada_ref[:, columns], NT) + dot(low, ada_ref[:, columns], NT)


def tail_kernel(direct, remote, *refs):
    give_ref, own_x, sib_x, mod_ref, lead_ref, gm_ref, dq_ref, dk_ref, dv_ref, w_ref = refs[:10]
    others = refs[10 : 10 + remote]
    early_sums, emb_ref, ada_ref = refs[10 + remote : 13 + remote]
    grad_ref, got_ref, full_ref, all_ref = refs[13 + remote : 17 + remote]
    gada_ref, gbada_ref, gemb_ref = refs[17 + remote : 20 + remote]
    refs = refs[20 + remote :]
    sums_s, other_s, got_s, sum_s, core_s, pieces_s, full_s, all_s = refs[:8]
    core_sems, piece_sems, back_sems, all_sems, grad_sems, local_sem = refs[8:]
    step, half = pl.program_id(0), pl.program_id(1)
    width = own_x.shape[2]
    core, me = direct.core(), direct.me()

    core_copy = direct.copy(
        give_ref.at[1 - core], core_s, core_sems.at[0], core_sems.at[1], direct.sibling()
    )

    def piece_copy(shift):
        other, device = direct.peer(shift)
        return direct.copy(
            sum_s.at[direct.rows(other)],
            pieces_s.at[shift],
            piece_sems.at[0, shift],
            piece_sems.at[1, shift],
            device,
        )

    def full_copy(shift, arriving):
        _, device = direct.peer(shift)
        owner = (me + direct.peers - shift) % direct.peers if arriving else me
        place = full_s.at[core, direct.rows(owner)]
        return direct.copy(place, place, back_sems.at[0, shift], back_sems.at[1, shift], device)

    def sums_copy(shift, arriving):
        _, device = direct.peer(shift)
        owner = (me + direct.peers - shift) % direct.peers if arriving else me
        place = all_s.at[core, owner]
        return direct.copy(place, place, all_sems.at[0, shift], all_sems.at[1, shift], device)

    def side_copy(values, which, side):
        place = values.at[side]
        return direct.copy(
            place, place, core_sems.at[which], core_sems.at[which + 1], direct.sibling()
        )

    def grad_copy(index):
        return direct.copy(
            other_s.at[index],
            got_s.at[index],
            grad_sems.at[0, index],
            grad_sems.at[1, index],
            direct.sibling(),
        )

    @pl.when((step == 0) & (half == 0))
    def _():
        direct.barrier()
        core_copy.start()
        sums_s[...] = jnp.zeros_like(sums_s)

    @pl.when((step == 0) & (half == 1))
    def _():
        core_copy.wait()
        real = core_s.shape[0]
        sum_s[:real] = (give_ref[core].astype(F32) + core_s[...].astype(F32)).astype(BF16)
        if direct.padded > real:
            sum_s[real:] = jnp.zeros_like(sum_s[real:])
        direct.each_peer(lambda shift: piece_copy(shift).start())

    x = jnp.where(half == 0, own_x[0], sib_x[0]).astype(F32)
    scale = mod_ref[pl.ds(step, 1), width : 2 * width]
    xhat, inverse = normalize(x)
    gy = dot(join_heads(dq_ref, dk_ref, dv_ref), w_ref[...], NT)
    for other in others:
        gy = gy + other[0, 0].astype(F32)
    grad = (gm_ref[0, 0] + norm_back(gy * (1.0 + scale), xhat, inverse)).astype(BF16)

    @pl.when(half == 0)
    def _():
        grad_ref[0] = grad

    @pl.when(half == 1)
    def _():
        other_s[step] = grad
        grad_copy(step).start()

    for kind, value in enumerate((gy, gy * xhat)):
        total = jnp.sum(value, axis=0, keepdims=True)
        for index in range(width // LANES):
            place = pl.ds((kind * 2 + step) * (width // LANES) + index, 1)
            sums_s[place, :] += total[:, index * LANES : (index + 1) * LANES]

    @pl.when((step == 1) & (half == 1))
    def _():
        for index in range(2):
            chosen = lane_index((1, LANES)) == lead_ref[0, first_step(2) + index]
            sums_s[12 + index : 13 + index, :] = jnp.where(chosen, 1.0, 0.0)
        all_s[core, me] = sums_s[...].astype(BF16)
        direct.each_peer(lambda shift: sums_copy(shift, False).start())
        direct.each_peer(lambda shift: piece_copy(shift).wait())

        def add(shift, total):
            return total + pieces_s[shift].astype(F32)

        total = lax.fori_loop(1, direct.peers, add, sum_s[direct.rows(me)].astype(F32))
        full_s[core, direct.rows(me)] = total.astype(BF16)
        direct.each_peer(lambda shift: full_copy(shift, False).start())
        grads = early_sums[...]
        leads = spread_leads(grads, lambda row: row % 2, emb_ref.shape[0])
        row = lane_index((1, grads.shape[0])) % 16
        part = jnp.zeros(gemb_ref.shape, F32)
        for index in range(4):
            columns = slice((2 + index) * width, (3 + index) * width)
            target = slice(index * width, (index + 1) * width)
            place = row // 2 == index
            part += lead_grads(
                emb_ref, ada_ref, grads, leads, place, columns, gada_ref, gbada_ref, target
            )
        gemb_ref[...] = part

        def arrived(shift):
            full_copy(shift, False).wait_send()
            full_copy(shift, True).wait_recv()
            sums_copy(shift, False).wait_send()
            sums_copy(shift, True).wait_recv()

        direct.each_peer(arrived)
        side_copy(full_s, 2, core).start()
        side_copy(all_s, 4, core).start()
        for index in range(2):
            grad_copy(index).wait()
        side_copy(full_s, 2, core).wait_send()
        side_copy(full_s, 2, 1 - core).wait_recv()
        side_copy(all_s, 4, core).wait_send()
        side_copy(all_s, 4, 1 - core).wait_recv()
        outs = [(got_s, got_ref), (full_s, full_ref), (all_s, all_ref)]
        copies = [
            pltpu.make_async_copy(source, target, local_sem.at[index])
            for index, (source, target) in enumerate(outs)
        ]
        for copy in copies:
            copy.start()
        for copy in copies:
            copy.wait()


def unstack(at, full_ref, targets, rows):
    row, end = 0, rows * len(targets)
    while row < end:
        group, inside, left = at(row)
        block, place = divmod(row, rows)
        count = min(left, rows - place)
        target, first_row, first_column = targets[block]
        columns = slice(first_column, first_column + full_ref.shape[2])
        value = full_ref[group, inside : inside + count, :].astype(F32)
        target[first_row + place : first_row + place + count, columns] = value
        row += count


def grouped(exchange):
    def at(row):
        group, inside = divmod(row, exchange.real)
        return group, inside, exchange.real - inside

    return at


def final_kernel(direct, *refs):
    late_sums, emb_ref, ada_ref, gada_part, gbada_part, gemb_part = refs[:6]
    late_ref, own_ref, got_ref = refs[6:9]
    grad_out, gemb_ref, gada_out, gbada_ref, gqkv_out = refs[9:14]
    gada_s, gbada_s, gqkv_s, late_s, own_s, got_s, sems = refs[14:]
    size = emb_ref.shape[1]
    mine = first_step(2)
    pairs = [(late_ref, late_s), (own_ref, own_s), (got_ref, got_s)]
    reads = [
        pltpu.make_async_copy(source, target, sems.at[index])
        for index, (source, target) in enumerate(pairs)
    ]
    for read in reads:
        read.start()
    copies = []

    def start(source, target):
        copy = pltpu.make_async_copy(source, target, sems.at[3 + len(copies)])
        copy.start()
        copies.append(copy)

    def halved(row):
        group, inside = divmod(row, direct.half)
        return group, inside, direct.half - inside

    start(gada_part, gada_out.at[:, pl.ds(2 * size, 4 * size)])
    columns = gqkv_s.shape[1] // LANES
    reads[0].wait()
    unstack(halved, late_s, [(gqkv_s, 0, block * LANES) for block in range(columns)], size)
    start(gqkv_s, gqkv_out)
    reads[1].wait()
    start(own_s, grad_out.at[pl.ds(mine, 2)])
    reads[2].wait()
    start(got_s, grad_out.at[pl.ds(2 - mine, 2)])

    table_rows = emb_ref.shape[0]
    table = emb_ref[...].astype(F32)
    gate = jax.nn.sigmoid(table)
    slope = gate * (1.0 + table * (1.0 - gate))
    total = gemb_part[...]
    grads = late_sums[...]
    parts = size // LANES
    leads = spread_leads(grads, lambda row: (row // parts) % 2, table_rows)
    row = lane_index((1, grads.shape[0])) % 16
    for index in range(2):
        for part in range(parts):
            place = (row // (2 * parts) == index) & (row % parts == part)
            columns = slice(index * size + part * LANES, index * size + (part + 1) * LANES)
            total += lead_grads(
                emb_ref, ada_ref, grads, leads, place, columns, gada_s, gbada_s, columns
            )
    gemb_ref[...] = total * slope
    start(gada_s, gada_out.at[:, pl.ds(0, 2 * size)])
    gbada_ref[: 2 * size] = gbada_s[0]
    gbada_ref[2 * size :] = gbada_part[0]
    for copy in copies:
        copy.wait()


def local(
    mesh_shape, inputs, cotangent, counts, lead_steps, emb_table, w_ada, b_ada, w_qkv, w_out, w_fc1, w_fc2
):
    slots, items, patches, width = inputs.shape
    chips = mesh_shape["seq"] // 2
    blocks = w_fc1.shape[1] // w_fc1.shape[0]
    steps = slots * items // 2
    hidden_width = w_fc1.shape[1]
    pairs = width // LANES
    rows = 2 * patches
    remote = 2 * (chips - 1)
    far_rows = remote * patches
    spot = lax.axis_index("seq")
    core = lax.rem(spot, 2)
    devices = 2 * chips

    def send(values, shift, cross):
        pairs_list = []
        for source in range(devices):
            chip, side = source // 2, source % 2
            pairs_list.append((source, ((chip + shift) % chips) * 2 + (1 - side if cross else side)))
        return lax.ppermute(values, "seq", pairs_list)

    x_steps = inputs.reshape(2, steps, patches, width)
    ct_steps = cotangent.reshape(2, steps, patches, width)
    own_x = lax.dynamic_index_in_dim(x_steps, core, 0, keepdims=False)
    other_x = lax.dynamic_index_in_dim(x_steps, 1 - core, 0, keepdims=False)
    own_ct = lax.dynamic_index_in_dim(ct_steps, core, 0, keepdims=False)
    other_ct = lax.dynamic_index_in_dim(ct_steps, 1 - core, 0, keepdims=False)
    sib_x = send(other_x, 0, True)
    far_x = []
    for step in range(steps):
        some = slice(step, step + 1)
        for shift in range(1, chips):
            far_x.append(send(own_x[some], shift, False))
            far_x.append(send(other_x[some], shift, True))
    sib_ct = send(other_ct, 0, True)

    step_block = pl.BlockSpec((1, patches, width), lambda j, i: (j, 0, 0))
    patch_block = pl.BlockSpec((1, 1, patches, width), lambda j, i: (j, i, 0, 0))

    def head_rows(count):
        return pl.BlockSpec((1, 1, count, LANES), lambda j, p: (j, p, 0, 0))

    def of_step(*shape):
        return pl.BlockSpec((1,) + shape, lambda j, p: (j,) + (0,) * len(shape))

    both_heads = pl.BlockSpec((1, 1, 2, rows, LANES), lambda j, p: (j, p, 0, 0, 0))
    piece = min(256, rows)
    near_work = 4 * steps * pairs * 2 * rows * LANES * rows
    near_heads = jax.ShapeDtypeStruct((steps, pairs, rows, LANES), BF16)
    mod, n1, q, k, v, acc = call(
        functools.partial(near_kernel, piece),
        "near",
        (steps, pairs),
        [scalars(), whole(emb_table.shape), whole(w_ada.shape), whole((1, 6 * width))]
        + [step_block] * 2
        + [whole(w_qkv.shape)],
        [whole((16, 6 * width)), of_step(rows, width)]
        + [of_step(pairs, rows, LANES)] * 3
        + [both_heads],
        [
            jax.ShapeDtypeStruct((16, 6 * width), F32),
            jax.ShapeDtypeStruct((steps, rows, width), BF16),
            near_heads,
            near_heads,
            near_heads,
            jax.ShapeDtypeStruct((steps, pairs, 2, rows, LANES), F32),
        ],
        [pltpu.VMEM((2, rows, LANES), BF16)],
        flops=near_work + 6 * steps * rows * width * width,
        exps=steps * pairs * 2 * rows * rows,
    )(lead_steps, emb_table, w_ada, b_ada.reshape(1, -1), own_x, sib_x, w_qkv)

    def far(step, before):
        some_x = far_x[step * remote : (step + 1) * remote]

        def at_step(*shape):
            return pl.BlockSpec((1,) + shape, lambda p: (step,) + (0,) * len(shape))

        def at_pair(*shape):
            return pl.BlockSpec((1, 1) + shape, lambda p: (step, p) + (0,) * len(shape))

        operands = [*some_x, mod, w_qkv, q, k, v, acc]
        return call(
            functools.partial(far_kernel, piece, step, remote),
            "far",
            (pairs,),
            [whole((1, patches, width))] * remote
            + [whole(mod.shape), whole(w_qkv.shape)]
            + [at_pair(rows, LANES)] * 3
            + [at_pair(2, rows, LANES)]
            + [pl.BlockSpec(memory_space=pl.ANY)] * len(before),
            [at_step(far_rows, width)]
            + [at_step(pairs, far_rows, LANES)] * 2
            + [at_pair(rows, LANES), at_pair(2, rows, LANES)],
            [
                jax.ShapeDtypeStruct((steps, far_rows, width), BF16),
                jax.ShapeDtypeStruct((steps, pairs, far_rows, LANES), BF16),
                jax.ShapeDtypeStruct((steps, pairs, far_rows, LANES), BF16),
                jax.ShapeDtypeStruct((steps, pairs, rows, LANES), F32),
                jax.ShapeDtypeStruct((steps, pairs, 2, rows, LANES), BF16),
            ],
            [pltpu.VMEM((2, far_rows, LANES), BF16), pltpu.VMEM((rows, LANES), F32)],
            flops=near_work // 2,
            exps=pairs * 2 * rows * far_rows,
            aliases={len(operands) + index: index for index in range(len(before))},
        )(*operands, *before)

    far_results = []
    for step in range(steps):
        far_results = far(step, far_results)
    n1r, kr, vr, o, qe = far_results

    block_rows = min(256, patches)
    outs = call(
        functools.partial(patch_kernel, block_rows, hidden_width),
        "patchwise",
        (steps, 2),
        [scalars()] * 2
        + [step_block] * 4
        + [
            whole(mod.shape),
            pl.BlockSpec((1, pairs, patches, LANES), lambda j, i: (j, 0, i, 0)),
            whole(w_out.shape),
            whole(w_fc1.shape),
            whole(w_fc2.shape),
        ],
        [
            step_block,
            step_block,
            patch_block,
            pl.BlockSpec((1, pairs, 2, patches, LANES), lambda j, i: (j, 0, 0, i, 0)),
            whole((16, width)),
            whole((blocks, width, width)),
            whole((blocks + 1, width, width)),
        ],
        [
            jax.ShapeDtypeStruct((steps, patches, width), BF16),
            jax.ShapeDtypeStruct((steps, patches, width), BF16),
            jax.ShapeDtypeStruct((steps, 2, patches, width), F32),
            jax.ShapeDtypeStruct((steps, pairs, 2, rows, LANES), BF16),
            jax.ShapeDtypeStruct((16, width), BF16),
            jax.ShapeDtypeStruct((blocks, width, width), BF16),
            jax.ShapeDtypeStruct((blocks + 1, width, width), BF16),
        ],
        [pltpu.VMEM((patches, hidden_width), BF16)] * 2
        + [pltpu.VMEM((patches, width), BF16)] * 4
        + [
            pltpu.VMEM((width, width), F32),
            pltpu.VMEM((width, hidden_width), F32),
            pltpu.VMEM((width, hidden_width), F32),
            pltpu.VMEM((16, width), F32),
        ],
        flops=6 * steps * rows * width * (2 * hidden_width + width),
        moved=steps * rows * width * 20,
        exps=2 * steps * rows * hidden_width,
    )(counts, lead_steps, own_x, sib_x, own_ct, sib_ct, mod, o, w_out, w_fc1, w_fc2)
    final_own, final_sib, gm, ge, sums, stack_one, stack_two = outs
    final_got = send(final_sib, 0, True)
    early = [Exchange(mesh_shape, blocks * width // 16, 0), Exchange(mesh_shape, (blocks + 1) * width // 16, 1)]
    gives = [g.reshape(e.groups, e.real, width) for e, g in zip(early, (stack_one, stack_two))]

    def attend_back(keys, values, extra, first, name):
        count = keys.shape[2]
        in_specs = [both_heads] * 2 + [head_rows(count)] * 2
        out_specs = [head_rows(rows), head_rows(count), head_rows(count)]
        out_shape = [
            jax.ShapeDtypeStruct((steps, pairs, rows, LANES), F32 if first else BF16),
            jax.ShapeDtypeStruct((steps, pairs, count, LANES), BF16),
            jax.ShapeDtypeStruct((steps, pairs, count, LANES), BF16),
        ]
        scratch = [pltpu.VMEM((LANES, rows), F32)]
        if not first:
            in_specs += [head_rows(rows)]
        for exchange in early:
            shape = (exchange.groups, exchange.padded, width)
            shard = (exchange.shard, width)
            sems = [pltpu.SemaphoreType.DMA((exchange.all_levels,))] * 2
            if first:
                in_specs += [whole((exchange.groups, exchange.real, width))]
                out_specs += [whole(shard)]
                out_shape += [jax.ShapeDtypeStruct(shard, BF16)]
                half = (exchange.groups // 2, exchange.padded, width)
                scratch += [pltpu.VMEM(half, BF16)] + sems + exchange.receive_scratch(width)
            else:
                in_specs += [whole(shard)]
                out_specs += [pl.BlockSpec(memory_space=pl.ANY)]
                out_shape += [jax.ShapeDtypeStruct(shape, BF16)]
                scratch += [pltpu.VMEM(shape, BF16)] + sems
        if first:
            every = (mesh_shape["dp"] * mesh_shape["seq"], 16, width)
            in_specs += [whole(sums.shape)]
            out_specs += [whole(every)]
            out_shape += [jax.ShapeDtypeStruct(every, BF16)]
            sems = [pltpu.SemaphoreType.DMA((early[0].all_levels,))] * 2
            scratch += [pltpu.VMEM(every, BF16)] + sems
        else:
            scratch += [pltpu.SemaphoreType.DMA] * len(early)
        return call(
            functools.partial(attend_back_kernel, min(512, count), first, early, steps * pairs),
            name,
            (steps, pairs),
            in_specs,
            out_specs,
            out_shape,
            scratch,
            flops=10 * steps * pairs * 2 * rows * count * LANES,
            exps=steps * pairs * 2 * rows * count,
            collective=1 if first else 2,
        )(qe, ge, keys, values, *extra)

    grad_block = pl.BlockSpec((1, pairs, patches, LANES), lambda j, i: (j, 0, i, 0))
    hbm = pl.BlockSpec(memory_space=pl.ANY)

    dq_part, dkr, dvr, shard_one, shard_two, early_all = attend_back(
        kr, vr, [*gives, sums], True, "attend_back_far"
    )
    dx_far, gw_part, outputs = call(
        project_back_far_kernel,
        "project_back_far",
        (steps, remote),
        [grad_block] * 2 + [patch_block, whole(w_qkv.shape), hbm, hbm],
        [patch_block, whole((width, 2 * width)), hbm],
        [
            jax.ShapeDtypeStruct((steps, remote, patches, width), BF16),
            jax.ShapeDtypeStruct((width, 2 * width), F32),
            jax.ShapeDtypeStruct((2 * steps, patches, width), BF16),
        ],
        [pltpu.VMEM((steps, patches, width), BF16)] * 2 + [pltpu.SemaphoreType.DMA((4,))],
        flops=4 * steps * far_rows * width * 2 * width,
        moved=steps * far_rows * width * 8,
    )(dkr, dvr, n1r.reshape(steps, remote, patches, width), w_qkv, final_own, final_got)
    dx_got = [send(dx_far[:, 2 * r - 2 : 2 * r], -r, False) for r in range(1, chips)]
    dq, dk, dv, *early_sums = attend_back(
        k, v, [dq_part, shard_one, shard_two], False, "attend_back_near"
    )
    columns = w_qkv.shape[1] // LANES
    early_weights = (w_fc1, w_fc2, w_out)
    give_late, g_fc1, g_fc2, g_out = call(
        functools.partial(weight_back_kernel, early),
        "weight_back",
        (steps, 2),
        [grad_block] * 3 + [patch_block, whole(gw_part.shape), hbm, hbm],
        [whole((columns, width, LANES))] + [hbm] * 3,
        [jax.ShapeDtypeStruct((columns, width, LANES), BF16)]
        + [jax.ShapeDtypeStruct(w.shape, F32) for w in early_weights],
        [pltpu.VMEM((width, columns * LANES), F32)]
        + [pltpu.VMEM(value.shape, BF16) for value in early_sums]
        + [pltpu.VMEM(w.shape, F32) for w in early_weights]
        + [pltpu.SemaphoreType.DMA((5,))],
        flops=2 * steps * rows * width * 3 * width,
        moved=steps * rows * width * 8,
    )(dq, dk, dv, n1.reshape(steps, 2, patches, width), gw_part, *early_sums)

    direct = Direct(mesh_shape, columns * width // 16)
    full_shape = (2, direct.padded, LANES)
    late_all_shape = (2, direct.peers, 16, LANES)
    early_all = early_all.reshape(-1, width)
    grad_own, grad_got, late_sum, late_all, *early_parts = call(
        functools.partial(tail_kernel, direct, len(dx_got)),
        "tail",
        (steps, 2),
        [whole((2, direct.half, LANES)), step_block, step_block, whole(mod.shape), scalars()]
        + [patch_block]
        + [grad_block] * 3
        + [whole(w_qkv.shape)]
        + [patch_block] * len(dx_got)
        + [whole(early_all.shape), whole(emb_table.shape), whole(w_ada.shape)],
        [step_block, hbm, hbm, hbm]
        + [whole((width, 4 * width)), whole((1, 4 * width)), whole(emb_table.shape)],
        [
            jax.ShapeDtypeStruct((steps, patches, width), BF16),
            jax.ShapeDtypeStruct((steps, patches, width), BF16),
            jax.ShapeDtypeStruct(full_shape, BF16),
            jax.ShapeDtypeStruct(late_all_shape, BF16),
            jax.ShapeDtypeStruct((width, 4 * width), F32),
            jax.ShapeDtypeStruct((1, 4 * width), F32),
            jax.ShapeDtypeStruct(emb_table.shape, F32),
        ],
        [
            pltpu.VMEM((16, LANES), F32),
            pltpu.VMEM((steps, patches, width), BF16),
            pltpu.VMEM((steps, patches, width), BF16),
            pltpu.VMEM((direct.padded, LANES), BF16),
            pltpu.VMEM((direct.half, LANES), BF16),
            pltpu.VMEM((direct.peers, direct.piece, LANES), BF16),
            pltpu.VMEM(full_shape, BF16),
            pltpu.VMEM(late_all_shape, BF16),
            pltpu.SemaphoreType.DMA((6,)),
            pltpu.SemaphoreType.DMA((2, direct.peers)),
            pltpu.SemaphoreType.DMA((2, direct.peers)),
            pltpu.SemaphoreType.DMA((2, direct.peers)),
            pltpu.SemaphoreType.DMA((2, steps)),
            pltpu.SemaphoreType.DMA((3,)),
        ],
        flops=2 * steps * rows * width * 3 * width,
        collective=3,
    )(
        give_late.reshape(2, direct.half, LANES),
        own_x,
        sib_x,
        mod,
        lead_steps,
        gm,
        dq,
        dk,
        dv,
        w_qkv,
        *dx_got,
        early_all,
        emb_table,
        w_ada,
    )

    late_all = late_all.reshape(-1, LANES)
    small = [late_all, emb_table, w_ada, *early_parts]
    large = [late_sum, grad_own, grad_got]
    out_shapes = [(slots * items, patches, width), emb_table.shape, w_ada.shape, b_ada.shape, w_qkv.shape]
    grad_inputs, g_emb, g_ada, g_bada, g_qkv = call(
        functools.partial(final_kernel, direct),
        "final",
        (),
        [whole(value.shape) for value in small] + [hbm] * len(large),
        [hbm, whole(emb_table.shape), hbm, whole(b_ada.shape), hbm],
        [
            jax.ShapeDtypeStruct(shape, F32 if index else BF16)
            for index, shape in enumerate(out_shapes)
        ],
        [pltpu.VMEM(shape, F32) for shape in ((width, 2 * width), (1, 2 * width), w_qkv.shape)]
        + [pltpu.VMEM(value.shape, BF16) for value in large]
        + [pltpu.SemaphoreType.DMA((8,))],
        flops=2 * late_all.shape[0] * width * 6 * width,
        moved=6 * w_ada.size,
    )(*small, *large)
    return (
        outputs.reshape(inputs.shape),
        grad_inputs.reshape(inputs.shape),
        g_emb,
        g_ada,
        g_bada,
        g_qkv,
        g_out,
        g_fc1,
        g_fc2,
    )


def solution(mesh):
    tokens = P(None, "dp", "seq", None)
    return jax.shard_map(
        functools.partial(local, dict(mesh.shape)),
        mesh=mesh,
        in_specs=(tokens, tokens, P("dp"), P("dp", None)) + (P(),) * 7,
        out_specs=(tokens, tokens) + (P(),) * 7,
        check_vma=False,
    )
```

```python
import functools

import jax
import jax.numpy as jnp
from jax import lax
from jax.experimental import pallas as pl
from jax.experimental.pallas import tpu as pltpu
from jax.sharding import PartitionSpec as P

HD = 64
LANES = 128
EPSILON = 1e-06
LOG2E = 1.4426950408889634
NN = (((1,), (0,)), ((), ()))
NT = (((1,), (1,)), ((), ()))
TN = (((0,), (0,)), ((), ()))
F32 = jnp.float32
BF16 = jnp.bfloat16
MIB = 1024 * 1024
GRANTS = {"patchwise": 20, "weight_back": 18}


def dot(a, b, dims=NN):
    return lax.dot_general(a, b, dims, preferred_element_type=F32)


def call(
    body,
    name,
    grid,
    in_specs,
    out_specs,
    out_shape,
    scratch=(),
    flops=0,
    moved=0,
    exps=0,
    collective=None,
    aliases=None,
):
    return pl.pallas_call(
        body,
        name=name,
        grid=grid,
        in_specs=in_specs,
        out_specs=out_specs,
        out_shape=out_shape,
        scratch_shapes=list(scratch),
        input_output_aliases=aliases or {},
        cost_estimate=pl.CostEstimate(flops=flops, bytes_accessed=moved, transcendentals=exps),
        compiler_params=pltpu.CompilerParams(
            vmem_limit_bytes=GRANTS.get(name, 16) * MIB,
            collective_id=collective,
            has_side_effects=collective is not None,
        ),
    )


def whole(shape):
    return pl.BlockSpec(shape, lambda *_: (0,) * len(shape))


def scalars():
    return pl.BlockSpec(memory_space=pltpu.SMEM)


def lane_index(shape):
    return lax.broadcasted_iota(jnp.int32, shape, 1)


def first_step(steps):
    return lax.rem(lax.axis_index("seq"), 2) * steps


def normalize(values):
    center = values - jnp.mean(values, axis=-1, keepdims=True)
    spread = jnp.mean(center * center, axis=-1, keepdims=True)
    inverse = lax.rsqrt(spread + EPSILON)
    return center * inverse, inverse


def norm_back(grad, xhat, inverse):
    first = jnp.mean(grad, axis=-1, keepdims=True)
    second = jnp.mean(grad * xhat, axis=-1, keepdims=True)
    return inverse * (grad - first - xhat * second)


def pick(refs, which):
    value = refs[0][0]
    for index in range(1, len(refs)):
        value = jnp.where(which == index, refs[index][0], value)
    return value


class Exchange:
    def __init__(self, mesh_shape, row_tiles, turn=0):
        bits = {"seq": [], "dp": []}
        for axis in bits:
            bit = 1
            while bit < mesh_shape[axis]:
                bits[axis].append((axis, bit))
                bit *= 2
        turned = bits["dp"][turn:] + bits["dp"][:turn]
        self.bits = bits["seq"][:1] + turned + bits["seq"][1:]
        self.all_levels = len(self.bits)
        self.levels = 1 + len(turned)
        self.even = 0
        while self.even < self.levels and row_tiles % 2 == 0:
            row_tiles //= 2
            self.even += 1
        unit = 2 ** (self.levels - self.even)
        self.groups = 2**self.even
        self.real = row_tiles * 16
        self.padded = -(-row_tiles // unit) * unit * 16
        self.shard = self.padded // unit

    def sizes(self, level):
        if level < self.even:
            return (self.groups >> (level + 1), self.real)
        return (1, self.padded >> (level - self.even + 1))

    def receive_scratch(self, width):
        last = self.levels - 1
        return [
            pltpu.VMEM(self.sizes(min(level, last)) + (width,), BF16)
            for level in range(self.all_levels)
        ]

    def place(self, level):
        axis, bit = self.bits[level]
        here = lax.axis_index(axis)
        value = (here // bit) % 2
        return value, {axis: here + bit * (1 - 2 * value)}

    def spot(self, level, first, flip):
        group, row = 0, 0
        for index in range(first, level + 1):
            value, _ = self.place(index)
            if flip and index == level:
                value = 1 - value
            if index < self.even:
                group = group + value * (self.groups >> (index + 1))
            else:
                row = row + value * (self.padded >> (index - self.even + 1))
        if level >= self.even:
            row = pl.multiple_of(row, 16)
        count, rows = self.sizes(level)
        return pl.ds(group, count), pl.ds(row, rows)

    def barrier(self):
        semaphore = pltpu.get_barrier_semaphore()
        for level in range(self.all_levels):
            _, partner = self.place(level)
            pl.semaphore_signal(
                semaphore, inc=1, device_id=partner, device_id_type=pl.DeviceIdType.MESH
            )
        pl.semaphore_wait(semaphore, self.all_levels)

    def copy(self, source, target, sends, recvs, level):
        _, partner = self.place(level)
        return pltpu.make_async_remote_copy(
            src_ref=source,
            dst_ref=target,
            send_sem=sends.at[level],
            recv_sem=recvs.at[level],
            device_id=partner,
            device_id_type=pl.DeviceIdType.MESH,
        )

    def reduce_copy(self, level, start_ref, acc_ref, got, sends, recvs):
        if level >= self.levels:
            return self.copy(self.own_shard(acc_ref, 1), got[level], sends, recvs, level)
        groups, rows = self.spot(level, min(level, 1), True)
        source = start_ref if level == 0 else acc_ref
        return self.copy(source.at[groups, rows], got[level], sends, recvs, level)

    def reduce_start(self, level, *refs):
        self.reduce_copy(level, *refs).start()

    def reduce_finish(self, level, start_ref, acc_ref, got, sends, recvs):
        self.reduce_copy(level, start_ref, acc_ref, got, sends, recvs).wait()
        if level >= self.levels:
            own = self.own_shard(acc_ref, 1)
            own[...] = (own[...].astype(F32) + got[level][...].astype(F32)).astype(BF16)
            return
        count, rows = self.sizes(level)
        groups, spots = self.spot(level, min(level, 1), False)
        if level == 0:
            target_groups, target_rows = pl.ds(0, count), pl.ds(0, rows)
            if self.padded > self.real:
                acc_ref[:, self.real :, :] = jnp.zeros_like(acc_ref[:, self.real :, :])
        else:
            target_groups, target_rows = groups, spots
        source = start_ref if level == 0 else acc_ref

        def add(index, carry):
            one = pl.ds(groups.start + index, 1)
            to = pl.ds(target_groups.start + index, 1)
            value = source[one, spots, :].astype(F32) + got[level][pl.ds(index, 1)].astype(F32)
            acc_ref[to, target_rows, :] = value.astype(BF16)
            return carry

        lax.fori_loop(0, count, add, 0)

    def own_shard(self, ref, first):
        if self.levels > self.even:
            return ref.at[self.spot(self.levels - 1, first, False)]
        groups, _ = self.spot(self.levels - 1, first, False)
        return ref.at[groups, pl.ds(0, self.shard)]

    def gather_copy(self, level, full_ref, sends, recvs):
        piece = full_ref.at[self.spot(level, 0, False)]
        return self.copy(piece, piece, sends, recvs, level)

    def gather_start(self, level, *refs):
        self.gather_copy(level, *refs).start()

    def gather_finish(self, level, *refs):
        self.gather_copy(level, *refs).wait()


def modulation(lead_ref, emb_ref, ada_ref, bias_ref):
    shape = (16, emb_ref.shape[0])
    rows = lax.broadcasted_iota(jnp.int32, shape, 0)
    columns = lane_index(shape)
    onehot = jnp.zeros(shape, F32)
    for step in range(2):
        lead = lead_ref[0, first_step(2) + step]
        onehot = jnp.where((rows == step) & (columns == lead), 1.0, onehot)
    condition = dot(onehot.astype(BF16), emb_ref[...])
    active = (condition * jax.nn.sigmoid(condition)).astype(BF16)
    return dot(active, ada_ref[...]) + bias_ref[...].astype(F32)


def project(x_refs, mod_ref, step, w_ref, normed_ref, head_refs):
    width = w_ref.shape[0]
    patches = x_refs[0].shape[1]
    rows = min(256, patches)
    shift = mod_ref[pl.ds(step, 1), 0:width]
    scale = mod_ref[pl.ds(step, 1), width : 2 * width]
    queries = len(head_refs) == 3
    for index, x_ref in enumerate(x_refs):

        def block(count, carry):
            start = pl.multiple_of(count * rows, rows)
            at = pl.ds(pl.multiple_of(index * patches + start, rows), rows)
            xhat, _ = normalize(x_ref[0, pl.ds(start, rows), :].astype(F32))
            normed = (xhat * (1.0 + scale) + shift).astype(BF16)
            normed_ref[0, at, :] = normed
            for part, head_ref in enumerate(head_refs):
                first = (part + (0 if queries else 1)) * width
                projected = dot(normed, w_ref[:, first : first + width])
                if queries and part == 0:
                    projected = projected.astype(BF16).astype(F32) * HD**-0.5
                projected = projected.astype(BF16)
                for pair in range(width // LANES):
                    head_ref[0, pair, at, :] = projected[:, pair * LANES : (pair + 1) * LANES]
            return carry

        lax.fori_loop(0, patches // rows, block, 0, unroll=True)


def with_ones(values):
    low = lane_index(values.shape) < HD
    one = jnp.ones_like(values)
    return jnp.where(low, values, one), jnp.where(low, one, values)


def exponentials(query, keys_ref, pair, width=256):
    count = keys_ref.shape[2]
    width = min(width, count)
    return jnp.concatenate(
        [
            jnp.exp(dot(query, keys_ref[0, pair, start : start + width, :], NT)).astype(BF16)
            for start in range(0, count, width)
        ],
        axis=-1,
    )


def masked(values):
    low = lane_index(values.shape) < HD
    zero = jnp.zeros_like(values)
    return jnp.where(low, values, zero), jnp.where(low, zero, values)


def near_kernel(rows, *refs):
    lead_ref, emb_ref, ada_ref, bias_ref, own_x, sib_x, w_ref = refs[:7]
    mod_ref, normed_ref, q_ref, k_ref, v_ref, acc_ref, ext_ref = refs[7:]
    step, pair = pl.program_id(0), pl.program_id(1)

    @pl.when((step == 0) & (pair == 0))
    def _():
        mod_ref[...] = modulation(lead_ref, emb_ref, ada_ref, bias_ref)

    @pl.when(pair == 0)
    def _():
        project([own_x, sib_x], mod_ref, step, w_ref, normed_ref, [q_ref, k_ref, v_ref])

    ext_ref[0], ext_ref[1] = with_ones(v_ref[0, pair])
    for start in range(0, q_ref.shape[2], rows):
        at = slice(start, start + rows)
        for head, query in enumerate(masked(q_ref[0, pair, at, :])):
            acc_ref[0, 0, head, at, :] = dot(exponentials(query, k_ref, pair), ext_ref[head])


def far_kernel(rows, step, sources, *refs):
    x_refs, refs = refs[:sources], refs[sources:]
    mod_ref, w_ref, q_ref, k_ref, v_ref, acc_ref = refs[:6]
    normed_ref, kr_ref, vr_ref, o_ref, qe_ref, ext_ref, total_ref = refs[-7:]
    pair = pl.program_id(0)

    @pl.when(pair == 0)
    def _():
        project(x_refs, mod_ref, step, w_ref, normed_ref, [kr_ref, vr_ref])

    ext_ref[0], ext_ref[1] = with_ones(vr_ref[0, pair])
    def finish(at, query, first, second, top_first, top_second):
        lane = lane_index(query.shape)
        low = lane < HD
        swapped = jnp.where(low, second, first)
        total = pltpu.roll(swapped, HD, 1)
        o_ref[0, 0, at, :] = jnp.where(low, first, second) / total
        log_total = jnp.log(swapped) + jnp.where(low, top_second, top_first)
        high = log_total.astype(BF16).astype(F32)
        middle = (log_total - high).astype(BF16).astype(F32)
        rest = log_total - high - middle
        spot = lane % HD
        extra = jnp.where(spot == 0, -high, jnp.where(spot == 1, -middle, -rest))
        extra = jnp.where(spot < 3, extra, 0.0).astype(BF16)
        qe_ref[0, 0, 0, at, :] = jnp.where(low, query, extra)
        qe_ref[0, 0, 1, at, :] = jnp.where(low, extra, query)
        return total

    def block(index, carry):
        at = pl.ds(pl.multiple_of(index * rows, rows), rows)
        query = q_ref[0, 0, at, :]
        sums = []
        for head, own in enumerate(masked(query)):
            more = dot(exponentials(own, kr_ref, pair), ext_ref[head])
            sums.append(acc_ref[0, 0, head, at, :] + more)
        total_ref[at, :] = finish(at, query, sums[0], sums[1], 0.0, 0.0)
        return carry

    lax.fori_loop(0, q_ref.shape[2] // rows, block, 0, unroll=True)
    total = total_ref[...]
    bad = jnp.sum(jnp.where((total > 1e-25) & (total < 1e25), 0.0, 1.0))

    @pl.when(bad > 0.0)
    def _():
        own_ext = with_ones(v_ref[0, 0])

        again_rows = min(32, q_ref.shape[2])

        def again(index, carry):
            at = pl.ds(pl.multiple_of(index * again_rows, again_rows), again_rows)
            query = q_ref[0, 0, at, :]
            sums, tops = [], []
            for head, own in enumerate(masked(query)):
                scores = dot(own, k_ref[0, 0], NT)
                others = dot(own, kr_ref[0, pair], NT)
                top = jnp.maximum(
                    jnp.max(scores, axis=-1, keepdims=True),
                    jnp.max(others, axis=-1, keepdims=True),
                )
                sums.append(
                    dot(jnp.exp(scores - top).astype(BF16), own_ext[head])
                    + dot(jnp.exp(others - top).astype(BF16), ext_ref[head])
                )
                tops.append(top)
            finish(at, query, sums[0], sums[1], tops[0], tops[1])
            return carry

        lax.fori_loop(0, q_ref.shape[2] // again_rows, again, 0)


def gelu_parts(values):
    cumulative = 0.5 * lax.erf(values * 0.7071067811865476) + 0.5
    bell = jnp.exp2(values * values * (-0.5 * LOG2E))
    return values * cumulative, cumulative + values * bell * 0.3989422804014327


def patch_kernel(
    rows,
    chunk,
    counts_ref,
    lead_ref,
    own_x,
    sib_x,
    own_ct,
    sib_ct,
    mod_ref,
    o_ref,
    out_w,
    fc1_w,
    fc2_w,
    final_own,
    final_sib,
    gm_ref,
    ge_ref,
    sums_ref,
    stack_one,
    stack_two,
    hidden_s,
    gpre_s,
    n2_s,
    g2_s,
    g1_s,
    mixed_s,
    gout_s,
    gfc1_s,
    gfc2_s,
    sums_s,
):
    step, half = pl.program_id(0), pl.program_id(1)
    width, hidden_width = fc1_w.shape
    patches = own_x.shape[1]
    slot = first_step(pl.num_programs(0)) + step
    active = (slot < counts_ref[0]).astype(F32)

    def piece(index):
        return mod_ref[pl.ds(step, 1), index * width : (index + 1) * width]

    gate1, shift2, scale2, gate2 = piece(2), piece(3), piece(4), piece(5)

    @pl.when((step == 0) & (half == 0))
    def _():
        sums_s[...] = jnp.zeros_like(sums_s)
        gout_s[...] = jnp.zeros_like(gout_s)
        gfc1_s[...] = jnp.zeros_like(gfc1_s)
        gfc2_s[...] = jnp.zeros_like(gfc2_s)

    def block(index, carry):
        at = pl.ds(pl.multiple_of(index * rows, rows), rows)
        x = jnp.where(half == 0, own_x[0, at, :], sib_x[0, at, :]).astype(F32)
        final_grad = jnp.where(half == 0, own_ct[0, at, :], sib_ct[0, at, :]).astype(F32) * active
        outs = [o_ref[0, pair, at, :] for pair in range(width // LANES)]
        mixed = jnp.concatenate([o.astype(BF16) for o in outs], axis=-1)
        mixed_s[at, :] = mixed
        branch_one = dot(mixed, out_w[...])
        middle = x + gate1 * branch_one
        xhat, inverse = normalize(middle)
        n2 = (xhat * (1.0 + scale2) + shift2).astype(BF16)
        n2_s[at, :] = n2
        g2 = (gate2 * final_grad).astype(BF16)
        g2_s[at, :] = g2
        branch_two = jnp.zeros((rows, width), F32)
        gy = jnp.zeros((rows, width), F32)
        for start in range(0, hidden_width, chunk):
            columns = slice(start, start + chunk)
            pre = dot(n2, fc1_w[:, columns])
            grad_hidden = dot(g2, fc2_w[columns, :], NT)
            hidden, slope = gelu_parts(pre)
            hidden = hidden.astype(BF16)
            grad_pre = (slope * grad_hidden).astype(BF16)
            hidden_s[at, columns] = hidden
            gpre_s[at, columns] = grad_pre
            branch_two += dot(hidden, fc2_w[columns, :])
            gy += dot(grad_pre, fc1_w[:, columns], NT)
        final = ((middle + gate2 * branch_two) * active).astype(BF16)

        @pl.when(half == 0)
        def _():
            final_own[0, at, :] = final

        @pl.when(half == 1)
        def _():
            final_sib[0, at, :] = final

        gm = final_grad + norm_back(gy * (1.0 + scale2), xhat, inverse)
        gm_ref[0, 0, at, :] = gm
        g1 = (gate1 * gm).astype(BF16)
        g1_s[at, :] = g1
        sums = [branch_one * gm, gy, gy * xhat, branch_two * final_grad]
        for row, value in enumerate(sums):
            place = pl.ds(2 * row + step, 1)
            sums_s[place, :] += jnp.sum(value, axis=0, keepdims=True)
        grad_mixed = dot(g1, out_w[...], NT).astype(BF16)
        lane = lane_index((rows, LANES))
        low = lane < HD
        spot = lane % HD
        for pair, o in enumerate(outs):
            grad = grad_mixed[:, pair * LANES : (pair + 1) * LANES]
            product = grad.astype(F32) * o
            first = jnp.sum(jnp.where(low, product, 0.0), axis=-1, keepdims=True)
            second = jnp.sum(jnp.where(low, 0.0, product), axis=-1, keepdims=True)
            inner = jnp.where(low, second, first)
            high = inner.astype(BF16).astype(F32)
            mid = (inner - high).astype(BF16).astype(F32)
            extra = jnp.where(spot == 0, -high, jnp.where(spot == 1, -mid, high + mid - inner))
            extra = jnp.where(spot < 3, extra, 0.0).astype(BF16)
            ge_ref[0, pair, 0, at, :] = jnp.where(low, grad, extra)
            ge_ref[0, pair, 1, at, :] = jnp.where(low, extra, grad)
        return carry

    lax.fori_loop(0, patches // rows, block, 0)
    gout_s[...] += dot(mixed_s[...], g1_s[...], TN)
    gfc1_s[...] += dot(n2_s[...], gpre_s[...], TN)
    gfc2_s[...] += dot(g2_s[...], hidden_s[...], TN)

    @pl.when((step == pl.num_programs(0) - 1) & (half == pl.num_programs(1) - 1))
    def _():
        for index in range(2):
            lead = lead_ref[0, first_step(2) + index]
            sums_s[12 + index : 13 + index, :] = jnp.where(lane_index((1, width)) == lead, 1.0, 0.0)
        sums_ref[...] = sums_s[...].astype(BF16)
        blocks = hidden_width // width
        for index in range(blocks):
            columns = slice(index * width, (index + 1) * width)
            stack_one[index] = gfc1_s[:, columns].astype(BF16)
            stack_two[index] = gfc2_s[:, columns].T.astype(BF16)
        stack_two[blocks] = gout_s[...].astype(BF16)


def attend_back_kernel(rows, first_pass, exchanges, grid_steps, *refs):
    count = len(exchanges)
    qe_ref, ge_ref, k_ref, v_ref = refs[:4]
    refs = refs[4:]
    if first_pass:
        gives, sums_ref, refs = refs[:count], refs[count], refs[count + 1 :]
        dq_ref, dk_ref, dv_ref = refs[:3]
        shards, all_ref, refs = refs[3 : 3 + count], refs[3 + count], refs[4 + count :]
        all_s, all_sends, all_recvs = refs[-3:]
    else:
        dq_in, shards, refs = refs[0], refs[1 : 1 + count], refs[1 + count :]
        dq_ref, dk_ref, dv_ref = refs[:3]
        fulls, refs = refs[3 : 3 + count], refs[3 + count :]
    dq_s, refs = refs[0], refs[1:]
    states = []
    for index, exchange in enumerate(exchanges):
        sends, recvs = refs[1], refs[2]
        if first_pass:
            got = refs[3 : 3 + exchange.all_levels]
            states.append((gives[index], refs[0], got, sends, recvs))
            refs = refs[3 + exchange.all_levels :]
        else:
            states.append((refs[0], sends, recvs))
            refs = refs[3:]
    per_step = k_ref.shape[2] // rows
    static_slots = grid_steps * per_step
    first_slot = (pl.program_id(0) * pl.num_programs(1) + pl.program_id(1)) * per_step
    levels = exchanges[0].all_levels if first_pass else exchanges[0].levels

    def all_copy(level):
        index = 0
        for lower in range(len(exchanges[0].bits)):
            index = index + exchanges[0].place(lower)[0] * (1 << lower)
        if level < 0:
            return all_s.at[pl.ds(index, 1)]
        size = 1 << level
        piece = all_s.at[pl.ds((index // size) * size, size)]
        return exchanges[0].copy(piece, piece, all_sends, all_recvs, level)

    def reduce_action(order):
        if order == 0:
            exchanges[0].barrier()
            own = all_copy(-1)
            own[...] = sums_ref[...][None]
        else:
            all_copy(order - 1).wait()
        if order < levels:
            all_copy(order).start()
        else:
            all_ref[...] = all_s[...]
        for exchange, state, shard in zip(exchanges, states, shards):
            if order > 0:
                exchange.reduce_finish(order - 1, *state)
            if order < levels:
                exchange.reduce_start(order, *state)
            else:
                shard[...] = exchange.own_shard(state[1], 1)[...][0]

    def gather_action(order):
        if order == 0:
            exchanges[0].barrier()
        for exchange, state, shard in zip(exchanges, states, shards):
            if order == 0:
                exchange.own_shard(state[0], 0)[...] = shard[...][None]
            else:
                exchange.gather_finish(levels - order, *state)
            if order < levels:
                exchange.gather_start(levels - 1 - order, *state)
        if order == levels:
            copies = [
                pltpu.make_async_copy(state[0], full, refs[index])
                for index, (state, full) in enumerate(zip(states, fulls))
            ]
            for copy in copies:
                copy.start()
            for copy in copies:
                copy.wait()

    action = reduce_action if first_pass else gather_action
    weights = [5.0, 10.0, 9.0, 6.0] + [4.0] * levels
    weights = weights[:levels] if first_pass else weights[:levels][::-1]
    marks, total = [0], 0.0
    for weight in weights:
        total += weight
        marks.append(total)
    last = static_slots - (2 if first_pass else 1)
    marks = [min(int(mark * last / total + 0.5), last) for mark in marks]

    dq_s[...] = jnp.zeros_like(dq_s) if first_pass else dq_in[0, 0].T

    def block(index, carry):
        for order, mark in enumerate(marks[:-1]):
            pl.when(first_slot + index == mark)(functools.partial(action, order))
        at = pl.ds(pl.multiple_of(index * rows, rows), rows)
        keys = k_ref[0, 0, at, :]
        values = v_ref[0, 0, at, :]
        lane = lane_index(keys.shape)
        low = lane < HD
        ones = jnp.where(lane % HD < 3, 1.0, 0.0).astype(BF16)
        zero = jnp.zeros_like(keys)
        grads = []
        for head in range(2):
            own = low if head == 0 else jnp.logical_not(low)
            query = qe_ref[0, 0, head]
            grad = ge_ref[0, 0, head]
            probs = jnp.exp(dot(jnp.where(own, keys, ones), query, NT))
            grad_probs = dot(jnp.where(own, values, ones), grad, NT)
            grad_scores = (probs * grad_probs).astype(BF16)
            grads.append((dot(grad_scores, query), dot(probs.astype(BF16), grad)))
            dq_s[...] += dot(jnp.where(own, keys, zero), grad_scores, TN)
        dk_ref[0, 0, at, :] = jnp.where(low, grads[0][0], grads[1][0]).astype(BF16)
        dv_ref[0, 0, at, :] = jnp.where(low, grads[0][1], grads[1][1]).astype(BF16)
        return carry

    lax.fori_loop(0, per_step, block, 0)
    if first_pass:
        dq_ref[0, 0] = dq_s[...].T
    else:
        dq_ref[0, 0] = (dq_s[...].T * HD**-0.5).astype(BF16)
    pl.when(first_slot + per_step == static_slots)(functools.partial(action, levels))


def joining(at, read, write, wait, own_ref, got_ref, out_ref, own_s, got_s, sems):
    mine = first_step(2)
    reads = [
        pltpu.make_async_copy(own_ref, own_s, sems.at[0]),
        pltpu.make_async_copy(got_ref, got_s, sems.at[1]),
    ]
    writes = [
        pltpu.make_async_copy(own_s, out_ref.at[pl.ds(mine, 2)], sems.at[2]),
        pltpu.make_async_copy(got_s, out_ref.at[pl.ds(2 - mine, 2)], sems.at[3]),
    ]

    @pl.when(at == read)
    def _():
        for copy in reads:
            copy.start()

    @pl.when(at == write)
    def _():
        for copy in reads:
            copy.wait()
        for copy in writes:
            copy.start()

    @pl.when(at == wait)
    def _():
        for copy in writes:
            copy.wait()


def project_back_far_kernel(
    dk_ref, dv_ref, normed_ref, w_ref, own_ref, got_ref, dx_ref, gw_ref, out_ref, own_s, got_s, sems
):
    width = w_ref.shape[0]
    at = pl.program_id(0) * pl.num_programs(1) + pl.program_id(1)
    joining(at, 0, 1, 3, own_ref, got_ref, out_ref, own_s, got_s, sems)
    joined = join_heads(dk_ref, dv_ref)
    dx_ref[0, 0] = dot(joined, w_ref[:, width:], NT).astype(BF16)

    @pl.when((pl.program_id(0) == 0) & (pl.program_id(1) == 0))
    def _():
        gw_ref[...] = jnp.zeros_like(gw_ref)

    gw_ref[...] += dot(normed_ref[0, 0], joined, TN)


def weight_back_kernel(early, *refs):
    dq_ref, dk_ref, dv_ref, normed_ref, far_ref, one_ref, two_ref = refs[:7]
    gw_ref, gfc1_ref, gfc2_ref, gout_ref = refs[7:11]
    gw_s, one_s, two_s, gfc1_s, gfc2_s, gout_s, sems = refs[11:]
    at = pl.program_id(0) * pl.num_programs(1) + pl.program_id(1)
    size = gout_s.shape[0]
    blocks = gfc1_s.shape[1] // size
    reads = [
        pltpu.make_async_copy(one_ref, one_s, sems.at[0]),
        pltpu.make_async_copy(two_ref, two_s, sems.at[1]),
    ]
    writes = [
        pltpu.make_async_copy(gfc1_s, gfc1_ref, sems.at[2]),
        pltpu.make_async_copy(gfc2_s, gfc2_ref, sems.at[3]),
        pltpu.make_async_copy(gout_s, gout_ref, sems.at[4]),
    ]

    @pl.when(at == 0)
    def _():
        for copy in reads:
            copy.start()

    @pl.when(at == 1)
    def _():
        reads[0].wait()
        unstack(
            grouped(early[0]), one_s, [(gfc1_s, 0, block * size) for block in range(blocks)], size
        )
        writes[0].start()

    @pl.when(at == 2)
    def _():
        reads[1].wait()
        rest = [(gfc2_s, block * size, 0) for block in range(blocks)] + [(gout_s, 0, 0)]
        unstack(grouped(early[1]), two_s, rest, size)
        writes[1].start()
        writes[2].start()

    @pl.when(at == pl.num_programs(0) * pl.num_programs(1) - 1)
    def _():
        for copy in writes:
            copy.wait()

    step, which = pl.program_id(0), pl.program_id(1)
    width = normed_ref.shape[3]

    @pl.when((step == 0) & (which == 0))
    def _():
        gw_s[:, :width] = jnp.zeros_like(gw_s[:, :width])
        gw_s[:, width:] = far_ref[...]

    gw_s[...] += dot(normed_ref[0, 0], join_heads(dq_ref, dk_ref, dv_ref), TN)

    @pl.when((step == pl.num_programs(0) - 1) & (which == pl.num_programs(1) - 1))
    def _():
        for block in range(gw_ref.shape[0]):
            gw_ref[block] = gw_s[:, block * LANES : (block + 1) * LANES].astype(BF16)


def join_heads(*grads):
    return jnp.concatenate([ref[0, pair] for ref in grads for pair in range(ref.shape[1])], axis=-1)


class Direct:
    def __init__(self, mesh_shape, row_tiles):
        self.chips = mesh_shape["seq"] // 2
        self.peers = mesh_shape["dp"] * self.chips
        self.half = row_tiles * 8
        self.piece = -(-row_tiles // (2 * self.peers)) * 16
        self.padded = self.piece * self.peers

    def me(self):
        return lax.axis_index("dp") * self.chips + lax.axis_index("seq") // 2

    def core(self):
        return lax.axis_index("seq") % 2

    def sibling(self):
        return {"seq": lax.axis_index("seq") + 1 - 2 * self.core()}

    def peer(self, shift):
        other = (self.me() + shift) % self.peers
        device = {"dp": other // self.chips, "seq": (other % self.chips) * 2 + self.core()}
        return other, device

    def rows(self, index):
        return pl.ds(pl.multiple_of(index * self.piece, 16), self.piece)

    def barrier(self):
        semaphore = pltpu.get_barrier_semaphore()

        def signal(device):
            pl.semaphore_signal(semaphore, 1, device_id=device, device_id_type=pl.DeviceIdType.MESH)

        signal(self.sibling())

        def greet(shift, carry):
            signal(self.peer(shift)[1])
            return carry

        lax.fori_loop(1, self.peers, greet, 0)
        pl.semaphore_wait(semaphore, self.peers)

    def copy(self, source, target, send, recv, device):
        return pltpu.make_async_remote_copy(
            src_ref=source,
            dst_ref=target,
            send_sem=send,
            recv_sem=recv,
            device_id=device,
            device_id_type=pl.DeviceIdType.MESH,
        )

    def each_peer(self, do):
        def one(shift, carry):
            do(shift)
            return carry

        lax.fori_loop(1, self.peers, one, 0)


def spread_leads(grads, step_of, table_rows):
    count = grads.shape[0]
    part = min(count, 512)
    row = lax.broadcasted_iota(jnp.int32, (part, part), 0)
    column = lane_index((part, part))
    chosen = (row // 16 == column // 16) & (row % 16 == 12 + step_of(column % 16))
    spread = jnp.where(chosen, 1.0, 0.0).astype(BF16)
    leads = [
        dot(grads[start : start + part, :LANES], spread, TN)[:table_rows]
        for start in range(0, count, part)
    ]
    return jnp.concatenate(leads, axis=-1)


def lead_grads(emb_ref, ada_ref, grads, leads, place, columns, gada_ref, gbada_ref, target):
    table = emb_ref[...].astype(F32)
    table_act = (table * jax.nn.sigmoid(table)).astype(BF16)
    chosen = jnp.where(place, leads, 0.0).astype(BF16)
    acts = dot(table_act, chosen, TN).astype(BF16)
    gada_ref[:, target] = dot(acts, grads)
    by_lead = dot(chosen, grads)
    gbada_ref[:, target] = jnp.sum(by_lead, axis=0, keepdims=True)
    high = by_lead.astype(BF16)
    low = (by_lead - high.astype(F32)).astype(BF16)
    return dot(high, ada_ref[:, columns], NT) + dot(low, ada_ref[:, columns], NT)


def tail_kernel(direct, remote, *refs):
    give_ref, own_x, sib_x, mod_ref, lead_ref, gm_ref, dq_ref, dk_ref, dv_ref, w_ref = refs[:10]
    others = refs[10 : 10 + remote]
    early_sums, emb_ref, ada_ref = refs[10 + remote : 13 + remote]
    grad_ref, got_ref, full_ref, all_ref = refs[13 + remote : 17 + remote]
    gada_ref, gbada_ref, gemb_ref = refs[17 + remote : 20 + remote]
    refs = refs[20 + remote :]
    sums_s, other_s, got_s, sum_s, core_s, pieces_s, full_s, all_s = refs[:8]
    core_sems, piece_sems, back_sems, all_sems, grad_sems, local_sem = refs[8:]
    step, half = pl.program_id(0), pl.program_id(1)
    width = own_x.shape[2]
    core, me = direct.core(), direct.me()

    core_copy = direct.copy(
        give_ref.at[1 - core], core_s, core_sems.at[0], core_sems.at[1], direct.sibling()
    )

    def piece_copy(shift):
        other, device = direct.peer(shift)
        return direct.copy(
            sum_s.at[direct.rows(other)],
            pieces_s.at[shift],
            piece_sems.at[0, shift],
            piece_sems.at[1, shift],
            device,
        )

    def full_copy(shift, arriving):
        _, device = direct.peer(shift)
        owner = (me + direct.peers - shift) % direct.peers if arriving else me
        place = full_s.at[core, direct.rows(owner)]
        return direct.copy(place, place, back_sems.at[0, shift], back_sems.at[1, shift], device)

    def sums_copy(shift, arriving):
        _, device = direct.peer(shift)
        owner = (me + direct.peers - shift) % direct.peers if arriving else me
        place = all_s.at[core, owner]
        return direct.copy(place, place, all_sems.at[0, shift], all_sems.at[1, shift], device)

    def side_copy(values, which, side):
        place = values.at[side]
        return direct.copy(
            place, place, core_sems.at[which], core_sems.at[which + 1], direct.sibling()
        )

    def grad_copy(index):
        return direct.copy(
            other_s.at[index],
            got_s.at[index],
            grad_sems.at[0, index],
            grad_sems.at[1, index],
            direct.sibling(),
        )

    @pl.when((step == 0) & (half == 0))
    def _():
        direct.barrier()
        core_copy.start()
        sums_s[...] = jnp.zeros_like(sums_s)

    @pl.when((step == 0) & (half == 1))
    def _():
        core_copy.wait()
        real = core_s.shape[0]
        sum_s[:real] = (give_ref[core].astype(F32) + core_s[...].astype(F32)).astype(BF16)
        if direct.padded > real:
            sum_s[real:] = jnp.zeros_like(sum_s[real:])
        direct.each_peer(lambda shift: piece_copy(shift).start())

    x = jnp.where(half == 0, own_x[0], sib_x[0]).astype(F32)
    scale = mod_ref[pl.ds(step, 1), width : 2 * width]
    xhat, inverse = normalize(x)
    gy = dot(join_heads(dq_ref, dk_ref, dv_ref), w_ref[...], NT)
    for other in others:
        gy = gy + other[0, 0].astype(F32)
    grad = (gm_ref[0, 0] + norm_back(gy * (1.0 + scale), xhat, inverse)).astype(BF16)

    @pl.when(half == 0)
    def _():
        grad_ref[0] = grad

    @pl.when(half == 1)
    def _():
        other_s[step] = grad
        grad_copy(step).start()

    for kind, value in enumerate((gy, gy * xhat)):
        total = jnp.sum(value, axis=0, keepdims=True)
        for index in range(width // LANES):
            place = pl.ds((kind * 2 + step) * (width // LANES) + index, 1)
            sums_s[place, :] += total[:, index * LANES : (index + 1) * LANES]

    @pl.when((step == 1) & (half == 1))
    def _():
        for index in range(2):
            chosen = lane_index((1, LANES)) == lead_ref[0, first_step(2) + index]
            sums_s[12 + index : 13 + index, :] = jnp.where(chosen, 1.0, 0.0)
        all_s[core, me] = sums_s[...].astype(BF16)
        direct.each_peer(lambda shift: sums_copy(shift, False).start())
        direct.each_peer(lambda shift: piece_copy(shift).wait())

        def add(shift, total):
            return total + pieces_s[shift].astype(F32)

        total = lax.fori_loop(1, direct.peers, add, sum_s[direct.rows(me)].astype(F32))
        full_s[core, direct.rows(me)] = total.astype(BF16)
        direct.each_peer(lambda shift: full_copy(shift, False).start())
        grads = early_sums[...]
        leads = spread_leads(grads, lambda row: row % 2, emb_ref.shape[0])
        row = lane_index((1, grads.shape[0])) % 16
        part = jnp.zeros(gemb_ref.shape, F32)
        for index in range(4):
            columns = slice((2 + index) * width, (3 + index) * width)
            target = slice(index * width, (index + 1) * width)
            place = row // 2 == index
            part += lead_grads(
                emb_ref, ada_ref, grads, leads, place, columns, gada_ref, gbada_ref, target
            )
        gemb_ref[...] = part

        def arrived(shift):
            full_copy(shift, False).wait_send()
            full_copy(shift, True).wait_recv()
            sums_copy(shift, False).wait_send()
            sums_copy(shift, True).wait_recv()

        direct.each_peer(arrived)
        side_copy(full_s, 2, core).start()
        side_copy(all_s, 4, core).start()
        for index in range(2):
            grad_copy(index).wait()
        side_copy(full_s, 2, core).wait_send()
        side_copy(full_s, 2, 1 - core).wait_recv()
        side_copy(all_s, 4, core).wait_send()
        side_copy(all_s, 4, 1 - core).wait_recv()
        outs = [(got_s, got_ref), (full_s, full_ref), (all_s, all_ref)]
        copies = [
            pltpu.make_async_copy(source, target, local_sem.at[index])
            for index, (source, target) in enumerate(outs)
        ]
        for copy in copies:
            copy.start()
        for copy in copies:
            copy.wait()


def unstack(at, full_ref, targets, rows):
    row, end = 0, rows * len(targets)
    while row < end:
        group, inside, left = at(row)
        block, place = divmod(row, rows)
        count = min(left, rows - place)
        target, first_row, first_column = targets[block]
        columns = slice(first_column, first_column + full_ref.shape[2])
        value = full_ref[group, inside : inside + count, :].astype(F32)
        target[first_row + place : first_row + place + count, columns] = value
        row += count


def grouped(exchange):
    def at(row):
        group, inside = divmod(row, exchange.real)
        return group, inside, exchange.real - inside

    return at


def final_kernel(direct, *refs):
    late_sums, emb_ref, ada_ref, gada_part, gbada_part, gemb_part = refs[:6]
    late_ref, own_ref, got_ref = refs[6:9]
    grad_out, gemb_ref, gada_out, gbada_ref, gqkv_out = refs[9:14]
    gada_s, gbada_s, gqkv_s, late_s, own_s, got_s, sems = refs[14:]
    size = emb_ref.shape[1]
    mine = first_step(2)
    pairs = [(late_ref, late_s), (own_ref, own_s), (got_ref, got_s)]
    reads = [
        pltpu.make_async_copy(source, target, sems.at[index])
        for index, (source, target) in enumerate(pairs)
    ]
    for read in reads:
        read.start()
    copies = []

    def start(source, target):
        copy = pltpu.make_async_copy(source, target, sems.at[3 + len(copies)])
        copy.start()
        copies.append(copy)

    def halved(row):
        group, inside = divmod(row, direct.half)
        return group, inside, direct.half - inside

    start(gada_part, gada_out.at[:, pl.ds(2 * size, 4 * size)])
    columns = gqkv_s.shape[1] // LANES
    reads[0].wait()
    unstack(halved, late_s, [(gqkv_s, 0, block * LANES) for block in range(columns)], size)
    start(gqkv_s, gqkv_out)
    reads[1].wait()
    start(own_s, grad_out.at[pl.ds(mine, 2)])
    reads[2].wait()
    start(got_s, grad_out.at[pl.ds(2 - mine, 2)])

    table_rows = emb_ref.shape[0]
    table = emb_ref[...].astype(F32)
    gate = jax.nn.sigmoid(table)
    slope = gate * (1.0 + table * (1.0 - gate))
    total = gemb_part[...]
    grads = late_sums[...]
    parts = size // LANES
    leads = spread_leads(grads, lambda row: (row // parts) % 2, table_rows)
    row = lane_index((1, grads.shape[0])) % 16
    for index in range(2):
        for part in range(parts):
            place = (row // (2 * parts) == index) & (row % parts == part)
            columns = slice(index * size + part * LANES, index * size + (part + 1) * LANES)
            total += lead_grads(
                emb_ref, ada_ref, grads, leads, place, columns, gada_s, gbada_s, columns
            )
    gemb_ref[...] = total * slope
    start(gada_s, gada_out.at[:, pl.ds(0, 2 * size)])
    gbada_ref[: 2 * size] = gbada_s[0]
    gbada_ref[2 * size :] = gbada_part[0]
    for copy in copies:
        copy.wait()


def local(
    mesh_shape, inputs, cotangent, counts, lead_steps, emb_table, w_ada, b_ada, w_qkv, w_out, w_fc1, w_fc2
):
    slots, items, patches, width = inputs.shape
    chips = mesh_shape["seq"] // 2
    blocks = w_fc1.shape[1] // w_fc1.shape[0]
    steps = slots * items // 2
    hidden_width = w_fc1.shape[1]
    pairs = width // LANES
    rows = 2 * patches
    remote = 2 * (chips - 1)
    far_rows = remote * patches
    spot = lax.axis_index("seq")
    core = lax.rem(spot, 2)
    devices = 2 * chips

    def send(values, shift, cross):
        pairs_list = []
        for source in range(devices):
            chip, side = source // 2, source % 2
            pairs_list.append((source, ((chip + shift) % chips) * 2 + (1 - side if cross else side)))
        return lax.ppermute(values, "seq", pairs_list)

    x_steps = inputs.reshape(2, steps, patches, width)
    ct_steps = cotangent.reshape(2, steps, patches, width)
    own_x = lax.dynamic_index_in_dim(x_steps, core, 0, keepdims=False)
    other_x = lax.dynamic_index_in_dim(x_steps, 1 - core, 0, keepdims=False)
    own_ct = lax.dynamic_index_in_dim(ct_steps, core, 0, keepdims=False)
    other_ct = lax.dynamic_index_in_dim(ct_steps, 1 - core, 0, keepdims=False)
    sib_x = send(other_x, 0, True)
    far_x = []
    for step in range(steps):
        some = slice(step, step + 1)
        for shift in range(1, chips):
            far_x.append(send(own_x[some], shift, False))
            far_x.append(send(other_x[some], shift, True))
    sib_ct = send(other_ct, 0, True)

    step_block = pl.BlockSpec((1, patches, width), lambda j, i: (j, 0, 0))
    patch_block = pl.BlockSpec((1, 1, patches, width), lambda j, i: (j, i, 0, 0))

    def head_rows(count):
        return pl.BlockSpec((1, 1, count, LANES), lambda j, p: (j, p, 0, 0))

    def of_step(*shape):
        return pl.BlockSpec((1,) + shape, lambda j, p: (j,) + (0,) * len(shape))

    both_heads = pl.BlockSpec((1, 1, 2, rows, LANES), lambda j, p: (j, p, 0, 0, 0))
    piece = min(256, rows)
    near_work = 4 * steps * pairs * 2 * rows * LANES * rows
    near_heads = jax.ShapeDtypeStruct((steps, pairs, rows, LANES), BF16)
    mod, n1, q, k, v, acc = call(
        functools.partial(near_kernel, piece),
        "near",
        (steps, pairs),
        [scalars(), whole(emb_table.shape), whole(w_ada.shape), whole((1, 6 * width))]
        + [step_block] * 2
        + [whole(w_qkv.shape)],
        [whole((16, 6 * width)), of_step(rows, width)]
        + [of_step(pairs, rows, LANES)] * 3
        + [both_heads],
        [
            jax.ShapeDtypeStruct((16, 6 * width), F32),
            jax.ShapeDtypeStruct((steps, rows, width), BF16),
            near_heads,
            near_heads,
            near_heads,
            jax.ShapeDtypeStruct((steps, pairs, 2, rows, LANES), F32),
        ],
        [pltpu.VMEM((2, rows, LANES), BF16)],
        flops=near_work + 6 * steps * rows * width * width,
        exps=steps * pairs * 2 * rows * rows,
    )(lead_steps, emb_table, w_ada, b_ada.reshape(1, -1), own_x, sib_x, w_qkv)

    def far(step, before):
        some_x = far_x[step * remote : (step + 1) * remote]

        def at_step(*shape):
            return pl.BlockSpec((1,) + shape, lambda p: (step,) + (0,) * len(shape))

        def at_pair(*shape):
            return pl.BlockSpec((1, 1) + shape, lambda p: (step, p) + (0,) * len(shape))

        operands = [*some_x, mod, w_qkv, q, k, v, acc]
        return call(
            functools.partial(far_kernel, piece, step, remote),
            "far",
            (pairs,),
            [whole((1, patches, width))] * remote
            + [whole(mod.shape), whole(w_qkv.shape)]
            + [at_pair(rows, LANES)] * 3
            + [at_pair(2, rows, LANES)]
            + [pl.BlockSpec(memory_space=pl.ANY)] * len(before),
            [at_step(far_rows, width)]
            + [at_step(pairs, far_rows, LANES)] * 2
            + [at_pair(rows, LANES), at_pair(2, rows, LANES)],
            [
                jax.ShapeDtypeStruct((steps, far_rows, width), BF16),
                jax.ShapeDtypeStruct((steps, pairs, far_rows, LANES), BF16),
                jax.ShapeDtypeStruct((steps, pairs, far_rows, LANES), BF16),
                jax.ShapeDtypeStruct((steps, pairs, rows, LANES), F32),
                jax.ShapeDtypeStruct((steps, pairs, 2, rows, LANES), BF16),
            ],
            [pltpu.VMEM((2, far_rows, LANES), BF16), pltpu.VMEM((rows, LANES), F32)],
            flops=near_work // 2,
            exps=pairs * 2 * rows * far_rows,
            aliases={len(operands) + index: index for index in range(len(before))},
        )(*operands, *before)

    far_results = []
    for step in range(steps):
        far_results = far(step, far_results)
    n1r, kr, vr, o, qe = far_results

    block_rows = min(256, patches)
    outs = call(
        functools.partial(patch_kernel, block_rows, hidden_width),
        "patchwise",
        (steps, 2),
        [scalars()] * 2
        + [step_block] * 4
        + [
            whole(mod.shape),
            pl.BlockSpec((1, pairs, patches, LANES), lambda j, i: (j, 0, i, 0)),
            whole(w_out.shape),
            whole(w_fc1.shape),
            whole(w_fc2.shape),
        ],
        [
            step_block,
            step_block,
            patch_block,
            pl.BlockSpec((1, pairs, 2, patches, LANES), lambda j, i: (j, 0, 0, i, 0)),
            whole((16, width)),
            whole((blocks, width, width)),
            whole((blocks + 1, width, width)),
        ],
        [
            jax.ShapeDtypeStruct((steps, patches, width), BF16),
            jax.ShapeDtypeStruct((steps, patches, width), BF16),
            jax.ShapeDtypeStruct((steps, 2, patches, width), F32),
            jax.ShapeDtypeStruct((steps, pairs, 2, rows, LANES), BF16),
            jax.ShapeDtypeStruct((16, width), BF16),
            jax.ShapeDtypeStruct((blocks, width, width), BF16),
            jax.ShapeDtypeStruct((blocks + 1, width, width), BF16),
        ],
        [pltpu.VMEM((patches, hidden_width), BF16)] * 2
        + [pltpu.VMEM((patches, width), BF16)] * 4
        + [
            pltpu.VMEM((width, width), F32),
            pltpu.VMEM((width, hidden_width), F32),
            pltpu.VMEM((width, hidden_width), F32),
            pltpu.VMEM((16, width), F32),
        ],
        flops=6 * steps * rows * width * (2 * hidden_width + width),
        moved=steps * rows * width * 20,
        exps=2 * steps * rows * hidden_width,
    )(counts, lead_steps, own_x, sib_x, own_ct, sib_ct, mod, o, w_out, w_fc1, w_fc2)
    final_own, final_sib, gm, ge, sums, stack_one, stack_two = outs
    final_got = send(final_sib, 0, True)
    early = [Exchange(mesh_shape, blocks * width // 16, 0), Exchange(mesh_shape, (blocks + 1) * width // 16, 1)]
    gives = [g.reshape(e.groups, e.real, width) for e, g in zip(early, (stack_one, stack_two))]

    def attend_back(keys, values, extra, first, name):
        count = keys.shape[2]
        in_specs = [both_heads] * 2 + [head_rows(count)] * 2
        out_specs = [head_rows(rows), head_rows(count), head_rows(count)]
        out_shape = [
            jax.ShapeDtypeStruct((steps, pairs, rows, LANES), F32 if first else BF16),
            jax.ShapeDtypeStruct((steps, pairs, count, LANES), BF16),
            jax.ShapeDtypeStruct((steps, pairs, count, LANES), BF16),
        ]
        scratch = [pltpu.VMEM((LANES, rows), F32)]
        if not first:
            in_specs += [head_rows(rows)]
        for exchange in early:
            shape = (exchange.groups, exchange.padded, width)
            shard = (exchange.shard, width)
            sems = [pltpu.SemaphoreType.DMA((exchange.all_levels,))] * 2
            if first:
                in_specs += [whole((exchange.groups, exchange.real, width))]
                out_specs += [whole(shard)]
                out_shape += [jax.ShapeDtypeStruct(shard, BF16)]
                half = (exchange.groups // 2, exchange.padded, width)
                scratch += [pltpu.VMEM(half, BF16)] + sems + exchange.receive_scratch(width)
            else:
                in_specs += [whole(shard)]
                out_specs += [pl.BlockSpec(memory_space=pl.ANY)]
                out_shape += [jax.ShapeDtypeStruct(shape, BF16)]
                scratch += [pltpu.VMEM(shape, BF16)] + sems
        if first:
            every = (mesh_shape["dp"] * mesh_shape["seq"], 16, width)
            in_specs += [whole(sums.shape)]
            out_specs += [whole(every)]
            out_shape += [jax.ShapeDtypeStruct(every, BF16)]
            sems = [pltpu.SemaphoreType.DMA((early[0].all_levels,))] * 2
            scratch += [pltpu.VMEM(every, BF16)] + sems
        else:
            scratch += [pltpu.SemaphoreType.DMA] * len(early)
        return call(
            functools.partial(attend_back_kernel, min(512, count), first, early, steps * pairs),
            name,
            (steps, pairs),
            in_specs,
            out_specs,
            out_shape,
            scratch,
            flops=10 * steps * pairs * 2 * rows * count * LANES,
            exps=steps * pairs * 2 * rows * count,
            collective=1 if first else 2,
        )(qe, ge, keys, values, *extra)

    grad_block = pl.BlockSpec((1, pairs, patches, LANES), lambda j, i: (j, 0, i, 0))
    hbm = pl.BlockSpec(memory_space=pl.ANY)

    dq_part, dkr, dvr, shard_one, shard_two, early_all = attend_back(
        kr, vr, [*gives, sums], True, "attend_back_far"
    )
    dx_far, gw_part, outputs = call(
        project_back_far_kernel,
        "project_back_far",
        (steps, remote),
        [grad_block] * 2 + [patch_block, whole(w_qkv.shape), hbm, hbm],
        [patch_block, whole((width, 2 * width)), hbm],
        [
            jax.ShapeDtypeStruct((steps, remote, patches, width), BF16),
            jax.ShapeDtypeStruct((width, 2 * width), F32),
            jax.ShapeDtypeStruct((2 * steps, patches, width), BF16),
        ],
        [pltpu.VMEM((steps, patches, width), BF16)] * 2 + [pltpu.SemaphoreType.DMA((4,))],
        flops=4 * steps * far_rows * width * 2 * width,
        moved=steps * far_rows * width * 8,
    )(dkr, dvr, n1r.reshape(steps, remote, patches, width), w_qkv, final_own, final_got)
    dx_got = [send(dx_far[:, 2 * r - 2 : 2 * r], -r, False) for r in range(1, chips)]
    dq, dk, dv, *early_sums = attend_back(
        k, v, [dq_part, shard_one, shard_two], False, "attend_back_near"
    )
    columns = w_qkv.shape[1] // LANES
    early_weights = (w_fc1, w_fc2, w_out)
    give_late, g_fc1, g_fc2, g_out = call(
        functools.partial(weight_back_kernel, early),
        "weight_back",
        (steps, 2),
        [grad_block] * 3 + [patch_block, whole(gw_part.shape), hbm, hbm],
        [whole((columns, width, LANES))] + [hbm] * 3,
        [jax.ShapeDtypeStruct((columns, width, LANES), BF16)]
        + [jax.ShapeDtypeStruct(w.shape, F32) for w in early_weights],
        [pltpu.VMEM((width, columns * LANES), F32)]
        + [pltpu.VMEM(value.shape, BF16) for value in early_sums]
        + [pltpu.VMEM(w.shape, F32) for w in early_weights]
        + [pltpu.SemaphoreType.DMA((5,))],
        flops=2 * steps * rows * width * 3 * width,
        moved=steps * rows * width * 8,
    )(dq, dk, dv, n1.reshape(steps, 2, patches, width), gw_part, *early_sums)

    direct = Direct(mesh_shape, columns * width // 16)
    full_shape = (2, direct.padded, LANES)
    late_all_shape = (2, direct.peers, 16, LANES)
    early_all = early_all.reshape(-1, width)
    grad_own, grad_got, late_sum, late_all, *early_parts = call(
        functools.partial(tail_kernel, direct, len(dx_got)),
        "tail",
        (steps, 2),
        [whole((2, direct.half, LANES)), step_block, step_block, whole(mod.shape), scalars()]
        + [patch_block]
        + [grad_block] * 3
        + [whole(w_qkv.shape)]
        + [patch_block] * len(dx_got)
        + [whole(early_all.shape), whole(emb_table.shape), whole(w_ada.shape)],
        [step_block, hbm, hbm, hbm]
        + [whole((width, 4 * width)), whole((1, 4 * width)), whole(emb_table.shape)],
        [
            jax.ShapeDtypeStruct((steps, patches, width), BF16),
            jax.ShapeDtypeStruct((steps, patches, width), BF16),
            jax.ShapeDtypeStruct(full_shape, BF16),
            jax.ShapeDtypeStruct(late_all_shape, BF16),
            jax.ShapeDtypeStruct((width, 4 * width), F32),
            jax.ShapeDtypeStruct((1, 4 * width), F32),
            jax.ShapeDtypeStruct(emb_table.shape, F32),
        ],
        [
            pltpu.VMEM((16, LANES), F32),
            pltpu.VMEM((steps, patches, width), BF16),
            pltpu.VMEM((steps, patches, width), BF16),
            pltpu.VMEM((direct.padded, LANES), BF16),
            pltpu.VMEM((direct.half, LANES), BF16),
            pltpu.VMEM((direct.peers, direct.piece, LANES), BF16),
            pltpu.VMEM(full_shape, BF16),
            pltpu.VMEM(late_all_shape, BF16),
            pltpu.SemaphoreType.DMA((6,)),
            pltpu.SemaphoreType.DMA((2, direct.peers)),
            pltpu.SemaphoreType.DMA((2, direct.peers)),
            pltpu.SemaphoreType.DMA((2, direct.peers)),
            pltpu.SemaphoreType.DMA((2, steps)),
            pltpu.SemaphoreType.DMA((3,)),
        ],
        flops=2 * steps * rows * width * 3 * width,
        collective=3,
    )(
        give_late.reshape(2, direct.half, LANES),
        own_x,
        sib_x,
        mod,
        lead_steps,
        gm,
        dq,
        dk,
        dv,
        w_qkv,
        *dx_got,
        early_all,
        emb_table,
        w_ada,
    )

    late_all = late_all.reshape(-1, LANES)
    small = [late_all, emb_table, w_ada, *early_parts]
    large = [late_sum, grad_own, grad_got]
    out_shapes = [(slots * items, patches, width), emb_table.shape, w_ada.shape, b_ada.shape, w_qkv.shape]
    grad_inputs, g_emb, g_ada, g_bada, g_qkv = call(
        functools.partial(final_kernel, direct),
        "final",
        (),
        [whole(value.shape) for value in small] + [hbm] * len(large),
        [hbm, whole(emb_table.shape), hbm, whole(b_ada.shape), hbm],
        [
            jax.ShapeDtypeStruct(shape, F32 if index else BF16)
            for index, shape in enumerate(out_shapes)
        ],
        [pltpu.VMEM(shape, F32) for shape in ((width, 2 * width), (1, 2 * width), w_qkv.shape)]
        + [pltpu.VMEM(value.shape, BF16) for value in large]
        + [pltpu.SemaphoreType.DMA((8,))],
        flops=2 * late_all.shape[0] * width * 6 * width,
        moved=6 * w_ada.size,
    )(*small, *large)
    return (
        outputs.reshape(inputs.shape),
        grad_inputs.reshape(inputs.shape),
        g_emb,
        g_ada,
        g_bada,
        g_qkv,
        g_out,
        g_fc1,
        g_fc2,
    )


def solution(mesh):
    tokens = P(None, "dp", "seq", None)
    return jax.shard_map(
        functools.partial(local, dict(mesh.shape)),
        mesh=mesh,
        in_specs=(tokens, tokens, P("dp"), P("dp", None)) + (P(),) * 7,
        out_specs=(tokens, tokens) + (P(),) * 7,
        check_vma=False,
    )
```
